32 devices in a mesh: gx: 4 (over y, x), gy: 2 (over core), col: 4 (over z).
Axes of the slice: x: 2, y: 2, z: 4, core: 2. Of those that a mesh axis runs over, the one named last changes fastest.
Arguments:
- iterate: float32 [3, 32, 16, 16, 512], P(None, None, 'gx', 'gy', 'col'), may hold values from -0.75 to 0.75
- residual: float32 [3, 32, 16, 16, 512], P(None, None, 'gx', 'gy', 'col'), may hold values from -8 to 8
- cell_ids: int32 [16, 16, 512], P('gx', 'gy', 'col'), may hold values from 0 to 15
- materials: float32 [2, 16], replicated, may hold values from 0.2 to 2
- eigen_counts: int32 [32], P(('gx', 'gy', 'col')), may hold values from 8 to 48, as said below
- coarse_rank: int32 [32], P(('gx', 'gy', 'col')), may hold values from 0 to 31, each once
- eigen_basis: float32 [48, 3, 16, 16, 512], P(None, None, 'gx', 'gy', 'col'), may hold values from -0.0546875 to 0.0546875
- coarse_inverse: bfloat16 [1024, 1024], P(('gx', 'col'))
Outputs:
- new_iterate: float32 [3, 32, 16, 16, 512], P(None, None, 'gx', 'gy', 'col')
- new_residual: float32 [3, 32, 16, 16, 512], P(None, None, 'gx', 'gy', 'col')
The draws below stay inside these ranges and needn't reach their ends.
Inputs may be any that keep to these rules, and one draw needn't show every extreme that they name: `eigen_counts`: the counts sum to 1024. `coarse_rank`: each subdomain has one position.
All inputs are finite; a program needn't handle non-finite values.
Results may differ from the reference program's by a relative error of at most 0.0027.
Values may be sent and summed in bfloat16 or wider, within the bound.
No kernel may reach another device: no remote copies, remote signals or barrier semaphores. Data moves between devices by JAX's collectives and lax.ppermute only.
A program may use at most 128 MiB of HBM per device.

```python
import math
import jax
import jax.numpy as jnp
from jax import lax

CX = 4
CY = 8
CZ = 128
NRHS = 32
NMAT = 16
KMAX = 48
KMIN = 8
KMEAN = 32
SWEEPS = 4
NX = 16
NY = 16
NZ = 512
NCOARSE = 1024
N_GX = 4
N_GY = 2
N_COL = 4
DEVICES = 32


def draw_eigen_counts(key, part):
    key = jax.random.fold_in(key, 7)
    groups = NCOARSE // KMEAN // 4
    first_key, second_key, third_key = jax.random.split(key, 3)
    middle = (4 * KMEAN - KMAX - KMIN) // 2
    spread = jax.random.randint(first_key, (groups,), 0, KMAX - KMIN + 1)
    spread = spread.at[0].set(0)
    swing = jax.random.randint(second_key, (groups,), 0, KMAX - middle + 1)
    quads = jnp.stack([KMAX - spread, KMIN + spread, middle + swing, middle - swing], axis=1).reshape(-1)
    order = jax.random.permutation(third_key, groups * 4)
    return quads[order].astype(jnp.int32)


def draw_coarse_inverse(key, part):
    key = jax.random.fold_in(key, 11)
    diag_key, noise_key = jax.random.split(key, 2)
    diag_values = jax.random.uniform(diag_key, (NCOARSE,), jnp.float32, 0.5, 1.5)
    noise = jax.random.normal(noise_key, (NCOARSE, NCOARSE), jnp.float32) * (0.6 / math.sqrt(NCOARSE))
    rows = lax_rows = jnp.arange(NCOARSE, dtype=jnp.int32)
    on_diag = rows[:, None] == lax_rows[None, :]
    return (noise + jnp.where(on_diag, diag_values[:, None], 0.0)).astype(jnp.bfloat16)


def touch_ends(entries, stream_key, smallest, top_value):
    longest = entries.shape.index(max(entries.shape))
    spots = []
    for shift in (0, 1):
        where = [jax.random.randint(jax.random.fold_in(stream_key, axis), (), 0, length) for axis, length in enumerate(entries.shape)]
        where[longest] = (where[longest] + shift) % entries.shape[longest]
        spots.append(tuple(where))
    return entries.at[spots[0]].set(smallest).at[spots[1]].set(top_value)


def block_levels(key, extent, cuts, least, high):
    def one(dim, shards_of):
        steps = jax.random.uniform(jax.random.fold_in(jax.random.fold_in(key, 6), dim), (shards_of,), jnp.float32, least / len(cuts), high / len(cuts))
        return jnp.repeat(jnp.exp(steps), extent[dim] // shards_of).reshape((-1,) + (1,) * (len(extent) - dim - 1))

    gain = one(*cuts[0])
    for cut in cuts[1:]:
        gain = gain * one(*cut)
    return gain


def normal_values(rng, extent, scale, limit, cuts=(), kind=jnp.bfloat16):
    entries = scale * jax.random.normal(rng, extent, jnp.float32)
    if cuts:
        entries = entries * block_levels(rng, extent, cuts, -0.22, 0.18)
    return jnp.clip(entries, -limit, limit).astype(kind)


def setup_inputs(seed: int = 0) -> dict:
    arg_keys = jax.random.split(jax.random.key(seed), 9)
    return {
        "iterate": normal_values(arg_keys[0], (3, NRHS, NX, NY, NZ), 0.05, 0.75, ((2, 4), (3, 2), (4, 4)), jnp.float32),
        "residual": normal_values(arg_keys[1], (3, NRHS, NX, NY, NZ), 1.0, 8.0, ((2, 4), (3, 2), (4, 4)), jnp.float32),
        "cell_ids": touch_ends(jax.random.randint(arg_keys[2], (NX, NY, NZ), 0, NMAT), jax.random.fold_in(arg_keys[2], 1), 0, NMAT - 1).astype(jnp.int32),
        "materials": jnp.clip(jnp.exp(jax.random.uniform(arg_keys[3], (2, NMAT), jnp.float32, math.log(0.2), math.log(2.0))), 0.2, 2.0),
        "eigen_counts": draw_eigen_counts(jax.random.fold_in(arg_keys[8], 71), 0),
        "coarse_rank": jax.random.permutation(arg_keys[5], DEVICES).astype(jnp.int32),
        "eigen_basis": normal_values(arg_keys[6], (KMAX, 3, NX, NY, NZ), (3 * CX * CY * CZ) ** -0.5, 0.0546875, ((2, 4), (3, 2), (4, 4)), jnp.float32),
        "coarse_inverse": draw_coarse_inverse(jax.random.fold_in(arg_keys[8], 71), 0),
    }


damping = 0.6

def face_coefs(mu_padded):
    center = mu_padded[1:-1, 1:-1, 1:-1]
    result = []
    for axis_pick in range(3):
        for side_pick in (0, 2):
            window_cut = [slice(1, -1)] * 3
            window_cut[axis_pick] = slice(side_pick, side_pick + center.shape[axis_pick])
            result.append(0.5 * (center + mu_padded[tuple(window_cut)]))
    return result

def apply_op(padded_field, coefs, lam_field):
    center = padded_field[:, :, 1:-1, 1:-1, 1:-1]
    result = center + lam_field * jnp.sum(center, axis=0, keepdims=True)
    shape_cells = center.shape[2:]
    position = 0
    for axis_pick in range(3):
        for side_pick in (0, 2):
            window_cut = [slice(1, -1)] * 3
            window_cut[axis_pick] = slice(side_pick, side_pick + shape_cells[axis_pick])
            neighbour = padded_field[(slice(None), slice(None)) + tuple(window_cut)]
            result = result + coefs[position] * (center - neighbour)
            position = position + 1
    return result

def pad_cells(field_value):
    return jnp.pad(field_value, ((0, 0), (0, 0), (1, 1), (1, 1), (1, 1)))

def local_solve(res_box, coefs, lam_box):
    diag_inv = damping / (1.0 + lam_box + sum(coefs))
    field_value = diag_inv * res_box
    for sweep_step in range(SWEEPS - 1):
        field_value = field_value + diag_inv * (res_box - apply_op(pad_cells(field_value), coefs, lam_box))
    return field_value[:, :, 1:-1, 1:-1, 1:-1]

def reference(iterate, residual, cell_ids, materials, eigen_counts, coarse_rank, eigen_basis, coarse_inverse):
    highest = lax.Precision.HIGHEST
    mu_grid = materials[0][cell_ids]
    lam_grid = materials[1][cell_ids]
    mu_wide = jnp.pad(mu_grid, 2)
    lam_pad = jnp.pad(lam_grid, 1)
    res_pad = pad_cells(residual)
    slot_ids = jnp.arange(KMAX, dtype=jnp.int32)
    starts = jnp.sum(eigen_counts[None, :] * (coarse_rank[None, :] < coarse_rank[:, None]).astype(jnp.int32), axis=1).astype(jnp.int32)

    def corner(subdomain):
        start_x = subdomain // (N_GY * N_COL) * CX
        start_y = subdomain // N_COL % N_GY * CY
        start_z = subdomain % N_COL * CZ
        return (start_x.astype(jnp.int32), start_y.astype(jnp.int32), start_z.astype(jnp.int32))

    def local_piece(subdomain):
        start_x, start_y, start_z = corner(subdomain)
        anchor = jnp.int32(0)
        res_box = lax.dynamic_slice(res_pad, (anchor, anchor, start_x, start_y, start_z), (3, NRHS, CX + 2, CY + 2, CZ + 2))
        mu_box = lax.dynamic_slice(mu_wide, (start_x, start_y, start_z), (CX + 4, CY + 4, CZ + 4))
        lam_box = lax.dynamic_slice(lam_pad, (start_x, start_y, start_z), (CX + 2, CY + 2, CZ + 2))
        near_part = local_solve(res_box, face_coefs(mu_box), lam_box)
        vectors = lax.dynamic_slice(eigen_basis, (anchor, anchor, start_x, start_y, start_z), (KMAX, 3, CX, CY, CZ))
        pieces = jnp.einsum('ecxyz,ckxyz->ek', vectors, res_box[:, :, 1:-1, 1:-1, 1:-1], precision=highest)
        live_slots = slot_ids < eigen_counts[subdomain]
        return (near_part, jnp.where(live_slots[:, None], pieces, 0.0))
    subdomains = jnp.arange(N_GX * N_GY * N_COL, dtype=jnp.int32)
    near_all, pieces_all = lax.map(local_piece, subdomains)
    live_all = slot_ids[None, :] < eigen_counts[:, None]
    target = jnp.where(live_all, starts[:, None] + slot_ids[None, :], NCOARSE + slot_ids[None, :]).astype(jnp.int32)
    assembled = jnp.zeros((NCOARSE + KMAX, NRHS), jnp.float32).at[target.reshape(-1)].add(pieces_all.reshape(-1, NRHS))
    coarse_vector = assembled[:NCOARSE].astype(jnp.bfloat16)
    coarse_coef = jnp.dot(coarse_inverse.astype(jnp.float32), coarse_vector.astype(jnp.float32), preferred_element_type=jnp.float32)
    padded_coef = jnp.concatenate([coarse_coef, jnp.zeros((KMAX, NRHS), jnp.float32)], axis=0)

    def coarse_part(subdomain):
        start_x, start_y, start_z = corner(subdomain)
        anchor = jnp.int32(0)
        vectors = lax.dynamic_slice(eigen_basis, (anchor, anchor, start_x, start_y, start_z), (KMAX, 3, CX, CY, CZ))
        own_coef = lax.dynamic_slice_in_dim(padded_coef, starts[subdomain], KMAX, 0)
        own_coef = jnp.where((slot_ids < eigen_counts[subdomain])[:, None], own_coef, 0.0)
        return jnp.einsum('ecxyz,ek->ckxyz', vectors, own_coef, precision=highest)
    corrections = lax.map(coarse_part, subdomains)
    blocks = near_all + corrections
    direction = blocks.reshape(N_GX, N_GY, N_COL, 3, NRHS, CX, CY, CZ).transpose(3, 4, 0, 5, 1, 6, 2, 7).reshape(3, NRHS, NX, NY, NZ)
    image_field = apply_op(pad_cells(direction), face_coefs(jnp.pad(mu_grid, 1)), lam_grid)
    energy = jnp.einsum('cjxyz,ckxyz->jk', direction, image_field, precision=highest)
    load_products = jnp.einsum('cjxyz,ckxyz->jk', direction, residual, precision=highest)
    factor = jnp.linalg.cholesky(energy)
    step_coef = jax.scipy.linalg.cho_solve((factor, True), load_products)
    new_iterate = iterate + jnp.einsum('cjxyz,jk->ckxyz', direction, step_coef, precision=highest)
    new_residual = residual - jnp.einsum('cjxyz,jk->ckxyz', image_field, step_coef, precision=highest)
    return (new_iterate, new_residual)
```

```python
import jax
import jax.numpy as jnp
from jax import lax
from jax.sharding import PartitionSpec as P

SWEEPS = 4


damping = 0.6


def extended(x, sides, width):
    for axis, dim in sides:
        devices, length = (lax.axis_size(axis), x.shape[dim])
        up = [(i, (i + 1) % devices) for i in range(devices - 1)]
        down = [(j, i) for i, j in up]
        last = lax.slice_in_dim(x, length - width, length, axis=dim)
        first = lax.slice_in_dim(x, 0, width, axis=dim)
        before = lax.ppermute(last, axis, up)
        after = lax.ppermute(first, axis, down)
        x = jnp.concatenate([before, x, after], axis=dim)
    return x


def face_coefs(mu_padded):
    center = mu_padded[1:-1, 1:-1, 1:-1]
    result = []
    for axis_pick in range(3):
        for side_pick in (0, 2):
            window_cut = [slice(1, -1)] * 3
            window_cut[axis_pick] = slice(side_pick, side_pick + center.shape[axis_pick])
            result.append(0.5 * (center + mu_padded[tuple(window_cut)]))
    return result


def apply_op(padded_field, coefs, lam_field):
    center = padded_field[:, :, 1:-1, 1:-1, 1:-1]
    result = center + lam_field * jnp.sum(center, axis=0, keepdims=True)
    shape_cells = center.shape[2:]
    position = 0
    for axis_pick in range(3):
        for side_pick in (0, 2):
            window_cut = [slice(1, -1)] * 3
            window_cut[axis_pick] = slice(side_pick, side_pick + shape_cells[axis_pick])
            neighbour = padded_field[(slice(None), slice(None)) + tuple(window_cut)]
            result = result + coefs[position] * (center - neighbour)
            position = position + 1
    return result


def pad_cells(field_value):
    return jnp.pad(field_value, ((0, 0), (0, 0), (1, 1), (1, 1), (1, 1)))


def local_solve(res_box, coefs, lam_box):
    diag_inv = damping / (1.0 + lam_box + sum(coefs))
    field_value = diag_inv * res_box
    for sweep_step in range(SWEEPS - 1):
        field_value = field_value + diag_inv * (
            res_box - apply_op(pad_cells(field_value), coefs, lam_box)
        )
    return field_value[:, :, 1:-1, 1:-1, 1:-1]


def lookup(ids_plus, materials):
    table_rows = materials.shape[1]
    onehot = (ids_plus[..., None] == jnp.arange(1, table_rows + 1, dtype=jnp.int32)).astype(
        jnp.float32
    )
    values = jnp.dot(onehot.reshape(-1, table_rows), materials.T, precision=lax.Precision.HIGHEST)
    values = values.reshape(ids_plus.shape + (2,))
    return (values[..., 0], values[..., 1])


def coarse_devices(axes):
    total = 1
    for axis in axes:
        total = total * lax.axis_size(axis)
    return total


def body(
    iterate, residual, cell_ids, materials, eigen_counts, coarse_rank, eigen_basis, coarse_inverse
):
    highest = lax.Precision.HIGHEST
    ids_wide = extended(cell_ids + 1, (("gx", 0), ("gy", 1), ("col", 2)), 2)
    mu_wide, lam_wide = lookup(ids_wide, materials)
    lam_box = lam_wide[1:-1, 1:-1, 1:-1]
    res_box = extended(residual, (("gx", 2), ("gy", 3), ("col", 4)), 1)
    box_coefs = face_coefs(mu_wide)
    near_part = local_solve(res_box, box_coefs, lam_box)
    slot_count = eigen_basis.shape[0]
    load_count = residual.shape[1]
    total_rows = coarse_inverse.shape[1]
    slot_ids = jnp.arange(slot_count, dtype=jnp.int32)
    live_slots = slot_ids < eigen_counts[0]
    pieces = jnp.einsum("ecxyz,ckxyz->ek", eigen_basis, residual, precision=highest)
    pieces = jnp.where(live_slots[:, None], pieces, 0.0)
    axes = ("gx", "gy", "col")
    devices = coarse_devices(axes)
    extra = jnp.zeros((16, load_count), jnp.float32)
    extra = extra.at[0].set(eigen_counts[0].astype(jnp.float32))
    extra = extra.at[1].set(coarse_rank[0].astype(jnp.float32))
    message = jnp.concatenate([pieces, extra], axis=0).astype(jnp.bfloat16)
    gathered = lax.all_to_all(
        jnp.broadcast_to(message[None], (devices,) + message.shape), axes, 0, 0, tiled=True
    )
    all_counts = gathered[:, slot_count, 0].astype(jnp.int32)
    all_ranks = gathered[:, slot_count + 1, 0].astype(jnp.int32)
    my_start = jnp.sum(all_counts * (all_ranks < coarse_rank[0]).astype(jnp.int32))
    starts = jnp.sum(
        all_counts[None, :] * (all_ranks[None, :] < all_ranks[:, None]).astype(jnp.int32), axis=1
    )
    target = jnp.where(
        slot_ids[None, :] < all_counts[:, None], starts[:, None] + slot_ids[None, :], -1
    ).reshape(-1)
    select = (jnp.arange(total_rows, dtype=jnp.int32)[:, None] == target[None, :]).astype(
        jnp.bfloat16
    )
    coarse_vector = jnp.dot(
        select,
        gathered[:, :slot_count].reshape(-1, load_count),
        preferred_element_type=jnp.float32,
    ).astype(jnp.bfloat16)
    partial_coef = jnp.dot(coarse_inverse, coarse_vector, preferred_element_type=jnp.float32)
    coarse_coef = lax.all_to_all(
        jnp.broadcast_to(partial_coef[None], (total_rows // partial_coef.shape[0],) + partial_coef.shape),
        ("gx", "col"), 0, 0, tiled=True,
    ).reshape(total_rows, load_count)
    padded_coef = jnp.concatenate(
        [coarse_coef, jnp.zeros((slot_count, load_count), jnp.float32)], axis=0
    )
    own_coef = lax.dynamic_slice_in_dim(padded_coef, my_start, slot_count, 0)
    own_coef = jnp.where(live_slots[:, None], own_coef, 0.0)
    direction = near_part + jnp.einsum("ecxyz,ek->ckxyz", eigen_basis, own_coef, precision=highest)
    inner_coefs = [coef_item[1:-1, 1:-1, 1:-1] for coef_item in box_coefs]
    lam_own = lam_box[1:-1, 1:-1, 1:-1]
    local_loads = jnp.einsum("cjxyz,ckxyz->jk", direction, residual, precision=highest)
    direction_pad = extended(direction, (("gx", 2), ("gy", 3), ("col", 4)), 1)
    image_field = apply_op(direction_pad, inner_coefs, lam_own)
    local_energy = jnp.einsum("cjxyz,ckxyz->jk", direction, image_field, precision=highest)
    sums = jnp.concatenate([local_energy, local_loads], axis=1)
    for axis in ("gy", "col", "gx"):
        step = 1
        while step < lax.axis_size(axis):
            pairs = [(i, i ^ step) for i in range(lax.axis_size(axis))]
            sums = sums + lax.ppermute(sums, axis, pairs)
            step = step * 2
    energy, load_products = sums[:, :load_count], sums[:, load_count:]
    factor = jnp.linalg.cholesky(energy)
    step_coef = jax.scipy.linalg.cho_solve((factor, True), load_products)
    new_iterate = iterate + jnp.einsum("cjxyz,jk->ckxyz", direction, step_coef, precision=highest)
    new_residual = residual - jnp.einsum(
        "cjxyz,jk->ckxyz", image_field, step_coef, precision=highest
    )
    return (new_iterate, new_residual)


def solution(mesh):
    placed = (
        P(None, None, "gx", "gy", "col"),
        P(None, None, "gx", "gy", "col"),
        P("gx", "gy", "col"),
        P(),
        P(("gx", "gy", "col")),
        P(("gx", "gy", "col")),
        P(None, None, "gx", "gy", "col"),
        P(("gx", "col"), None),
    )
    return jax.shard_map(
        body,
        mesh=mesh,
        in_specs=placed,
        out_specs=(P(None, None, "gx", "gy", "col"), P(None, None, "gx", "gy", "col")),
        check_vma=False,
    )
```

```python
import jax
import jax.numpy as jnp
from jax import lax
from jax.experimental import pallas as pl
from jax.experimental.pallas import tpu as pltpu
from jax.sharding import PartitionSpec as P

DAMPING = 0.6
F32 = jnp.float32
BF16 = jnp.bfloat16
LANES = 128
HALO_IDS = 16
AXES = ("gx", "gy", "col")
TRANSPOSED = (((1,), (1,)), ((), ()))


def split_hi_lo(value):
    hi = value.astype(BF16)
    return hi, (value - hi.astype(F32)).astype(BF16)


def paired_left(value, width, parts):
    rows = value.shape[0]
    hi, lo = split_hi_lo(value)
    parts[pl.ds(0, rows), :] = hi
    parts[pl.ds(rows, rows), :] = lo
    high = parts[pl.ds(0, rows), :].astype(F32)
    low = parts[pl.ds(rows, rows), :].astype(F32)
    return jnp.concatenate([high + roll_lanes(high, width), low], axis=0).astype(BF16)


def lane_ids(rows):
    return lax.broadcasted_iota(jnp.int32, (rows, LANES), 1)


def roll_lanes(value, shift):
    if isinstance(shift, int):
        shift = shift % LANES
        if shift == 0:
            return value
    return pltpu.roll(value, shift, axis=1)


def vmem_call(name, kernel, outs, scratch, limit_mib, flops, moved, operands, spaces=None):
    spaces = spaces or [pltpu.VMEM] * len(operands)
    return pl.pallas_call(
        kernel,
        name=name,
        out_shape=outs,
        in_specs=[pl.BlockSpec(memory_space=space) for space in spaces],
        out_specs=jax.tree.map(lambda _: pl.BlockSpec(memory_space=pltpu.VMEM), outs),
        scratch_shapes=scratch,
        compiler_params=pltpu.CompilerParams(vmem_limit_bytes=limit_mib << 20),
        cost_estimate=pl.CostEstimate(flops=flops, bytes_accessed=moved, transcendentals=0),
    )(*operands)


class Sizes:
    def __init__(self, residual, eigen_basis, coarse_inverse):
        self.comps, self.loads, self.cx, self.cy, _ = residual.shape
        self.slots = eigen_basis.shape[0]
        self.block_rows, self.total_rows = coarse_inverse.shape
        self.cells = self.cx * self.cy
        self.bx, self.by = self.cx + 2, self.cy + 2
        self.box = self.bx * self.by
        self.tiles = self.comps * self.cells
        self.face_x = self.comps * self.cy * self.loads
        self.face_y = self.comps * self.bx * self.loads
        self.inner_y = self.comps * self.cx * self.loads
        self.face_z = self.comps * self.loads
        self.pitch = 16


def own_rows(sz, ref, comp, cell):
    start = comp * sz.loads * sz.cells + cell
    return ref[pl.ds(start, sz.loads, stride=sz.cells), :]


def pack_x(sz, res, ids, lo, hi):
    for comp in range(sz.comps):
        for y in range(sz.cy):
            rows = pl.ds((comp * sz.cy + y) * sz.loads, sz.loads)
            lo[rows, :] = own_rows(sz, res, comp, y).astype(BF16)
            hi[rows, :] = own_rows(sz, res, comp, (sz.cx - 1) * sz.cy + y).astype(BF16)
    two = 2 * sz.cy
    lo[pl.ds(sz.face_x, two), :] = (ids[pl.ds(0, two), :] + 1).astype(F32).astype(BF16)
    hi[pl.ds(sz.face_x, two), :] = (
        (ids[pl.ds(sz.cells - two, two), :] + 1).astype(F32).astype(BF16)
    )


def make_pieces(sz, count, rank, basis, res, message, split, wide):
    slots, loads = sz.slots, sz.loads

    def step(index, carry):
        both, low = carry
        basis_hi, basis_lo, res_hi, res_both = [], [], [], []
        for half in range(2):
            tile = index * 2 + half
            comp = tile // sz.cells
            hi, lo = split_hi_lo(basis[pl.ds(tile, slots, stride=sz.tiles), :])
            split[tile, pl.ds(0, slots), :] = hi
            split[tile, pl.ds(slots, slots), :] = lo
            value_hi, value_lo = split_hi_lo(own_rows(sz, res, comp, tile - comp * sz.cells))
            basis_hi.append(hi)
            basis_lo.append(lo)
            res_hi.append(value_hi)
            res_both.append(jnp.concatenate([value_hi, value_lo], axis=0))
        both = both + lax.dot_general(
            jnp.concatenate(res_both, axis=1),
            jnp.concatenate(basis_hi, axis=1),
            TRANSPOSED,
            preferred_element_type=F32,
        )
        low = low + lax.dot_general(
            jnp.concatenate(res_hi, axis=1),
            jnp.concatenate(basis_lo, axis=1),
            TRANSPOSED,
            preferred_element_type=F32,
        )
        return both, low

    both, low = lax.fori_loop(
        0,
        sz.tiles // 2,
        step,
        (jnp.zeros((2 * loads, slots), F32), jnp.zeros((loads, slots), F32)),
        unroll=4,
    )
    pieces = both[:loads] + both[loads:] + low
    slot = lax.broadcasted_iota(jnp.int32, pieces.shape, 1)
    wide[...] = jnp.zeros_like(wide)
    wide[:, pl.ds(0, slots)] = jnp.where(slot < count[0], pieces, 0.0)
    half = loads // 2
    lane = lane_ids(half)
    packed = jnp.where(lane < 64, wide[:half, :], roll_lanes(wide[half:, :], 64))
    packed = jnp.where(lane == slots, count[0].astype(F32), packed)
    packed = jnp.where(lane == slots + 1, rank[0].astype(F32), packed).astype(BF16)
    for device in range(message.shape[0]):
        message[device] = packed


def pack_y(sz, swap, res, ids, below, above, *refs):
    outs, side = refs[:-1], refs[-1]
    last = sz.cy - 1
    if swap:
        faces = [jnp.where(lax.axis_index("gy") == 0, last, 0)]
    else:
        faces = [0, last]
    ids_below = below[pl.ds(sz.face_x, 2 * sz.cy), :].astype(F32)
    ids_above = above[pl.ds(sz.face_x, 2 * sz.cy), :].astype(F32)
    for out, y in zip(outs, faces):
        dynamic = not isinstance(y, int)
        for comp in range(sz.comps):
            for x in range(sz.bx):
                rows = pl.ds((comp * sz.bx + x) * sz.loads, sz.loads)
                if 0 < x < sz.bx - 1:
                    value = own_rows(sz, res, comp, (x - 1) * sz.cy + y).astype(BF16)
                else:
                    source = below if x == 0 else above
                    start = (comp * sz.cy + y) * sz.loads
                    if dynamic:
                        start = pl.multiple_of(start, sz.loads)
                    value = source[pl.ds(start, sz.loads), :]
                out[rows, :] = value
        for x in range(sz.cx + 4):
            for j in range(2):
                if 2 <= x < sz.cx + 2:
                    first = (ids[pl.ds((x - 2) * sz.cy + j, 1), :] + 1).astype(F32)
                    end = (ids[pl.ds((x - 2) * sz.cy + last - 1 + j, 1), :] + 1).astype(F32)
                else:
                    source, base = (ids_below, x * sz.cy) if x < 2 else (
                        ids_above, (x - sz.cx - 2) * sz.cy)
                    first = source[base + j : base + j + 1]
                    end = source[base + last - 1 + j : base + last + j]
                if dynamic:
                    row = jnp.where(y == 0, first, end)
                else:
                    row = first if y == 0 else end
                side[pl.ds(x * 2 + j, 1), :] = row
        out[pl.ds(sz.face_y, HALO_IDS), :] = side[...].astype(BF16)


def side_flags(swap):
    if not swap:
        return None, None
    upper = lax.axis_index("gy") == 1
    return jnp.where(upper, 1.0, 0.0).astype(F32), jnp.where(upper, 0.0, 1.0).astype(F32)


def flagged(value, flag):
    value = value.astype(F32)
    return value if flag is None else value * flag


def box_tile(sz, res, below, above, ylow, yhigh, flags, comp, x, y):
    if y == 0 or y == sz.by - 1:
        source, flag = (ylow, flags[0]) if y == 0 else (yhigh, flags[1])
        return flagged(source[pl.ds((comp * sz.bx + x) * sz.loads, sz.loads), :], flag)
    if x == 0 or x == sz.bx - 1:
        source = below if x == 0 else above
        return source[pl.ds((comp * sz.cy + y - 1) * sz.loads, sz.loads), :].astype(F32)
    return own_rows(sz, res, comp, (x - 1) * sz.cy + y - 1)


def pack_z(sz, swap, res, ids, below, above, ylow, yhigh, out, id_box, star, outer):
    flags = side_flags(swap)
    pitch = sz.pitch
    id_box[...] = jnp.zeros_like(id_box)
    two = 2 * sz.cy
    ids_below = below[pl.ds(sz.face_x, two), :].astype(F32)
    ids_above = above[pl.ds(sz.face_x, two), :].astype(F32)
    ids_low = flagged(ylow[pl.ds(sz.face_y, HALO_IDS), :], flags[0])
    ids_high = flagged(yhigh[pl.ds(sz.face_y, HALO_IDS), :], flags[1])
    for x in range(sz.cx + 4):
        if x < 2:
            rows = ids_below[x * sz.cy : (x + 1) * sz.cy]
        elif x >= sz.cx + 2:
            rows = ids_above[(x - sz.cx - 2) * sz.cy : (x - sz.cx - 1) * sz.cy]
        else:
            rows = (ids[pl.ds((x - 2) * sz.cy, sz.cy), :] + 1).astype(F32)
        id_box[pl.ds(x * pitch + 2, sz.cy), :] = rows
        id_box[pl.ds(x * pitch, 2), :] = ids_low[2 * x : 2 * x + 2]
        id_box[pl.ds(x * pitch + sz.cy + 2, 2), :] = ids_high[2 * x : 2 * x + 2]
    values = id_box[...]
    lane = lane_ids(values.shape[0])
    outer[...] = jnp.where(lane == LANES - 1, roll_lanes(values, 1), roll_lanes(values, -1))
    star[...] = jnp.zeros_like(star)
    lane8 = lane_ids(8)
    taken = jnp.zeros((8, LANES), F32)
    for x in range(sz.bx):
        for y in range(sz.by):
            place = x * sz.by + y
            row = (x + 1) * pitch + y + 1
            for j, shift in enumerate((0, -pitch, pitch, -1, 1)):
                star[pl.ds(place * 8 + j, 1), :] = id_box[pl.ds(row + shift, 1), :]
            star[pl.ds(place * 8 + 5, 1), :] = outer[pl.ds(row, 1), :]
    for place in range(sz.box):
        picked = roll_lanes(star[pl.ds(place * 8, 8), :], 2 * place + 1)
        taken = jnp.where((lane8 >> 1) == place, picked, taken)
    out[pl.ds(sz.face_z, HALO_IDS), :] = jnp.concatenate(
        [taken, jnp.zeros((HALO_IDS - 8, LANES), F32)], axis=0
    ).astype(BF16)
    lane_k = lane_ids(sz.loads)
    for comp in range(sz.comps):
        total = jnp.zeros((sz.loads, LANES), F32)
        for x in range(sz.bx):
            for y in range(sz.by):
                place = x * sz.by + y
                tile = box_tile(sz, res, below, above, ylow, yhigh, flags, comp, x, y)
                total = jnp.where(
                    (lane_k >> 1) == place, roll_lanes(tile, 2 * place + 1), total
                )
        out[pl.ds(comp * sz.loads, sz.loads), :] = total.astype(BF16)


def place_pieces(sz, starts, gathered, inverse, message, vector, wide):
    half = sz.loads // 2
    lane = lane_ids(half)
    vector[...] = jnp.zeros_like(vector)

    def place(device, carry):
        start = starts[device]
        block = start // LANES
        offset = start - block * LANES
        packed = gathered[device].astype(F32)
        low = jnp.where(lane < sz.slots, packed, 0.0)
        high = jnp.where((lane >= 64) & (lane < 64 + sz.slots), packed, 0.0)
        both = jnp.concatenate(
            [
                pltpu.roll(low, offset, axis=1),
                pltpu.roll(high, lax.rem(offset + 64, LANES), axis=1),
            ],
            axis=0,
        )
        wide_lane = lane_ids(sz.loads)
        vector[block] = vector[block] + jnp.where(wide_lane >= offset, both, 0.0)
        vector[block + 1] = vector[block + 1] + jnp.where(wide_lane < offset, both, 0.0)
        return carry

    lax.fori_loop(0, gathered.shape[0], place, 0)
    total = jnp.zeros((sz.loads, sz.block_rows), F32)
    for block in range(sz.total_rows // LANES):
        total = total + lax.dot_general(
            vector[block].astype(BF16),
            inverse[:, pl.ds(block * LANES, LANES)],
            TRANSPOSED,
            preferred_element_type=F32,
        )
    if sz.block_rows == 64:
        wide[...] = jnp.zeros_like(wide)
        wide[:, pl.ds(0, 64)] = total
        packed = jnp.where(lane < 64, wide[:half, :], roll_lanes(wide[half:, :], 64))
        for device in range(message.shape[0]):
            message[device, 0] = packed
    else:
        for device in range(message.shape[0]):
            for block in range(sz.block_rows // LANES):
                message[device, block] = total[:, block * LANES : (block + 1) * LANES]


def own_coefs(sz, coefs, start):
    if sz.block_rows == 64:
        half = sz.loads // 2
        block = start // 64
        offset = start - block * 64
        first = coefs[block]
        second = coefs[jnp.minimum(block + 1, coefs.shape[0] - 1)]
        lane = lane_ids(half)
        top = jnp.where(lane < 64, first, roll_lanes(second, 64))
        bottom = jnp.where(lane < 64, roll_lanes(first, 64), second)
        both = jnp.concatenate([top, bottom], axis=0)
    else:
        block = start // LANES
        offset = start - block * LANES
        first = coefs[block]
        second = coefs[jnp.minimum(block + 1, coefs.shape[0] - 1)]
        both = jnp.where(lane_ids(sz.loads) >= offset, first, second)
    return pltpu.roll(both, lax.rem(LANES - offset, LANES), axis=1)


def look_up(table, row, ids):
    result = jnp.zeros_like(ids)
    for material in range(table.shape[1]):
        result = jnp.where(ids == material + 1, table[row, material], result)
    return result


DINV, KEEP, DLAM, WXM, WXP, WYM, WYP, WZM, WZP = range(9)


def spread_row(ref, index, row):
    return jnp.broadcast_to(ref[index, pl.ds(row, 1), :], (8, LANES))


def make_coefs(sz, table, id_box, halo_ids, coefs, halo_coefs, own, mu_box, halo_mu):
    pitch = sz.pitch
    mu_box[...] = look_up(table, 0, id_box[...])
    lam_box = look_up(table, 1, id_box[...])
    mu_halo = look_up(table, 0, halo_ids)
    lam_halo = look_up(table, 1, halo_ids)
    lane8 = lane_ids(8)
    center = jnp.broadcast_to(mu_halo[0:1], (8, LANES))
    inner = jnp.zeros((8, LANES), F32)
    for place in range(sz.box):
        row = (place // sz.by + 1) * pitch + place % sz.by + 1
        halo_mu[pl.ds(row, 1), :] = roll_lanes(center, -2 * place)[0:1]
        spread = jnp.broadcast_to(mu_box[pl.ds(row, 1), :], (8, LANES))
        here = (((lane8 + 1) >> 1) & 63) == place
        inner = jnp.where(here, roll_lanes(spread, 2 * place), inner)
    rows_id = lax.broadcasted_iota(jnp.int32, (pitch, LANES), 0)
    lane = lane_ids(pitch)
    for x in range(1, sz.bx + 1):
        mu = mu_box[pl.ds(x * pitch, pitch), :]
        edge = halo_mu[pl.ds(x * pitch, pitch), :]
        lam = lam_box[x * pitch : (x + 1) * pitch]
        faces = [
            0.5 * (mu + mu_box[pl.ds((x - 1) * pitch, pitch), :]),
            0.5 * (mu + mu_box[pl.ds((x + 1) * pitch, pitch), :]),
            0.5 * (mu + mu_box[pl.ds(x * pitch - 1, pitch), :]),
            0.5 * (mu + mu_box[pl.ds(x * pitch + 1, pitch), :]),
            0.5 * (mu + jnp.where(lane == 0, edge, roll_lanes(mu, 1))),
            0.5 * (mu + jnp.where(lane == LANES - 1, edge, roll_lanes(mu, -1))),
        ]
        diag = 1.0 + sum(faces)
        dinv = DAMPING / (diag + lam)
        rows = pl.ds(x * pitch, pitch)
        coefs[DINV, rows, :] = dinv
        coefs[KEEP, rows, :] = (1.0 - DAMPING) + dinv * lam
        coefs[DLAM, rows, :] = dinv * lam
        weights = [dinv * face for face in faces]
        if x == 1:
            weights[0] = jnp.zeros_like(dinv)
        if x == sz.bx:
            weights[1] = jnp.zeros_like(dinv)
        weights[2] = jnp.where(rows_id == 1, 0.0, weights[2])
        weights[3] = jnp.where(rows_id == sz.by, 0.0, weights[3])
        for j in range(6):
            coefs[WXM + j, rows, :] = weights[j]
        if 2 <= x <= sz.cx + 1:
            target = pl.ds((x - 2) * sz.cy, sz.cy)
            for j, value in enumerate([diag, lam] + faces):
                own[j, target, :] = value[2 : 2 + sz.cy]
    place = ((lane8 + 1) >> 1) & 63
    column = jnp.zeros_like(place)
    for x in range(1, sz.bx):
        column = column + (place >= x * sz.by).astype(jnp.int32)
    y_place = place - column * sz.by
    others = [jnp.broadcast_to(mu_halo[j : j + 1], (8, LANES)) for j in range(1, 6)]
    faces = [0.5 * (center + other) for other in others] + [0.5 * (center + inner)]
    lam = jnp.broadcast_to(lam_halo[0:1], (8, LANES))
    dinv = DAMPING / (1.0 + lam + sum(faces))
    live = place < sz.box
    keep = [
        live & (column > 0),
        live & (column < sz.bx - 1),
        live & (y_place > 0),
        live & (y_place < sz.by - 1),
        None,
        live,
    ]
    halo_coefs[DINV] = dinv
    halo_coefs[KEEP] = (1.0 - DAMPING) + dinv * lam
    halo_coefs[DLAM] = dinv * lam
    for j, target in ((0, WXM), (1, WXP), (2, WYM), (3, WYP), (5, WZM)):
        halo_coefs[target] = jnp.where(keep[j], dinv * faces[j], 0.0)


def solve_and_direct(
    sz, swap, start, count, table, res, below, above, ylow, yhigh, zdown, zup, id_box, coarse,
    split, *rest,
):
    if swap:
        direction, xlo, xhi, yface, zface, own = rest[:6]
        yfaces = [yface]
        rest = rest[6:]
    else:
        direction, xlo, xhi, ylo_out, yhi_out, zface, own = rest[:7]
        yfaces = [ylo_out, yhi_out]
        rest = rest[7:]
    first, second, third, halos, inner, coefs, halo_coefs, mu_box, halo_mu, left = rest
    loads, comps = sz.loads, sz.comps
    groups = loads // 8
    flags = side_flags(swap)
    lane8 = lane_ids(8)
    even8 = (lane8 & 1) == 0

    def halo_rows(row, size):
        down = zdown[pl.ds(row, size), :].astype(F32)
        up = zup[pl.ds(row, size), :].astype(F32)
        even = (lane_ids(size) & 1) == 0
        return jnp.where(even, down, roll_lanes(up, -2))

    halo_mu[...] = jnp.zeros_like(halo_mu)
    inner[1] = jnp.zeros((comps, loads, LANES), F32)
    make_coefs(
        sz, table, id_box, halo_rows(sz.face_z, HALO_IDS)[:8], coefs, halo_coefs, own, mu_box,
        halo_mu,
    )
    here_of = lambda place: (((lane8 + 1) >> 1) & 63) == place

    for comp in range(comps):
        halo = halo_rows(comp * loads, loads)
        dinv = jnp.concatenate([halo_coefs[DINV]] * groups, axis=0)
        halos[0, comp] = dinv * halo
        total = jnp.zeros((loads, LANES), F32)
        lane_k = lane_ids(loads)
        for x in range(sz.bx):
            for y in range(sz.by):
                place = x * sz.by + y
                row = (x + 1) * sz.pitch + y + 1
                tile = box_tile(sz, res, below, above, ylow, yhigh, flags, comp, x, y)
                value = tile * jnp.broadcast_to(coefs[DINV, pl.ds(row, 1), :], (loads, LANES))
                first[comp, place] = value
                here = (((lane_k + 1) >> 1) & 63) == place
                total = jnp.where(here, roll_lanes(value, 2 * place), total)
        inner[0, comp] = total

    def relax(source, level, place, row):
        coef = [spread_row(coefs, j, row) for j in range(9)]
        xm, xp = jnp.maximum(place - sz.by, 0), jnp.minimum(place + sz.by, sz.box - 1)
        ym, yp = jnp.maximum(place - 1, 0), jnp.minimum(place + 1, sz.box - 1)
        back = lax.rem(LANES - 2 * place + LANES, LANES)
        result = {}
        for group in range(groups):
            rows = pl.ds(group * 8, 8)
            center = [source[comp, place, rows, :] for comp in range(comps)]
            coupled = coef[DLAM] * sum(center)
            for comp in range(comps):
                value = center[comp]
                edge = pltpu.roll(halos[level, comp, rows, :], back, axis=1)
                zm = jnp.where(lane8 == 0, edge, roll_lanes(value, 1))
                zp = jnp.where(lane8 == LANES - 1, edge, roll_lanes(value, -1))
                out = (first[comp, place, rows, :] - coupled) + coef[KEEP] * value
                out = out + coef[WXM] * source[comp, xm, rows, :]
                out = out + coef[WXP] * source[comp, xp, rows, :]
                out = out + coef[WYM] * source[comp, ym, rows, :]
                out = out + coef[WYP] * source[comp, yp, rows, :]
                out = out + coef[WZM] * zm
                out = out + coef[WZP] * zp
                result[comp, group] = out
        return result

    def sweep(source, target, level):
        def at(place, carry):
            x = place // sz.by
            row = (x + 1) * sz.pitch + place - x * sz.by + 1
            result = relax(source, level, place, row)
            for (comp, group), out in result.items():
                rows = pl.ds(group * 8, 8)
                target[comp, place, rows, :] = out
                if level == 0:
                    inner[1, comp, rows, :] = jnp.where(
                        here_of(place), pltpu.roll(out, 2 * place, axis=1),
                        inner[1, comp, rows, :],
                    )
            return carry

        lax.fori_loop(0, sz.box, at, 0)
        coef = [halo_coefs[j] for j in range(8)]
        for group in range(groups):
            rows = pl.ds(group * 8, 8)
            center = [halos[level, comp, rows, :] for comp in range(comps)]
            coupled = coef[DLAM] * sum(center)
            for comp in range(comps):
                value = center[comp]
                out = (halos[0, comp, rows, :] - coupled) + coef[KEEP] * value
                out = out + coef[WXM] * roll_lanes(value, 2 * sz.by)
                out = out + coef[WXP] * roll_lanes(value, -2 * sz.by)
                out = out + coef[WYM] * roll_lanes(value, 2)
                out = out + coef[WYP] * roll_lanes(value, -2)
                out = out + coef[WZM] * inner[level, comp, rows, :]
                halos[level + 1, comp, rows, :] = out

    sweep(first, second, 0)
    sweep(second, third, 1)

    mine = own_coefs(sz, coarse, start[0])
    mine = jnp.where(lane_ids(loads) < jnp.minimum(count[0], sz.slots), mine, 0.0)
    left[...] = paired_left(mine, sz.slots, left)
    zface[...] = jnp.zeros_like(zface)

    def final(cell, carry):
        x = cell // sz.cy
        y = cell - x * sz.cy
        place = (x + 1) * sz.by + y + 1
        result = relax(third, 2, place, (x + 2) * sz.pitch + y + 2)
        for comp in range(comps):
            tile = comp * sz.cells + cell
            part = jnp.dot(
                left[:, : 2 * sz.slots], split[tile], preferred_element_type=F32
            )
            for group in range(groups):
                rows = pl.ds(group * 8, 8)
                value = result[comp, group] + (
                    part[group * 8 : group * 8 + 8]
                    + part[loads + group * 8 : loads + group * 8 + 8]
                )
                direction[comp, cell, rows, :] = value
                zrows = pl.ds(comp * loads + group * 8, 8)
                zface[zrows, :] = jnp.where(
                    (lane8 >> 1) == place,
                    pltpu.roll(value, 2 * place + 1, axis=1),
                    zface[zrows, :],
                )
        return carry

    lax.fori_loop(0, sz.cells, final, 0)
    for comp in range(comps):
        for y in range(sz.cy):
            rows = pl.ds((comp * sz.cy + y) * loads, loads)
            xlo[rows, :] = direction[comp, y].astype(BF16)
            xhi[rows, :] = direction[comp, (sz.cx - 1) * sz.cy + y].astype(BF16)
        for x in range(sz.cx):
            rows = pl.ds((comp * sz.cx + x) * loads, loads)
            if swap:
                y = jnp.where(lax.axis_index("gy") == 0, sz.cy - 1, 0)
                yfaces[0][rows, :] = direction[comp, x * sz.cy + y].astype(BF16)
            else:
                yfaces[0][rows, :] = direction[comp, x * sz.cy].astype(BF16)
                yfaces[1][rows, :] = direction[comp, x * sz.cy + sz.cy - 1].astype(BF16)


def make_image(
    sz, swap, res, own, direction, below, above, ylow, yhigh, zdown, zup, dir_split,
    image_split, message, box, halo, sem,
):
    loads, comps = sz.loads, sz.comps
    groups = loads // 8
    copies = []
    for comp in range(comps):
        for x in range(sz.cx):
            copies.append(
                pltpu.make_async_copy(
                    direction.at[comp, pl.ds(x * sz.cy, sz.cy)],
                    box.at[comp, pl.ds((x + 1) * sz.by + 1, sz.cy)],
                    sem.at[comp, x],
                )
            )
    for copy in copies:
        copy.start()
    flags = side_flags(swap)
    for comp in range(comps):
        for y in range(sz.cy):
            rows = pl.ds((comp * sz.cy + y) * loads, loads)
            box[comp, y + 1] = below[rows, :].astype(F32)
            box[comp, (sz.bx - 1) * sz.by + y + 1] = above[rows, :].astype(F32)
        for x in range(sz.cx):
            rows = pl.ds((comp * sz.cx + x) * loads, loads)
            box[comp, (x + 1) * sz.by] = flagged(ylow[rows, :], flags[0])
            box[comp, (x + 1) * sz.by + sz.by - 1] = flagged(yhigh[rows, :], flags[1])
        rows = pl.ds(comp * loads, loads)
        even = (lane_ids(loads) & 1) == 0
        halo[comp] = jnp.where(
            even, zdown[rows, :].astype(F32), roll_lanes(zup[rows, :].astype(F32), -2)
        )
    for copy in copies:
        copy.wait()
    lane8 = lane_ids(8)

    def at(cell, total):
        x = cell // sz.cy
        y = cell - x * sz.cy
        place = (x + 1) * sz.by + y + 1
        back = lax.rem(LANES - 2 * place + LANES, LANES)
        coef = [spread_row(own, j, cell) for j in range(8)]
        parts = {}
        for group in range(groups):
            rows = pl.ds(group * 8, 8)
            center = [box[comp, place, rows, :] for comp in range(comps)]
            coupled = coef[1] * sum(center)
            for comp in range(comps):
                value = center[comp]
                edge = pltpu.roll(halo[comp, rows, :], back, axis=1)
                zm = jnp.where(lane8 == 0, edge, roll_lanes(value, 1))
                zp = jnp.where(lane8 == LANES - 1, edge, roll_lanes(value, -1))
                out = coef[0] * value + coupled
                out = out - coef[2] * box[comp, place - sz.by, rows, :]
                out = out - coef[3] * box[comp, place + sz.by, rows, :]
                out = out - coef[4] * box[comp, place - 1, rows, :]
                out = out - coef[5] * box[comp, place + 1, rows, :]
                out = out - coef[6] * zm
                parts[comp, group] = out - coef[7] * zp
        for comp in range(comps):
            tile = comp * sz.cells + cell
            dir_hi, dir_lo = split_hi_lo(box[comp, place])
            field = jnp.concatenate([parts[comp, group] for group in range(groups)], axis=0)
            field_hi, field_lo = split_hi_lo(field)
            res_hi, res_lo = split_hi_lo(own_rows(sz, res, comp, cell))
            left = jnp.concatenate([dir_hi, dir_lo], axis=0)
            field_both = jnp.concatenate([field_hi, field_lo], axis=0)
            dir_split[tile] = left
            image_split[tile] = field_both
            total = total + lax.dot_general(
                left,
                jnp.concatenate([field_both, res_hi, res_lo], axis=0),
                TRANSPOSED,
                preferred_element_type=F32,
            )
        return total

    total = lax.fori_loop(0, sz.cells, at, jnp.zeros((2 * loads, 4 * loads), F32))
    high, low = total[:loads], total[loads:]
    sums = high + roll_lanes(high, -loads) + low
    half = loads // 2
    lane = lane_ids(half)
    packed = jnp.where((lane & (2 * loads - 1)) < loads, sums[:half], roll_lanes(sums[half:], loads))
    for device in range(message.shape[0]):
        message[device] = packed


def finish(
    sz, sums, iterate, res, dir_split, image_split, new_iterate, new_residual, parts
):
    loads = sz.loads
    half = loads // 2
    total = sums[0]
    for device in range(1, sums.shape[0]):
        total = total + sums[device]
    system = jnp.concatenate([total, roll_lanes(total, -loads)], axis=0)
    lane = lane_ids(loads)
    system = jnp.where((lane & (2 * loads - 1)) < loads, system, 0.0)
    row_ids = lax.broadcasted_iota(jnp.int32, (loads, LANES), 0)
    for i in range(loads):
        row = system[i : i + 1, :]
        row = row / row[:, i : i + 1]
        system = jnp.where(row_ids == i, row, system - system[:, i : i + 1] * row)
    step = jnp.transpose(system)[2 * loads : 3 * loads, :]
    padded = jnp.concatenate([step, jnp.zeros((loads, LANES - loads), F32)], axis=1) if (
        step.shape[1] < LANES
    ) else step
    left = paired_left(padded, loads, parts)[:, : 2 * loads]

    def at(cell, carry):
        for comp in range(sz.comps):
            tile = comp * sz.cells + cell
            right = jnp.concatenate([dir_split[tile], image_split[tile]], axis=1)
            part = jnp.dot(left, right, preferred_element_type=F32)
            part = part[:loads] + part[loads:]
            rows = pl.ds(comp * loads * sz.cells + cell, loads, stride=sz.cells)
            new_iterate[rows, :] = iterate[rows, :] + part[:, :LANES]
            new_residual[rows, :] = res[rows, :] - part[:, LANES:]
        return carry

    lax.fori_loop(0, sz.cells, at, 0, unroll=2)


def exchange(low, high, axis):
    devices = lax.axis_size(axis)
    up = [(i, i + 1) for i in range(devices - 1)]
    down = [(j, i) for i, j in up]
    return lax.ppermute(high, axis, up), lax.ppermute(low, axis, down)


def exchange_y(faces, swap):
    if swap:
        got = lax.ppermute(faces[0], "gy", [(0, 1), (1, 0)])
        return got, got
    return exchange(faces[0], faces[1], "gy")


def body(
    iterate, residual, cell_ids, materials, eigen_counts, coarse_rank, eigen_basis, coarse_inverse
):
    sz = Sizes(residual, eigen_basis, coarse_inverse)
    shape = jax.ShapeDtypeStruct
    swap = lax.axis_size("gy") == 2
    devices = 1
    for axis in AXES:
        devices = devices * lax.axis_size(axis)
    blocks = sz.total_rows // sz.block_rows
    smem, vmem = pltpu.SMEM, pltpu.VMEM
    res = residual.reshape(-1, LANES)
    old = iterate.reshape(-1, LANES)
    basis = eigen_basis.reshape(-1, LANES)
    ids = cell_ids.reshape(-1, LANES)

    def call(name, kernel, *args, **kwargs):
        return vmem_call(name, lambda *refs: kernel(sz, *refs), *args, **kwargs)

    def call_swap(name, kernel, *args, **kwargs):
        return vmem_call(name, lambda *refs: kernel(sz, swap, *refs), *args, **kwargs)

    face = shape((sz.face_x + 2 * sz.cy, LANES), BF16)
    xlo, xhi = call("pack_x", pack_x, [face, face], [], 16, 1 << 20, 2 << 20, [res, ids])
    below, above = exchange(xlo, xhi, "gx")

    message, split = call(
        "pieces",
        make_pieces,
        [
            shape((devices, sz.loads // 2, LANES), BF16),
            shape((sz.tiles, 2 * sz.slots, LANES), BF16),
        ],
        [pltpu.VMEM((sz.loads, LANES), F32)],
        20,
        1 << 27,
        7 << 20,
        [eigen_counts, coarse_rank, basis, res],
        spaces=[smem, smem, vmem, vmem],
    )
    gathered = lax.all_to_all(message, AXES, 0, 0, tiled=True)
    all_counts = gathered[:, 0, sz.slots].astype(jnp.int32)
    all_ranks = gathered[:, 0, sz.slots + 1].astype(jnp.int32)
    starts = jnp.sum(
        all_counts[None, :] * (all_ranks[None, :] < all_ranks[:, None]).astype(jnp.int32), axis=1
    )
    my_start = jnp.sum(
        all_counts * (all_ranks < coarse_rank[0]).astype(jnp.int32), keepdims=True
    )

    side = [pltpu.VMEM((HALO_IDS, LANES), F32)]
    yface = shape((sz.face_y + HALO_IDS, LANES), BF16)
    faces = call_swap(
        "pack_y", pack_y, [yface] * (1 if swap else 2), side, 16, 1 << 20, 2 << 20,
        [res, ids, below, above],
    )
    ylow, yhigh = exchange_y(faces, swap)
    rows = (sz.cx + 4) * sz.pitch
    zmessage, id_box = call_swap(
        "pack_z",
        pack_z,
        [shape((sz.face_z + HALO_IDS, LANES), BF16), shape((rows, LANES), F32)],
        [pltpu.VMEM((sz.box * 8, LANES), F32), pltpu.VMEM((rows, LANES), F32)],
        16,
        1 << 22,
        3 << 20,
        [res, ids, below, above, ylow, yhigh],
    )
    zdown, zup = exchange(zmessage, zmessage, "col")

    packed = sz.block_rows == 64
    tile = (1, sz.loads // 2, LANES) if packed else (sz.block_rows // LANES, sz.loads, LANES)
    partial = call(
        "coarse",
        place_pieces,
        shape((blocks,) + tile, F32),
        [
            pltpu.VMEM((sz.total_rows // LANES + 1, sz.loads, LANES), F32),
            pltpu.VMEM((sz.loads, LANES), F32),
        ],
        20,
        1 << 23,
        1 << 20,
        [starts, gathered, coarse_inverse],
        spaces=[smem, vmem, vmem],
    )
    coarse = lax.all_to_all(partial, ("gx", "col"), 0, 0, tiled=True)
    coarse = coarse.reshape((-1,) + tile[1:])

    dface = shape((sz.face_x, LANES), BF16)
    dyface = shape((sz.inner_y, LANES), BF16)
    field = pltpu.VMEM((sz.comps, sz.box, sz.loads, LANES), F32)
    results = call_swap(
        "solve",
        solve_and_direct,
        [shape((sz.comps, sz.cells, sz.loads, LANES), F32), dface, dface]
        + [dyface] * (1 if swap else 2)
        + [shape((sz.face_z, LANES), F32), shape((8, sz.cells, LANES), F32)],
        [
            field,
            field,
            field,
            pltpu.VMEM((3, sz.comps, sz.loads, LANES), F32),
            pltpu.VMEM((2, sz.comps, sz.loads, LANES), F32),
            pltpu.VMEM((9, rows, LANES), F32),
            pltpu.VMEM((9, 8, LANES), F32),
            pltpu.VMEM((rows, LANES), F32),
            pltpu.VMEM((rows, LANES), F32),
            pltpu.VMEM((2 * sz.loads, LANES), BF16),
        ],
        40,
        1 << 28,
        8 << 20,
        [
            my_start, eigen_counts, materials, res, below, above, ylow, yhigh, zdown, zup, id_box,
            coarse, split,
        ],
        spaces=[smem, smem, smem] + [vmem] * 10,
    )
    direction, dxlo, dxhi = results[:3]
    dfaces, zface, own = results[3:-2], results[-2], results[-1]
    dbelow, dabove = exchange(dxlo, dxhi, "gx")
    dylow, dyhigh = exchange_y(dfaces, swap)
    dzdown, dzup = exchange(zface, zface, "col")

    dir_split, image_split, energy = call_swap(
        "image",
        make_image,
        [
            shape((sz.tiles, 2 * sz.loads, LANES), BF16),
            shape((sz.tiles, 2 * sz.loads, LANES), BF16),
            shape((devices, sz.loads // 2, LANES), F32),
        ],
        [
            field,
            pltpu.VMEM((sz.comps, sz.loads, LANES), F32),
            pltpu.SemaphoreType.DMA((sz.comps, sz.cx)),
        ],
        32,
        1 << 28,
        8 << 20,
        [res, own, direction, dbelow, dabove, dylow, dyhigh, dzdown, dzup],
        spaces=[vmem, vmem, pl.ANY] + [vmem] * 6,
    )
    sums = lax.all_to_all(energy, AXES, 0, 0, tiled=True)
    flat = shape(res.shape, F32)
    new_iterate, new_residual = call(
        "finish",
        finish,
        [flat, flat],
        [pltpu.VMEM((2 * sz.loads, LANES), BF16)],
        32,
        1 << 27,
        9 << 20,
        [sums, old, res, dir_split, image_split],
    )
    return (new_iterate.reshape(iterate.shape), new_residual.reshape(residual.shape))


def solution(mesh):
    placed = (
        P(None, None, "gx", "gy", "col"),
        P(None, None, "gx", "gy", "col"),
        P("gx", "gy", "col"),
        P(),
        P(("gx", "gy", "col")),
        P(("gx", "gy", "col")),
        P(None, None, "gx", "gy", "col"),
        P(("gx", "col"), None),
    )
    return jax.shard_map(
        body,
        mesh=mesh,
        in_specs=placed,
        out_specs=(P(None, None, "gx", "gy", "col"), P(None, None, "gx", "gy", "col")),
        check_vma=False,
    )
```

```python
import jax
import jax.numpy as jnp
from jax import lax
from jax.experimental import pallas as pl
from jax.experimental.pallas import tpu as pltpu
from jax.sharding import PartitionSpec as P

DAMPING = 0.6
F32 = jnp.float32
BF16 = jnp.bfloat16
LANES = 128
HALO_IDS = 16
AXES = ("gx", "gy", "col")
TRANSPOSED = (((1,), (1,)), ((), ()))


def split_hi_lo(value):
    hi = value.astype(BF16)
    return hi, (value - hi.astype(F32)).astype(BF16)


def paired_left(value, width, parts):
    rows = value.shape[0]
    hi, lo = split_hi_lo(value)
    parts[pl.ds(0, rows), :] = hi
    parts[pl.ds(rows, rows), :] = lo
    high = parts[pl.ds(0, rows), :].astype(F32)
    low = parts[pl.ds(rows, rows), :].astype(F32)
    return jnp.concatenate([high + roll_lanes(high, width), low], axis=0).astype(BF16)


def lane_ids(rows):
    return lax.broadcasted_iota(jnp.int32, (rows, LANES), 1)


def roll_lanes(value, shift):
    if isinstance(shift, int):
        shift = shift % LANES
        if shift == 0:
            return value
    return pltpu.roll(value, shift, axis=1)


def vmem_call(name, kernel, outs, scratch, limit_mib, flops, moved, operands, spaces=None):
    spaces = spaces or [pltpu.VMEM] * len(operands)
    return pl.pallas_call(
        kernel,
        name=name,
        out_shape=outs,
        in_specs=[pl.BlockSpec(memory_space=space) for space in spaces],
        out_specs=jax.tree.map(lambda _: pl.BlockSpec(memory_space=pltpu.VMEM), outs),
        scratch_shapes=scratch,
        compiler_params=pltpu.CompilerParams(vmem_limit_bytes=limit_mib << 20),
        cost_estimate=pl.CostEstimate(flops=flops, bytes_accessed=moved, transcendentals=0),
    )(*operands)


def own_index():
    index = 0
    for axis in AXES:
        index = index * lax.axis_size(axis) + lax.axis_index(axis)
    return index


class Sizes:
    def __init__(self, residual, eigen_basis, coarse_inverse):
        self.comps, self.loads, self.cx, self.cy, _ = residual.shape
        self.slots = eigen_basis.shape[0]
        self.block_rows, self.total_rows = coarse_inverse.shape
        self.cells = self.cx * self.cy
        self.bx, self.by = self.cx + 2, self.cy + 2
        self.box = self.bx * self.by
        self.tiles = self.comps * self.cells
        self.face_x = self.comps * self.cy * self.loads
        self.face_y = self.comps * self.bx * self.loads
        self.inner_y = self.comps * self.cx * self.loads
        self.face_z = self.comps * self.loads
        self.pitch = 16


def own_rows(sz, ref, comp, cell):
    start = comp * sz.loads * sz.cells + cell
    return ref[pl.ds(start, sz.loads, stride=sz.cells), :]


def pack_x(sz, res, ids, lo, hi):
    for comp in range(sz.comps):
        for y in range(sz.cy):
            rows = pl.ds((comp * sz.cy + y) * sz.loads, sz.loads)
            lo[rows, :] = own_rows(sz, res, comp, y).astype(BF16)
            hi[rows, :] = own_rows(sz, res, comp, (sz.cx - 1) * sz.cy + y).astype(BF16)
    two = 2 * sz.cy
    lo[pl.ds(sz.face_x, two), :] = (ids[pl.ds(0, two), :] + 1).astype(F32).astype(BF16)
    hi[pl.ds(sz.face_x, two), :] = (
        (ids[pl.ds(sz.cells - two, two), :] + 1).astype(F32).astype(BF16)
    )


def make_pieces(sz, count, rank, basis, res, after, message, split, wide):
    del after
    slots, loads = sz.slots, sz.loads

    def step(index, carry):
        both, low = carry
        basis_hi, basis_lo, res_hi, res_both = [], [], [], []
        for half in range(2):
            tile = index * 2 + half
            comp = tile // sz.cells
            hi, lo = split_hi_lo(basis[pl.ds(tile, slots, stride=sz.tiles), :])
            split[tile, pl.ds(0, slots), :] = hi
            split[tile, pl.ds(slots, slots), :] = lo
            value_hi, value_lo = split_hi_lo(own_rows(sz, res, comp, tile - comp * sz.cells))
            basis_hi.append(hi)
            basis_lo.append(lo)
            res_hi.append(value_hi)
            res_both.append(jnp.concatenate([value_hi, value_lo], axis=0))
        both = both + lax.dot_general(
            jnp.concatenate(res_both, axis=1),
            jnp.concatenate(basis_hi, axis=1),
            TRANSPOSED,
            preferred_element_type=F32,
        )
        low = low + lax.dot_general(
            jnp.concatenate(res_hi, axis=1),
            jnp.concatenate(basis_lo, axis=1),
            TRANSPOSED,
            preferred_element_type=F32,
        )
        return both, low

    both, low = lax.fori_loop(
        0,
        sz.tiles // 2,
        step,
        (jnp.zeros((2 * loads, slots), F32), jnp.zeros((loads, slots), F32)),
        unroll=4,
    )
    pieces = both[:loads] + both[loads:] + low
    slot = lax.broadcasted_iota(jnp.int32, pieces.shape, 1)
    wide[...] = jnp.zeros_like(wide)
    wide[:, pl.ds(0, slots)] = jnp.where(slot < count[0], pieces, 0.0)
    half = loads // 2
    lane = lane_ids(half)
    packed = jnp.where(lane < 64, wide[:half, :], roll_lanes(wide[half:, :], 64))
    packed = jnp.where(lane == slots, count[0].astype(F32), packed)
    packed = jnp.where(lane == slots + 1, rank[0].astype(F32), packed).astype(BF16)
    for device in range(message.shape[0]):
        message[device] = packed


def pack_y(sz, swap, res, ids, below, above, *refs):
    outs, side = refs[:-1], refs[-1]
    last = sz.cy - 1
    if swap:
        faces = [jnp.where(lax.axis_index("gy") == 0, last, 0)]
    else:
        faces = [0, last]
    ids_below = below[pl.ds(sz.face_x, 2 * sz.cy), :].astype(F32)
    ids_above = above[pl.ds(sz.face_x, 2 * sz.cy), :].astype(F32)
    for out, y in zip(outs, faces):
        dynamic = not isinstance(y, int)
        for comp in range(sz.comps):
            for x in range(sz.bx):
                rows = pl.ds((comp * sz.bx + x) * sz.loads, sz.loads)
                if 0 < x < sz.bx - 1:
                    value = own_rows(sz, res, comp, (x - 1) * sz.cy + y).astype(BF16)
                else:
                    source = below if x == 0 else above
                    start = (comp * sz.cy + y) * sz.loads
                    if dynamic:
                        start = pl.multiple_of(start, sz.loads)
                    value = source[pl.ds(start, sz.loads), :]
                out[rows, :] = value
        for x in range(sz.cx + 4):
            for j in range(2):
                if 2 <= x < sz.cx + 2:
                    first = (ids[pl.ds((x - 2) * sz.cy + j, 1), :] + 1).astype(F32)
                    end = (ids[pl.ds((x - 2) * sz.cy + last - 1 + j, 1), :] + 1).astype(F32)
                else:
                    source, base = (ids_below, x * sz.cy) if x < 2 else (
                        ids_above, (x - sz.cx - 2) * sz.cy)
                    first = source[base + j : base + j + 1]
                    end = source[base + last - 1 + j : base + last + j]
                if dynamic:
                    row = jnp.where(y == 0, first, end)
                else:
                    row = first if y == 0 else end
                side[pl.ds(x * 2 + j, 1), :] = row
        out[pl.ds(sz.face_y, HALO_IDS), :] = side[...].astype(BF16)


def side_flags(swap):
    if not swap:
        return None, None
    upper = lax.axis_index("gy") == 1
    return jnp.where(upper, 1.0, 0.0).astype(F32), jnp.where(upper, 0.0, 1.0).astype(F32)


def flagged(value, flag):
    value = value.astype(F32)
    return value if flag is None else value * flag


def box_tile(sz, res, below, above, ylow, yhigh, flags, comp, x, y):
    if y == 0 or y == sz.by - 1:
        source, flag = (ylow, flags[0]) if y == 0 else (yhigh, flags[1])
        return flagged(source[pl.ds((comp * sz.bx + x) * sz.loads, sz.loads), :], flag)
    if x == 0 or x == sz.bx - 1:
        source = below if x == 0 else above
        return source[pl.ds((comp * sz.cy + y - 1) * sz.loads, sz.loads), :].astype(F32)
    return own_rows(sz, res, comp, (x - 1) * sz.cy + y - 1)


def pack_z(sz, swap, res, ids, below, above, ylow, yhigh, out, id_box, star, outer):
    flags = side_flags(swap)
    pitch = sz.pitch
    id_box[...] = jnp.zeros_like(id_box)
    two = 2 * sz.cy
    ids_below = below[pl.ds(sz.face_x, two), :].astype(F32)
    ids_above = above[pl.ds(sz.face_x, two), :].astype(F32)
    ids_low = flagged(ylow[pl.ds(sz.face_y, HALO_IDS), :], flags[0])
    ids_high = flagged(yhigh[pl.ds(sz.face_y, HALO_IDS), :], flags[1])
    for x in range(sz.cx + 4):
        if x < 2:
            rows = ids_below[x * sz.cy : (x + 1) * sz.cy]
        elif x >= sz.cx + 2:
            rows = ids_above[(x - sz.cx - 2) * sz.cy : (x - sz.cx - 1) * sz.cy]
        else:
            rows = (ids[pl.ds((x - 2) * sz.cy, sz.cy), :] + 1).astype(F32)
        id_box[pl.ds(x * pitch + 2, sz.cy), :] = rows
        id_box[pl.ds(x * pitch, 2), :] = ids_low[2 * x : 2 * x + 2]
        id_box[pl.ds(x * pitch + sz.cy + 2, 2), :] = ids_high[2 * x : 2 * x + 2]
    values = id_box[...]
    lane = lane_ids(values.shape[0])
    outer[...] = jnp.where(lane == LANES - 1, roll_lanes(values, 1), roll_lanes(values, -1))
    star[...] = jnp.zeros_like(star)
    lane8 = lane_ids(8)
    taken = jnp.zeros((8, LANES), F32)
    for x in range(sz.bx):
        for y in range(sz.by):
            place = x * sz.by + y
            row = (x + 1) * pitch + y + 1
            for j, shift in enumerate((0, -pitch, pitch, -1, 1)):
                star[pl.ds(place * 8 + j, 1), :] = id_box[pl.ds(row + shift, 1), :]
            star[pl.ds(place * 8 + 5, 1), :] = outer[pl.ds(row, 1), :]
    for place in range(sz.box):
        picked = roll_lanes(star[pl.ds(place * 8, 8), :], 2 * place + 1)
        taken = jnp.where((lane8 >> 1) == place, picked, taken)
    out[pl.ds(sz.face_z, HALO_IDS), :] = jnp.concatenate(
        [taken, jnp.zeros((HALO_IDS - 8, LANES), F32)], axis=0
    ).astype(BF16)
    lane_k = lane_ids(sz.loads)
    for comp in range(sz.comps):
        total = jnp.zeros((sz.loads, LANES), F32)
        for x in range(sz.bx):
            for y in range(sz.by):
                place = x * sz.by + y
                tile = box_tile(sz, res, below, above, ylow, yhigh, flags, comp, x, y)
                total = jnp.where(
                    (lane_k >> 1) == place, roll_lanes(tile, 2 * place + 1), total
                )
        out[pl.ds(comp * sz.loads, sz.loads), :] = total.astype(BF16)


def place_pieces(sz, starts, gathered, inverse, message, vector, wide):
    half = sz.loads // 2
    lane = lane_ids(half)
    vector[...] = jnp.zeros_like(vector)

    def place(device, carry):
        start = starts[device]
        block = start // LANES
        offset = start - block * LANES
        packed = gathered[device].astype(F32)
        low = jnp.where(lane < sz.slots, packed, 0.0)
        high = jnp.where((lane >= 64) & (lane < 64 + sz.slots), packed, 0.0)
        both = jnp.concatenate(
            [
                pltpu.roll(low, offset, axis=1),
                pltpu.roll(high, lax.rem(offset + 64, LANES), axis=1),
            ],
            axis=0,
        )
        wide_lane = lane_ids(sz.loads)
        vector[block] = vector[block] + jnp.where(wide_lane >= offset, both, 0.0)
        vector[block + 1] = vector[block + 1] + jnp.where(wide_lane < offset, both, 0.0)
        return carry

    lax.fori_loop(0, gathered.shape[0], place, 0, unroll=8)
    total = jnp.zeros((sz.loads, sz.block_rows), F32)
    for block in range(sz.total_rows // LANES):
        total = total + lax.dot_general(
            vector[block].astype(BF16),
            inverse[:, pl.ds(block * LANES, LANES)],
            TRANSPOSED,
            preferred_element_type=F32,
        )
    if sz.block_rows == 64:
        wide[...] = jnp.zeros_like(wide)
        wide[:, pl.ds(0, 64)] = total
        packed = jnp.where(lane < 64, wide[:half, :], roll_lanes(wide[half:, :], 64))
        for device in range(message.shape[0]):
            message[device, 0] = packed.astype(BF16)
    else:
        for device in range(message.shape[0]):
            for block in range(sz.block_rows // LANES):
                message[device, block] = total[:, block * LANES : (block + 1) * LANES].astype(BF16)


def own_coefs(sz, coefs, start):
    if sz.block_rows == 64:
        half = sz.loads // 2
        block = start // 64
        offset = start - block * 64
        first = coefs[block].astype(F32)
        second = coefs[jnp.minimum(block + 1, coefs.shape[0] - 1)].astype(F32)
        lane = lane_ids(half)
        top = jnp.where(lane < 64, first, roll_lanes(second, 64))
        bottom = jnp.where(lane < 64, roll_lanes(first, 64), second)
        both = jnp.concatenate([top, bottom], axis=0)
    else:
        block = start // LANES
        offset = start - block * LANES
        first = coefs[block].astype(F32)
        second = coefs[jnp.minimum(block + 1, coefs.shape[0] - 1)].astype(F32)
        both = jnp.where(lane_ids(sz.loads) >= offset, first, second)
    return pltpu.roll(both, lax.rem(LANES - offset, LANES), axis=1)


def look_up(table, row, ids):
    result = jnp.zeros_like(ids)
    for material in range(table.shape[1]):
        result = jnp.where(ids == material + 1, table[row, material], result)
    return result


DINV, KEEP, DLAM, WXM, WXP, WYM, WYP, WZM, WZP = range(9)


def spread_row(ref, index, row):
    return jnp.broadcast_to(ref[index, pl.ds(row, 1), :], (8, LANES))


def make_coefs(sz, table, id_box, halo_ids, coefs, halo_coefs, own, mu_box, halo_mu):
    pitch = sz.pitch
    mu_box[...] = look_up(table, 0, id_box[...])
    lam_box = look_up(table, 1, id_box[...])
    mu_halo = look_up(table, 0, halo_ids)
    lam_halo = look_up(table, 1, halo_ids)
    lane8 = lane_ids(8)
    center = jnp.broadcast_to(mu_halo[0:1], (8, LANES))
    inner = jnp.zeros((8, LANES), F32)
    for place in range(sz.box):
        row = (place // sz.by + 1) * pitch + place % sz.by + 1
        halo_mu[pl.ds(row, 1), :] = roll_lanes(center, -2 * place)[0:1]
        spread = jnp.broadcast_to(mu_box[pl.ds(row, 1), :], (8, LANES))
        here = (((lane8 + 1) >> 1) & 63) == place
        inner = jnp.where(here, roll_lanes(spread, 2 * place), inner)
    rows_id = lax.broadcasted_iota(jnp.int32, (pitch, LANES), 0)
    lane = lane_ids(pitch)
    for x in range(1, sz.bx + 1):
        mu = mu_box[pl.ds(x * pitch, pitch), :]
        edge = halo_mu[pl.ds(x * pitch, pitch), :]
        lam = lam_box[x * pitch : (x + 1) * pitch]
        faces = [
            0.5 * (mu + mu_box[pl.ds((x - 1) * pitch, pitch), :]),
            0.5 * (mu + mu_box[pl.ds((x + 1) * pitch, pitch), :]),
            0.5 * (mu + mu_box[pl.ds(x * pitch - 1, pitch), :]),
            0.5 * (mu + mu_box[pl.ds(x * pitch + 1, pitch), :]),
            0.5 * (mu + jnp.where(lane == 0, edge, roll_lanes(mu, 1))),
            0.5 * (mu + jnp.where(lane == LANES - 1, edge, roll_lanes(mu, -1))),
        ]
        diag = 1.0 + sum(faces)
        dinv = DAMPING / (diag + lam)
        rows = pl.ds(x * pitch, pitch)
        coefs[DINV, rows, :] = dinv
        coefs[KEEP, rows, :] = (1.0 - DAMPING) + dinv * lam
        coefs[DLAM, rows, :] = dinv * lam
        weights = [dinv * face for face in faces]
        if x == 1:
            weights[0] = jnp.zeros_like(dinv)
        if x == sz.bx:
            weights[1] = jnp.zeros_like(dinv)
        weights[2] = jnp.where(rows_id == 1, 0.0, weights[2])
        weights[3] = jnp.where(rows_id == sz.by, 0.0, weights[3])
        for j in range(6):
            coefs[WXM + j, rows, :] = weights[j]
        if 2 <= x <= sz.cx + 1:
            target = pl.ds((x - 2) * sz.cy, sz.cy)
            for j, value in enumerate([diag, lam] + faces):
                own[j, target, :] = value[2 : 2 + sz.cy]
    place = ((lane8 + 1) >> 1) & 63
    column = jnp.zeros_like(place)
    for x in range(1, sz.bx):
        column = column + (place >= x * sz.by).astype(jnp.int32)
    y_place = place - column * sz.by
    others = [jnp.broadcast_to(mu_halo[j : j + 1], (8, LANES)) for j in range(1, 6)]
    faces = [0.5 * (center + other) for other in others] + [0.5 * (center + inner)]
    lam = jnp.broadcast_to(lam_halo[0:1], (8, LANES))
    dinv = DAMPING / (1.0 + lam + sum(faces))
    live = place < sz.box
    keep = [
        live & (column > 0),
        live & (column < sz.bx - 1),
        live & (y_place > 0),
        live & (y_place < sz.by - 1),
        None,
        live,
    ]
    halo_coefs[DINV] = dinv
    halo_coefs[KEEP] = (1.0 - DAMPING) + dinv * lam
    halo_coefs[DLAM] = dinv * lam
    for j, target in ((0, WXM), (1, WXP), (2, WYM), (3, WYP), (5, WZM)):
        halo_coefs[target] = jnp.where(keep[j], dinv * faces[j], 0.0)


def solve_and_direct(
    sz, swap, starts, count, table, res, below, above, ylow, yhigh, zdown, zup, id_box, coarse,
    split, *rest,
):
    if swap:
        direction, xlo, xhi, yface, zface, own = rest[:6]
        yfaces = [yface]
        rest = rest[6:]
    else:
        direction, xlo, xhi, ylo_out, yhi_out, zface, own = rest[:7]
        yfaces = [ylo_out, yhi_out]
        rest = rest[7:]
    first, second, third, halos, inner, coefs, halo_coefs, mu_box, halo_mu, left, zedge = rest
    loads, comps = sz.loads, sz.comps
    groups = loads // 8
    flags = side_flags(swap)
    lane8 = lane_ids(8)
    even8 = (lane8 & 1) == 0

    def halo_rows(row, size):
        down = zdown[pl.ds(row, size), :].astype(F32)
        up = zup[pl.ds(row, size), :].astype(F32)
        even = (lane_ids(size) & 1) == 0
        return jnp.where(even, down, roll_lanes(up, -2))

    halo_mu[...] = jnp.zeros_like(halo_mu)
    inner[1] = jnp.zeros((comps, loads, LANES), F32)
    make_coefs(
        sz, table, id_box, halo_rows(sz.face_z, HALO_IDS)[:8], coefs, halo_coefs, own, mu_box,
        halo_mu,
    )
    here_of = lambda place: (((lane8 + 1) >> 1) & 63) == place

    for comp in range(comps):
        halo = halo_rows(comp * loads, loads)
        dinv = jnp.concatenate([halo_coefs[DINV]] * groups, axis=0)
        halos[0, comp] = dinv * halo
        total = jnp.zeros((loads, LANES), F32)
        lane_k = lane_ids(loads)
        for x in range(sz.bx):
            for y in range(sz.by):
                place = x * sz.by + y
                row = (x + 1) * sz.pitch + y + 1
                tile = box_tile(sz, res, below, above, ylow, yhigh, flags, comp, x, y)
                value = tile * jnp.broadcast_to(coefs[DINV, pl.ds(row, 1), :], (loads, LANES))
                first[comp, place] = value
                here = (((lane_k + 1) >> 1) & 63) == place
                total = jnp.where(here, roll_lanes(value, 2 * place), total)
        inner[0, comp] = total

    def relax(source, level, place, row):
        coef = [spread_row(coefs, j, row) for j in range(9)]
        xm, xp = jnp.maximum(place - sz.by, 0), jnp.minimum(place + sz.by, sz.box - 1)
        ym, yp = jnp.maximum(place - 1, 0), jnp.minimum(place + 1, sz.box - 1)
        back = lax.rem(LANES - 2 * place + LANES, LANES)
        result = {}
        for group in range(groups):
            rows = pl.ds(group * 8, 8)
            center = [source[comp, place, rows, :] for comp in range(comps)]
            coupled = coef[DLAM] * sum(center)
            for comp in range(comps):
                value = center[comp]
                edge = pltpu.roll(halos[level, comp, rows, :], back, axis=1)
                zm = jnp.where(lane8 == 0, edge, roll_lanes(value, 1))
                zp = jnp.where(lane8 == LANES - 1, edge, roll_lanes(value, -1))
                out = (first[comp, place, rows, :] - coupled) + coef[KEEP] * value
                out = out + coef[WXM] * source[comp, xm, rows, :]
                out = out + coef[WXP] * source[comp, xp, rows, :]
                out = out + coef[WYM] * source[comp, ym, rows, :]
                out = out + coef[WYP] * source[comp, yp, rows, :]
                out = out + coef[WZM] * zm
                out = out + coef[WZP] * zp
                result[comp, group] = out
        return result

    def sweep(source, target, level):
        def at(place, carry):
            x = place // sz.by
            row = (x + 1) * sz.pitch + place - x * sz.by + 1
            result = relax(source, level, place, row)
            for (comp, group), out in result.items():
                rows = pl.ds(group * 8, 8)
                target[comp, place, rows, :] = out
                if level == 0:
                    pltpu.store(
                        inner.at[1, comp, rows, :],
                        pltpu.roll(out, 2 * place, axis=1),
                        mask=here_of(place),
                    )
            return carry

        lax.fori_loop(0, sz.box, at, 0, unroll=4)
        coef = [halo_coefs[j] for j in range(8)]
        for group in range(groups):
            rows = pl.ds(group * 8, 8)
            center = [halos[level, comp, rows, :] for comp in range(comps)]
            coupled = coef[DLAM] * sum(center)
            for comp in range(comps):
                value = center[comp]
                out = (halos[0, comp, rows, :] - coupled) + coef[KEEP] * value
                out = out + coef[WXM] * roll_lanes(value, 2 * sz.by)
                out = out + coef[WXP] * roll_lanes(value, -2 * sz.by)
                out = out + coef[WYM] * roll_lanes(value, 2)
                out = out + coef[WYP] * roll_lanes(value, -2)
                out = out + coef[WZM] * inner[level, comp, rows, :]
                halos[level + 1, comp, rows, :] = out

    sweep(first, second, 0)
    sweep(second, third, 1)

    mine = own_coefs(sz, coarse, starts[own_index()])
    mine = jnp.where(lane_ids(loads) < jnp.minimum(count[0], sz.slots), mine, 0.0)
    left[...] = paired_left(mine, sz.slots, left)
    zedge[...] = jnp.zeros_like(zedge)

    def final(cell, carry):
        x = cell // sz.cy
        y = cell - x * sz.cy
        place = (x + 1) * sz.by + y + 1
        result = relax(third, 2, place, (x + 2) * sz.pitch + y + 2)
        for comp in range(comps):
            tile = comp * sz.cells + cell
            part = jnp.dot(
                left[:, : 2 * sz.slots], split[tile], preferred_element_type=F32
            )
            for group in range(groups):
                rows = pl.ds(group * 8, 8)
                value = result[comp, group] + (
                    part[group * 8 : group * 8 + 8]
                    + part[loads + group * 8 : loads + group * 8 + 8]
                )
                direction[comp, cell, rows, :] = value
                zrows = pl.ds(comp * loads + group * 8, 8)
                pltpu.store(
                    zedge.at[zrows, :],
                    pltpu.roll(value, 2 * place + 1, axis=1),
                    mask=(lane8 >> 1) == place,
                )
        return carry

    lax.fori_loop(0, sz.cells, final, 0, unroll=4)
    zface[...] = zedge[...].astype(BF16)
    for comp in range(comps):
        for y in range(sz.cy):
            rows = pl.ds((comp * sz.cy + y) * loads, loads)
            xlo[rows, :] = direction[comp, y].astype(BF16)
            xhi[rows, :] = direction[comp, (sz.cx - 1) * sz.cy + y].astype(BF16)
        for x in range(sz.cx):
            rows = pl.ds((comp * sz.cx + x) * loads, loads)
            if swap:
                y = jnp.where(lax.axis_index("gy") == 0, sz.cy - 1, 0)
                yfaces[0][rows, :] = direction[comp, x * sz.cy + y].astype(BF16)
            else:
                yfaces[0][rows, :] = direction[comp, x * sz.cy].astype(BF16)
                yfaces[1][rows, :] = direction[comp, x * sz.cy + sz.cy - 1].astype(BF16)


def make_image(
    sz, swap, res, own, direction, below, above, ylow, yhigh, zdown, zup, dir_split,
    image_split, message, box, halo, sem,
):
    loads, comps = sz.loads, sz.comps
    groups = loads // 8
    copies = []
    for comp in range(comps):
        for x in range(sz.cx):
            copies.append(
                pltpu.make_async_copy(
                    direction.at[comp, pl.ds(x * sz.cy, sz.cy)],
                    box.at[comp, pl.ds((x + 1) * sz.by + 1, sz.cy)],
                    sem.at[comp, x],
                )
            )
    for copy in copies:
        copy.start()
    flags = side_flags(swap)
    for comp in range(comps):
        for y in range(sz.cy):
            rows = pl.ds((comp * sz.cy + y) * loads, loads)
            box[comp, y + 1] = below[rows, :].astype(F32)
            box[comp, (sz.bx - 1) * sz.by + y + 1] = above[rows, :].astype(F32)
        for x in range(sz.cx):
            rows = pl.ds((comp * sz.cx + x) * loads, loads)
            box[comp, (x + 1) * sz.by] = flagged(ylow[rows, :], flags[0])
            box[comp, (x + 1) * sz.by + sz.by - 1] = flagged(yhigh[rows, :], flags[1])
        rows = pl.ds(comp * loads, loads)
        even = (lane_ids(loads) & 1) == 0
        halo[comp] = jnp.where(
            even, zdown[rows, :].astype(F32), roll_lanes(zup[rows, :].astype(F32), -2)
        )
    for copy in copies:
        copy.wait()
    lane8 = lane_ids(8)

    def at(cell, total):
        x = cell // sz.cy
        y = cell - x * sz.cy
        place = (x + 1) * sz.by + y + 1
        back = lax.rem(LANES - 2 * place + LANES, LANES)
        coef = [spread_row(own, j, cell) for j in range(8)]
        parts = {}
        for group in range(groups):
            rows = pl.ds(group * 8, 8)
            center = [box[comp, place, rows, :] for comp in range(comps)]
            coupled = coef[1] * sum(center)
            for comp in range(comps):
                value = center[comp]
                edge = pltpu.roll(halo[comp, rows, :], back, axis=1)
                zm = jnp.where(lane8 == 0, edge, roll_lanes(value, 1))
                zp = jnp.where(lane8 == LANES - 1, edge, roll_lanes(value, -1))
                out = coef[0] * value + coupled
                out = out - coef[2] * box[comp, place - sz.by, rows, :]
                out = out - coef[3] * box[comp, place + sz.by, rows, :]
                out = out - coef[4] * box[comp, place - 1, rows, :]
                out = out - coef[5] * box[comp, place + 1, rows, :]
                out = out - coef[6] * zm
                parts[comp, group] = out - coef[7] * zp
        for comp in range(comps):
            tile = comp * sz.cells + cell
            dir_hi, dir_lo = split_hi_lo(box[comp, place])
            field = jnp.concatenate([parts[comp, group] for group in range(groups)], axis=0)
            field_hi, field_lo = split_hi_lo(field)
            res_hi, res_lo = split_hi_lo(own_rows(sz, res, comp, cell))
            left = jnp.concatenate([dir_hi, dir_lo], axis=0)
            field_both = jnp.concatenate([field_hi, field_lo], axis=0)
            dir_split[tile] = left
            image_split[tile] = field_both
            total = total + lax.dot_general(
                left,
                jnp.concatenate([field_both, res_hi, res_lo], axis=0),
                TRANSPOSED,
                preferred_element_type=F32,
            )
        return total

    total = lax.fori_loop(
        0, sz.cells, at, jnp.zeros((2 * loads, 4 * loads), F32), unroll=4
    )
    high, low = total[:loads], total[loads:]
    sums = high + roll_lanes(high, -loads) + low
    if message.shape[1] == 1:
        for device in range(message.shape[0]):
            message[device] = sums[device : device + 1]
    else:
        for device in range(message.shape[0]):
            message[device] = sums


def add_rows(sz, parts, message):
    total = parts[0]
    for device in range(1, parts.shape[0]):
        total = total + parts[device]
    for device in range(message.shape[0]):
        message[device] = total


def finish(
    sz, sums, iterate, res, dir_split, image_split, new_iterate, new_residual, parts
):
    loads = sz.loads
    if sums.shape[1] == 1:
        system = jnp.concatenate([sums[device] for device in range(sums.shape[0])], axis=0)
    else:
        system = sums[0]
        for device in range(1, sums.shape[0]):
            system = system + sums[device]
    lane = lane_ids(loads)
    system = jnp.where((lane & (2 * loads - 1)) < loads, system, 0.0)
    row_ids = lax.broadcasted_iota(jnp.int32, (loads, LANES), 0)
    for base in range(0, loads, 8):
        columns = [
            jnp.broadcast_to(system[:, i : i + 1], (loads, LANES)) for i in range(base, base + 8)
        ]
        for j in range(8):
            i = base + j
            here = row_ids == i
            scale = 1.0 / columns[j][i : i + 1, :]
            row = system[i : i + 1, :] * scale
            system = jnp.where(here, row, system - columns[j] * row)
            for other in range(j + 1, 8):
                entry = columns[other][i : i + 1, :] * scale
                columns[other] = jnp.where(here, entry, columns[other] - columns[j] * entry)
    step = jnp.transpose(system)[2 * loads : 3 * loads, :]
    padded = jnp.concatenate([step, jnp.zeros((loads, LANES - loads), F32)], axis=1) if (
        step.shape[1] < LANES
    ) else step
    left = paired_left(padded, loads, parts)[:, : 2 * loads]

    def at(cell, carry):
        for comp in range(sz.comps):
            tile = comp * sz.cells + cell
            right = jnp.concatenate([dir_split[tile], image_split[tile]], axis=1)
            part = jnp.dot(left, right, preferred_element_type=F32)
            part = part[:loads] + part[loads:]
            rows = pl.ds(comp * loads * sz.cells + cell, loads, stride=sz.cells)
            new_iterate[rows, :] = iterate[rows, :] + part[:, :LANES]
            new_residual[rows, :] = res[rows, :] - part[:, LANES:]
        return carry

    lax.fori_loop(0, sz.cells, at, 0, unroll=4)


def exchange(low, high, axis):
    devices = lax.axis_size(axis)
    up = [(i, i + 1) for i in range(devices - 1)]
    down = [(j, i) for i, j in up]
    return lax.ppermute(high, axis, up), lax.ppermute(low, axis, down)


def exchange_y(faces, swap):
    if swap:
        got = lax.ppermute(faces[0], "gy", [(0, 1), (1, 0)])
        return got, got
    return exchange(faces[0], faces[1], "gy")


def body(
    iterate, residual, cell_ids, materials, eigen_counts, coarse_rank, eigen_basis, coarse_inverse
):
    sz = Sizes(residual, eigen_basis, coarse_inverse)
    shape = jax.ShapeDtypeStruct
    swap = lax.axis_size("gy") == 2
    devices = 1
    for axis in AXES:
        devices = devices * lax.axis_size(axis)
    blocks = sz.total_rows // sz.block_rows
    scatter = devices == sz.loads
    smem, vmem = pltpu.SMEM, pltpu.VMEM
    res = residual.reshape(-1, LANES)
    old = iterate.reshape(-1, LANES)
    basis = eigen_basis.reshape(-1, LANES)
    ids = cell_ids.reshape(-1, LANES)

    def call(name, kernel, *args, **kwargs):
        return vmem_call(name, lambda *refs: kernel(sz, *refs), *args, **kwargs)

    def call_swap(name, kernel, *args, **kwargs):
        return vmem_call(name, lambda *refs: kernel(sz, swap, *refs), *args, **kwargs)

    face = shape((sz.face_x + 2 * sz.cy, LANES), BF16)
    xlo, xhi = call("pack_x", pack_x, [face, face], [], 16, 1 << 20, 2 << 20, [res, ids])
    below, above = exchange(xlo, xhi, "gx")

    message, split = call(
        "pieces",
        make_pieces,
        [
            shape((devices, sz.loads // 2, LANES), BF16),
            shape((sz.tiles, 2 * sz.slots, LANES), BF16),
        ],
        [pltpu.VMEM((sz.loads, LANES), F32)],
        20,
        1 << 27,
        7 << 20,
        [eigen_counts, coarse_rank, basis, res, xhi],
        spaces=[smem, smem, vmem, vmem, pl.ANY],
    )
    gathered = lax.all_to_all(message, AXES, 0, 0, tiled=True)
    all_counts = gathered[:, 0, sz.slots].astype(jnp.int32)
    all_ranks = gathered[:, 0, sz.slots + 1].astype(jnp.int32)
    starts = jnp.sum(
        all_counts[None, :] * (all_ranks[None, :] < all_ranks[:, None]).astype(jnp.int32), axis=1
    )

    side = [pltpu.VMEM((HALO_IDS, LANES), F32)]
    yface = shape((sz.face_y + HALO_IDS, LANES), BF16)
    faces = call_swap(
        "pack_y", pack_y, [yface] * (1 if swap else 2), side, 16, 1 << 20, 2 << 20,
        [res, ids, below, above],
    )
    ylow, yhigh = exchange_y(faces, swap)
    rows = (sz.cx + 4) * sz.pitch
    zmessage, id_box = call_swap(
        "pack_z",
        pack_z,
        [shape((sz.face_z + HALO_IDS, LANES), BF16), shape((rows, LANES), F32)],
        [pltpu.VMEM((sz.box * 8, LANES), F32), pltpu.VMEM((rows, LANES), F32)],
        16,
        1 << 22,
        3 << 20,
        [res, ids, below, above, ylow, yhigh],
    )
    zdown, zup = exchange(zmessage, zmessage, "col")

    packed = sz.block_rows == 64
    tile = (1, sz.loads // 2, LANES) if packed else (sz.block_rows // LANES, sz.loads, LANES)
    partial = call(
        "coarse",
        place_pieces,
        shape((blocks,) + tile, BF16),
        [
            pltpu.VMEM((sz.total_rows // LANES + 1, sz.loads, LANES), F32),
            pltpu.VMEM((sz.loads, LANES), F32),
        ],
        20,
        1 << 23,
        1 << 20,
        [starts, gathered, coarse_inverse],
        spaces=[smem, vmem, vmem],
    )
    coarse = lax.all_to_all(partial, ("gx", "col"), 0, 0, tiled=True)
    coarse = coarse.reshape((-1,) + tile[1:])

    dface = shape((sz.face_x, LANES), BF16)
    dyface = shape((sz.inner_y, LANES), BF16)
    field = pltpu.VMEM((sz.comps, sz.box, sz.loads, LANES), F32)
    results = call_swap(
        "solve",
        solve_and_direct,
        [shape((sz.comps, sz.cells, sz.loads, LANES), F32), dface, dface]
        + [dyface] * (1 if swap else 2)
        + [shape((sz.face_z, LANES), BF16), shape((8, sz.cells, LANES), F32)],
        [
            field,
            field,
            field,
            pltpu.VMEM((3, sz.comps, sz.loads, LANES), F32),
            pltpu.VMEM((2, sz.comps, sz.loads, LANES), F32),
            pltpu.VMEM((9, rows, LANES), F32),
            pltpu.VMEM((9, 8, LANES), F32),
            pltpu.VMEM((rows, LANES), F32),
            pltpu.VMEM((rows, LANES), F32),
            pltpu.VMEM((2 * sz.loads, LANES), BF16),
            pltpu.VMEM((sz.face_z, LANES), F32),
        ],
        28,
        1 << 28,
        8 << 20,
        [
            starts, eigen_counts, materials, res, below, above, ylow, yhigh, zdown, zup, id_box,
            coarse, split,
        ],
        spaces=[smem, smem, smem] + [vmem] * 10,
    )
    direction, dxlo, dxhi = results[:3]
    dfaces, zface, own = results[3:-2], results[-2], results[-1]
    dbelow, dabove = exchange(dxlo, dxhi, "gx")
    dylow, dyhigh = exchange_y(dfaces, swap)
    dzdown, dzup = exchange(zface, zface, "col")

    dir_split, image_split, energy = call_swap(
        "image",
        make_image,
        [
            shape((sz.tiles, 2 * sz.loads, LANES), BF16),
            shape((sz.tiles, 2 * sz.loads, LANES), BF16),
            shape((devices, 1 if scatter else sz.loads, LANES), F32),
        ],
        [
            field,
            pltpu.VMEM((sz.comps, sz.loads, LANES), F32),
            pltpu.SemaphoreType.DMA((sz.comps, sz.cx)),
        ],
        20,
        1 << 28,
        8 << 20,
        [res, own, direction, dbelow, dabove, dylow, dyhigh, dzdown, dzup],
        spaces=[vmem, vmem, pl.ANY] + [vmem] * 6,
    )
    sums = lax.all_to_all(energy, AXES, 0, 0, tiled=True)
    if scatter:
        whole = call(
            "add_rows", add_rows, shape(sums.shape, F32), [], 4, 1 << 12, 1 << 15, [sums]
        )
        sums = lax.all_to_all(whole, AXES, 0, 0, tiled=True)
    flat = shape(res.shape, F32)
    new_iterate, new_residual = call(
        "finish",
        finish,
        [flat, flat],
        [pltpu.VMEM((2 * sz.loads, LANES), BF16)],
        20,
        1 << 27,
        9 << 20,
        [sums, old, res, dir_split, image_split],
    )
    return (new_iterate.reshape(iterate.shape), new_residual.reshape(residual.shape))


def solution(mesh):
    placed = (
        P(None, None, "gx", "gy", "col"),
        P(None, None, "gx", "gy", "col"),
        P("gx", "gy", "col"),
        P(),
        P(("gx", "gy", "col")),
        P(("gx", "gy", "col")),
        P(None, None, "gx", "gy", "col"),
        P(("gx", "col"), None),
    )
    return jax.shard_map(
        body,
        mesh=mesh,
        in_specs=placed,
        out_specs=(P(None, None, "gx", "gy", "col"), P(None, None, "gx", "gy", "col")),
        check_vma=False,
    )
```

```python
import jax
import jax.numpy as jnp
from jax import lax
from jax.experimental import pallas as pl
from jax.experimental.pallas import tpu as pltpu
from jax.sharding import PartitionSpec as P

DAMPING = 0.6
F32 = jnp.float32
BF16 = jnp.bfloat16
LANES = 128
HALO_IDS = 16
AXES = ("gx", "gy", "col")
TRANSPOSED = (((1,), (1,)), ((), ()))


def split_hi_lo(value):
    hi = value.astype(BF16)
    return hi, (value - hi.astype(F32)).astype(BF16)


def paired_left(value, width, parts):
    rows = value.shape[0]
    hi, lo = split_hi_lo(value)
    parts[pl.ds(0, rows), :] = hi
    parts[pl.ds(rows, rows), :] = lo
    high = parts[pl.ds(0, rows), :].astype(F32)
    low = parts[pl.ds(rows, rows), :].astype(F32)
    return jnp.concatenate([high + roll_lanes(high, width), low], axis=0).astype(BF16)


def lane_ids(rows):
    return lax.broadcasted_iota(jnp.int32, (rows, LANES), 1)


def roll_lanes(value, shift):
    if isinstance(shift, int):
        shift = shift % LANES
        if shift == 0:
            return value
    return pltpu.roll(value, shift, axis=1)


def vmem_call(name, kernel, outs, scratch, limit_mib, flops, moved, operands, spaces=None):
    spaces = spaces or [pltpu.VMEM] * len(operands)
    return pl.pallas_call(
        kernel,
        name=name,
        out_shape=outs,
        in_specs=[pl.BlockSpec(memory_space=space) for space in spaces],
        out_specs=jax.tree.map(lambda _: pl.BlockSpec(memory_space=pltpu.VMEM), outs),
        scratch_shapes=scratch,
        compiler_params=pltpu.CompilerParams(vmem_limit_bytes=limit_mib << 20),
        cost_estimate=pl.CostEstimate(flops=flops, bytes_accessed=moved, transcendentals=0),
    )(*operands)


def own_index():
    index = 0
    for axis in AXES:
        index = index * lax.axis_size(axis) + lax.axis_index(axis)
    return index


class Sizes:
    def __init__(self, residual, eigen_basis, coarse_inverse):
        self.comps, self.loads, self.cx, self.cy, _ = residual.shape
        self.slots = eigen_basis.shape[0]
        self.block_rows, self.total_rows = coarse_inverse.shape
        self.cells = self.cx * self.cy
        self.bx, self.by = self.cx + 2, self.cy + 2
        self.box = self.bx * self.by
        self.tiles = self.comps * self.cells
        self.face_x = self.comps * self.cy * self.loads
        self.face_y = self.comps * self.bx * self.loads
        self.inner_y = self.comps * self.cx * self.loads
        self.face_z = self.comps * self.loads
        self.pitch = 16


class Halo:
    def __init__(self, axis, refs):
        self.refs = refs
        self.even = lax.rem(lax.axis_index(axis), 2) == 0

    def side(self, rows, first):
        value = self.refs[0][rows, :].astype(F32)
        other = self.refs[1][rows, :].astype(F32) if len(self.refs) > 1 else jnp.zeros_like(value)
        return jnp.where(self.even, value, other) if first else jnp.where(self.even, other, value)

    def below(self, rows):
        return self.side(rows, False)

    def above(self, rows):
        return self.side(rows, True)

    def send(self, rows, low, high):
        self.refs[0][rows, :] = jnp.where(self.even, high, low).astype(BF16)
        if len(self.refs) > 1:
            self.refs[1][rows, :] = jnp.where(self.even, low, high).astype(BF16)


def swaps(axis):
    return 1 if lax.axis_size(axis) == 2 else 2


def exchange(faces, axis):
    devices = lax.axis_size(axis)
    result = []
    for parity in range(swaps(axis)):
        pairs = []
        for low in range(parity, devices - 1, 2):
            pairs += [(low, low + 1), (low + 1, low)]
        result.append(lax.ppermute(faces[parity], axis, pairs))
    return result


def take_halos(refs, *axes):
    refs = list(refs)
    halos = []
    for axis in axes:
        count = swaps(axis)
        halos.append(Halo(axis, refs[:count]))
        refs = refs[count:]
    return halos + [refs]


def own_rows(sz, ref, comp, cell):
    start = comp * sz.loads * sz.cells + cell
    return ref[pl.ds(start, sz.loads, stride=sz.cells), :]


def pack_x(sz, res, ids, *refs):
    xsend, (low, high, id_rows, sem) = take_halos(refs, "gx")
    copies = [
        pltpu.make_async_copy(res.at[:, pl.ds(0, sz.cy)], low, sem.at[0]),
        pltpu.make_async_copy(res.at[:, pl.ds(sz.cells - sz.cy, sz.cy)], high, sem.at[1]),
        pltpu.make_async_copy(ids, id_rows, sem.at[2]),
    ]
    for copy in copies:
        copy.start()
    for copy in copies:
        copy.wait()
    low, high = (ref.reshape(sz.comps * sz.loads * sz.cy, LANES) for ref in (low, high))
    for comp in range(sz.comps):
        for y in range(sz.cy):
            rows = pl.ds((comp * sz.cy + y) * sz.loads, sz.loads)
            taken = pl.ds(comp * sz.loads * sz.cy + y, sz.loads, stride=sz.cy)
            xsend.send(rows, low[taken, :], high[taken, :])
    two = 2 * sz.cy
    first = (id_rows[pl.ds(0, two), :] + 1).astype(F32)
    last = (id_rows[pl.ds(sz.cells - two, two), :] + 1).astype(F32)
    xsend.send(pl.ds(sz.face_x, two), first, last)


def make_pieces(
    sz, count, rank, basis_in, res_in, after, message, split, wide, basis_rows, res_rows, sem
):
    del after
    slots, loads = sz.slots, sz.loads
    copies = []
    for comp in range(sz.comps):
        part = pl.ds(comp * sz.cells, sz.cells)
        copies.append(
            (
                pltpu.make_async_copy(
                    basis_in.at[:, part], basis_rows.at[:, part], sem.at[0, comp]
                ),
                pltpu.make_async_copy(res_in.at[comp], res_rows.at[comp], sem.at[1, comp]),
            )
        )
    for pair in copies:
        for copy in pair:
            copy.start()
    basis = basis_rows.reshape(slots * sz.tiles, LANES)
    res = res_rows.reshape(sz.tiles * loads, LANES)

    def step(index, carry):
        both, low = carry
        basis_hi, basis_lo, res_hi, res_both = [], [], [], []
        for half in range(2):
            tile = index * 2 + half
            comp = tile // sz.cells
            hi, lo = split_hi_lo(basis[pl.ds(tile, slots, stride=sz.tiles), :])
            split[tile, pl.ds(0, slots), :] = hi
            split[tile, pl.ds(slots, slots), :] = lo
            value_hi, value_lo = split_hi_lo(own_rows(sz, res, comp, tile - comp * sz.cells))
            basis_hi.append(hi)
            basis_lo.append(lo)
            res_hi.append(value_hi)
            res_both.append(jnp.concatenate([value_hi, value_lo], axis=0))
        both = both + lax.dot_general(
            jnp.concatenate(res_both, axis=1),
            jnp.concatenate(basis_hi, axis=1),
            TRANSPOSED,
            preferred_element_type=F32,
        )
        low = low + lax.dot_general(
            jnp.concatenate(res_hi, axis=1),
            jnp.concatenate(basis_lo, axis=1),
            TRANSPOSED,
            preferred_element_type=F32,
        )
        return both, low

    carry = (jnp.zeros((2 * loads, slots), F32), jnp.zeros((loads, slots), F32))
    for comp in range(sz.comps):
        for copy in copies[comp]:
            copy.wait()
        carry = lax.fori_loop(
            comp * sz.cells // 2, (comp + 1) * sz.cells // 2, step, carry, unroll=4
        )
    both, low = carry
    pieces = both[:loads] + both[loads:] + low
    slot = lax.broadcasted_iota(jnp.int32, pieces.shape, 1)
    wide[...] = jnp.zeros_like(wide)
    wide[:, pl.ds(0, slots)] = jnp.where(slot < count[0], pieces, 0.0)
    half = loads // 2
    lane = lane_ids(half)
    packed = jnp.where(lane < 64, wide[:half, :], roll_lanes(wide[half:, :], 64))
    packed = jnp.where(lane == slots, count[0].astype(F32), packed)
    packed = jnp.where(lane == slots + 1, rank[0].astype(F32), packed)
    message[...] = packed.astype(BF16)


def pack_y(sz, res, ids, packed, *refs):
    xhalo, refs = take_halos(refs, "gx")
    message = refs[0]
    ysend, (side_low, side_high) = take_halos(refs[1:], "gy")
    for device in range(message.shape[0]):
        message[device] = packed[...]
    last = sz.cy - 1
    for comp in range(sz.comps):
        for x in range(sz.bx):
            rows = pl.ds((comp * sz.bx + x) * sz.loads, sz.loads)
            if 0 < x < sz.bx - 1:
                low, high = (own_rows(sz, res, comp, (x - 1) * sz.cy + y) for y in (0, last))
            else:
                side = xhalo.below if x == 0 else xhalo.above
                low, high = (
                    side(pl.ds((comp * sz.cy + y) * sz.loads, sz.loads)) for y in (0, last)
                )
            ysend.send(rows, low, high)
    ids_below = xhalo.below(pl.ds(sz.face_x, 2 * sz.cy))
    ids_above = xhalo.above(pl.ds(sz.face_x, 2 * sz.cy))
    for x in range(sz.cx + 4):
        if x < 2:
            rows = ids_below[x * sz.cy : (x + 1) * sz.cy]
        elif x >= sz.cx + 2:
            rows = ids_above[(x - sz.cx - 2) * sz.cy : (x - sz.cx - 1) * sz.cy]
        else:
            rows = (ids[pl.ds((x - 2) * sz.cy, sz.cy), :] + 1).astype(F32)
        side_low[pl.ds(2 * x, 2), :] = rows[:2]
        side_high[pl.ds(2 * x, 2), :] = rows[sz.cy - 2 :]
    ysend.send(pl.ds(sz.face_y, HALO_IDS), side_low[...], side_high[...])


def box_tile(sz, res, xhalo, yhalo, comp, x, y):
    if y == 0 or y == sz.by - 1:
        side = yhalo.below if y == 0 else yhalo.above
        return side(pl.ds((comp * sz.bx + x) * sz.loads, sz.loads))
    if x == 0 or x == sz.bx - 1:
        side = xhalo.below if x == 0 else xhalo.above
        return side(pl.ds((comp * sz.cy + y - 1) * sz.loads, sz.loads))
    return own_rows(sz, res, comp, (x - 1) * sz.cy + y - 1)


def pack_z(sz, res, ids, *refs):
    xhalo, yhalo, (out, id_box, star, outer) = take_halos(refs, "gx", "gy")
    pitch = sz.pitch
    id_box[...] = jnp.zeros_like(id_box)
    two = 2 * sz.cy
    ids_below = xhalo.below(pl.ds(sz.face_x, two))
    ids_above = xhalo.above(pl.ds(sz.face_x, two))
    ids_low = yhalo.below(pl.ds(sz.face_y, HALO_IDS))
    ids_high = yhalo.above(pl.ds(sz.face_y, HALO_IDS))
    for x in range(sz.cx + 4):
        if x < 2:
            rows = ids_below[x * sz.cy : (x + 1) * sz.cy]
        elif x >= sz.cx + 2:
            rows = ids_above[(x - sz.cx - 2) * sz.cy : (x - sz.cx - 1) * sz.cy]
        else:
            rows = (ids[pl.ds((x - 2) * sz.cy, sz.cy), :] + 1).astype(F32)
        id_box[pl.ds(x * pitch + 2, sz.cy), :] = rows
        id_box[pl.ds(x * pitch, 2), :] = ids_low[2 * x : 2 * x + 2]
        id_box[pl.ds(x * pitch + sz.cy + 2, 2), :] = ids_high[2 * x : 2 * x + 2]
    values = id_box[...]
    lane = lane_ids(values.shape[0])
    outer[...] = jnp.where(lane == LANES - 1, roll_lanes(values, 1), roll_lanes(values, -1))
    star[...] = jnp.zeros_like(star)
    lane8 = lane_ids(8)
    taken = jnp.zeros((8, LANES), F32)
    for x in range(sz.bx):
        for y in range(sz.by):
            place = x * sz.by + y
            row = (x + 1) * pitch + y + 1
            for j, shift in enumerate((0, -pitch, pitch, -1, 1)):
                star[pl.ds(place * 8 + j, 1), :] = id_box[pl.ds(row + shift, 1), :]
            star[pl.ds(place * 8 + 5, 1), :] = outer[pl.ds(row, 1), :]
    for place in range(sz.box):
        picked = roll_lanes(star[pl.ds(place * 8, 8), :], 2 * place + 1)
        taken = jnp.where((lane8 >> 1) == place, picked, taken)
    out[pl.ds(sz.face_z, HALO_IDS), :] = jnp.concatenate(
        [taken, jnp.zeros((HALO_IDS - 8, LANES), F32)], axis=0
    ).astype(BF16)
    lane_k = lane_ids(sz.loads)
    for comp in range(sz.comps):
        total = jnp.zeros((sz.loads, LANES), F32)
        for x in range(sz.bx):
            for y in range(sz.by):
                place = x * sz.by + y
                tile = box_tile(sz, res, xhalo, yhalo, comp, x, y)
                total = jnp.where(
                    (lane_k >> 1) == place, roll_lanes(tile, 2 * place + 1), total
                )
        out[pl.ds(comp * sz.loads, sz.loads), :] = total.astype(BF16)


def place_pieces(sz, starts, gathered, inverse, message, vector, wide):
    half = sz.loads // 2
    lane = lane_ids(half)
    vector[...] = jnp.zeros_like(vector)

    def place(device, carry):
        start = starts[device]
        block = start // LANES
        offset = start - block * LANES
        packed = gathered[device].astype(F32)
        low = jnp.where(lane < sz.slots, packed, 0.0)
        high = jnp.where((lane >= 64) & (lane < 64 + sz.slots), packed, 0.0)
        both = jnp.concatenate(
            [
                pltpu.roll(low, offset, axis=1),
                pltpu.roll(high, lax.rem(offset + 64, LANES), axis=1),
            ],
            axis=0,
        )
        wide_lane = lane_ids(sz.loads)
        vector[block] = vector[block] + jnp.where(wide_lane >= offset, both, 0.0)
        vector[block + 1] = vector[block + 1] + jnp.where(wide_lane < offset, both, 0.0)
        return carry

    lax.fori_loop(0, gathered.shape[0], place, 0, unroll=8)
    total = jnp.zeros((sz.loads, sz.block_rows), F32)
    for block in range(sz.total_rows // LANES):
        total = total + lax.dot_general(
            vector[block].astype(BF16),
            inverse[:, pl.ds(block * LANES, LANES)],
            TRANSPOSED,
            preferred_element_type=F32,
        )
    if sz.block_rows == 64:
        wide[...] = jnp.zeros_like(wide)
        wide[:, pl.ds(0, 64)] = total
        packed = jnp.where(lane < 64, wide[:half, :], roll_lanes(wide[half:, :], 64))
        for device in range(message.shape[0]):
            message[device, 0] = packed
    else:
        for device in range(message.shape[0]):
            for block in range(sz.block_rows // LANES):
                message[device, block] = total[:, block * LANES : (block + 1) * LANES]


def own_coefs(sz, coefs, start):
    if sz.block_rows == 64:
        half = sz.loads // 2
        block = start // 64
        offset = start - block * 64
        first = coefs[block]
        second = coefs[jnp.minimum(block + 1, coefs.shape[0] - 1)]
        lane = lane_ids(half)
        top = jnp.where(lane < 64, first, roll_lanes(second, 64))
        bottom = jnp.where(lane < 64, roll_lanes(first, 64), second)
        both = jnp.concatenate([top, bottom], axis=0)
    else:
        block = start // LANES
        offset = start - block * LANES
        first = coefs[block]
        second = coefs[jnp.minimum(block + 1, coefs.shape[0] - 1)]
        both = jnp.where(lane_ids(sz.loads) >= offset, first, second)
    return pltpu.roll(both, lax.rem(LANES - offset, LANES), axis=1)


def look_up(table, row, ids):
    result = jnp.zeros_like(ids)
    for material in range(table.shape[1]):
        result = jnp.where(ids == material + 1, table[row, material], result)
    return result


DINV, KEEP, DLAM, WXM, WXP, WYM, WYP, WZM, WZP = range(9)


def spread_row(ref, index, row):
    return jnp.broadcast_to(ref[index, pl.ds(row, 1), :], (8, LANES))


def make_coefs(sz, table, id_box, halo_ids, coefs, halo_coefs, own, mu_box, halo_mu):
    pitch = sz.pitch
    mu_box[...] = look_up(table, 0, id_box[...])
    lam_box = look_up(table, 1, id_box[...])
    mu_halo = look_up(table, 0, halo_ids)
    lam_halo = look_up(table, 1, halo_ids)
    lane8 = lane_ids(8)
    center = jnp.broadcast_to(mu_halo[0:1], (8, LANES))
    inner = jnp.zeros((8, LANES), F32)
    for place in range(sz.box):
        row = (place // sz.by + 1) * pitch + place % sz.by + 1
        halo_mu[pl.ds(row, 1), :] = roll_lanes(center, -2 * place)[0:1]
        spread = jnp.broadcast_to(mu_box[pl.ds(row, 1), :], (8, LANES))
        here = (((lane8 + 1) >> 1) & 63) == place
        inner = jnp.where(here, roll_lanes(spread, 2 * place), inner)
    rows_id = lax.broadcasted_iota(jnp.int32, (pitch, LANES), 0)
    lane = lane_ids(pitch)
    for x in range(1, sz.bx + 1):
        mu = mu_box[pl.ds(x * pitch, pitch), :]
        edge = halo_mu[pl.ds(x * pitch, pitch), :]
        lam = lam_box[x * pitch : (x + 1) * pitch]
        faces = [
            0.5 * (mu + mu_box[pl.ds((x - 1) * pitch, pitch), :]),
            0.5 * (mu + mu_box[pl.ds((x + 1) * pitch, pitch), :]),
            0.5 * (mu + mu_box[pl.ds(x * pitch - 1, pitch), :]),
            0.5 * (mu + mu_box[pl.ds(x * pitch + 1, pitch), :]),
            0.5 * (mu + jnp.where(lane == 0, edge, roll_lanes(mu, 1))),
            0.5 * (mu + jnp.where(lane == LANES - 1, edge, roll_lanes(mu, -1))),
        ]
        diag = 1.0 + sum(faces)
        dinv = DAMPING / (diag + lam)
        rows = pl.ds(x * pitch, pitch)
        coefs[DINV, rows, :] = dinv
        coefs[KEEP, rows, :] = (1.0 - DAMPING) + dinv * lam
        coefs[DLAM, rows, :] = dinv * lam
        weights = [dinv * face for face in faces]
        if x == 1:
            weights[0] = jnp.zeros_like(dinv)
        if x == sz.bx:
            weights[1] = jnp.zeros_like(dinv)
        weights[2] = jnp.where(rows_id == 1, 0.0, weights[2])
        weights[3] = jnp.where(rows_id == sz.by, 0.0, weights[3])
        for j in range(6):
            coefs[WXM + j, rows, :] = weights[j]
        if 2 <= x <= sz.cx + 1:
            target = pl.ds((x - 2) * sz.cy, sz.cy)
            for j, value in enumerate([diag, lam] + faces):
                own[j, target, :] = value[2 : 2 + sz.cy]
    place = ((lane8 + 1) >> 1) & 63
    column = jnp.zeros_like(place)
    for x in range(1, sz.bx):
        column = column + (place >= x * sz.by).astype(jnp.int32)
    y_place = place - column * sz.by
    others = [jnp.broadcast_to(mu_halo[j : j + 1], (8, LANES)) for j in range(1, 6)]
    faces = [0.5 * (center + other) for other in others] + [0.5 * (center + inner)]
    lam = jnp.broadcast_to(lam_halo[0:1], (8, LANES))
    dinv = DAMPING / (1.0 + lam + sum(faces))
    live = place < sz.box
    keep = [
        live & (column > 0),
        live & (column < sz.bx - 1),
        live & (y_place > 0),
        live & (y_place < sz.by - 1),
        None,
        live,
    ]
    halo_coefs[DINV] = dinv
    halo_coefs[KEEP] = (1.0 - DAMPING) + dinv * lam
    halo_coefs[DLAM] = dinv * lam
    for j, target in ((0, WXM), (1, WXP), (2, WYM), (3, WYP), (5, WZM)):
        halo_coefs[target] = jnp.where(keep[j], dinv * faces[j], 0.0)


def z_halo(zhalo, rows):
    down, up = zhalo.below(rows), zhalo.above(rows)
    even = (lane_ids(down.shape[0]) & 1) == 0
    return jnp.where(even, down, roll_lanes(up, -2))


def solve_and_direct(sz, starts, count, table, res, id_box, coarse, split, *refs):
    xhalo, yhalo, zhalo, refs = take_halos(refs, "gx", "gy", "col")
    direction, own, zface = refs[:3]
    xsend, ysend, refs = take_halos(refs[3:], "gx", "gy")
    first, second, third, halos, inner, coefs, halo_coefs, mu_box, halo_mu, left, zedge = refs
    loads, comps = sz.loads, sz.comps
    groups = loads // 8
    lane8 = lane_ids(8)

    halo_mu[...] = jnp.zeros_like(halo_mu)
    inner[1] = jnp.zeros((comps, loads, LANES), F32)
    make_coefs(
        sz, table, id_box, z_halo(zhalo, pl.ds(sz.face_z, HALO_IDS))[:8], coefs, halo_coefs, own,
        mu_box, halo_mu,
    )

    def here_of(place):
        return (((lane8 + 1) >> 1) & 63) == place

    for comp in range(comps):
        halo = z_halo(zhalo, pl.ds(comp * loads, loads))
        dinv = jnp.concatenate([halo_coefs[DINV]] * groups, axis=0)
        halos[0, comp] = dinv * halo
        total = jnp.zeros((loads, LANES), F32)
        lane_k = lane_ids(loads)
        for x in range(sz.bx):
            for y in range(sz.by):
                place = x * sz.by + y
                row = (x + 1) * sz.pitch + y + 1
                tile = box_tile(sz, res, xhalo, yhalo, comp, x, y)
                value = tile * jnp.broadcast_to(coefs[DINV, pl.ds(row, 1), :], (loads, LANES))
                first[comp, place] = value
                here = (((lane_k + 1) >> 1) & 63) == place
                total = jnp.where(here, roll_lanes(value, 2 * place), total)
        inner[0, comp] = total

    def relax(source, level, place, row):
        coef = [spread_row(coefs, j, row) for j in range(9)]
        xm, xp = jnp.maximum(place - sz.by, 0), jnp.minimum(place + sz.by, sz.box - 1)
        ym, yp = jnp.maximum(place - 1, 0), jnp.minimum(place + 1, sz.box - 1)
        back = lax.rem(LANES - 2 * place + LANES, LANES)
        result = {}
        for group in range(groups):
            rows = pl.ds(group * 8, 8)
            center = [source[comp, place, rows, :] for comp in range(comps)]
            coupled = coef[DLAM] * sum(center)
            for comp in range(comps):
                value = center[comp]
                edge = pltpu.roll(halos[level, comp, rows, :], back, axis=1)
                zm = jnp.where(lane8 == 0, edge, roll_lanes(value, 1))
                zp = jnp.where(lane8 == LANES - 1, edge, roll_lanes(value, -1))
                out = (first[comp, place, rows, :] - coupled) + coef[KEEP] * value
                out = out + coef[WXM] * source[comp, xm, rows, :]
                out = out + coef[WXP] * source[comp, xp, rows, :]
                out = out + coef[WYM] * source[comp, ym, rows, :]
                out = out + coef[WYP] * source[comp, yp, rows, :]
                out = out + coef[WZM] * zm
                out = out + coef[WZP] * zp
                result[comp, group] = out
        return result

    def sweep(source, target, level):
        def at(place, carry):
            x = place // sz.by
            row = (x + 1) * sz.pitch + place - x * sz.by + 1
            result = relax(source, level, place, row)
            for (comp, group), out in result.items():
                rows = pl.ds(group * 8, 8)
                target[comp, place, rows, :] = out
                if level == 0:
                    pltpu.store(
                        inner.at[1, comp, rows, :],
                        pltpu.roll(out, 2 * place, axis=1),
                        mask=here_of(place),
                    )
            return carry

        lax.fori_loop(0, sz.box, at, 0, unroll=6)
        coef = [halo_coefs[j] for j in range(8)]
        for group in range(groups):
            rows = pl.ds(group * 8, 8)
            center = [halos[level, comp, rows, :] for comp in range(comps)]
            coupled = coef[DLAM] * sum(center)
            for comp in range(comps):
                value = center[comp]
                out = (halos[0, comp, rows, :] - coupled) + coef[KEEP] * value
                out = out + coef[WXM] * roll_lanes(value, 2 * sz.by)
                out = out + coef[WXP] * roll_lanes(value, -2 * sz.by)
                out = out + coef[WYM] * roll_lanes(value, 2)
                out = out + coef[WYP] * roll_lanes(value, -2)
                out = out + coef[WZM] * inner[level, comp, rows, :]
                halos[level + 1, comp, rows, :] = out

    sweep(first, second, 0)
    sweep(second, third, 1)

    mine = own_coefs(sz, coarse, starts[own_index()])
    mine = jnp.where(lane_ids(loads) < jnp.minimum(count[0], sz.slots), mine, 0.0)
    left[...] = paired_left(mine, sz.slots, left)
    zedge[...] = jnp.zeros_like(zedge)

    def final(cell, carry):
        x = cell // sz.cy
        y = cell - x * sz.cy
        place = (x + 1) * sz.by + y + 1
        result = relax(third, 2, place, (x + 2) * sz.pitch + y + 2)
        for comp in range(comps):
            tile = comp * sz.cells + cell
            part = jnp.dot(
                left[:, : 2 * sz.slots], split[tile], preferred_element_type=F32
            )
            for group in range(groups):
                rows = pl.ds(group * 8, 8)
                value = result[comp, group] + (
                    part[group * 8 : group * 8 + 8]
                    + part[loads + group * 8 : loads + group * 8 + 8]
                )
                direction[comp, cell, rows, :] = value
                zrows = pl.ds(comp * loads + group * 8, 8)
                pltpu.store(
                    zedge.at[zrows, :],
                    pltpu.roll(value, 2 * place + 1, axis=1),
                    mask=(lane8 >> 1) == place,
                )
        return carry

    lax.fori_loop(0, sz.cells, final, 0, unroll=4)
    zface[...] = zedge[...].astype(BF16)
    for comp in range(comps):
        for y in range(sz.cy):
            rows = pl.ds((comp * sz.cy + y) * loads, loads)
            xsend.send(rows, direction[comp, y], direction[comp, (sz.cx - 1) * sz.cy + y])
        for x in range(sz.cx):
            rows = pl.ds((comp * sz.cx + x) * loads, loads)
            ysend.send(rows, direction[comp, x * sz.cy], direction[comp, (x + 1) * sz.cy - 1])


def make_image(sz, res, own, direction, *refs):
    xhalo, yhalo, zhalo, refs = take_halos(refs, "gx", "gy", "col")
    dir_split, image_split, message, box, halo, sem = refs
    loads, comps = sz.loads, sz.comps
    groups = loads // 8
    copies = []
    for comp in range(comps):
        for x in range(sz.cx):
            copies.append(
                pltpu.make_async_copy(
                    direction.at[comp, pl.ds(x * sz.cy, sz.cy)],
                    box.at[comp, pl.ds((x + 1) * sz.by + 1, sz.cy)],
                    sem.at[comp, x],
                )
            )
    for copy in copies:
        copy.start()
    for comp in range(comps):
        for y in range(sz.cy):
            rows = pl.ds((comp * sz.cy + y) * loads, loads)
            box[comp, y + 1] = xhalo.below(rows)
            box[comp, (sz.bx - 1) * sz.by + y + 1] = xhalo.above(rows)
        for x in range(sz.cx):
            rows = pl.ds((comp * sz.cx + x) * loads, loads)
            box[comp, (x + 1) * sz.by] = yhalo.below(rows)
            box[comp, (x + 1) * sz.by + sz.by - 1] = yhalo.above(rows)
        halo[comp] = z_halo(zhalo, pl.ds(comp * loads, loads))
    for copy in copies:
        copy.wait()
    lane8 = lane_ids(8)

    def at(cell, total):
        x = cell // sz.cy
        y = cell - x * sz.cy
        place = (x + 1) * sz.by + y + 1
        back = lax.rem(LANES - 2 * place + LANES, LANES)
        coef = [spread_row(own, j, cell) for j in range(8)]
        parts = {}
        for group in range(groups):
            rows = pl.ds(group * 8, 8)
            center = [box[comp, place, rows, :] for comp in range(comps)]
            coupled = coef[1] * sum(center)
            for comp in range(comps):
                value = center[comp]
                edge = pltpu.roll(halo[comp, rows, :], back, axis=1)
                zm = jnp.where(lane8 == 0, edge, roll_lanes(value, 1))
                zp = jnp.where(lane8 == LANES - 1, edge, roll_lanes(value, -1))
                out = coef[0] * value + coupled
                out = out - coef[2] * box[comp, place - sz.by, rows, :]
                out = out - coef[3] * box[comp, place + sz.by, rows, :]
                out = out - coef[4] * box[comp, place - 1, rows, :]
                out = out - coef[5] * box[comp, place + 1, rows, :]
                out = out - coef[6] * zm
                parts[comp, group] = out - coef[7] * zp
        for comp in range(comps):
            tile = comp * sz.cells + cell
            dir_hi, dir_lo = split_hi_lo(box[comp, place])
            field = jnp.concatenate([parts[comp, group] for group in range(groups)], axis=0)
            field_hi, field_lo = split_hi_lo(field)
            res_hi, res_lo = split_hi_lo(own_rows(sz, res, comp, cell))
            left = jnp.concatenate([dir_hi, dir_lo], axis=0)
            field_both = jnp.concatenate([field_hi, field_lo], axis=0)
            dir_split[tile] = left
            image_split[tile] = field_both
            total = total + lax.dot_general(
                left,
                jnp.concatenate([field_both, res_hi, res_lo], axis=0),
                TRANSPOSED,
                preferred_element_type=F32,
            )
        return total

    total = lax.fori_loop(
        0, sz.cells, at, jnp.zeros((2 * loads, 4 * loads), F32), unroll=4
    )
    high, low = total[:loads], total[loads:]
    sums = high + roll_lanes(high, -loads) + low
    half = loads // 2
    lane = lane_ids(half)
    packed = jnp.where((lane & (2 * loads - 1)) < loads, sums[:half], roll_lanes(sums[half:], loads))
    message[...] = packed


def share_sums(sz, mine, *refs):
    message = refs[-1]
    total = mine[...]
    for other in refs[:-1]:
        total = total + other[...]
    for device in range(message.shape[0]):
        message[device] = total


def finish(
    sz, sums, iterate, res, dir_split, image_split, new_iterate, new_residual, parts
):
    loads = sz.loads
    total = sums[0]
    for device in range(1, sums.shape[0]):
        total = total + sums[device]
    system = jnp.concatenate([total, roll_lanes(total, -loads)], axis=0)
    lane = lane_ids(loads)
    system = jnp.where((lane & (2 * loads - 1)) < loads, system, 0.0)
    row_ids = lax.broadcasted_iota(jnp.int32, (loads, LANES), 0)
    for base in range(0, loads, 8):
        columns = [
            jnp.broadcast_to(system[:, i : i + 1], (loads, LANES)) for i in range(base, base + 8)
        ]
        for j in range(8):
            i = base + j
            here = row_ids == i
            scale = 1.0 / columns[j][i : i + 1, :]
            row = system[i : i + 1, :] * scale
            system = jnp.where(here, row, system - columns[j] * row)
            for other in range(j + 1, 8):
                entry = columns[other][i : i + 1, :] * scale
                columns[other] = jnp.where(here, entry, columns[other] - columns[j] * entry)
    step = jnp.transpose(system)[2 * loads : 3 * loads, :]
    padded = jnp.concatenate([step, jnp.zeros((loads, LANES - loads), F32)], axis=1) if (
        step.shape[1] < LANES
    ) else step
    left = paired_left(padded, loads, parts)[:, : 2 * loads]

    def at(cell, carry):
        for comp in range(sz.comps):
            tile = comp * sz.cells + cell
            right = jnp.concatenate([dir_split[tile], image_split[tile]], axis=1)
            part = jnp.dot(left, right, preferred_element_type=F32)
            part = part[:loads] + part[loads:]
            rows = pl.ds(comp * loads * sz.cells + cell, loads, stride=sz.cells)
            new_iterate[rows, :] = iterate[rows, :] + part[:, :LANES]
            new_residual[rows, :] = res[rows, :] - part[:, LANES:]
        return carry

    lax.fori_loop(0, sz.cells, at, 0, unroll=4)


def body(
    iterate, residual, cell_ids, materials, eigen_counts, coarse_rank, eigen_basis, coarse_inverse
):
    sz = Sizes(residual, eigen_basis, coarse_inverse)
    shape = jax.ShapeDtypeStruct
    devices = 1
    for axis in AXES:
        devices = devices * lax.axis_size(axis)
    blocks = sz.total_rows // sz.block_rows
    smem, vmem, scratch, dma = pltpu.SMEM, pltpu.VMEM, pltpu.VMEM, pltpu.SemaphoreType.DMA
    res = residual.reshape(-1, LANES)
    old = iterate.reshape(-1, LANES)
    ids = cell_ids.reshape(-1, LANES)

    def call(name, kernel, *args, **kwargs):
        return vmem_call(name, lambda *refs: kernel(sz, *refs), *args, **kwargs)

    face = shape((sz.face_x + 2 * sz.cy, LANES), BF16)
    faces = call(
        "pack_x",
        pack_x,
        [face] * swaps("gx"),
        [scratch((sz.comps * sz.loads, sz.cy, LANES), F32)] * 2
        + [scratch((sz.cells, LANES), jnp.int32), dma((3,))],
        8,
        1 << 20,
        2 << 20,
        [residual.reshape(-1, sz.cells, LANES), ids],
        spaces=[pl.ANY, pl.ANY],
    )
    xhalo = exchange(faces, "gx")

    packed, split = call(
        "pieces",
        make_pieces,
        [
            shape((sz.loads // 2, LANES), BF16),
            shape((sz.tiles, 2 * sz.slots, LANES), BF16),
        ],
        [
            scratch((sz.loads, LANES), F32),
            scratch((sz.slots, sz.tiles, LANES), F32),
            scratch((sz.comps, sz.loads * sz.cells, LANES), F32),
            dma((2, sz.comps)),
        ],
        12,
        1 << 27,
        7 << 20,
        [
            eigen_counts,
            coarse_rank,
            eigen_basis.reshape(sz.slots, sz.tiles, LANES),
            residual.reshape(sz.comps, -1, LANES),
            faces[0],
        ],
        spaces=[smem, smem, pl.ANY, pl.ANY, pl.ANY],
    )

    yface = shape((sz.face_y + HALO_IDS, LANES), BF16)
    message, *faces = call(
        "pack_y",
        pack_y,
        [shape((devices,) + packed.shape, BF16)] + [yface] * swaps("gy"),
        [scratch((HALO_IDS, LANES), F32)] * 2,
        8,
        1 << 20,
        2 << 20,
        [res, ids, packed] + xhalo,
    )
    yhalo = exchange(faces, "gy")
    gathered = lax.all_to_all(message, AXES, 0, 0, tiled=True)
    all_counts = gathered[:, 0, sz.slots].astype(jnp.int32)
    all_ranks = gathered[:, 0, sz.slots + 1].astype(jnp.int32)
    starts = jnp.sum(
        all_counts[None, :] * (all_ranks[None, :] < all_ranks[:, None]).astype(jnp.int32), axis=1
    )
    rows = (sz.cx + 4) * sz.pitch
    zmessage, id_box = call(
        "pack_z",
        pack_z,
        [shape((sz.face_z + HALO_IDS, LANES), BF16), shape((rows, LANES), F32)],
        [scratch((sz.box * 8, LANES), F32), scratch((rows, LANES), F32)],
        8,
        1 << 22,
        3 << 20,
        [res, ids] + xhalo + yhalo,
    )
    zhalo = exchange([zmessage] * 2, "col")

    tile = (1, sz.loads // 2, LANES)
    if sz.block_rows != 64:
        tile = (sz.block_rows // LANES, sz.loads, LANES)
    partial = call(
        "coarse",
        place_pieces,
        shape((blocks,) + tile, F32),
        [
            scratch((sz.total_rows // LANES + 1, sz.loads, LANES), F32),
            scratch((sz.loads, LANES), F32),
        ],
        12,
        1 << 23,
        1 << 20,
        [starts, gathered, coarse_inverse],
        spaces=[smem, vmem, vmem],
    )
    coarse = lax.all_to_all(partial, ("gx", "col"), 0, 0, tiled=True)
    coarse = coarse.reshape((-1,) + tile[1:])

    field = scratch((sz.comps, sz.box, sz.loads, LANES), F32)
    direction, own, zface, *faces = call(
        "solve",
        solve_and_direct,
        [
            shape((sz.comps, sz.cells, sz.loads, LANES), F32),
            shape((8, sz.cells, LANES), F32),
            shape((sz.face_z, LANES), BF16),
        ]
        + [shape((sz.face_x, LANES), BF16)] * swaps("gx")
        + [shape((sz.inner_y, LANES), BF16)] * swaps("gy"),
        [
            field,
            field,
            field,
            scratch((3, sz.comps, sz.loads, LANES), F32),
            scratch((2, sz.comps, sz.loads, LANES), F32),
            scratch((9, rows, LANES), F32),
            scratch((9, 8, LANES), F32),
            scratch((rows, LANES), F32),
            scratch((rows, LANES), F32),
            scratch((2 * sz.loads, LANES), BF16),
            scratch((sz.face_z, LANES), F32),
        ],
        20,
        1 << 28,
        8 << 20,
        [starts, eigen_counts, materials, res, id_box, coarse, split] + xhalo + yhalo + zhalo,
        spaces=[smem, smem, smem] + [vmem] * (4 + len(xhalo + yhalo + zhalo)),
    )
    xhalo = exchange(faces[: swaps("gx")], "gx")
    yhalo = exchange(faces[swaps("gx") :], "gy")
    zhalo = exchange([zface] * 2, "col")
    sums_shape = (sz.loads // 2, LANES)
    dir_split, image_split, sums = call(
        "image",
        make_image,
        [
            shape((sz.tiles, 2 * sz.loads, LANES), BF16),
            shape((sz.tiles, 2 * sz.loads, LANES), BF16),
            shape(sums_shape, F32),
        ],
        [field, scratch((sz.comps, sz.loads, LANES), F32), dma((sz.comps, sz.cx))],
        16,
        1 << 28,
        8 << 20,
        [res, own, direction] + xhalo + yhalo + zhalo,
        spaces=[vmem, vmem, pl.ANY] + [vmem] * len(xhalo + yhalo + zhalo),
    )
    over, operands = AXES, [sums]
    if lax.axis_size("gy") == 2:
        over = ("gx", "col")
        operands += exchange([sums], "gy")
        devices = devices // 2
    spread = call(
        "share_sums", share_sums, shape((devices,) + sums_shape, F32), [], 4, 1 << 12, 1 << 17,
        operands,
    )
    sums = lax.all_to_all(spread, over, 0, 0, tiled=True)
    flat = shape(res.shape, F32)
    new_iterate, new_residual = call(
        "finish",
        finish,
        [flat, flat],
        [scratch((2 * sz.loads, LANES), BF16)],
        16,
        1 << 27,
        9 << 20,
        [sums, old, res, dir_split, image_split],
    )
    return (new_iterate.reshape(iterate.shape), new_residual.reshape(residual.shape))


def solution(mesh):
    placed = (
        P(None, None, "gx", "gy", "col"),
        P(None, None, "gx", "gy", "col"),
        P("gx", "gy", "col"),
        P(),
        P(("gx", "gy", "col")),
        P(("gx", "gy", "col")),
        P(None, None, "gx", "gy", "col"),
        P(("gx", "col"), None),
    )
    return jax.shard_map(
        body,
        mesh=mesh,
        in_specs=placed,
        out_specs=(P(None, None, "gx", "gy", "col"), P(None, None, "gx", "gy", "col")),
        check_vma=False,
    )
```

```python
import jax
import jax.numpy as jnp
from jax import lax
from jax.experimental import pallas as pl
from jax.experimental.pallas import tpu as pltpu
from jax.sharding import PartitionSpec as P

DAMPING = 0.6
F32 = jnp.float32
BF16 = jnp.bfloat16
LANES = 128
HALO_IDS = 16
AXES = ("gx", "gy", "col")
TRANSPOSED = (((1,), (1,)), ((), ()))


def split_hi_lo(value):
    hi = value.astype(BF16)
    return hi, (value - hi.astype(F32)).astype(BF16)


def paired_left(value, width, parts):
    rows = value.shape[0]
    hi, lo = split_hi_lo(value)
    parts[pl.ds(0, rows), :] = hi
    parts[pl.ds(rows, rows), :] = lo
    high = parts[pl.ds(0, rows), :].astype(F32)
    low = parts[pl.ds(rows, rows), :].astype(F32)
    return jnp.concatenate([high + roll_lanes(high, width), low], axis=0).astype(BF16)


def lane_ids(rows):
    return lax.broadcasted_iota(jnp.int32, (rows, LANES), 1)


def roll_lanes(value, shift):
    if isinstance(shift, int):
        shift = shift % LANES
        if shift == 0:
            return value
    return pltpu.roll(value, shift, axis=1)


def vmem_call(
    name, kernel, outs, scratch, limit_mib, flops, moved, operands, spaces=None, direct=1 << 60
):
    spaces = spaces or [pltpu.VMEM] * len(operands)
    return pl.pallas_call(
        kernel,
        name=name,
        out_shape=outs,
        in_specs=[pl.BlockSpec(memory_space=space) for space in spaces],
        out_specs=jax.tree.map(
            lambda out: pl.BlockSpec(memory_space=pl.ANY if out.size >= direct else pltpu.VMEM), outs
        ),
        scratch_shapes=scratch,
        compiler_params=pltpu.CompilerParams(vmem_limit_bytes=limit_mib << 20),
        cost_estimate=pl.CostEstimate(flops=flops, bytes_accessed=moved, transcendentals=0),
    )(*operands)


def own_index():
    index = 0
    for axis in AXES:
        index = index * lax.axis_size(axis) + lax.axis_index(axis)
    return index


class Sizes:
    def __init__(self, residual, eigen_basis, coarse_inverse):
        self.comps, self.loads, self.cx, self.cy, _ = residual.shape
        self.slots = eigen_basis.shape[0]
        self.block_rows, self.total_rows = coarse_inverse.shape
        self.cells = self.cx * self.cy
        self.bx, self.by = self.cx + 2, self.cy + 2
        self.box = self.bx * self.by
        self.tiles = self.comps * self.cells
        self.face_x = self.comps * self.cy * self.loads
        self.face_y = self.comps * self.bx * self.loads
        self.inner_y = self.comps * self.cx * self.loads
        self.face_z = self.comps * self.loads
        self.pitch = 16


class Halo:
    def __init__(self, axis, refs):
        self.refs = refs
        self.even = lax.rem(lax.axis_index(axis), 2) == 0

    def side(self, rows, first):
        value = self.refs[0][rows, :].astype(F32)
        other = self.refs[1][rows, :].astype(F32) if len(self.refs) > 1 else jnp.zeros_like(value)
        return jnp.where(self.even, value, other) if first else jnp.where(self.even, other, value)

    def below(self, rows):
        return self.side(rows, False)

    def above(self, rows):
        return self.side(rows, True)

    def send(self, rows, low, high):
        self.refs[0][rows, :] = jnp.where(self.even, high, low).astype(BF16)
        if len(self.refs) > 1:
            self.refs[1][rows, :] = jnp.where(self.even, low, high).astype(BF16)


def swaps(axis):
    return 1 if lax.axis_size(axis) == 2 else 2


def exchange(faces, axis):
    devices = lax.axis_size(axis)
    result = []
    for parity in range(swaps(axis)):
        pairs = []
        for low in range(parity, devices - 1, 2):
            pairs += [(low, low + 1), (low + 1, low)]
        result.append(lax.ppermute(faces[parity], axis, pairs))
    return result


def take_halos(refs, *axes):
    refs = list(refs)
    halos = []
    for axis in axes:
        count = swaps(axis)
        halos.append(Halo(axis, refs[:count]))
        refs = refs[count:]
    return halos + [refs]


def own_rows(sz, ref, comp, cell):
    start = comp * sz.loads * sz.cells + cell
    return ref[pl.ds(start, sz.loads, stride=sz.cells), :]


def pack_x(sz, res, ids, *refs):
    xsend, (low, high, id_rows, sem) = take_halos(refs, "gx")
    copies = [
        pltpu.make_async_copy(res.at[:, pl.ds(0, sz.cy)], low, sem.at[0]),
        pltpu.make_async_copy(res.at[:, pl.ds(sz.cells - sz.cy, sz.cy)], high, sem.at[1]),
        pltpu.make_async_copy(ids, id_rows, sem.at[2]),
    ]
    for copy in copies:
        copy.start()
    for copy in copies:
        copy.wait()
    low, high = (ref.reshape(sz.comps * sz.loads * sz.cy, LANES) for ref in (low, high))
    for comp in range(sz.comps):
        for y in range(sz.cy):
            rows = pl.ds((comp * sz.cy + y) * sz.loads, sz.loads)
            taken = pl.ds(comp * sz.loads * sz.cy + y, sz.loads, stride=sz.cy)
            xsend.send(rows, low[taken, :], high[taken, :])
    two = 2 * sz.cy
    first = (id_rows[pl.ds(0, two), :] + 1).astype(F32)
    last = (id_rows[pl.ds(sz.cells - two, two), :] + 1).astype(F32)
    xsend.send(pl.ds(sz.face_x, two), first, last)


def make_pieces(
    sz, count, rank, basis_in, res_in, after, message, wide, basis_rows, res_rows, sem
):
    del after
    slots, loads = sz.slots, sz.loads
    copies = []
    for comp in range(sz.comps):
        part = pl.ds(comp * sz.cells, sz.cells)
        copies.append(
            (
                pltpu.make_async_copy(
                    basis_in.at[:, part], basis_rows.at[:, part], sem.at[0, comp]
                ),
                pltpu.make_async_copy(res_in.at[comp], res_rows.at[comp], sem.at[1, comp]),
            )
        )
    for pair in copies:
        for copy in pair:
            copy.start()
    basis = basis_rows.reshape(slots * sz.tiles, LANES)
    res = res_rows.reshape(sz.tiles * loads, LANES)

    def step(index, carry):
        both, low = carry
        basis_hi, basis_lo, res_hi, res_both = [], [], [], []
        for half in range(2):
            tile = index * 2 + half
            comp = tile // sz.cells
            hi, lo = split_hi_lo(basis[pl.ds(tile, slots, stride=sz.tiles), :])
            value_hi, value_lo = split_hi_lo(own_rows(sz, res, comp, tile - comp * sz.cells))
            basis_hi.append(hi)
            basis_lo.append(lo)
            res_hi.append(value_hi)
            res_both.append(jnp.concatenate([value_hi, value_lo], axis=0))
        both = both + lax.dot_general(
            jnp.concatenate(res_both, axis=1),
            jnp.concatenate(basis_hi, axis=1),
            TRANSPOSED,
            preferred_element_type=F32,
        )
        low = low + lax.dot_general(
            jnp.concatenate(res_hi, axis=1),
            jnp.concatenate(basis_lo, axis=1),
            TRANSPOSED,
            preferred_element_type=F32,
        )
        return both, low

    carry = (jnp.zeros((2 * loads, slots), F32), jnp.zeros((loads, slots), F32))
    for comp in range(sz.comps):
        for copy in copies[comp]:
            copy.wait()
        carry = lax.fori_loop(
            comp * sz.cells // 2, (comp + 1) * sz.cells // 2, step, carry, unroll=4
        )
    both, low = carry
    pieces = both[:loads] + both[loads:] + low
    slot = lax.broadcasted_iota(jnp.int32, pieces.shape, 1)
    wide[...] = jnp.zeros_like(wide)
    wide[:, pl.ds(0, slots)] = jnp.where(slot < count[0], pieces, 0.0)
    half = loads // 2
    lane = lane_ids(half)
    packed = jnp.where(lane < 64, wide[:half, :], roll_lanes(wide[half:, :], 64))
    packed = jnp.where(lane == slots, count[0].astype(F32), packed)
    packed = jnp.where(lane == slots + 1, rank[0].astype(F32), packed)
    message[...] = packed.astype(BF16)


def pack_y(sz, res, ids, packed, *refs):
    xhalo, refs = take_halos(refs, "gx")
    message = refs[0]
    ysend, (side_low, side_high) = take_halos(refs[1:], "gy")
    for device in range(message.shape[0]):
        message[device] = packed[...]
    last = sz.cy - 1
    for comp in range(sz.comps):
        for x in range(sz.bx):
            rows = pl.ds((comp * sz.bx + x) * sz.loads, sz.loads)
            if 0 < x < sz.bx - 1:
                low, high = (own_rows(sz, res, comp, (x - 1) * sz.cy + y) for y in (0, last))
            else:
                side = xhalo.below if x == 0 else xhalo.above
                low, high = (
                    side(pl.ds((comp * sz.cy + y) * sz.loads, sz.loads)) for y in (0, last)
                )
            ysend.send(rows, low, high)
    ids_below = xhalo.below(pl.ds(sz.face_x, 2 * sz.cy))
    ids_above = xhalo.above(pl.ds(sz.face_x, 2 * sz.cy))
    for x in range(sz.cx + 4):
        if x < 2:
            rows = ids_below[x * sz.cy : (x + 1) * sz.cy]
        elif x >= sz.cx + 2:
            rows = ids_above[(x - sz.cx - 2) * sz.cy : (x - sz.cx - 1) * sz.cy]
        else:
            rows = (ids[pl.ds((x - 2) * sz.cy, sz.cy), :] + 1).astype(F32)
        side_low[pl.ds(2 * x, 2), :] = rows[:2]
        side_high[pl.ds(2 * x, 2), :] = rows[sz.cy - 2 :]
    ysend.send(pl.ds(sz.face_y, HALO_IDS), side_low[...], side_high[...])


def box_tile(sz, res, xhalo, yhalo, comp, x, y):
    if y == 0 or y == sz.by - 1:
        side = yhalo.below if y == 0 else yhalo.above
        return side(pl.ds((comp * sz.bx + x) * sz.loads, sz.loads))
    if x == 0 or x == sz.bx - 1:
        side = xhalo.below if x == 0 else xhalo.above
        return side(pl.ds((comp * sz.cy + y - 1) * sz.loads, sz.loads))
    return own_rows(sz, res, comp, (x - 1) * sz.cy + y - 1)


def pack_z(sz, res, ids, *refs):
    xhalo, yhalo, (out, id_box, star, outer) = take_halos(refs, "gx", "gy")
    pitch = sz.pitch
    id_box[...] = jnp.zeros_like(id_box)
    two = 2 * sz.cy
    ids_below = xhalo.below(pl.ds(sz.face_x, two))
    ids_above = xhalo.above(pl.ds(sz.face_x, two))
    ids_low = yhalo.below(pl.ds(sz.face_y, HALO_IDS))
    ids_high = yhalo.above(pl.ds(sz.face_y, HALO_IDS))
    for x in range(sz.cx + 4):
        if x < 2:
            rows = ids_below[x * sz.cy : (x + 1) * sz.cy]
        elif x >= sz.cx + 2:
            rows = ids_above[(x - sz.cx - 2) * sz.cy : (x - sz.cx - 1) * sz.cy]
        else:
            rows = (ids[pl.ds((x - 2) * sz.cy, sz.cy), :] + 1).astype(F32)
        id_box[pl.ds(x * pitch + 2, sz.cy), :] = rows
        id_box[pl.ds(x * pitch, 2), :] = ids_low[2 * x : 2 * x + 2]
        id_box[pl.ds(x * pitch + sz.cy + 2, 2), :] = ids_high[2 * x : 2 * x + 2]
    values = id_box[...]
    lane = lane_ids(values.shape[0])
    outer[...] = jnp.where(lane == LANES - 1, roll_lanes(values, 1), roll_lanes(values, -1))
    star[...] = jnp.zeros_like(star)
    lane8 = lane_ids(8)
    taken = jnp.zeros((8, LANES), F32)
    for x in range(sz.bx):
        for y in range(sz.by):
            place = x * sz.by + y
            row = (x + 1) * pitch + y + 1
            for j, shift in enumerate((0, -pitch, pitch, -1, 1)):
                star[pl.ds(place * 8 + j, 1), :] = id_box[pl.ds(row + shift, 1), :]
            star[pl.ds(place * 8 + 5, 1), :] = outer[pl.ds(row, 1), :]
    for place in range(sz.box):
        picked = roll_lanes(star[pl.ds(place * 8, 8), :], 2 * place + 1)
        taken = jnp.where((lane8 >> 1) == place, picked, taken)
    out[pl.ds(sz.face_z, HALO_IDS), :] = jnp.concatenate(
        [taken, jnp.zeros((HALO_IDS - 8, LANES), F32)], axis=0
    ).astype(BF16)
    lane_k = lane_ids(sz.loads)
    for comp in range(sz.comps):
        total = jnp.zeros((sz.loads, LANES), F32)
        for x in range(sz.bx):
            for y in range(sz.by):
                place = x * sz.by + y
                tile = box_tile(sz, res, xhalo, yhalo, comp, x, y)
                total = jnp.where(
                    (lane_k >> 1) == place, roll_lanes(tile, 2 * place + 1), total
                )
        out[pl.ds(comp * sz.loads, sz.loads), :] = total.astype(BF16)


def place_pieces(
    sz, gathered, inverse, after, message, starts_out, vector, wide, heads, starts, sem
):
    del after
    devices = gathered.shape[0]
    for device in range(devices):
        heads[pl.ds(device, 1), :] = gathered[device].astype(F32)[0:1]
    values = heads[...]
    ranks = jnp.transpose(values)[sz.slots + 1 : sz.slots + 2, :]
    earlier = values[:, sz.slots + 1 : sz.slots + 2] < ranks
    total = jnp.sum(jnp.where(earlier, values[:, sz.slots : sz.slots + 1], 0.0), axis=0, keepdims=True)
    starts_out[...] = jnp.zeros_like(starts_out)
    starts_out[:, pl.ds(0, devices)] = jnp.broadcast_to(total.astype(jnp.int32), (8, devices))
    copy = pltpu.make_async_copy(starts_out, starts, sem)
    copy.start()
    half = sz.loads // 2
    lane = lane_ids(half)
    vector[...] = jnp.zeros_like(vector)
    copy.wait()

    def place(device, carry):
        start = starts[0, device]
        block = start // LANES
        offset = start - block * LANES
        packed = gathered[device].astype(F32)
        low = jnp.where(lane < sz.slots, packed, 0.0)
        high = jnp.where((lane >= 64) & (lane < 64 + sz.slots), packed, 0.0)
        both = jnp.concatenate(
            [
                pltpu.roll(low, offset, axis=1),
                pltpu.roll(high, lax.rem(offset + 64, LANES), axis=1),
            ],
            axis=0,
        )
        wide_lane = lane_ids(sz.loads)
        vector[block] = vector[block] + jnp.where(wide_lane >= offset, both, 0.0)
        vector[block + 1] = vector[block + 1] + jnp.where(wide_lane < offset, both, 0.0)
        return carry

    lax.fori_loop(0, gathered.shape[0], place, 0, unroll=8)
    total = jnp.zeros((sz.loads, sz.block_rows), F32)
    for block in range(sz.total_rows // LANES):
        total = total + lax.dot_general(
            vector[block].astype(BF16),
            inverse[:, pl.ds(block * LANES, LANES)],
            TRANSPOSED,
            preferred_element_type=F32,
        )
    if sz.block_rows == 64:
        wide[...] = jnp.zeros_like(wide)
        wide[:, pl.ds(0, 64)] = total
        packed = jnp.where(lane < 64, wide[:half, :], roll_lanes(wide[half:, :], 64))
        for device in range(message.shape[0]):
            message[device, 0] = packed
    else:
        for device in range(message.shape[0]):
            for block in range(sz.block_rows // LANES):
                message[device, block] = total[:, block * LANES : (block + 1) * LANES]


def own_coefs(sz, coefs, start):
    if sz.block_rows == 64:
        half = sz.loads // 2
        block = start // 64
        offset = start - block * 64
        first = coefs[block]
        second = coefs[jnp.minimum(block + 1, coefs.shape[0] - 1)]
        lane = lane_ids(half)
        top = jnp.where(lane < 64, first, roll_lanes(second, 64))
        bottom = jnp.where(lane < 64, roll_lanes(first, 64), second)
        both = jnp.concatenate([top, bottom], axis=0)
    else:
        block = start // LANES
        offset = start - block * LANES
        first = coefs[block]
        second = coefs[jnp.minimum(block + 1, coefs.shape[0] - 1)]
        both = jnp.where(lane_ids(sz.loads) >= offset, first, second)
    return pltpu.roll(both, lax.rem(LANES - offset, LANES), axis=1)


def look_up(table, row, ids):
    result = jnp.zeros_like(ids)
    for material in range(table.shape[1]):
        result = jnp.where(ids == material + 1, table[row, material], result)
    return result


DINV, KEEP, DLAM, WXM, WXP, WYM, WYP, WZM, WZP = range(9)


def spread_row(ref, index, row):
    return ref[index, pl.ds(row, 8, stride=0), :]


def make_coefs(sz, table, id_box, halo_ids, coefs, halo_coefs, own, mu_box, halo_mu):
    pitch = sz.pitch
    mu_box[...] = look_up(table, 0, id_box[...])
    lam_box = look_up(table, 1, id_box[...])
    mu_halo = look_up(table, 0, halo_ids)
    lam_halo = look_up(table, 1, halo_ids)
    lane8 = lane_ids(8)
    center = jnp.broadcast_to(mu_halo[0:1], (8, LANES))
    inner = jnp.zeros((8, LANES), F32)
    for place in range(sz.box):
        row = (place // sz.by + 1) * pitch + place % sz.by + 1
        halo_mu[pl.ds(row, 1), :] = roll_lanes(center, -2 * place)[0:1]
        spread = jnp.broadcast_to(mu_box[pl.ds(row, 1), :], (8, LANES))
        here = (((lane8 + 1) >> 1) & 63) == place
        inner = jnp.where(here, roll_lanes(spread, 2 * place), inner)
    rows_id = lax.broadcasted_iota(jnp.int32, (pitch, LANES), 0)
    lane = lane_ids(pitch)
    for x in range(1, sz.bx + 1):
        mu = mu_box[pl.ds(x * pitch, pitch), :]
        edge = halo_mu[pl.ds(x * pitch, pitch), :]
        lam = lam_box[x * pitch : (x + 1) * pitch]
        faces = [
            0.5 * (mu + mu_box[pl.ds((x - 1) * pitch, pitch), :]),
            0.5 * (mu + mu_box[pl.ds((x + 1) * pitch, pitch), :]),
            0.5 * (mu + mu_box[pl.ds(x * pitch - 1, pitch), :]),
            0.5 * (mu + mu_box[pl.ds(x * pitch + 1, pitch), :]),
            0.5 * (mu + jnp.where(lane == 0, edge, roll_lanes(mu, 1))),
            0.5 * (mu + jnp.where(lane == LANES - 1, edge, roll_lanes(mu, -1))),
        ]
        diag = 1.0 + sum(faces)
        dinv = DAMPING / (diag + lam)
        rows = pl.ds(x * pitch, pitch)
        coefs[DINV, rows, :] = dinv
        coefs[KEEP, rows, :] = (1.0 - DAMPING) + dinv * lam
        coefs[DLAM, rows, :] = dinv * lam
        weights = [dinv * face for face in faces]
        if x == 1:
            weights[0] = jnp.zeros_like(dinv)
        if x == sz.bx:
            weights[1] = jnp.zeros_like(dinv)
        weights[2] = jnp.where(rows_id == 1, 0.0, weights[2])
        weights[3] = jnp.where(rows_id == sz.by, 0.0, weights[3])
        for j in range(6):
            coefs[WXM + j, rows, :] = weights[j]
        if 2 <= x <= sz.cx + 1:
            target = pl.ds((x - 2) * sz.cy, sz.cy)
            for j, value in enumerate([diag, lam] + faces):
                own[j, target, :] = value[2 : 2 + sz.cy]
    place = ((lane8 + 1) >> 1) & 63
    column = jnp.zeros_like(place)
    for x in range(1, sz.bx):
        column = column + (place >= x * sz.by).astype(jnp.int32)
    y_place = place - column * sz.by
    others = [jnp.broadcast_to(mu_halo[j : j + 1], (8, LANES)) for j in range(1, 6)]
    faces = [0.5 * (center + other) for other in others] + [0.5 * (center + inner)]
    lam = jnp.broadcast_to(lam_halo[0:1], (8, LANES))
    dinv = DAMPING / (1.0 + lam + sum(faces))
    live = place < sz.box
    keep = [
        live & (column > 0),
        live & (column < sz.bx - 1),
        live & (y_place > 0),
        live & (y_place < sz.by - 1),
        None,
        live,
    ]
    halo_coefs[DINV] = dinv
    halo_coefs[KEEP] = (1.0 - DAMPING) + dinv * lam
    halo_coefs[DLAM] = dinv * lam
    for j, target in ((0, WXM), (1, WXP), (2, WYM), (3, WYP), (5, WZM)):
        halo_coefs[target] = jnp.where(keep[j], dinv * faces[j], 0.0)


def z_halo(zhalo, rows):
    down, up = zhalo.below(rows), zhalo.above(rows)
    even = (lane_ids(down.shape[0]) & 1) == 0
    return jnp.where(even, down, roll_lanes(up, -2))


def solve_and_direct(sz, count, table, starts_in, res, id_box, coarse, basis_in, *refs):
    xhalo, yhalo, zhalo, refs = take_halos(refs, "gx", "gy", "col")
    direction, own, zface = refs[:3]
    xsend, ysend, refs = take_halos(refs[3:], "gx", "gy")
    first, second, third, halos, inner, coefs, halo_coefs, mu_box, halo_mu, left, zedge = refs[:11]
    basis_rows, starts, sem = refs[11:]
    copies = [
        pltpu.make_async_copy(starts_in, starts, sem.at[0]),
        pltpu.make_async_copy(basis_in, basis_rows, sem.at[1]),
    ]
    for copy in copies:
        copy.start()
    basis = basis_rows.reshape(sz.slots * sz.tiles, LANES)
    loads, comps = sz.loads, sz.comps
    groups = loads // 8
    lane8 = lane_ids(8)

    halo_mu[...] = jnp.zeros_like(halo_mu)
    inner[1] = jnp.zeros((comps, loads, LANES), F32)
    make_coefs(
        sz, table, id_box, z_halo(zhalo, pl.ds(sz.face_z, HALO_IDS))[:8], coefs, halo_coefs, own,
        mu_box, halo_mu,
    )

    def here_of(place):
        return (((lane8 + 1) >> 1) & 63) == place

    for comp in range(comps):
        halo = z_halo(zhalo, pl.ds(comp * loads, loads))
        dinv = jnp.concatenate([halo_coefs[DINV]] * groups, axis=0)
        halos[0, comp] = dinv * halo
        total = jnp.zeros((loads, LANES), F32)
        lane_k = lane_ids(loads)
        for x in range(sz.bx):
            for y in range(sz.by):
                place = x * sz.by + y
                row = (x + 1) * sz.pitch + y + 1
                tile = box_tile(sz, res, xhalo, yhalo, comp, x, y)
                value = tile * coefs[DINV, pl.ds(row, loads, stride=0), :]
                first[comp, place] = value
                here = (((lane_k + 1) >> 1) & 63) == place
                total = jnp.where(here, roll_lanes(value, 2 * place), total)
        inner[0, comp] = total

    def relax(source, level, place, row):
        coef = [spread_row(coefs, j, row) for j in range(9)]
        xm, xp = jnp.maximum(place - sz.by, 0), jnp.minimum(place + sz.by, sz.box - 1)
        ym, yp = jnp.maximum(place - 1, 0), jnp.minimum(place + 1, sz.box - 1)
        back = lax.rem(LANES - 2 * place + LANES, LANES)
        result = {}
        for group in range(groups):
            rows = pl.ds(group * 8, 8)
            center = [source[comp, place, rows, :] for comp in range(comps)]
            coupled = coef[DLAM] * sum(center)
            for comp in range(comps):
                value = center[comp]
                edge = pltpu.roll(halos[level, comp, rows, :], back, axis=1)
                zm = jnp.where(lane8 == 0, edge, roll_lanes(value, 1))
                zp = jnp.where(lane8 == LANES - 1, edge, roll_lanes(value, -1))
                out = (first[comp, place, rows, :] - coupled) + coef[KEEP] * value
                out = out + coef[WXM] * source[comp, xm, rows, :]
                out = out + coef[WXP] * source[comp, xp, rows, :]
                out = out + coef[WYM] * source[comp, ym, rows, :]
                out = out + coef[WYP] * source[comp, yp, rows, :]
                out = out + coef[WZM] * zm
                out = out + coef[WZP] * zp
                result[comp, group] = out
        return result

    def sweep(source, target, level):
        def at(place, carry):
            x = place // sz.by
            row = (x + 1) * sz.pitch + place - x * sz.by + 1
            result = relax(source, level, place, row)
            for (comp, group), out in result.items():
                rows = pl.ds(group * 8, 8)
                target[comp, place, rows, :] = out
                if level == 0:
                    pltpu.store(
                        inner.at[1, comp, rows, :],
                        pltpu.roll(out, 2 * place, axis=1),
                        mask=here_of(place),
                    )
            return carry

        lax.fori_loop(0, sz.box, at, 0, unroll=6)
        coef = [halo_coefs[j] for j in range(8)]
        for group in range(groups):
            rows = pl.ds(group * 8, 8)
            center = [halos[level, comp, rows, :] for comp in range(comps)]
            coupled = coef[DLAM] * sum(center)
            for comp in range(comps):
                value = center[comp]
                out = (halos[0, comp, rows, :] - coupled) + coef[KEEP] * value
                out = out + coef[WXM] * roll_lanes(value, 2 * sz.by)
                out = out + coef[WXP] * roll_lanes(value, -2 * sz.by)
                out = out + coef[WYM] * roll_lanes(value, 2)
                out = out + coef[WYP] * roll_lanes(value, -2)
                out = out + coef[WZM] * inner[level, comp, rows, :]
                halos[level + 1, comp, rows, :] = out

    sweep(first, second, 0)
    sweep(second, third, 1)

    for copy in copies:
        copy.wait()
    mine = own_coefs(sz, coarse, starts[0, own_index()])
    mine = jnp.where(lane_ids(loads) < jnp.minimum(count[0], sz.slots), mine, 0.0)
    left[...] = paired_left(mine, sz.slots, left)
    zedge[...] = jnp.zeros_like(zedge)

    def final(cell, carry):
        x = cell // sz.cy
        y = cell - x * sz.cy
        place = (x + 1) * sz.by + y + 1
        result = relax(third, 2, place, (x + 2) * sz.pitch + y + 2)
        for comp in range(comps):
            tile = comp * sz.cells + cell
            both = split_hi_lo(basis[pl.ds(tile, sz.slots, stride=sz.tiles), :])
            part = jnp.dot(
                left[:, : 2 * sz.slots],
                jnp.concatenate(both, axis=0),
                preferred_element_type=F32,
            )
            for group in range(groups):
                rows = pl.ds(group * 8, 8)
                value = result[comp, group] + (
                    part[group * 8 : group * 8 + 8]
                    + part[loads + group * 8 : loads + group * 8 + 8]
                )
                direction[comp, cell, rows, :] = value
                zrows = pl.ds(comp * loads + group * 8, 8)
                pltpu.store(
                    zedge.at[zrows, :],
                    pltpu.roll(value, 2 * place + 1, axis=1),
                    mask=(lane8 >> 1) == place,
                )
        return carry

    lax.fori_loop(0, sz.cells, final, 0, unroll=4)
    zface[...] = zedge[...].astype(BF16)
    for comp in range(comps):
        for y in range(sz.cy):
            rows = pl.ds((comp * sz.cy + y) * loads, loads)
            xsend.send(rows, direction[comp, y], direction[comp, (sz.cx - 1) * sz.cy + y])
        for x in range(sz.cx):
            rows = pl.ds((comp * sz.cx + x) * loads, loads)
            ysend.send(rows, direction[comp, x * sz.cy], direction[comp, (x + 1) * sz.cy - 1])


def make_image(sz, res, own, direction, *refs):
    xhalo, yhalo, zhalo, refs = take_halos(refs, "gx", "gy", "col")
    dir_out, image_out, message, box, halo, dir_split, image_split, sem, out_sem = refs
    loads, comps = sz.loads, sz.comps
    groups = loads // 8
    copies = []
    for comp in range(comps):
        for x in range(sz.cx):
            copies.append(
                pltpu.make_async_copy(
                    direction.at[comp, pl.ds(x * sz.cy, sz.cy)],
                    box.at[comp, pl.ds((x + 1) * sz.by + 1, sz.cy)],
                    sem.at[comp, x],
                )
            )
    for copy in copies:
        copy.start()
    for comp in range(comps):
        for y in range(sz.cy):
            rows = pl.ds((comp * sz.cy + y) * loads, loads)
            box[comp, y + 1] = xhalo.below(rows)
            box[comp, (sz.bx - 1) * sz.by + y + 1] = xhalo.above(rows)
        for x in range(sz.cx):
            rows = pl.ds((comp * sz.cx + x) * loads, loads)
            box[comp, (x + 1) * sz.by] = yhalo.below(rows)
            box[comp, (x + 1) * sz.by + sz.by - 1] = yhalo.above(rows)
        halo[comp] = z_halo(zhalo, pl.ds(comp * loads, loads))
    for copy in copies:
        copy.wait()
    lane8 = lane_ids(8)

    def at(cell, total):
        x = cell // sz.cy
        y = cell - x * sz.cy
        place = (x + 1) * sz.by + y + 1
        back = lax.rem(LANES - 2 * place + LANES, LANES)
        coef = [spread_row(own, j, cell) for j in range(8)]
        parts = {}
        for group in range(groups):
            rows = pl.ds(group * 8, 8)
            center = [box[comp, place, rows, :] for comp in range(comps)]
            coupled = coef[1] * sum(center)
            for comp in range(comps):
                value = center[comp]
                edge = pltpu.roll(halo[comp, rows, :], back, axis=1)
                zm = jnp.where(lane8 == 0, edge, roll_lanes(value, 1))
                zp = jnp.where(lane8 == LANES - 1, edge, roll_lanes(value, -1))
                out = coef[0] * value + coupled
                out = out - coef[2] * box[comp, place - sz.by, rows, :]
                out = out - coef[3] * box[comp, place + sz.by, rows, :]
                out = out - coef[4] * box[comp, place - 1, rows, :]
                out = out - coef[5] * box[comp, place + 1, rows, :]
                out = out - coef[6] * zm
                parts[comp, group] = out - coef[7] * zp
        for comp in range(comps):
            tile = comp * sz.cells + cell
            dir_hi, dir_lo = split_hi_lo(box[comp, place])
            field = jnp.concatenate([parts[comp, group] for group in range(groups)], axis=0)
            field_hi, field_lo = split_hi_lo(field)
            res_hi, res_lo = split_hi_lo(own_rows(sz, res, comp, cell))
            left = jnp.concatenate([dir_hi, dir_lo], axis=0)
            field_both = jnp.concatenate([field_hi, field_lo], axis=0)
            dir_split[tile] = left
            image_split[tile] = field_both
            total = total + lax.dot_general(
                left,
                jnp.concatenate([field_both, res_hi, res_lo], axis=0),
                TRANSPOSED,
                preferred_element_type=F32,
            )
        return total

    total = jnp.zeros((2 * loads, 4 * loads), F32)
    copies = []
    for x in range(sz.cx):
        total = lax.fori_loop(x * sz.cy, (x + 1) * sz.cy, at, total, unroll=4)
        for comp in range(comps):
            part = pl.ds(comp * sz.cells + x * sz.cy, sz.cy)
            for j, (source, out) in enumerate(((dir_split, dir_out), (image_split, image_out))):
                copies.append(
                    pltpu.make_async_copy(source.at[part], out.at[part], out_sem.at[j, comp, x])
                )
                copies[-1].start()
    high, low = total[:loads], total[loads:]
    sums = high + roll_lanes(high, -loads) + low
    half = loads // 2
    lane = lane_ids(half)
    packed = jnp.where((lane & (2 * loads - 1)) < loads, sums[:half], roll_lanes(sums[half:], loads))
    message[...] = packed
    for copy in copies:
        copy.wait()


def share_sums(sz, mine, *refs):
    message = refs[-1]
    total = mine[...]
    for other in refs[:-1]:
        total = total + other[...]
    for device in range(message.shape[0]):
        message[device] = total


def finish(sz, sums, *refs):
    sources, outs, refs = refs[:4], refs[4:6], refs[6:]
    locals_in, (new_iterate, new_residual), (parts, sem, out_sem) = refs[:4], refs[4:6], refs[6:]
    iterate, res, dir_split, image_split = locals_in
    loads = sz.loads
    copies = []
    for comp in range(sz.comps):
        copies.append([])
        for j, (source, target) in enumerate(zip(sources, locals_in)):
            length = source.shape[0] // sz.comps
            part = pl.ds(comp * length, length)
            copies[comp].append(
                pltpu.make_async_copy(source.at[part], target.at[part], sem.at[j, comp])
            )
            copies[comp][-1].start()
    total = sums[0]
    for device in range(1, sums.shape[0]):
        total = total + sums[device]
    system = jnp.concatenate([total, roll_lanes(total, -loads)], axis=0)
    lane = lane_ids(loads)
    system = jnp.where((lane & (2 * loads - 1)) < loads, system, 0.0)
    row_ids = lax.broadcasted_iota(jnp.int32, (loads, LANES), 0)
    for base in range(0, loads, 8):
        columns = [
            jnp.broadcast_to(system[:, i : i + 1], (loads, LANES)) for i in range(base, base + 8)
        ]
        for j in range(8):
            i = base + j
            here = row_ids == i
            scale = 1.0 / columns[j][i : i + 1, :]
            row = system[i : i + 1, :] * scale
            system = jnp.where(here, row, system - columns[j] * row)
            for other in range(j + 1, 8):
                entry = columns[other][i : i + 1, :] * scale
                columns[other] = jnp.where(here, entry, columns[other] - columns[j] * entry)
    step = jnp.transpose(system)[2 * loads : 3 * loads, :]
    padded = jnp.concatenate([step, jnp.zeros((loads, LANES - loads), F32)], axis=1) if (
        step.shape[1] < LANES
    ) else step
    left = paired_left(padded, loads, parts)[:, : 2 * loads]

    writes = []
    for comp in range(sz.comps):
        for copy in copies[comp]:
            copy.wait()

        def at(cell, carry, comp=comp):
            tile = comp * sz.cells + cell
            right = jnp.concatenate([dir_split[tile], image_split[tile]], axis=1)
            part = jnp.dot(left, right, preferred_element_type=F32)
            part = part[:loads] + part[loads:]
            rows = pl.ds(comp * loads * sz.cells + cell, loads, stride=sz.cells)
            new_iterate[rows, :] = iterate[rows, :] + part[:, :LANES]
            new_residual[rows, :] = res[rows, :] - part[:, LANES:]
            return carry

        lax.fori_loop(0, sz.cells, at, 0, unroll=8)
        part = pl.ds(comp * loads * sz.cells, loads * sz.cells)
        for j, (source, target) in enumerate(zip((new_iterate, new_residual), outs)):
            writes.append(
                pltpu.make_async_copy(source.at[part], target.at[part], out_sem.at[j, comp])
            )
            writes[-1].start()
    for copy in writes:
        copy.wait()


def body(
    iterate, residual, cell_ids, materials, eigen_counts, coarse_rank, eigen_basis, coarse_inverse
):
    sz = Sizes(residual, eigen_basis, coarse_inverse)
    shape = jax.ShapeDtypeStruct
    devices = 1
    for axis in AXES:
        devices = devices * lax.axis_size(axis)
    blocks = sz.total_rows // sz.block_rows
    smem, vmem, scratch, dma = pltpu.SMEM, pltpu.VMEM, pltpu.VMEM, pltpu.SemaphoreType.DMA
    res = residual.reshape(-1, LANES)
    old = iterate.reshape(-1, LANES)
    ids = cell_ids.reshape(-1, LANES)

    def call(name, kernel, *args, **kwargs):
        return vmem_call(name, lambda *refs: kernel(sz, *refs), *args, **kwargs)

    face = shape((sz.face_x + 2 * sz.cy, LANES), BF16)
    faces = call(
        "pack_x",
        pack_x,
        [face] * swaps("gx"),
        [scratch((sz.comps * sz.loads, sz.cy, LANES), F32)] * 2
        + [scratch((sz.cells, LANES), jnp.int32), dma((3,))],
        60,
        1 << 20,
        2 << 20,
        [residual.reshape(-1, sz.cells, LANES), ids],
        spaces=[pl.ANY, pl.ANY],
    )
    xhalo = exchange(faces, "gx")

    vectors = eigen_basis.reshape(sz.slots, sz.tiles, LANES)
    packed = call(
        "pieces",
        make_pieces,
        shape((sz.loads // 2, LANES), BF16),
        [
            scratch((sz.loads, LANES), F32),
            scratch((sz.slots, sz.tiles, LANES), F32),
            scratch((sz.comps, sz.loads * sz.cells, LANES), F32),
            dma((2, sz.comps)),
        ],
        60,
        1 << 27,
        7 << 20,
        [
            eigen_counts,
            coarse_rank,
            vectors,
            residual.reshape(sz.comps, -1, LANES),
            faces[0],
        ],
        spaces=[smem, smem, pl.ANY, pl.ANY, pl.ANY],
    )

    yface = shape((sz.face_y + HALO_IDS, LANES), BF16)
    message, *faces = call(
        "pack_y",
        pack_y,
        [shape((devices,) + packed.shape, BF16)] + [yface] * swaps("gy"),
        [scratch((HALO_IDS, LANES), F32)] * 2,
        8,
        1 << 20,
        2 << 20,
        [res, ids, packed] + xhalo,
    )
    yhalo = exchange(faces, "gy")
    gathered = lax.all_to_all(message, AXES, 0, 0, tiled=True)
    rows = (sz.cx + 4) * sz.pitch
    zmessage, id_box = call(
        "pack_z",
        pack_z,
        [shape((sz.face_z + HALO_IDS, LANES), BF16), shape((rows, LANES), F32)],
        [scratch((sz.box * 8, LANES), F32), scratch((rows, LANES), F32)],
        8,
        1 << 22,
        3 << 20,
        [res, ids] + xhalo + yhalo,
    )
    zhalo = exchange([zmessage] * 2, "col")

    tile = (1, sz.loads // 2, LANES)
    if sz.block_rows != 64:
        tile = (sz.block_rows // LANES, sz.loads, LANES)
    wide = (8, max(LANES, devices))
    partial, starts = call(
        "coarse",
        place_pieces,
        [shape((blocks,) + tile, F32), shape(wide, jnp.int32)],
        [
            scratch((sz.total_rows // LANES + 1, sz.loads, LANES), F32),
            scratch((sz.loads, LANES), F32),
            scratch((devices, LANES), F32),
            smem(wide, jnp.int32),
            dma,
        ],
        12,
        1 << 23,
        1 << 20,
        [gathered, coarse_inverse, zmessage],
        spaces=[vmem, vmem, pl.ANY],
    )
    coarse = lax.all_to_all(partial, ("gx", "col"), 0, 0, tiled=True)
    coarse = coarse.reshape((-1,) + tile[1:])

    field = scratch((sz.comps, sz.box, sz.loads, LANES), F32)
    direction, own, zface, *faces = call(
        "solve",
        solve_and_direct,
        [
            shape((sz.comps, sz.cells, sz.loads, LANES), F32),
            shape((8, sz.cells, LANES), F32),
            shape((sz.face_z, LANES), BF16),
        ]
        + [shape((sz.face_x, LANES), BF16)] * swaps("gx")
        + [shape((sz.inner_y, LANES), BF16)] * swaps("gy"),
        [
            field,
            field,
            field,
            scratch((3, sz.comps, sz.loads, LANES), F32),
            scratch((2, sz.comps, sz.loads, LANES), F32),
            scratch((9, rows, LANES), F32),
            scratch((9, 8, LANES), F32),
            scratch((rows, LANES), F32),
            scratch((rows, LANES), F32),
            scratch((2 * sz.loads, LANES), BF16),
            scratch((sz.face_z, LANES), F32),
            scratch((sz.slots, sz.tiles, LANES), F32),
            smem(starts.shape, jnp.int32),
            dma((2,)),
        ],
        56,
        1 << 28,
        8 << 20,
        [eigen_counts, materials, starts, res, id_box, coarse, vectors] + xhalo + yhalo + zhalo,
        spaces=[smem, smem, pl.ANY, vmem, vmem, vmem, pl.ANY]
        + [vmem] * len(xhalo + yhalo + zhalo),
    )
    xhalo = exchange(faces[: swaps("gx")], "gx")
    yhalo = exchange(faces[swaps("gx") :], "gy")
    zhalo = exchange([zface] * 2, "col")
    sums_shape = (sz.loads // 2, LANES)
    dir_split, image_split, sums = call(
        "image",
        make_image,
        [
            shape((sz.tiles, 2 * sz.loads, LANES), BF16),
            shape((sz.tiles, 2 * sz.loads, LANES), BF16),
            shape(sums_shape, F32),
        ],
        [
            field,
            scratch((sz.comps, sz.loads, LANES), F32),
            scratch((sz.tiles, 2 * sz.loads, LANES), BF16),
            scratch((sz.tiles, 2 * sz.loads, LANES), BF16),
            dma((sz.comps, sz.cx)),
            dma((2, sz.comps, sz.cx)),
        ],
        56,
        1 << 28,
        8 << 20,
        [res, own, direction] + xhalo + yhalo + zhalo,
        spaces=[vmem, vmem, pl.ANY] + [vmem] * len(xhalo + yhalo + zhalo),
        direct=1 << 16,
    )
    over, operands = AXES, [sums]
    if lax.axis_size("gy") == 2:
        over = ("gx", "col")
        operands += exchange([sums], "gy")
        devices = devices // 2
    spread = call(
        "share_sums", share_sums, shape((devices,) + sums_shape, F32), [], 4, 1 << 12, 1 << 17,
        operands,
    )
    sums = lax.all_to_all(spread, over, 0, 0, tiled=True)
    flat = shape(res.shape, F32)
    new_iterate, new_residual = call(
        "finish",
        finish,
        [flat, flat],
        [scratch(res.shape, F32)] * 2
        + [scratch(dir_split.shape, BF16)] * 2
        + [scratch(res.shape, F32)] * 2
        + [scratch((2 * sz.loads, LANES), BF16), dma((4, sz.comps)), dma((2, sz.comps))],
        60,
        1 << 27,
        9 << 20,
        [sums, old, res, dir_split, image_split],
        spaces=[vmem] + [pl.ANY] * 4,
        direct=1 << 16,
    )
    return (new_iterate.reshape(iterate.shape), new_residual.reshape(residual.shape))


def solution(mesh):
    placed = (
        P(None, None, "gx", "gy", "col"),
        P(None, None, "gx", "gy", "col"),
        P("gx", "gy", "col"),
        P(),
        P(("gx", "gy", "col")),
        P(("gx", "gy", "col")),
        P(None, None, "gx", "gy", "col"),
        P(("gx", "col"), None),
    )
    return jax.shard_map(
        body,
        mesh=mesh,
        in_specs=placed,
        out_specs=(P(None, None, "gx", "gy", "col"), P(None, None, "gx", "gy", "col")),
        check_vma=False,
    )
```

```python
import jax
import jax.numpy as jnp
from jax import lax
from jax.experimental import pallas as pl
from jax.experimental.pallas import tpu as pltpu
from jax.sharding import PartitionSpec as P

DAMPING = 0.6
F32 = jnp.float32
BF16 = jnp.bfloat16
LANES = 128
HALO_IDS = 16
AXES = ("gx", "gy", "col")
TRANSPOSED = (((1,), (1,)), ((), ()))


def split_hi_lo(value):
    hi = value.astype(BF16)
    return hi, (value - hi.astype(F32)).astype(BF16)


def paired_left(value, width, parts):
    rows = value.shape[0]
    hi, lo = split_hi_lo(value)
    parts[pl.ds(0, rows), :] = hi
    parts[pl.ds(rows, rows), :] = lo
    high = parts[pl.ds(0, rows), :].astype(F32)
    low = parts[pl.ds(rows, rows), :].astype(F32)
    return jnp.concatenate([high + roll_lanes(high, width), low], axis=0).astype(BF16)


def lane_ids(rows):
    return lax.broadcasted_iota(jnp.int32, (rows, LANES), 1)


def roll_lanes(value, shift):
    if isinstance(shift, int):
        shift = shift % LANES
        if shift == 0:
            return value
    return pltpu.roll(value, shift, axis=1)


def vmem_call(name, kernel, outs, scratch, limit_mib, flops, moved, operands, spaces=None):
    spaces = spaces or [pltpu.VMEM] * len(operands)
    return pl.pallas_call(
        kernel,
        name=name,
        out_shape=outs,
        in_specs=[pl.BlockSpec(memory_space=space) for space in spaces],
        out_specs=jax.tree.map(lambda _: pl.BlockSpec(memory_space=pltpu.VMEM), outs),
        scratch_shapes=scratch,
        compiler_params=pltpu.CompilerParams(vmem_limit_bytes=limit_mib << 20),
        cost_estimate=pl.CostEstimate(flops=flops, bytes_accessed=moved, transcendentals=0),
    )(*operands)


def own_index():
    index = 0
    for axis in AXES:
        index = index * lax.axis_size(axis) + lax.axis_index(axis)
    return index


class Sizes:
    def __init__(self, residual, eigen_basis, coarse_inverse):
        self.comps, self.loads, self.cx, self.cy, _ = residual.shape
        self.slots = eigen_basis.shape[0]
        self.block_rows, self.total_rows = coarse_inverse.shape
        self.cells = self.cx * self.cy
        self.bx, self.by = self.cx + 2, self.cy + 2
        self.box = self.bx * self.by
        self.tiles = self.comps * self.cells
        self.face_x = self.comps * self.cy * self.loads
        self.face_y = self.comps * self.bx * self.loads
        self.inner_y = self.comps * self.cx * self.loads
        self.face_z = self.comps * self.loads
        self.pitch = 16


class Halo:
    def __init__(self, axis, refs):
        self.refs = refs
        self.even = lax.rem(lax.axis_index(axis), 2) == 0

    def side(self, rows, first):
        value = self.refs[0][rows, :].astype(F32)
        other = self.refs[1][rows, :].astype(F32) if len(self.refs) > 1 else jnp.zeros_like(value)
        return jnp.where(self.even, value, other) if first else jnp.where(self.even, other, value)

    def below(self, rows):
        return self.side(rows, False)

    def above(self, rows):
        return self.side(rows, True)

    def send(self, rows, low, high):
        self.refs[0][rows, :] = jnp.where(self.even, high, low).astype(BF16)
        if len(self.refs) > 1:
            self.refs[1][rows, :] = jnp.where(self.even, low, high).astype(BF16)


def swaps(axis):
    return 1 if lax.axis_size(axis) == 2 else 2


def exchange(faces, axis):
    devices = lax.axis_size(axis)
    result = []
    for parity in range(swaps(axis)):
        pairs = []
        for low in range(parity, devices - 1, 2):
            pairs += [(low, low + 1), (low + 1, low)]
        result.append(lax.ppermute(faces[parity], axis, pairs))
    return result


def take_halos(refs, *axes):
    refs = list(refs)
    halos = []
    for axis in axes:
        count = swaps(axis)
        halos.append(Halo(axis, refs[:count]))
        refs = refs[count:]
    return halos + [refs]


def own_rows(sz, ref, comp, cell):
    start = comp * sz.loads * sz.cells + cell
    return ref[pl.ds(start, sz.loads, stride=sz.cells), :]


def pack_x(sz, res, ids, *refs):
    xsend, (low, high, id_rows, sem) = take_halos(refs, "gx")
    copies = [
        pltpu.make_async_copy(res.at[:, pl.ds(0, sz.cy)], low, sem.at[0]),
        pltpu.make_async_copy(res.at[:, pl.ds(sz.cells - sz.cy, sz.cy)], high, sem.at[1]),
        pltpu.make_async_copy(ids, id_rows, sem.at[2]),
    ]
    for copy in copies:
        copy.start()
    for copy in copies:
        copy.wait()
    low, high = (ref.reshape(sz.comps * sz.loads * sz.cy, LANES) for ref in (low, high))
    for comp in range(sz.comps):
        for y in range(sz.cy):
            rows = pl.ds((comp * sz.cy + y) * sz.loads, sz.loads)
            taken = pl.ds(comp * sz.loads * sz.cy + y, sz.loads, stride=sz.cy)
            xsend.send(rows, low[taken, :], high[taken, :])
    two = 2 * sz.cy
    first = (id_rows[pl.ds(0, two), :] + 1).astype(F32)
    last = (id_rows[pl.ds(sz.cells - two, two), :] + 1).astype(F32)
    xsend.send(pl.ds(sz.face_x, two), first, last)


def make_pieces(
    sz, count, rank, basis_in, res_in, after, message, split, wide, basis_rows, res_rows, sem
):
    del after
    slots, loads = sz.slots, sz.loads
    copies = []
    for comp in range(sz.comps):
        part = pl.ds(comp * sz.cells, sz.cells)
        copies.append(
            (
                pltpu.make_async_copy(
                    basis_in.at[:, part], basis_rows.at[:, part], sem.at[0, comp]
                ),
                pltpu.make_async_copy(res_in.at[comp], res_rows.at[comp], sem.at[1, comp]),
            )
        )
    for pair in copies:
        for copy in pair:
            copy.start()
    basis = basis_rows.reshape(slots * sz.tiles, LANES)
    res = res_rows.reshape(sz.tiles * loads, LANES)

    def step(index, carry):
        both, low = carry
        basis_hi, basis_lo, res_hi, res_both = [], [], [], []
        for half in range(2):
            tile = index * 2 + half
            comp = tile // sz.cells
            hi, lo = split_hi_lo(basis[pl.ds(tile, slots, stride=sz.tiles), :])
            split[tile, pl.ds(0, slots), :] = hi
            split[tile, pl.ds(slots, slots), :] = lo
            value_hi, value_lo = split_hi_lo(own_rows(sz, res, comp, tile - comp * sz.cells))
            basis_hi.append(hi)
            basis_lo.append(lo)
            res_hi.append(value_hi)
            res_both.append(jnp.concatenate([value_hi, value_lo], axis=0))
        both = both + lax.dot_general(
            jnp.concatenate(res_both, axis=1),
            jnp.concatenate(basis_hi, axis=1),
            TRANSPOSED,
            preferred_element_type=F32,
        )
        low = low + lax.dot_general(
            jnp.concatenate(res_hi, axis=1),
            jnp.concatenate(basis_lo, axis=1),
            TRANSPOSED,
            preferred_element_type=F32,
        )
        return both, low

    carry = (jnp.zeros((2 * loads, slots), F32), jnp.zeros((loads, slots), F32))
    for comp in range(sz.comps):
        for copy in copies[comp]:
            copy.wait()
        carry = lax.fori_loop(
            comp * sz.cells // 2, (comp + 1) * sz.cells // 2, step, carry, unroll=4
        )
    both, low = carry
    pieces = both[:loads] + both[loads:] + low
    slot = lax.broadcasted_iota(jnp.int32, pieces.shape, 1)
    wide[...] = jnp.zeros_like(wide)
    wide[:, pl.ds(0, slots)] = jnp.where(slot < count[0], pieces, 0.0)
    half = loads // 2
    lane = lane_ids(half)
    packed = jnp.where(lane < 64, wide[:half, :], roll_lanes(wide[half:, :], 64))
    packed = jnp.where(lane == slots, count[0].astype(F32), packed)
    packed = jnp.where(lane == slots + 1, rank[0].astype(F32), packed)
    message[...] = packed.astype(BF16)


def pack_y(sz, res, ids, packed, *refs):
    xhalo, refs = take_halos(refs, "gx")
    message = refs[0]
    ysend, (side_low, side_high) = take_halos(refs[1:], "gy")
    for device in range(message.shape[0]):
        message[device] = packed[...]
    last = sz.cy - 1
    for comp in range(sz.comps):
        for x in range(sz.bx):
            rows = pl.ds((comp * sz.bx + x) * sz.loads, sz.loads)
            if 0 < x < sz.bx - 1:
                low, high = (own_rows(sz, res, comp, (x - 1) * sz.cy + y) for y in (0, last))
            else:
                side = xhalo.below if x == 0 else xhalo.above
                low, high = (
                    side(pl.ds((comp * sz.cy + y) * sz.loads, sz.loads)) for y in (0, last)
                )
            ysend.send(rows, low, high)
    ids_below = xhalo.below(pl.ds(sz.face_x, 2 * sz.cy))
    ids_above = xhalo.above(pl.ds(sz.face_x, 2 * sz.cy))
    for x in range(sz.cx + 4):
        if x < 2:
            rows = ids_below[x * sz.cy : (x + 1) * sz.cy]
        elif x >= sz.cx + 2:
            rows = ids_above[(x - sz.cx - 2) * sz.cy : (x - sz.cx - 1) * sz.cy]
        else:
            rows = (ids[pl.ds((x - 2) * sz.cy, sz.cy), :] + 1).astype(F32)
        side_low[pl.ds(2 * x, 2), :] = rows[:2]
        side_high[pl.ds(2 * x, 2), :] = rows[sz.cy - 2 :]
    ysend.send(pl.ds(sz.face_y, HALO_IDS), side_low[...], side_high[...])


def box_tile(sz, res, xhalo, yhalo, comp, x, y):
    if y == 0 or y == sz.by - 1:
        side = yhalo.below if y == 0 else yhalo.above
        return side(pl.ds((comp * sz.bx + x) * sz.loads, sz.loads))
    if x == 0 or x == sz.bx - 1:
        side = xhalo.below if x == 0 else xhalo.above
        return side(pl.ds((comp * sz.cy + y - 1) * sz.loads, sz.loads))
    return own_rows(sz, res, comp, (x - 1) * sz.cy + y - 1)


def pack_z(sz, res, ids, *refs):
    xhalo, yhalo, (out, id_box, star, outer) = take_halos(refs, "gx", "gy")
    pitch = sz.pitch
    id_box[...] = jnp.zeros_like(id_box)
    two = 2 * sz.cy
    ids_below = xhalo.below(pl.ds(sz.face_x, two))
    ids_above = xhalo.above(pl.ds(sz.face_x, two))
    ids_low = yhalo.below(pl.ds(sz.face_y, HALO_IDS))
    ids_high = yhalo.above(pl.ds(sz.face_y, HALO_IDS))
    for x in range(sz.cx + 4):
        if x < 2:
            rows = ids_below[x * sz.cy : (x + 1) * sz.cy]
        elif x >= sz.cx + 2:
            rows = ids_above[(x - sz.cx - 2) * sz.cy : (x - sz.cx - 1) * sz.cy]
        else:
            rows = (ids[pl.ds((x - 2) * sz.cy, sz.cy), :] + 1).astype(F32)
        id_box[pl.ds(x * pitch + 2, sz.cy), :] = rows
        id_box[pl.ds(x * pitch, 2), :] = ids_low[2 * x : 2 * x + 2]
        id_box[pl.ds(x * pitch + sz.cy + 2, 2), :] = ids_high[2 * x : 2 * x + 2]
    values = id_box[...]
    lane = lane_ids(values.shape[0])
    outer[...] = jnp.where(lane == LANES - 1, roll_lanes(values, 1), roll_lanes(values, -1))
    star[...] = jnp.zeros_like(star)
    lane8 = lane_ids(8)
    taken = jnp.zeros((8, LANES), F32)
    for x in range(sz.bx):
        for y in range(sz.by):
            place = x * sz.by + y
            row = (x + 1) * pitch + y + 1
            for j, shift in enumerate((0, -pitch, pitch, -1, 1)):
                star[pl.ds(place * 8 + j, 1), :] = id_box[pl.ds(row + shift, 1), :]
            star[pl.ds(place * 8 + 5, 1), :] = outer[pl.ds(row, 1), :]
    for place in range(sz.box):
        picked = roll_lanes(star[pl.ds(place * 8, 8), :], 2 * place + 1)
        taken = jnp.where((lane8 >> 1) == place, picked, taken)
    out[pl.ds(sz.face_z, HALO_IDS), :] = jnp.concatenate(
        [taken, jnp.zeros((HALO_IDS - 8, LANES), F32)], axis=0
    ).astype(BF16)
    lane_k = lane_ids(sz.loads)
    for comp in range(sz.comps):
        total = jnp.zeros((sz.loads, LANES), F32)
        for x in range(sz.bx):
            for y in range(sz.by):
                place = x * sz.by + y
                tile = box_tile(sz, res, xhalo, yhalo, comp, x, y)
                total = jnp.where(
                    (lane_k >> 1) == place, roll_lanes(tile, 2 * place + 1), total
                )
        out[pl.ds(comp * sz.loads, sz.loads), :] = total.astype(BF16)


def place_pieces(
    sz, gathered, inverse, after, message, starts_out, vector, wide, heads, starts, sem
):
    del after
    devices = gathered.shape[0]
    for device in range(devices):
        heads[pl.ds(device, 1), :] = gathered[device].astype(F32)[0:1]
    values = heads[...]
    ranks = jnp.transpose(values)[sz.slots + 1 : sz.slots + 2, :]
    earlier = values[:, sz.slots + 1 : sz.slots + 2] < ranks
    total = jnp.sum(jnp.where(earlier, values[:, sz.slots : sz.slots + 1], 0.0), axis=0, keepdims=True)
    starts_out[...] = jnp.zeros_like(starts_out)
    starts_out[:, pl.ds(0, devices)] = jnp.broadcast_to(total.astype(jnp.int32), (8, devices))
    copy = pltpu.make_async_copy(starts_out, starts, sem)
    copy.start()
    half = sz.loads // 2
    lane = lane_ids(half)
    vector[...] = jnp.zeros_like(vector)
    copy.wait()

    def place(device, carry):
        start = starts[0, device]
        block = start // LANES
        offset = start - block * LANES
        packed = gathered[device].astype(F32)
        low = jnp.where(lane < sz.slots, packed, 0.0)
        high = jnp.where((lane >= 64) & (lane < 64 + sz.slots), packed, 0.0)
        both = jnp.concatenate(
            [
                pltpu.roll(low, offset, axis=1),
                pltpu.roll(high, lax.rem(offset + 64, LANES), axis=1),
            ],
            axis=0,
        )
        wide_lane = lane_ids(sz.loads)
        vector[block] = vector[block] + jnp.where(wide_lane >= offset, both, 0.0)
        vector[block + 1] = vector[block + 1] + jnp.where(wide_lane < offset, both, 0.0)
        return carry

    lax.fori_loop(0, gathered.shape[0], place, 0, unroll=8)
    total = jnp.zeros((sz.loads, sz.block_rows), F32)
    for block in range(sz.total_rows // LANES):
        total = total + lax.dot_general(
            vector[block].astype(BF16),
            inverse[:, pl.ds(block * LANES, LANES)],
            TRANSPOSED,
            preferred_element_type=F32,
        )
    if sz.block_rows == 64:
        wide[...] = jnp.zeros_like(wide)
        wide[:, pl.ds(0, 64)] = total
        packed = jnp.where(lane < 64, wide[:half, :], roll_lanes(wide[half:, :], 64))
        for device in range(message.shape[0]):
            message[device, 0] = packed
    else:
        for device in range(message.shape[0]):
            for block in range(sz.block_rows // LANES):
                message[device, block] = total[:, block * LANES : (block + 1) * LANES]


def own_coefs(sz, coefs, start):
    if sz.block_rows == 64:
        half = sz.loads // 2
        block = start // 64
        offset = start - block * 64
        first = coefs[block]
        second = coefs[jnp.minimum(block + 1, coefs.shape[0] - 1)]
        lane = lane_ids(half)
        top = jnp.where(lane < 64, first, roll_lanes(second, 64))
        bottom = jnp.where(lane < 64, roll_lanes(first, 64), second)
        both = jnp.concatenate([top, bottom], axis=0)
    else:
        block = start // LANES
        offset = start - block * LANES
        first = coefs[block]
        second = coefs[jnp.minimum(block + 1, coefs.shape[0] - 1)]
        both = jnp.where(lane_ids(sz.loads) >= offset, first, second)
    return pltpu.roll(both, lax.rem(LANES - offset, LANES), axis=1)


def look_up(table, row, ids):
    result = jnp.zeros_like(ids)
    for material in range(table.shape[1]):
        result = jnp.where(ids == material + 1, table[row, material], result)
    return result


DINV, KEEP, DLAM, WXM, WXP, WYM, WYP, WZM, WZP = range(9)


def spread_row(ref, index, row):
    return ref[index, pl.ds(row, 8, stride=0), :]


def make_coefs(sz, table, id_box, halo_ids, coefs, halo_coefs, own, mu_box, halo_mu):
    pitch = sz.pitch
    mu_box[...] = look_up(table, 0, id_box[...])
    lam_box = look_up(table, 1, id_box[...])
    mu_halo = look_up(table, 0, halo_ids)
    lam_halo = look_up(table, 1, halo_ids)
    lane8 = lane_ids(8)
    center = jnp.broadcast_to(mu_halo[0:1], (8, LANES))
    inner = jnp.zeros((8, LANES), F32)
    for place in range(sz.box):
        row = (place // sz.by + 1) * pitch + place % sz.by + 1
        halo_mu[pl.ds(row, 1), :] = roll_lanes(center, -2 * place)[0:1]
        spread = jnp.broadcast_to(mu_box[pl.ds(row, 1), :], (8, LANES))
        here = (((lane8 + 1) >> 1) & 63) == place
        inner = jnp.where(here, roll_lanes(spread, 2 * place), inner)
    rows_id = lax.broadcasted_iota(jnp.int32, (pitch, LANES), 0)
    lane = lane_ids(pitch)
    for x in range(1, sz.bx + 1):
        mu = mu_box[pl.ds(x * pitch, pitch), :]
        edge = halo_mu[pl.ds(x * pitch, pitch), :]
        lam = lam_box[x * pitch : (x + 1) * pitch]
        faces = [
            0.5 * (mu + mu_box[pl.ds((x - 1) * pitch, pitch), :]),
            0.5 * (mu + mu_box[pl.ds((x + 1) * pitch, pitch), :]),
            0.5 * (mu + mu_box[pl.ds(x * pitch - 1, pitch), :]),
            0.5 * (mu + mu_box[pl.ds(x * pitch + 1, pitch), :]),
            0.5 * (mu + jnp.where(lane == 0, edge, roll_lanes(mu, 1))),
            0.5 * (mu + jnp.where(lane == LANES - 1, edge, roll_lanes(mu, -1))),
        ]
        diag = 1.0 + sum(faces)
        dinv = DAMPING / (diag + lam)
        rows = pl.ds(x * pitch, pitch)
        coefs[DINV, rows, :] = dinv
        coefs[KEEP, rows, :] = (1.0 - DAMPING) + dinv * lam
        coefs[DLAM, rows, :] = dinv * lam
        weights = [dinv * face for face in faces]
        if x == 1:
            weights[0] = jnp.zeros_like(dinv)
        if x == sz.bx:
            weights[1] = jnp.zeros_like(dinv)
        weights[2] = jnp.where(rows_id == 1, 0.0, weights[2])
        weights[3] = jnp.where(rows_id == sz.by, 0.0, weights[3])
        for j in range(6):
            coefs[WXM + j, rows, :] = weights[j]
        if 2 <= x <= sz.cx + 1:
            target = pl.ds((x - 2) * sz.cy, sz.cy)
            for j, value in enumerate([diag, lam] + faces):
                own[j, target, :] = value[2 : 2 + sz.cy]
    place = ((lane8 + 1) >> 1) & 63
    column = jnp.zeros_like(place)
    for x in range(1, sz.bx):
        column = column + (place >= x * sz.by).astype(jnp.int32)
    y_place = place - column * sz.by
    others = [jnp.broadcast_to(mu_halo[j : j + 1], (8, LANES)) for j in range(1, 6)]
    faces = [0.5 * (center + other) for other in others] + [0.5 * (center + inner)]
    lam = jnp.broadcast_to(lam_halo[0:1], (8, LANES))
    dinv = DAMPING / (1.0 + lam + sum(faces))
    live = place < sz.box
    keep = [
        live & (column > 0),
        live & (column < sz.bx - 1),
        live & (y_place > 0),
        live & (y_place < sz.by - 1),
        None,
        live,
    ]
    halo_coefs[DINV] = dinv
    halo_coefs[KEEP] = (1.0 - DAMPING) + dinv * lam
    halo_coefs[DLAM] = dinv * lam
    for j, target in ((0, WXM), (1, WXP), (2, WYM), (3, WYP), (5, WZM)):
        halo_coefs[target] = jnp.where(keep[j], dinv * faces[j], 0.0)


def neighbour_matrix(copies, spread):
    width = (3 if spread else 2) * LANES
    parts = []
    for copy in range(copies + 1):
        row = lax.broadcasted_iota(jnp.int32, (LANES, width), 0)
        lane = lax.broadcasted_iota(jnp.int32, (LANES, width), 1)
        even = (row & 1) == 0
        if copy < copies:
            hit = ((lane < LANES) & (row == lane - 1)) | (
                (lane >= LANES) & (lane < 2 * LANES) & (row == lane - LANES + 1)
            )
            if spread:
                source = jnp.where((lane & 1) == 0, 0, LANES - 1)
                hit = hit | ((lane >= 2 * LANES) & (row == source))
        else:
            hit = ((lane == 0) & even) | ((lane == 2 * LANES - 1) & jnp.logical_not(even))
        parts.append(jnp.where(hit, 1.0, 0.0).astype(BF16))
    return jnp.concatenate(parts, axis=0)


def z_halo(zhalo, rows):
    down, up = zhalo.below(rows), zhalo.above(rows)
    even = (lane_ids(down.shape[0]) & 1) == 0
    return jnp.where(even, down, roll_lanes(up, -2))


def solve_and_direct(sz, count, table, starts_in, res, id_box, coarse, split, *refs):
    xhalo, yhalo, zhalo, refs = take_halos(refs, "gx", "gy", "col")
    direction, own, zface = refs[:3]
    xsend, ysend, refs = take_halos(refs[3:], "gx", "gy")
    first, second, third, halos, inner, coefs, halo_coefs, mu_box, halo_mu, left, zedge = refs[:11]
    wide, own_rows_coef, weights, lhs, near, starts, sem = refs[11:]
    copy = pltpu.make_async_copy(starts_in, starts, sem)
    copy.start()
    loads, comps = sz.loads, sz.comps
    groups = loads // 8
    lane8 = lane_ids(8)

    halo_mu[...] = jnp.zeros_like(halo_mu)
    inner[...] = jnp.zeros_like(inner)
    make_coefs(
        sz, table, id_box, z_halo(zhalo, pl.ds(sz.face_z, HALO_IDS))[:8], coefs, halo_coefs, own_rows_coef,
        mu_box, halo_mu,
    )

    weights[...] = neighbour_matrix(1, True)

    def spread(place, carry):
        x = place // sz.by
        row = (x + 1) * sz.pitch + place - x * sz.by + 1
        for j in range(9):
            wide[j, place] = jnp.broadcast_to(coefs[j, pl.ds(row, 1), :], (8, LANES))
        return carry

    lax.fori_loop(0, sz.box, spread, 0, unroll=4)

    def spread_own(cell, carry):
        for j in range(8):
            own[j, cell] = jnp.broadcast_to(own_rows_coef[j, pl.ds(cell, 1), :], (8, LANES))
        return carry

    lax.fori_loop(0, sz.cells, spread_own, 0, unroll=4)

    for comp in range(comps):
        halo = z_halo(zhalo, pl.ds(comp * loads, loads))
        dinv = jnp.concatenate([halo_coefs[DINV]] * groups, axis=0)
        halos[0, comp] = dinv * halo
        for x in range(sz.bx):
            for y in range(sz.by):
                place = x * sz.by + y
                tile = box_tile(sz, res, xhalo, yhalo, comp, x, y)
                first[comp, place] = tile * jnp.concatenate([wide[DINV, place]] * groups, axis=0)

    lane_k = lane_ids(loads)

    def relax(source, level, x, ys, put):
        count = len(ys)
        for j, y in enumerate(ys):
            place = x * sz.by + y
            here = (((lane_k + 1) >> 1) & 63) == place
            for comp in range(comps):
                rows = pl.ds((j * comps + comp) * loads, loads)
                lhs[rows, pl.ds(0, LANES)] = source[comp, place].astype(BF16)
                lhs[rows, pl.ds(LANES, LANES)] = jnp.where(here, halos[level, comp], 0.0).astype(BF16)
        size = count * comps * loads
        cut = 3 * LANES if level < 2 else 2 * LANES
        near[pl.ds(0, size), pl.ds(0, cut)] = jnp.dot(
            lhs[pl.ds(0, size), :], weights[:, pl.ds(0, cut)], preferred_element_type=F32
        )
        for j, y in enumerate(ys):
            place = x * sz.by + y
            coef = [wide[i, place] for i in range(9)]
            here = (((lane8 + 1) >> 1) & 63) == place
            xm, xp = jnp.maximum(place - sz.by, 0), jnp.minimum(place + sz.by, sz.box - 1)
            ym, yp = jnp.maximum(place - 1, 0), jnp.minimum(place + 1, sz.box - 1)
            for group in range(groups):
                rows = pl.ds(group * 8, 8)
                center = [source[comp, place, rows, :] for comp in range(comps)]
                coupled = coef[DLAM] * (center[0] + center[1] + center[2])
                for comp in range(comps):
                    value = center[comp]
                    at = pl.ds((j * comps + comp) * loads + group * 8, 8)
                    out = (first[comp, place, rows, :] - coupled) + coef[KEEP] * value
                    out = out + coef[WXM] * source[comp, xm, rows, :]
                    out = out + coef[WXP] * source[comp, xp, rows, :]
                    out = out + coef[WYM] * source[comp, ym, rows, :]
                    out = out + coef[WYP] * source[comp, yp, rows, :]
                    out = out + coef[WZM] * near[at, pl.ds(0, LANES)]
                    out = out + coef[WZP] * near[at, pl.ds(LANES, LANES)]
                    put(j, place, comp, group, out)
                    if level < 2:
                        pltpu.store(
                            inner.at[level, comp, rows, :],
                            near[at, pl.ds(2 * LANES, LANES)],
                            mask=here,
                        )

    def sweep(source, target, level):
        def put(j, place, comp, group, out):
            target[comp, place, pl.ds(group * 8, 8), :] = out

        def at(x, carry):
            relax(source, level, x, range(sz.by), put)
            return carry

        lax.fori_loop(0, sz.bx, at, 0)
        coef = [halo_coefs[j] for j in range(8)]
        for group in range(groups):
            rows = pl.ds(group * 8, 8)
            center = [halos[level, comp, rows, :] for comp in range(comps)]
            coupled = coef[DLAM] * (center[0] + center[1] + center[2])
            for comp in range(comps):
                value = center[comp]
                out = (halos[0, comp, rows, :] - coupled) + coef[KEEP] * value
                out = out + coef[WXM] * roll_lanes(value, 2 * sz.by)
                out = out + coef[WXP] * roll_lanes(value, -2 * sz.by)
                out = out + coef[WYM] * roll_lanes(value, 2)
                out = out + coef[WYP] * roll_lanes(value, -2)
                out = out + coef[WZM] * inner[level, comp, rows, :]
                halos[level + 1, comp, rows, :] = out

    sweep(first, second, 0)
    sweep(second, third, 1)

    copy.wait()
    mine = own_coefs(sz, coarse, starts[0, own_index()])
    mine = jnp.where(lane_ids(loads) < jnp.minimum(count[0], sz.slots), mine, 0.0)
    left[...] = paired_left(mine, sz.slots, left)
    zedge[...] = jnp.zeros_like(zedge)

    def final(x, carry):
        def put(j, place, comp, group, out):
            direction[comp, x * sz.cy + j, pl.ds(group * 8, 8), :] = out

        relax(third, 2, x + 1, range(1, sz.cy + 1), put)
        for y in range(sz.cy):
            cell = x * sz.cy + y
            place = (x + 1) * sz.by + y + 1
            for comp in range(comps):
                part = jnp.dot(
                    left[:, : 2 * sz.slots],
                    split[comp * sz.cells + cell],
                    preferred_element_type=F32,
                )
                value = direction[comp, cell] + (part[:loads] + part[loads:])
                direction[comp, cell] = value
                lhs[pl.ds((y * comps + comp) * loads, loads), pl.ds(0, LANES)] = value.astype(BF16)
        size = sz.cy * comps * loads
        near[pl.ds(0, size), pl.ds(0, LANES)] = jnp.dot(
            lhs[pl.ds(0, size), pl.ds(0, LANES)], edges, preferred_element_type=F32
        )
        for y in range(sz.cy):
            place = (x + 1) * sz.by + y + 1
            for comp in range(comps):
                pltpu.store(
                    zedge.at[pl.ds(comp * loads, loads), :],
                    near[pl.ds((y * comps + comp) * loads, loads), pl.ds(0, LANES)],
                    mask=(lane_k >> 1) == place,
                )
        return carry

    edge_row = lax.broadcasted_iota(jnp.int32, (LANES, LANES), 0)
    even_lane = (lane_ids(LANES) & 1) == 0
    edges = jnp.where(jnp.where(even_lane, LANES - 1, 0) == edge_row, 1.0, 0.0).astype(BF16)
    lax.fori_loop(0, sz.cx, final, 0)
    zface[...] = zedge[...].astype(BF16)
    for comp in range(comps):
        for y in range(sz.cy):
            rows = pl.ds((comp * sz.cy + y) * loads, loads)
            xsend.send(rows, direction[comp, y], direction[comp, (sz.cx - 1) * sz.cy + y])
        for x in range(sz.cx):
            rows = pl.ds((comp * sz.cx + x) * loads, loads)
            ysend.send(rows, direction[comp, x * sz.cy], direction[comp, (x + 1) * sz.cy - 1])


def make_image(sz, res, own, direction, *refs):
    xhalo, yhalo, zhalo, refs = take_halos(refs, "gx", "gy", "col")
    dir_split, image_split, message, box, halo, weights, lhs, near, sem = refs
    weights[...] = neighbour_matrix(2, False)
    loads, comps = sz.loads, sz.comps
    groups = loads // 8
    copies = []
    for comp in range(comps):
        for x in range(sz.cx):
            copies.append(
                pltpu.make_async_copy(
                    direction.at[comp, pl.ds(x * sz.cy, sz.cy)],
                    box.at[comp, pl.ds((x + 1) * sz.by + 1, sz.cy)],
                    sem.at[comp, x],
                )
            )
    for copy in copies:
        copy.start()
    for comp in range(comps):
        for y in range(sz.cy):
            rows = pl.ds((comp * sz.cy + y) * loads, loads)
            box[comp, y + 1] = xhalo.below(rows)
            box[comp, (sz.bx - 1) * sz.by + y + 1] = xhalo.above(rows)
        for x in range(sz.cx):
            rows = pl.ds((comp * sz.cx + x) * loads, loads)
            box[comp, (x + 1) * sz.by] = yhalo.below(rows)
            box[comp, (x + 1) * sz.by + sz.by - 1] = yhalo.above(rows)
        halo[comp] = z_halo(zhalo, pl.ds(comp * loads, loads))
    for copy in copies:
        copy.wait()
    lane_k = lane_ids(loads)

    def at(x, total):
        for y in range(sz.cy):
            cell = x * sz.cy + y
            place = (x + 1) * sz.by + y + 1
            here = (((lane_k + 1) >> 1) & 63) == place
            for comp in range(comps):
                hi, lo = split_hi_lo(box[comp, place])
                dir_split[comp * sz.cells + cell] = jnp.concatenate([hi, lo], axis=0)
                rows = pl.ds((y * comps + comp) * loads, loads)
                lhs[rows, pl.ds(0, LANES)] = hi
                lhs[rows, pl.ds(LANES, LANES)] = lo
                lhs[rows, pl.ds(2 * LANES, LANES)] = jnp.where(here, halo[comp], 0.0).astype(BF16)
        near[...] = jnp.dot(lhs[...], weights[...], preferred_element_type=F32)
        sides = {}
        for y in range(sz.cy):
            cell = x * sz.cy + y
            place = (x + 1) * sz.by + y + 1
            coef = [own[j, cell] for j in range(8)]
            parts = {}
            for group in range(groups):
                rows = pl.ds(group * 8, 8)
                center = [box[comp, place, rows, :] for comp in range(comps)]
                coupled = coef[1] * (center[0] + center[1] + center[2])
                for comp in range(comps):
                    line = pl.ds((y * comps + comp) * loads + group * 8, 8)
                    out = coef[0] * center[comp] + coupled
                    out = out - coef[2] * box[comp, place - sz.by, rows, :]
                    out = out - coef[3] * box[comp, place + sz.by, rows, :]
                    out = out - coef[4] * box[comp, place - 1, rows, :]
                    out = out - coef[5] * box[comp, place + 1, rows, :]
                    out = out - coef[6] * near[line, pl.ds(0, LANES)]
                    parts[comp, group] = out - coef[7] * near[line, pl.ds(LANES, LANES)]
            for comp in range(comps):
                tile = comp * sz.cells + cell
                field = jnp.concatenate([parts[comp, group] for group in range(groups)], axis=0)
                both = jnp.concatenate(split_hi_lo(field), axis=0)
                image_split[tile] = both
                right = jnp.concatenate((both,) + split_hi_lo(own_rows(sz, res, comp, cell)), axis=0)
                sides[y, comp] = (dir_split[tile], right)
            if y % 2 == 1:
                for comp in range(comps):
                    pair = zip(sides[y - 1, comp], sides[y, comp])
                    left, right = (jnp.concatenate(items, axis=1) for items in pair)
                    total = total + lax.dot_general(
                        left, right, TRANSPOSED, preferred_element_type=F32
                    )
        return total

    total = lax.fori_loop(0, sz.cx, at, jnp.zeros((2 * loads, 4 * loads), F32))
    high, low = total[:loads], total[loads:]
    sums = high + roll_lanes(high, -loads) + low
    half = loads // 2
    lane = lane_ids(half)
    packed = jnp.where((lane & (2 * loads - 1)) < loads, sums[:half], roll_lanes(sums[half:], loads))
    message[...] = packed


def share_sums(sz, mine, *refs):
    message = refs[-1]
    total = mine[...]
    for other in refs[:-1]:
        total = total + other[...]
    for device in range(message.shape[0]):
        message[device] = total


def finish(
    sz, sums, iterate, res, dir_split, image_split, new_iterate, new_residual, parts
):
    loads = sz.loads
    total = sums[0]
    for device in range(1, sums.shape[0]):
        total = total + sums[device]
    system = jnp.concatenate([total, roll_lanes(total, -loads)], axis=0)
    lane = lane_ids(loads)
    system = jnp.where((lane & (2 * loads - 1)) < loads, system, 0.0)
    row_ids = lax.broadcasted_iota(jnp.int32, (loads, LANES), 0)
    for base in range(0, loads, 8):
        columns = [
            jnp.broadcast_to(system[:, i : i + 1], (loads, LANES)) for i in range(base, base + 8)
        ]
        for j in range(8):
            i = base + j
            here = row_ids == i
            scale = 1.0 / columns[j][i : i + 1, :]
            row = system[i : i + 1, :] * scale
            system = jnp.where(here, row, system - columns[j] * row)
            for other in range(j + 1, 8):
                entry = columns[other][i : i + 1, :] * scale
                columns[other] = jnp.where(here, entry, columns[other] - columns[j] * entry)
    step = jnp.transpose(system)[2 * loads : 3 * loads, :]
    padded = jnp.concatenate([step, jnp.zeros((loads, LANES - loads), F32)], axis=1) if (
        step.shape[1] < LANES
    ) else step
    left = paired_left(padded, loads, parts)[:, : 2 * loads]

    def at(cell, carry):
        for comp in range(sz.comps):
            tile = comp * sz.cells + cell
            right = jnp.concatenate([dir_split[tile], image_split[tile]], axis=1)
            part = jnp.dot(left, right, preferred_element_type=F32)
            part = part[:loads] + part[loads:]
            rows = pl.ds(comp * loads * sz.cells + cell, loads, stride=sz.cells)
            new_iterate[rows, :] = iterate[rows, :] + part[:, :LANES]
            new_residual[rows, :] = res[rows, :] - part[:, LANES:]
        return carry

    lax.fori_loop(0, sz.cells, at, 0, unroll=4)


def body(
    iterate, residual, cell_ids, materials, eigen_counts, coarse_rank, eigen_basis, coarse_inverse
):
    sz = Sizes(residual, eigen_basis, coarse_inverse)
    shape = jax.ShapeDtypeStruct
    devices = 1
    for axis in AXES:
        devices = devices * lax.axis_size(axis)
    blocks = sz.total_rows // sz.block_rows
    smem, vmem, scratch, dma = pltpu.SMEM, pltpu.VMEM, pltpu.VMEM, pltpu.SemaphoreType.DMA
    res = residual.reshape(-1, LANES)
    old = iterate.reshape(-1, LANES)
    ids = cell_ids.reshape(-1, LANES)

    def call(name, kernel, *args, **kwargs):
        return vmem_call(name, lambda *refs: kernel(sz, *refs), *args, **kwargs)

    face = shape((sz.face_x + 2 * sz.cy, LANES), BF16)
    faces = call(
        "pack_x",
        pack_x,
        [face] * swaps("gx"),
        [scratch((sz.comps * sz.loads, sz.cy, LANES), F32)] * 2
        + [scratch((sz.cells, LANES), jnp.int32), dma((3,))],
        8,
        1 << 20,
        2 << 20,
        [residual.reshape(-1, sz.cells, LANES), ids],
        spaces=[pl.ANY, pl.ANY],
    )
    xhalo = exchange(faces, "gx")

    packed, split = call(
        "pieces",
        make_pieces,
        [
            shape((sz.loads // 2, LANES), BF16),
            shape((sz.tiles, 2 * sz.slots, LANES), BF16),
        ],
        [
            scratch((sz.loads, LANES), F32),
            scratch((sz.slots, sz.tiles, LANES), F32),
            scratch((sz.comps, sz.loads * sz.cells, LANES), F32),
            dma((2, sz.comps)),
        ],
        12,
        1 << 27,
        7 << 20,
        [
            eigen_counts,
            coarse_rank,
            eigen_basis.reshape(sz.slots, sz.tiles, LANES),
            residual.reshape(sz.comps, -1, LANES),
            faces[0],
        ],
        spaces=[smem, smem, pl.ANY, pl.ANY, pl.ANY],
    )

    yface = shape((sz.face_y + HALO_IDS, LANES), BF16)
    message, *faces = call(
        "pack_y",
        pack_y,
        [shape((devices,) + packed.shape, BF16)] + [yface] * swaps("gy"),
        [scratch((HALO_IDS, LANES), F32)] * 2,
        8,
        1 << 20,
        2 << 20,
        [res, ids, packed] + xhalo,
    )
    yhalo = exchange(faces, "gy")
    gathered = lax.all_to_all(message, AXES, 0, 0, tiled=True)
    rows = (sz.cx + 4) * sz.pitch
    zmessage, id_box = call(
        "pack_z",
        pack_z,
        [shape((sz.face_z + HALO_IDS, LANES), BF16), shape((rows, LANES), F32)],
        [scratch((sz.box * 8, LANES), F32), scratch((rows, LANES), F32)],
        8,
        1 << 22,
        3 << 20,
        [res, ids] + xhalo + yhalo,
    )
    zhalo = exchange([zmessage] * 2, "col")

    tile = (1, sz.loads // 2, LANES)
    if sz.block_rows != 64:
        tile = (sz.block_rows // LANES, sz.loads, LANES)
    wide = (8, max(LANES, devices))
    partial, starts = call(
        "coarse",
        place_pieces,
        [shape((blocks,) + tile, F32), shape(wide, jnp.int32)],
        [
            scratch((sz.total_rows // LANES + 1, sz.loads, LANES), F32),
            scratch((sz.loads, LANES), F32),
            scratch((devices, LANES), F32),
            smem(wide, jnp.int32),
            dma,
        ],
        12,
        1 << 23,
        1 << 20,
        [gathered, coarse_inverse, zmessage],
        spaces=[vmem, vmem, pl.ANY],
    )
    coarse = lax.all_to_all(partial, ("gx", "col"), 0, 0, tiled=True)
    coarse = coarse.reshape((-1,) + tile[1:])

    field = scratch((sz.comps, sz.box, sz.loads, LANES), F32)
    direction, own, zface, *faces = call(
        "solve",
        solve_and_direct,
        [
            shape((sz.comps, sz.cells, sz.loads, LANES), F32),
            shape((8, sz.cells, 8, LANES), F32),
            shape((sz.face_z, LANES), BF16),
        ]
        + [shape((sz.face_x, LANES), BF16)] * swaps("gx")
        + [shape((sz.inner_y, LANES), BF16)] * swaps("gy"),
        [
            field,
            field,
            field,
            scratch((3, sz.comps, sz.loads, LANES), F32),
            scratch((2, sz.comps, sz.loads, LANES), F32),
            scratch((9, rows, LANES), F32),
            scratch((9, 8, LANES), F32),
            scratch((rows, LANES), F32),
            scratch((rows, LANES), F32),
            scratch((2 * sz.loads, LANES), BF16),
            scratch((sz.face_z, LANES), F32),
            scratch((9, sz.box, 8, LANES), F32),
            scratch((8, sz.cells, LANES), F32),
            scratch((2 * LANES, 3 * LANES), BF16),
            scratch((sz.by * sz.comps * sz.loads, 2 * LANES), BF16),
            scratch((sz.by * sz.comps * sz.loads, 3 * LANES), F32),
            smem(starts.shape, jnp.int32),
            dma,
        ],
        26,
        1 << 28,
        8 << 20,
        [eigen_counts, materials, starts, res, id_box, coarse, split] + xhalo + yhalo + zhalo,
        spaces=[smem, smem, pl.ANY] + [vmem] * (4 + len(xhalo + yhalo + zhalo)),
    )
    xhalo = exchange(faces[: swaps("gx")], "gx")
    yhalo = exchange(faces[swaps("gx") :], "gy")
    zhalo = exchange([zface] * 2, "col")
    sums_shape = (sz.loads // 2, LANES)
    dir_split, image_split, sums = call(
        "image",
        make_image,
        [
            shape((sz.tiles, 2 * sz.loads, LANES), BF16),
            shape((sz.tiles, 2 * sz.loads, LANES), BF16),
            shape(sums_shape, F32),
        ],
        [
            field,
            scratch((sz.comps, sz.loads, LANES), F32),
            scratch((3 * LANES, 2 * LANES), BF16),
            scratch((sz.cy * sz.comps * sz.loads, 3 * LANES), BF16),
            scratch((sz.cy * sz.comps * sz.loads, 2 * LANES), F32),
            dma((sz.comps, sz.cx)),
        ],
        20,
        1 << 28,
        8 << 20,
        [res, own, direction] + xhalo + yhalo + zhalo,
        spaces=[vmem, vmem, pl.ANY] + [vmem] * len(xhalo + yhalo + zhalo),
    )
    over, operands = AXES, [sums]
    if lax.axis_size("gy") == 2:
        over = ("gx", "col")
        operands += exchange([sums], "gy")
        devices = devices // 2
    spread = call(
        "share_sums", share_sums, shape((devices,) + sums_shape, F32), [], 4, 1 << 12, 1 << 17,
        operands,
    )
    sums = lax.all_to_all(spread, over, 0, 0, tiled=True)
    flat = shape(res.shape, F32)
    new_iterate, new_residual = call(
        "finish",
        finish,
        [flat, flat],
        [scratch((2 * sz.loads, LANES), BF16)],
        16,
        1 << 27,
        9 << 20,
        [sums, old, res, dir_split, image_split],
    )
    return (new_iterate.reshape(iterate.shape), new_residual.reshape(residual.shape))


def solution(mesh):
    placed = (
        P(None, None, "gx", "gy", "col"),
        P(None, None, "gx", "gy", "col"),
        P("gx", "gy", "col"),
        P(),
        P(("gx", "gy", "col")),
        P(("gx", "gy", "col")),
        P(None, None, "gx", "gy", "col"),
        P(("gx", "col"), None),
    )
    return jax.shard_map(
        body,
        mesh=mesh,
        in_specs=placed,
        out_specs=(P(None, None, "gx", "gy", "col"), P(None, None, "gx", "gy", "col")),
        check_vma=False,
    )
```

```python
import jax
import jax.numpy as jnp
from jax import lax
from jax.experimental import pallas as pl
from jax.experimental.pallas import tpu as pltpu
from jax.sharding import PartitionSpec as P

DAMPING = 0.6
F32 = jnp.float32
BF16 = jnp.bfloat16
LANES = 128
HALO_IDS = 16
AXES = ("gx", "gy", "col")
TRANSPOSED = (((1,), (1,)), ((), ()))


def split_hi_lo(value):
    hi = value.astype(BF16)
    return hi, (value - hi.astype(F32)).astype(BF16)


def paired_left(value, width, parts):
    rows = value.shape[0]
    hi, lo = split_hi_lo(value)
    parts[pl.ds(0, rows), :] = hi
    parts[pl.ds(rows, rows), :] = lo
    high = parts[pl.ds(0, rows), :].astype(F32)
    low = parts[pl.ds(rows, rows), :].astype(F32)
    return jnp.concatenate([high + roll_lanes(high, width), low], axis=0).astype(BF16)


def lane_ids(rows):
    return lax.broadcasted_iota(jnp.int32, (rows, LANES), 1)


def roll_lanes(value, shift):
    if isinstance(shift, int):
        shift = shift % LANES
        if shift == 0:
            return value
    return pltpu.roll(value, shift, axis=1)


def vmem_call(name, kernel, outs, scratch, limit_mib, flops, moved, operands, spaces=None):
    spaces = spaces or [pltpu.VMEM] * len(operands)
    return pl.pallas_call(
        kernel,
        name=name,
        out_shape=outs,
        in_specs=[pl.BlockSpec(memory_space=space) for space in spaces],
        out_specs=jax.tree.map(lambda _: pl.BlockSpec(memory_space=pltpu.VMEM), outs),
        scratch_shapes=scratch,
        compiler_params=pltpu.CompilerParams(vmem_limit_bytes=limit_mib << 20),
        cost_estimate=pl.CostEstimate(flops=flops, bytes_accessed=moved, transcendentals=0),
    )(*operands)


def own_index():
    index = 0
    for axis in AXES:
        index = index * lax.axis_size(axis) + lax.axis_index(axis)
    return index


class Sizes:
    def __init__(self, residual, eigen_basis, coarse_inverse):
        self.comps, self.loads, self.cx, self.cy, _ = residual.shape
        self.slots = eigen_basis.shape[0]
        self.block_rows, self.total_rows = coarse_inverse.shape
        self.cells = self.cx * self.cy
        self.bx, self.by = self.cx + 2, self.cy + 2
        self.box = self.bx * self.by
        self.tiles = self.comps * self.cells
        self.face_x = self.comps * self.cy * self.loads
        self.face_y = self.comps * self.bx * self.loads
        self.inner_y = self.comps * self.cx * self.loads
        self.face_z = self.comps * self.loads
        self.pitch = 16


class Halo:
    def __init__(self, axis, refs):
        self.refs = refs
        self.even = lax.rem(lax.axis_index(axis), 2) == 0

    def side(self, rows, first):
        value = self.refs[0][rows, :].astype(F32)
        other = self.refs[1][rows, :].astype(F32) if len(self.refs) > 1 else jnp.zeros_like(value)
        return jnp.where(self.even, value, other) if first else jnp.where(self.even, other, value)

    def below(self, rows):
        return self.side(rows, False)

    def above(self, rows):
        return self.side(rows, True)

    def send(self, rows, low, high):
        self.refs[0][rows, :] = jnp.where(self.even, high, low).astype(BF16)
        if len(self.refs) > 1:
            self.refs[1][rows, :] = jnp.where(self.even, low, high).astype(BF16)


def swaps(axis):
    return 1 if lax.axis_size(axis) == 2 else 2


def exchange(faces, axis):
    devices = lax.axis_size(axis)
    result = []
    for parity in range(swaps(axis)):
        pairs = []
        for low in range(parity, devices - 1, 2):
            pairs += [(low, low + 1), (low + 1, low)]
        result.append(lax.ppermute(faces[parity], axis, pairs))
    return result


def take_halos(refs, *axes):
    refs = list(refs)
    halos = []
    for axis in axes:
        count = swaps(axis)
        halos.append(Halo(axis, refs[:count]))
        refs = refs[count:]
    return halos + [refs]


def own_rows(sz, ref, comp, cell):
    start = comp * sz.loads * sz.cells + cell
    return ref[pl.ds(start, sz.loads, stride=sz.cells), :]


def pack_x(sz, res, ids, *refs):
    xsend, (low, high, id_rows, sem) = take_halos(refs, "gx")
    copies = [
        pltpu.make_async_copy(res.at[:, pl.ds(0, sz.cy)], low, sem.at[0]),
        pltpu.make_async_copy(res.at[:, pl.ds(sz.cells - sz.cy, sz.cy)], high, sem.at[1]),
        pltpu.make_async_copy(ids, id_rows, sem.at[2]),
    ]
    for copy in copies:
        copy.start()
    for copy in copies:
        copy.wait()
    low, high = (ref.reshape(sz.comps * sz.loads * sz.cy, LANES) for ref in (low, high))
    for comp in range(sz.comps):
        for y in range(sz.cy):
            rows = pl.ds((comp * sz.cy + y) * sz.loads, sz.loads)
            taken = pl.ds(comp * sz.loads * sz.cy + y, sz.loads, stride=sz.cy)
            xsend.send(rows, low[taken, :], high[taken, :])
    two = 2 * sz.cy
    first = (id_rows[pl.ds(0, two), :] + 1).astype(F32)
    last = (id_rows[pl.ds(sz.cells - two, two), :] + 1).astype(F32)
    xsend.send(pl.ds(sz.face_x, two), first, last)


def make_pieces(
    sz, count, rank, basis_in, res_in, after, message, split, wide, basis_rows, res_rows, sem
):
    del after
    slots, loads = sz.slots, sz.loads
    copies = []
    for comp in range(sz.comps):
        part = pl.ds(comp * sz.cells, sz.cells)
        copies.append(
            (
                pltpu.make_async_copy(
                    basis_in.at[:, part], basis_rows.at[:, part], sem.at[0, comp]
                ),
                pltpu.make_async_copy(res_in.at[comp], res_rows.at[comp], sem.at[1, comp]),
            )
        )
    for pair in copies:
        for copy in pair:
            copy.start()
    basis = basis_rows.reshape(slots * sz.tiles, LANES)
    res = res_rows.reshape(sz.tiles * loads, LANES)

    def step(index, carry):
        both, low = carry
        basis_hi, basis_lo, res_hi, res_both = [], [], [], []
        for half in range(2):
            tile = index * 2 + half
            comp = tile // sz.cells
            hi, lo = split_hi_lo(basis[pl.ds(tile, slots, stride=sz.tiles), :])
            split[tile, pl.ds(0, slots), :] = hi
            split[tile, pl.ds(slots, slots), :] = lo
            value_hi, value_lo = split_hi_lo(own_rows(sz, res, comp, tile - comp * sz.cells))
            basis_hi.append(hi)
            basis_lo.append(lo)
            res_hi.append(value_hi)
            res_both.append(jnp.concatenate([value_hi, value_lo], axis=0))
        both = both + lax.dot_general(
            jnp.concatenate(res_both, axis=1),
            jnp.concatenate(basis_hi, axis=1),
            TRANSPOSED,
            preferred_element_type=F32,
        )
        low = low + lax.dot_general(
            jnp.concatenate(res_hi, axis=1),
            jnp.concatenate(basis_lo, axis=1),
            TRANSPOSED,
            preferred_element_type=F32,
        )
        return both, low

    carry = (jnp.zeros((2 * loads, slots), F32), jnp.zeros((loads, slots), F32))
    for comp in range(sz.comps):
        for copy in copies[comp]:
            copy.wait()
        carry = lax.fori_loop(
            comp * sz.cells // 2, (comp + 1) * sz.cells // 2, step, carry, unroll=4
        )
    both, low = carry
    pieces = both[:loads] + both[loads:] + low
    slot = lax.broadcasted_iota(jnp.int32, pieces.shape, 1)
    wide[...] = jnp.zeros_like(wide)
    wide[:, pl.ds(0, slots)] = jnp.where(slot < count[0], pieces, 0.0)
    half = loads // 2
    lane = lane_ids(half)
    packed = jnp.where(lane < 64, wide[:half, :], roll_lanes(wide[half:, :], 64))
    packed = jnp.where(lane == slots, count[0].astype(F32), packed)
    packed = jnp.where(lane == slots + 1, rank[0].astype(F32), packed)
    message[...] = packed.astype(BF16)


def pack_y(sz, res, ids, packed, *refs):
    xhalo, refs = take_halos(refs, "gx")
    message = refs[0]
    ysend, (side_low, side_high) = take_halos(refs[1:], "gy")
    for device in range(message.shape[0]):
        message[device] = packed[...]
    last = sz.cy - 1
    for comp in range(sz.comps):
        for x in range(sz.bx):
            rows = pl.ds((comp * sz.bx + x) * sz.loads, sz.loads)
            if 0 < x < sz.bx - 1:
                low, high = (own_rows(sz, res, comp, (x - 1) * sz.cy + y) for y in (0, last))
            else:
                side = xhalo.below if x == 0 else xhalo.above
                low, high = (
                    side(pl.ds((comp * sz.cy + y) * sz.loads, sz.loads)) for y in (0, last)
                )
            ysend.send(rows, low, high)
    ids_below = xhalo.below(pl.ds(sz.face_x, 2 * sz.cy))
    ids_above = xhalo.above(pl.ds(sz.face_x, 2 * sz.cy))
    for x in range(sz.cx + 4):
        if x < 2:
            rows = ids_below[x * sz.cy : (x + 1) * sz.cy]
        elif x >= sz.cx + 2:
            rows = ids_above[(x - sz.cx - 2) * sz.cy : (x - sz.cx - 1) * sz.cy]
        else:
            rows = (ids[pl.ds((x - 2) * sz.cy, sz.cy), :] + 1).astype(F32)
        side_low[pl.ds(2 * x, 2), :] = rows[:2]
        side_high[pl.ds(2 * x, 2), :] = rows[sz.cy - 2 :]
    ysend.send(pl.ds(sz.face_y, HALO_IDS), side_low[...], side_high[...])


def box_tile(sz, res, xhalo, yhalo, comp, x, y):
    if y == 0 or y == sz.by - 1:
        side = yhalo.below if y == 0 else yhalo.above
        return side(pl.ds((comp * sz.bx + x) * sz.loads, sz.loads))
    if x == 0 or x == sz.bx - 1:
        side = xhalo.below if x == 0 else xhalo.above
        return side(pl.ds((comp * sz.cy + y - 1) * sz.loads, sz.loads))
    return own_rows(sz, res, comp, (x - 1) * sz.cy + y - 1)


def pack_z(sz, res, ids, *refs):
    xhalo, yhalo, (out, id_box, star, outer) = take_halos(refs, "gx", "gy")
    pitch = sz.pitch
    id_box[...] = jnp.zeros_like(id_box)
    two = 2 * sz.cy
    ids_below = xhalo.below(pl.ds(sz.face_x, two))
    ids_above = xhalo.above(pl.ds(sz.face_x, two))
    ids_low = yhalo.below(pl.ds(sz.face_y, HALO_IDS))
    ids_high = yhalo.above(pl.ds(sz.face_y, HALO_IDS))
    for x in range(sz.cx + 4):
        if x < 2:
            rows = ids_below[x * sz.cy : (x + 1) * sz.cy]
        elif x >= sz.cx + 2:
            rows = ids_above[(x - sz.cx - 2) * sz.cy : (x - sz.cx - 1) * sz.cy]
        else:
            rows = (ids[pl.ds((x - 2) * sz.cy, sz.cy), :] + 1).astype(F32)
        id_box[pl.ds(x * pitch + 2, sz.cy), :] = rows
        id_box[pl.ds(x * pitch, 2), :] = ids_low[2 * x : 2 * x + 2]
        id_box[pl.ds(x * pitch + sz.cy + 2, 2), :] = ids_high[2 * x : 2 * x + 2]
    values = id_box[...]
    lane = lane_ids(values.shape[0])
    outer[...] = jnp.where(lane == LANES - 1, roll_lanes(values, 1), roll_lanes(values, -1))
    star[...] = jnp.zeros_like(star)
    lane8 = lane_ids(8)
    taken = jnp.zeros((8, LANES), F32)
    for x in range(sz.bx):
        for y in range(sz.by):
            place = x * sz.by + y
            row = (x + 1) * pitch + y + 1
            for j, shift in enumerate((0, -pitch, pitch, -1, 1)):
                star[pl.ds(place * 8 + j, 1), :] = id_box[pl.ds(row + shift, 1), :]
            star[pl.ds(place * 8 + 5, 1), :] = outer[pl.ds(row, 1), :]
    for place in range(sz.box):
        picked = roll_lanes(star[pl.ds(place * 8, 8), :], 2 * place + 1)
        taken = jnp.where((lane8 >> 1) == place, picked, taken)
    out[pl.ds(sz.face_z, HALO_IDS), :] = jnp.concatenate(
        [taken, jnp.zeros((HALO_IDS - 8, LANES), F32)], axis=0
    ).astype(BF16)
    lane_k = lane_ids(sz.loads)
    for comp in range(sz.comps):
        total = jnp.zeros((sz.loads, LANES), F32)
        for x in range(sz.bx):
            for y in range(sz.by):
                place = x * sz.by + y
                tile = box_tile(sz, res, xhalo, yhalo, comp, x, y)
                total = jnp.where(
                    (lane_k >> 1) == place, roll_lanes(tile, 2 * place + 1), total
                )
        out[pl.ds(comp * sz.loads, sz.loads), :] = total.astype(BF16)


def place_pieces(
    sz, gathered, inverse, *refs
):
    message, starts_out, vector, wide, heads, starts, sem = refs[-7:]
    devices = gathered.shape[0]
    for device in range(devices):
        heads[pl.ds(device, 1), :] = gathered[device].astype(F32)[0:1]
    values = heads[...]
    ranks = jnp.transpose(values)[sz.slots + 1 : sz.slots + 2, :]
    earlier = values[:, sz.slots + 1 : sz.slots + 2] < ranks
    total = jnp.sum(jnp.where(earlier, values[:, sz.slots : sz.slots + 1], 0.0), axis=0, keepdims=True)
    starts_out[...] = jnp.zeros_like(starts_out)
    starts_out[:, pl.ds(0, devices)] = jnp.broadcast_to(total.astype(jnp.int32), (8, devices))
    copy = pltpu.make_async_copy(starts_out, starts, sem)
    copy.start()
    half = sz.loads // 2
    lane = lane_ids(half)
    vector[...] = jnp.zeros_like(vector)
    copy.wait()

    def place(device, carry):
        start = starts[0, device]
        block = start // LANES
        offset = start - block * LANES
        packed = gathered[device].astype(F32)
        low = jnp.where(lane < sz.slots, packed, 0.0)
        high = jnp.where((lane >= 64) & (lane < 64 + sz.slots), packed, 0.0)
        both = jnp.concatenate(
            [
                pltpu.roll(low, offset, axis=1),
                pltpu.roll(high, lax.rem(offset + 64, LANES), axis=1),
            ],
            axis=0,
        )
        wide_lane = lane_ids(sz.loads)
        vector[block] = vector[block] + jnp.where(wide_lane >= offset, both, 0.0)
        vector[block + 1] = vector[block + 1] + jnp.where(wide_lane < offset, both, 0.0)
        return carry

    lax.fori_loop(0, gathered.shape[0], place, 0, unroll=8)
    total = jnp.zeros((sz.loads, sz.block_rows), F32)
    for block in range(sz.total_rows // LANES):
        total = total + lax.dot_general(
            vector[block].astype(BF16),
            inverse[:, pl.ds(block * LANES, LANES)],
            TRANSPOSED,
            preferred_element_type=F32,
        )
    if sz.block_rows == 64:
        wide[...] = jnp.zeros_like(wide)
        wide[:, pl.ds(0, 64)] = total
        packed = jnp.where(lane < 64, wide[:half, :], roll_lanes(wide[half:, :], 64))
        for device in range(message.shape[0]):
            message[device, 0] = packed
    else:
        for device in range(message.shape[0]):
            for block in range(sz.block_rows // LANES):
                message[device, block] = total[:, block * LANES : (block + 1) * LANES]


def own_coefs(sz, coefs, start):
    if sz.block_rows == 64:
        half = sz.loads // 2
        block = start // 64
        offset = start - block * 64
        first = coefs[block]
        second = coefs[jnp.minimum(block + 1, coefs.shape[0] - 1)]
        lane = lane_ids(half)
        top = jnp.where(lane < 64, first, roll_lanes(second, 64))
        bottom = jnp.where(lane < 64, roll_lanes(first, 64), second)
        both = jnp.concatenate([top, bottom], axis=0)
    else:
        block = start // LANES
        offset = start - block * LANES
        first = coefs[block]
        second = coefs[jnp.minimum(block + 1, coefs.shape[0] - 1)]
        both = jnp.where(lane_ids(sz.loads) >= offset, first, second)
    return pltpu.roll(both, lax.rem(LANES - offset, LANES), axis=1)


def look_up(table, row, ids):
    result = jnp.zeros_like(ids)
    for material in range(table.shape[1]):
        result = jnp.where(ids == material + 1, table[row, material], result)
    return result


DINV, KEEP, DLAM, WXM, WXP, WYM, WYP, WZM, WZP = range(9)


def spread_row(ref, index, row):
    return ref[index, pl.ds(row, 8, stride=0), :]


def make_coefs(sz, table, id_box, halo_ids, coefs, halo_coefs, own, mu_box, halo_mu):
    pitch = sz.pitch
    mu_box[...] = look_up(table, 0, id_box[...])
    lam_box = look_up(table, 1, id_box[...])
    mu_halo = look_up(table, 0, halo_ids)
    lam_halo = look_up(table, 1, halo_ids)
    lane8 = lane_ids(8)
    center = jnp.broadcast_to(mu_halo[0:1], (8, LANES))
    inner = jnp.zeros((8, LANES), F32)
    for place in range(sz.box):
        row = (place // sz.by + 1) * pitch + place % sz.by + 1
        halo_mu[pl.ds(row, 1), :] = roll_lanes(center, -2 * place)[0:1]
        spread = jnp.broadcast_to(mu_box[pl.ds(row, 1), :], (8, LANES))
        here = (((lane8 + 1) >> 1) & 63) == place
        inner = jnp.where(here, roll_lanes(spread, 2 * place), inner)
    rows_id = lax.broadcasted_iota(jnp.int32, (pitch, LANES), 0)
    lane = lane_ids(pitch)
    for x in range(1, sz.bx + 1):
        mu = mu_box[pl.ds(x * pitch, pitch), :]
        edge = halo_mu[pl.ds(x * pitch, pitch), :]
        lam = lam_box[x * pitch : (x + 1) * pitch]
        faces = [
            0.5 * (mu + mu_box[pl.ds((x - 1) * pitch, pitch), :]),
            0.5 * (mu + mu_box[pl.ds((x + 1) * pitch, pitch), :]),
            0.5 * (mu + mu_box[pl.ds(x * pitch - 1, pitch), :]),
            0.5 * (mu + mu_box[pl.ds(x * pitch + 1, pitch), :]),
            0.5 * (mu + jnp.where(lane == 0, edge, roll_lanes(mu, 1))),
            0.5 * (mu + jnp.where(lane == LANES - 1, edge, roll_lanes(mu, -1))),
        ]
        diag = 1.0 + sum(faces)
        dinv = DAMPING / (diag + lam)
        rows = pl.ds(x * pitch, pitch)
        coefs[DINV, rows, :] = dinv
        coefs[KEEP, rows, :] = (1.0 - DAMPING) + dinv * lam
        coefs[DLAM, rows, :] = dinv * lam
        weights = [dinv * face for face in faces]
        if x == 1:
            weights[0] = jnp.zeros_like(dinv)
        if x == sz.bx:
            weights[1] = jnp.zeros_like(dinv)
        weights[2] = jnp.where(rows_id == 1, 0.0, weights[2])
        weights[3] = jnp.where(rows_id == sz.by, 0.0, weights[3])
        for j in range(6):
            coefs[WXM + j, rows, :] = weights[j]
        if 2 <= x <= sz.cx + 1:
            target = pl.ds((x - 2) * sz.cy, sz.cy)
            for j, value in enumerate([diag, lam] + faces):
                own[j, target, :] = value[2 : 2 + sz.cy]
    place = ((lane8 + 1) >> 1) & 63
    column = jnp.zeros_like(place)
    for x in range(1, sz.bx):
        column = column + (place >= x * sz.by).astype(jnp.int32)
    y_place = place - column * sz.by
    others = [jnp.broadcast_to(mu_halo[j : j + 1], (8, LANES)) for j in range(1, 6)]
    faces = [0.5 * (center + other) for other in others] + [0.5 * (center + inner)]
    lam = jnp.broadcast_to(lam_halo[0:1], (8, LANES))
    dinv = DAMPING / (1.0 + lam + sum(faces))
    live = place < sz.box
    keep = [
        live & (column > 0),
        live & (column < sz.bx - 1),
        live & (y_place > 0),
        live & (y_place < sz.by - 1),
        None,
        live,
    ]
    halo_coefs[DINV] = dinv
    halo_coefs[KEEP] = (1.0 - DAMPING) + dinv * lam
    halo_coefs[DLAM] = dinv * lam
    for j, target in ((0, WXM), (1, WXP), (2, WYM), (3, WYP), (5, WZM)):
        halo_coefs[target] = jnp.where(keep[j], dinv * faces[j], 0.0)


def neighbour_matrix(copies, spread):
    width = (3 if spread else 2) * LANES
    parts = []
    for copy in range(copies + 1):
        row = lax.broadcasted_iota(jnp.int32, (LANES, width), 0)
        lane = lax.broadcasted_iota(jnp.int32, (LANES, width), 1)
        even = (row & 1) == 0
        if copy < copies:
            hit = ((lane < LANES) & (row == lane - 1)) | (
                (lane >= LANES) & (lane < 2 * LANES) & (row == lane - LANES + 1)
            )
            if spread:
                source = jnp.where((lane & 1) == 0, 0, LANES - 1)
                hit = hit | ((lane >= 2 * LANES) & (row == source))
        else:
            hit = ((lane == 0) & even) | ((lane == 2 * LANES - 1) & jnp.logical_not(even))
        parts.append(jnp.where(hit, 1.0, 0.0).astype(BF16))
    return jnp.concatenate(parts, axis=0)


def z_halo(zhalo, rows):
    down, up = zhalo.below(rows), zhalo.above(rows)
    even = (lane_ids(down.shape[0]) & 1) == 0
    return jnp.where(even, down, roll_lanes(up, -2))


def relax_box(sz, table, res, id_box, *refs):
    xhalo, yhalo, zhalo, refs = take_halos(refs, "gx", "gy", "col")
    near_part, own = refs[:2]
    first, second, third, halos, inner, coefs, halo_coefs, mu_box, halo_mu = refs[2:11]
    wide, own_rows_coef, weights, lhs, near = refs[11:]
    loads, comps = sz.loads, sz.comps
    groups = loads // 8
    lane8 = lane_ids(8)

    halo_mu[...] = jnp.zeros_like(halo_mu)
    inner[...] = jnp.zeros_like(inner)
    make_coefs(
        sz, table, id_box, z_halo(zhalo, pl.ds(sz.face_z, HALO_IDS))[:8], coefs, halo_coefs, own_rows_coef,
        mu_box, halo_mu,
    )

    weights[...] = neighbour_matrix(1, True)

    def spread(place, carry):
        x = place // sz.by
        row = (x + 1) * sz.pitch + place - x * sz.by + 1
        for j in range(9):
            wide[j, place] = jnp.broadcast_to(coefs[j, pl.ds(row, 1), :], (8, LANES))
        return carry

    lax.fori_loop(0, sz.box, spread, 0, unroll=4)

    def spread_own(cell, carry):
        for j in range(8):
            own[j, cell] = jnp.broadcast_to(own_rows_coef[j, pl.ds(cell, 1), :], (8, LANES))
        return carry

    lax.fori_loop(0, sz.cells, spread_own, 0, unroll=4)

    for comp in range(comps):
        halo = z_halo(zhalo, pl.ds(comp * loads, loads))
        dinv = jnp.concatenate([halo_coefs[DINV]] * groups, axis=0)
        halos[0, comp] = dinv * halo
        for x in range(sz.bx):
            for y in range(sz.by):
                place = x * sz.by + y
                tile = box_tile(sz, res, xhalo, yhalo, comp, x, y)
                first[comp, place] = tile * jnp.concatenate([wide[DINV, place]] * groups, axis=0)

    lane_k = lane_ids(loads)

    def relax(source, level, x, ys, put):
        count = len(ys)
        for j, y in enumerate(ys):
            place = x * sz.by + y
            here = (((lane_k + 1) >> 1) & 63) == place
            for comp in range(comps):
                rows = pl.ds((j * comps + comp) * loads, loads)
                lhs[rows, pl.ds(0, LANES)] = source[comp, place].astype(BF16)
                lhs[rows, pl.ds(LANES, LANES)] = jnp.where(here, halos[level, comp], 0.0).astype(BF16)
        size = count * comps * loads
        cut = 3 * LANES if level < 2 else 2 * LANES
        near[pl.ds(0, size), pl.ds(0, cut)] = jnp.dot(
            lhs[pl.ds(0, size), :], weights[:, pl.ds(0, cut)], preferred_element_type=F32
        )
        for j, y in enumerate(ys):
            place = x * sz.by + y
            coef = [wide[i, place] for i in range(9)]
            here = (((lane8 + 1) >> 1) & 63) == place
            xm, xp = jnp.maximum(place - sz.by, 0), jnp.minimum(place + sz.by, sz.box - 1)
            ym, yp = jnp.maximum(place - 1, 0), jnp.minimum(place + 1, sz.box - 1)
            for group in range(groups):
                rows = pl.ds(group * 8, 8)
                center = [source[comp, place, rows, :] for comp in range(comps)]
                coupled = coef[DLAM] * (center[0] + center[1] + center[2])
                for comp in range(comps):
                    value = center[comp]
                    at = pl.ds((j * comps + comp) * loads + group * 8, 8)
                    out = (first[comp, place, rows, :] - coupled) + coef[KEEP] * value
                    out = out + coef[WXM] * source[comp, xm, rows, :]
                    out = out + coef[WXP] * source[comp, xp, rows, :]
                    out = out + coef[WYM] * source[comp, ym, rows, :]
                    out = out + coef[WYP] * source[comp, yp, rows, :]
                    out = out + coef[WZM] * near[at, pl.ds(0, LANES)]
                    out = out + coef[WZP] * near[at, pl.ds(LANES, LANES)]
                    put(j, place, comp, group, out)
                    if level < 2:
                        pltpu.store(
                            inner.at[level, comp, rows, :],
                            near[at, pl.ds(2 * LANES, LANES)],
                            mask=here,
                        )

    def sweep(source, target, level):
        def put(j, place, comp, group, out):
            target[comp, place, pl.ds(group * 8, 8), :] = out

        def at(x, carry):
            relax(source, level, x, range(sz.by), put)
            return carry

        lax.fori_loop(0, sz.bx, at, 0)
        coef = [halo_coefs[j] for j in range(8)]
        for group in range(groups):
            rows = pl.ds(group * 8, 8)
            center = [halos[level, comp, rows, :] for comp in range(comps)]
            coupled = coef[DLAM] * (center[0] + center[1] + center[2])
            for comp in range(comps):
                value = center[comp]
                out = (halos[0, comp, rows, :] - coupled) + coef[KEEP] * value
                out = out + coef[WXM] * roll_lanes(value, 2 * sz.by)
                out = out + coef[WXP] * roll_lanes(value, -2 * sz.by)
                out = out + coef[WYM] * roll_lanes(value, 2)
                out = out + coef[WYP] * roll_lanes(value, -2)
                out = out + coef[WZM] * inner[level, comp, rows, :]
                halos[level + 1, comp, rows, :] = out

    sweep(first, second, 0)
    sweep(second, third, 1)

    def final(x, carry):
        def put(j, place, comp, group, out):
            near_part[comp, x * sz.cy + j, pl.ds(group * 8, 8), :] = out

        relax(third, 2, x + 1, range(1, sz.cy + 1), put)
        return carry

    lax.fori_loop(0, sz.cx, final, 0)


def make_direction(sz, count, starts_in, coarse, split, near_part, *refs):
    direction, zface = refs[:2]
    xsend, ysend, (left, zedge, lhs, near, starts, sem) = take_halos(refs[2:], "gx", "gy")
    loads, comps = sz.loads, sz.comps
    copy = pltpu.make_async_copy(starts_in, starts, sem)
    copy.start()
    lane_k = lane_ids(loads)
    copy.wait()
    mine = own_coefs(sz, coarse, starts[0, own_index()])
    mine = jnp.where(lane_ids(loads) < jnp.minimum(count[0], sz.slots), mine, 0.0)
    left[...] = paired_left(mine, sz.slots, left)
    zedge[...] = jnp.zeros_like(zedge)

    def final(x, carry):
        for y in range(sz.cy):
            cell = x * sz.cy + y
            place = (x + 1) * sz.by + y + 1
            for comp in range(comps):
                part = jnp.dot(
                    left[:, : 2 * sz.slots],
                    split[comp * sz.cells + cell],
                    preferred_element_type=F32,
                )
                value = near_part[comp, cell] + (part[:loads] + part[loads:])
                direction[comp, cell] = value
                lhs[pl.ds((y * comps + comp) * loads, loads), :] = value.astype(BF16)
        near[...] = jnp.dot(lhs[...], edges, preferred_element_type=F32)
        for y in range(sz.cy):
            place = (x + 1) * sz.by + y + 1
            for comp in range(comps):
                pltpu.store(
                    zedge.at[pl.ds(comp * loads, loads), :],
                    near[pl.ds((y * comps + comp) * loads, loads), :],
                    mask=(lane_k >> 1) == place,
                )
        return carry

    edge_row = lax.broadcasted_iota(jnp.int32, (LANES, LANES), 0)
    even_lane = (lane_ids(LANES) & 1) == 0
    edges = jnp.where(jnp.where(even_lane, LANES - 1, 0) == edge_row, 1.0, 0.0).astype(BF16)
    lax.fori_loop(0, sz.cx, final, 0)
    zface[...] = zedge[...].astype(BF16)
    for comp in range(comps):
        for y in range(sz.cy):
            rows = pl.ds((comp * sz.cy + y) * loads, loads)
            xsend.send(rows, direction[comp, y], direction[comp, (sz.cx - 1) * sz.cy + y])
        for x in range(sz.cx):
            rows = pl.ds((comp * sz.cx + x) * loads, loads)
            ysend.send(rows, direction[comp, x * sz.cy], direction[comp, (x + 1) * sz.cy - 1])


def make_image(sz, res, own, direction, *refs):
    xhalo, yhalo, zhalo, refs = take_halos(refs, "gx", "gy", "col")
    dir_split, image_split, message, box, halo, weights, lhs, near, sem = refs
    weights[...] = neighbour_matrix(2, False)
    loads, comps = sz.loads, sz.comps
    groups = loads // 8
    copies = []
    for comp in range(comps):
        for x in range(sz.cx):
            copies.append(
                pltpu.make_async_copy(
                    direction.at[comp, pl.ds(x * sz.cy, sz.cy)],
                    box.at[comp, pl.ds((x + 1) * sz.by + 1, sz.cy)],
                    sem.at[comp, x],
                )
            )
    for copy in copies:
        copy.start()
    for comp in range(comps):
        for y in range(sz.cy):
            rows = pl.ds((comp * sz.cy + y) * loads, loads)
            box[comp, y + 1] = xhalo.below(rows)
            box[comp, (sz.bx - 1) * sz.by + y + 1] = xhalo.above(rows)
        for x in range(sz.cx):
            rows = pl.ds((comp * sz.cx + x) * loads, loads)
            box[comp, (x + 1) * sz.by] = yhalo.below(rows)
            box[comp, (x + 1) * sz.by + sz.by - 1] = yhalo.above(rows)
        halo[comp] = z_halo(zhalo, pl.ds(comp * loads, loads))
    for copy in copies:
        copy.wait()
    lane_k = lane_ids(loads)

    part_cells = sz.cy // 2

    def at(step, total):
        x = step // 2
        first_y = (step - 2 * x) * part_cells
        for y in range(part_cells):
            cell = step * part_cells + y
            place = (x + 1) * sz.by + first_y + y + 1
            here = (((lane_k + 1) >> 1) & 63) == place
            for comp in range(comps):
                hi, lo = split_hi_lo(box[comp, place])
                dir_split[comp * sz.cells + cell] = jnp.concatenate([hi, lo], axis=0)
                rows = pl.ds((y * comps + comp) * loads, loads)
                lhs[rows, pl.ds(0, LANES)] = hi
                lhs[rows, pl.ds(LANES, LANES)] = lo
                lhs[rows, pl.ds(2 * LANES, LANES)] = jnp.where(here, halo[comp], 0.0).astype(BF16)
        near[...] = jnp.dot(lhs[...], weights[...], preferred_element_type=F32)
        sides = {}
        for y in range(part_cells):
            cell = step * part_cells + y
            place = (x + 1) * sz.by + first_y + y + 1
            coef = [own[j, cell] for j in range(8)]
            parts = {}
            for group in range(groups):
                rows = pl.ds(group * 8, 8)
                center = [box[comp, place, rows, :] for comp in range(comps)]
                coupled = coef[1] * (center[0] + center[1] + center[2])
                for comp in range(comps):
                    line = pl.ds((y * comps + comp) * loads + group * 8, 8)
                    out = coef[0] * center[comp] + coupled
                    out = out - coef[2] * box[comp, place - sz.by, rows, :]
                    out = out - coef[3] * box[comp, place + sz.by, rows, :]
                    out = out - coef[4] * box[comp, place - 1, rows, :]
                    out = out - coef[5] * box[comp, place + 1, rows, :]
                    out = out - coef[6] * near[line, pl.ds(0, LANES)]
                    parts[comp, group] = out - coef[7] * near[line, pl.ds(LANES, LANES)]
            for comp in range(comps):
                tile = comp * sz.cells + cell
                field = jnp.concatenate([parts[comp, group] for group in range(groups)], axis=0)
                both = jnp.concatenate(split_hi_lo(field), axis=0)
                image_split[tile] = both
                right = jnp.concatenate((both,) + split_hi_lo(own_rows(sz, res, comp, cell)), axis=0)
                sides[y, comp] = (dir_split[tile], right)
            if y % 2 == 1:
                for comp in range(comps):
                    pair = zip(sides[y - 1, comp], sides[y, comp])
                    left, right = (jnp.concatenate(items, axis=1) for items in pair)
                    total = total + lax.dot_general(
                        left, right, TRANSPOSED, preferred_element_type=F32
                    )
        return total

    total = lax.fori_loop(0, 2 * sz.cx, at, jnp.zeros((2 * loads, 4 * loads), F32))
    high, low = total[:loads], total[loads:]
    sums = high + roll_lanes(high, -loads) + low
    half = loads // 2
    lane = lane_ids(half)
    packed = jnp.where((lane & (2 * loads - 1)) < loads, sums[:half], roll_lanes(sums[half:], loads))
    message[...] = packed


def share_sums(sz, mine, *refs):
    message = refs[-1]
    total = mine[...]
    for other in refs[:-1]:
        total = total + other[...]
    for device in range(message.shape[0]):
        message[device] = total


def finish(
    sz, sums, iterate, res, dir_split, image_split, new_iterate, new_residual, parts
):
    loads = sz.loads
    total = sums[0]
    for device in range(1, sums.shape[0]):
        total = total + sums[device]
    system = jnp.concatenate([total, roll_lanes(total, -loads)], axis=0)
    lane = lane_ids(loads)
    system = jnp.where((lane & (2 * loads - 1)) < loads, system, 0.0)
    row_ids = lax.broadcasted_iota(jnp.int32, (loads, LANES), 0)
    for base in range(0, loads, 8):
        columns = [
            jnp.broadcast_to(system[:, i : i + 1], (loads, LANES)) for i in range(base, base + 8)
        ]
        for j in range(8):
            i = base + j
            here = row_ids == i
            scale = 1.0 / columns[j][i : i + 1, :]
            row = system[i : i + 1, :] * scale
            system = jnp.where(here, row, system - columns[j] * row)
            for other in range(j + 1, 8):
                entry = columns[other][i : i + 1, :] * scale
                columns[other] = jnp.where(here, entry, columns[other] - columns[j] * entry)
    step = jnp.transpose(system)[2 * loads : 3 * loads, :]
    padded = jnp.concatenate([step, jnp.zeros((loads, LANES - loads), F32)], axis=1) if (
        step.shape[1] < LANES
    ) else step
    left = paired_left(padded, loads, parts)[:, : 2 * loads]

    def at(cell, carry):
        for comp in range(sz.comps):
            tile = comp * sz.cells + cell
            right = jnp.concatenate([dir_split[tile], image_split[tile]], axis=1)
            part = jnp.dot(left, right, preferred_element_type=F32)
            part = part[:loads] + part[loads:]
            rows = pl.ds(comp * loads * sz.cells + cell, loads, stride=sz.cells)
            new_iterate[rows, :] = iterate[rows, :] + part[:, :LANES]
            new_residual[rows, :] = res[rows, :] - part[:, LANES:]
        return carry

    lax.fori_loop(0, sz.cells, at, 0, unroll=2)


def body(
    iterate, residual, cell_ids, materials, eigen_counts, coarse_rank, eigen_basis, coarse_inverse
):
    sz = Sizes(residual, eigen_basis, coarse_inverse)
    shape = jax.ShapeDtypeStruct
    devices = 1
    for axis in AXES:
        devices = devices * lax.axis_size(axis)
    blocks = sz.total_rows // sz.block_rows
    smem, vmem, scratch, dma = pltpu.SMEM, pltpu.VMEM, pltpu.VMEM, pltpu.SemaphoreType.DMA
    res = residual.reshape(-1, LANES)
    old = iterate.reshape(-1, LANES)
    ids = cell_ids.reshape(-1, LANES)

    def call(name, kernel, *args, **kwargs):
        return vmem_call(name, lambda *refs: kernel(sz, *refs), *args, **kwargs)

    face = shape((sz.face_x + 2 * sz.cy, LANES), BF16)
    faces = call(
        "pack_x",
        pack_x,
        [face] * swaps("gx"),
        [scratch((sz.comps * sz.loads, sz.cy, LANES), F32)] * 2
        + [scratch((sz.cells, LANES), jnp.int32), dma((3,))],
        8,
        1 << 20,
        2 << 20,
        [residual.reshape(-1, sz.cells, LANES), ids],
        spaces=[pl.ANY, pl.ANY],
    )
    xhalo = exchange(faces, "gx")

    packed, split = call(
        "pieces",
        make_pieces,
        [
            shape((sz.loads // 2, LANES), BF16),
            shape((sz.tiles, 2 * sz.slots, LANES), BF16),
        ],
        [
            scratch((sz.loads, LANES), F32),
            scratch((sz.slots, sz.tiles, LANES), F32),
            scratch((sz.comps, sz.loads * sz.cells, LANES), F32),
            dma((2, sz.comps)),
        ],
        12,
        1 << 27,
        7 << 20,
        [
            eigen_counts,
            coarse_rank,
            eigen_basis.reshape(sz.slots, sz.tiles, LANES),
            residual.reshape(sz.comps, -1, LANES),
            faces[0],
        ],
        spaces=[smem, smem, pl.ANY, pl.ANY, pl.ANY],
    )

    yface = shape((sz.face_y + HALO_IDS, LANES), BF16)
    message, *faces = call(
        "pack_y",
        pack_y,
        [shape((devices,) + packed.shape, BF16)] + [yface] * swaps("gy"),
        [scratch((HALO_IDS, LANES), F32)] * 2,
        8,
        1 << 20,
        2 << 20,
        [res, ids, packed] + xhalo,
    )
    yhalo = exchange(faces, "gy")
    gathered = lax.all_to_all(message, AXES, 0, 0, tiled=True)
    rows = (sz.cx + 4) * sz.pitch
    zmessage, id_box = call(
        "pack_z",
        pack_z,
        [shape((sz.face_z + HALO_IDS, LANES), BF16), shape((rows, LANES), F32)],
        [scratch((sz.box * 8, LANES), F32), scratch((rows, LANES), F32)],
        8,
        1 << 22,
        3 << 20,
        [res, ids] + xhalo + yhalo,
    )
    zhalo = exchange([zmessage] * 2, "col")

    tile = (1, sz.loads // 2, LANES)
    if sz.block_rows != 64:
        tile = (sz.block_rows // LANES, sz.loads, LANES)
    wide = (8, max(LANES, devices))
    partial, starts = call(
        "coarse",
        place_pieces,
        [shape((blocks,) + tile, F32), shape(wide, jnp.int32)],
        [
            scratch((sz.total_rows // LANES + 1, sz.loads, LANES), F32),
            scratch((sz.loads, LANES), F32),
            scratch((devices, LANES), F32),
            smem(wide, jnp.int32),
            dma,
        ],
        12,
        1 << 23,
        1 << 20,
        [gathered, coarse_inverse] + zhalo,
        spaces=[vmem, vmem] + [pl.ANY] * len(zhalo),
    )
    coarse = lax.all_to_all(partial, ("gx", "col"), 0, 0, tiled=True)
    coarse = coarse.reshape((-1,) + tile[1:])

    field = scratch((sz.comps, sz.box, sz.loads, LANES), F32)
    halos = xhalo + yhalo + zhalo
    near_part, own = call(
        "sweeps",
        relax_box,
        [
            shape((sz.comps, sz.cells, sz.loads, LANES), F32),
            shape((8, sz.cells, 8, LANES), F32),
        ],
        [
            field,
            field,
            field,
            scratch((3, sz.comps, sz.loads, LANES), F32),
            scratch((2, sz.comps, sz.loads, LANES), F32),
            scratch((9, rows, LANES), F32),
            scratch((9, 8, LANES), F32),
            scratch((rows, LANES), F32),
            scratch((rows, LANES), F32),
            scratch((9, sz.box, 8, LANES), F32),
            scratch((8, sz.cells, LANES), F32),
            scratch((2 * LANES, 3 * LANES), BF16),
            scratch((sz.by * sz.comps * sz.loads, 2 * LANES), BF16),
            scratch((sz.by * sz.comps * sz.loads, 3 * LANES), F32),
        ],
        24,
        1 << 28,
        8 << 20,
        [materials, res, id_box] + halos,
        spaces=[smem] + [vmem] * (2 + len(halos)),
    )
    plane = sz.cy * sz.comps * sz.loads
    direction, zface, *faces = call(
        "direct",
        make_direction,
        [
            shape((sz.comps, sz.cells, sz.loads, LANES), F32),
            shape((sz.face_z, LANES), BF16),
        ]
        + [shape((sz.face_x, LANES), BF16)] * swaps("gx")
        + [shape((sz.inner_y, LANES), BF16)] * swaps("gy"),
        [
            scratch((2 * sz.loads, LANES), BF16),
            scratch((sz.face_z, LANES), F32),
            scratch((plane, LANES), BF16),
            scratch((plane, LANES), F32),
            smem(starts.shape, jnp.int32),
            dma,
        ],
        14,
        1 << 26,
        8 << 20,
        [eigen_counts, starts, coarse, split, near_part],
        spaces=[smem, pl.ANY, vmem, vmem, vmem],
    )
    xhalo = exchange(faces[: swaps("gx")], "gx")
    yhalo = exchange(faces[swaps("gx") :], "gy")
    zhalo = exchange([zface] * 2, "col")
    sums_shape = (sz.loads // 2, LANES)
    dir_split, image_split, sums = call(
        "image",
        make_image,
        [
            shape((sz.tiles, 2 * sz.loads, LANES), BF16),
            shape((sz.tiles, 2 * sz.loads, LANES), BF16),
            shape(sums_shape, F32),
        ],
        [
            field,
            scratch((sz.comps, sz.loads, LANES), F32),
            scratch((3 * LANES, 2 * LANES), BF16),
            scratch((plane // 2, 3 * LANES), BF16),
            scratch((plane // 2, 2 * LANES), F32),
            dma((sz.comps, sz.cx)),
        ],
        20,
        1 << 28,
        8 << 20,
        [res, own, direction] + xhalo + yhalo + zhalo,
        spaces=[vmem, vmem, pl.ANY] + [vmem] * len(xhalo + yhalo + zhalo),
    )
    over, operands = AXES, [sums]
    if lax.axis_size("gy") == 2:
        over = ("gx", "col")
        operands += exchange([sums], "gy")
        devices = devices // 2
    spread = call(
        "share_sums", share_sums, shape((devices,) + sums_shape, F32), [], 4, 1 << 12, 1 << 17,
        operands,
    )
    sums = lax.all_to_all(spread, over, 0, 0, tiled=True)
    flat = shape(res.shape, F32)
    new_iterate, new_residual = call(
        "finish",
        finish,
        [flat, flat],
        [scratch((2 * sz.loads, LANES), BF16)],
        16,
        1 << 27,
        9 << 20,
        [sums, old, res, dir_split, image_split],
    )
    return (new_iterate.reshape(iterate.shape), new_residual.reshape(residual.shape))


def solution(mesh):
    placed = (
        P(None, None, "gx", "gy", "col"),
        P(None, None, "gx", "gy", "col"),
        P("gx", "gy", "col"),
        P(),
        P(("gx", "gy", "col")),
        P(("gx", "gy", "col")),
        P(None, None, "gx", "gy", "col"),
        P(("gx", "col"), None),
    )
    return jax.shard_map(
        body,
        mesh=mesh,
        in_specs=placed,
        out_specs=(P(None, None, "gx", "gy", "col"), P(None, None, "gx", "gy", "col")),
        check_vma=False,
    )
```

```python
import jax
import jax.numpy as jnp
from jax import lax
from jax.experimental import pallas as pl
from jax.experimental.pallas import tpu as pltpu
from jax.sharding import PartitionSpec as P

DAMPING = 0.6
F32 = jnp.float32
BF16 = jnp.bfloat16
LANES = 128
HALO_IDS = 16
AXES = ("gx", "gy", "col")
TRANSPOSED = (((1,), (1,)), ((), ()))


def split_hi_lo(value):
    hi = value.astype(BF16)
    return hi, (value - hi.astype(F32)).astype(BF16)


def paired_left(value, width, parts):
    rows = value.shape[0]
    hi, lo = split_hi_lo(value)
    parts[pl.ds(0, rows), :] = hi
    parts[pl.ds(rows, rows), :] = lo
    high = parts[pl.ds(0, rows), :].astype(F32)
    low = parts[pl.ds(rows, rows), :].astype(F32)
    return jnp.concatenate([high + roll_lanes(high, width), low], axis=0).astype(BF16)


def lane_ids(rows):
    return lax.broadcasted_iota(jnp.int32, (rows, LANES), 1)


def roll_lanes(value, shift):
    if isinstance(shift, int):
        shift = shift % LANES
        if shift == 0:
            return value
    return pltpu.roll(value, shift, axis=1)


def vmem_call(name, kernel, outs, scratch, limit_mib, flops, moved, operands, spaces=None):
    spaces = spaces or [pltpu.VMEM] * len(operands)
    return pl.pallas_call(
        kernel,
        name=name,
        out_shape=outs,
        in_specs=[pl.BlockSpec(memory_space=space) for space in spaces],
        out_specs=jax.tree.map(lambda _: pl.BlockSpec(memory_space=pltpu.VMEM), outs),
        scratch_shapes=scratch,
        compiler_params=pltpu.CompilerParams(vmem_limit_bytes=limit_mib << 20),
        cost_estimate=pl.CostEstimate(flops=flops, bytes_accessed=moved, transcendentals=0),
    )(*operands)


def own_index():
    index = 0
    for axis in AXES:
        index = index * lax.axis_size(axis) + lax.axis_index(axis)
    return index


class Sizes:
    def __init__(self, residual, eigen_basis, coarse_inverse):
        self.comps, self.loads, self.cx, self.cy, _ = residual.shape
        self.slots = eigen_basis.shape[0]
        self.block_rows, self.total_rows = coarse_inverse.shape
        self.cells = self.cx * self.cy
        self.bx, self.by = self.cx + 2, self.cy + 2
        self.box = self.bx * self.by
        self.tiles = self.comps * self.cells
        self.face_x = self.comps * self.cy * self.loads
        self.face_y = self.comps * self.bx * self.loads
        self.inner_y = self.comps * self.cx * self.loads
        self.face_z = self.comps * self.loads
        self.pitch = 16


class Halo:
    def __init__(self, axis, refs):
        self.refs = refs
        self.even = lax.rem(lax.axis_index(axis), 2) == 0

    def side(self, rows, first):
        value = self.refs[0][rows, :].astype(F32)
        other = self.refs[1][rows, :].astype(F32) if len(self.refs) > 1 else jnp.zeros_like(value)
        return jnp.where(self.even, value, other) if first else jnp.where(self.even, other, value)

    def below(self, rows):
        return self.side(rows, False)

    def above(self, rows):
        return self.side(rows, True)

    def send(self, rows, low, high):
        self.refs[0][rows, :] = jnp.where(self.even, high, low).astype(BF16)
        if len(self.refs) > 1:
            self.refs[1][rows, :] = jnp.where(self.even, low, high).astype(BF16)


def swaps(axis):
    return 1 if lax.axis_size(axis) == 2 else 2


def exchange(faces, axis):
    devices = lax.axis_size(axis)
    result = []
    for parity in range(swaps(axis)):
        pairs = []
        for low in range(parity, devices - 1, 2):
            pairs += [(low, low + 1), (low + 1, low)]
        result.append(lax.ppermute(faces[parity], axis, pairs))
    return result


def take_halos(refs, *axes):
    refs = list(refs)
    halos = []
    for axis in axes:
        count = swaps(axis)
        halos.append(Halo(axis, refs[:count]))
        refs = refs[count:]
    return halos + [refs]


def own_rows(sz, ref, comp, cell):
    start = comp * sz.loads * sz.cells + cell
    return ref[pl.ds(start, sz.loads, stride=sz.cells), :]


def pack_x(sz, res, ids, *refs):
    xsend, (low, high, id_rows, sem) = take_halos(refs, "gx")
    copies = [
        pltpu.make_async_copy(res.at[:, pl.ds(0, sz.cy)], low, sem.at[0]),
        pltpu.make_async_copy(res.at[:, pl.ds(sz.cells - sz.cy, sz.cy)], high, sem.at[1]),
        pltpu.make_async_copy(ids, id_rows, sem.at[2]),
    ]
    for copy in copies:
        copy.start()
    for copy in copies:
        copy.wait()
    low, high = (ref.reshape(sz.comps * sz.loads * sz.cy, LANES) for ref in (low, high))
    for comp in range(sz.comps):
        for y in range(sz.cy):
            rows = pl.ds((comp * sz.cy + y) * sz.loads, sz.loads)
            taken = pl.ds(comp * sz.loads * sz.cy + y, sz.loads, stride=sz.cy)
            xsend.send(rows, low[taken, :], high[taken, :])
    two = 2 * sz.cy
    first = (id_rows[pl.ds(0, two), :] + 1).astype(F32)
    last = (id_rows[pl.ds(sz.cells - two, two), :] + 1).astype(F32)
    xsend.send(pl.ds(sz.face_x, two), first, last)


def make_pieces(
    sz, count, rank, basis_in, res_in, after, message, split, wide, basis_rows, res_rows, sem
):
    del after
    slots, loads = sz.slots, sz.loads
    copies = []
    for comp in range(sz.comps):
        part = pl.ds(comp * sz.cells, sz.cells)
        copies.append(
            (
                pltpu.make_async_copy(
                    basis_in.at[:, part], basis_rows.at[:, part], sem.at[0, comp]
                ),
                pltpu.make_async_copy(res_in.at[comp], res_rows.at[comp], sem.at[1, comp]),
            )
        )
    for pair in copies:
        for copy in pair:
            copy.start()
    basis = basis_rows.reshape(slots * sz.tiles, LANES)
    res = res_rows.reshape(sz.tiles * loads, LANES)

    def step(index, carry):
        both, low = carry
        basis_hi, basis_lo, res_hi, res_both = [], [], [], []
        for half in range(2):
            tile = index * 2 + half
            comp = tile // sz.cells
            hi, lo = split_hi_lo(basis[pl.ds(tile, slots, stride=sz.tiles), :])
            split[tile] = hi
            value_hi, value_lo = split_hi_lo(own_rows(sz, res, comp, tile - comp * sz.cells))
            basis_hi.append(hi)
            basis_lo.append(lo)
            res_hi.append(value_hi)
            res_both.append(jnp.concatenate([value_hi, value_lo], axis=0))
        both = both + lax.dot_general(
            jnp.concatenate(res_both, axis=1),
            jnp.concatenate(basis_hi, axis=1),
            TRANSPOSED,
            preferred_element_type=F32,
        )
        low = low + lax.dot_general(
            jnp.concatenate(res_hi, axis=1),
            jnp.concatenate(basis_lo, axis=1),
            TRANSPOSED,
            preferred_element_type=F32,
        )
        return both, low

    carry = (jnp.zeros((2 * loads, slots), F32), jnp.zeros((loads, slots), F32))
    for comp in range(sz.comps):
        for copy in copies[comp]:
            copy.wait()
        carry = lax.fori_loop(
            comp * sz.cells // 2, (comp + 1) * sz.cells // 2, step, carry, unroll=8
        )
    both, low = carry
    pieces = both[:loads] + both[loads:] + low
    slot = lax.broadcasted_iota(jnp.int32, pieces.shape, 1)
    wide[...] = jnp.zeros_like(wide)
    wide[:, pl.ds(0, slots)] = jnp.where(slot < count[0], pieces, 0.0)
    half = loads // 2
    lane = lane_ids(half)
    packed = jnp.where(lane < 64, wide[:half, :], roll_lanes(wide[half:, :], 64))
    packed = jnp.where(lane == slots, count[0].astype(F32), packed)
    packed = jnp.where(lane == slots + 1, rank[0].astype(F32), packed)
    message[...] = packed.astype(BF16)


def pack_y(sz, res, ids, packed, *refs):
    xhalo, refs = take_halos(refs, "gx")
    message = refs[0]
    ysend, (side_low, side_high) = take_halos(refs[1:], "gy")
    for device in range(message.shape[0]):
        message[device] = packed[...]
    last = sz.cy - 1
    for comp in range(sz.comps):
        for x in range(sz.bx):
            rows = pl.ds((comp * sz.bx + x) * sz.loads, sz.loads)
            if 0 < x < sz.bx - 1:
                low, high = (own_rows(sz, res, comp, (x - 1) * sz.cy + y) for y in (0, last))
            else:
                side = xhalo.below if x == 0 else xhalo.above
                low, high = (
                    side(pl.ds((comp * sz.cy + y) * sz.loads, sz.loads)) for y in (0, last)
                )
            ysend.send(rows, low, high)
    ids_below = xhalo.below(pl.ds(sz.face_x, 2 * sz.cy))
    ids_above = xhalo.above(pl.ds(sz.face_x, 2 * sz.cy))
    for x in range(sz.cx + 4):
        if x < 2:
            rows = ids_below[x * sz.cy : (x + 1) * sz.cy]
        elif x >= sz.cx + 2:
            rows = ids_above[(x - sz.cx - 2) * sz.cy : (x - sz.cx - 1) * sz.cy]
        else:
            rows = (ids[pl.ds((x - 2) * sz.cy, sz.cy), :] + 1).astype(F32)
        side_low[pl.ds(2 * x, 2), :] = rows[:2]
        side_high[pl.ds(2 * x, 2), :] = rows[sz.cy - 2 :]
    ysend.send(pl.ds(sz.face_y, HALO_IDS), side_low[...], side_high[...])


def box_tile(sz, res, xhalo, yhalo, comp, x, y):
    if y == 0 or y == sz.by - 1:
        side = yhalo.below if y == 0 else yhalo.above
        return side(pl.ds((comp * sz.bx + x) * sz.loads, sz.loads))
    if x == 0 or x == sz.bx - 1:
        side = xhalo.below if x == 0 else xhalo.above
        return side(pl.ds((comp * sz.cy + y - 1) * sz.loads, sz.loads))
    return own_rows(sz, res, comp, (x - 1) * sz.cy + y - 1)


def pack_z(sz, res, ids, *refs):
    xhalo, yhalo, (out, id_box, star, outer) = take_halos(refs, "gx", "gy")
    pitch = sz.pitch
    id_box[...] = jnp.zeros_like(id_box)
    two = 2 * sz.cy
    ids_below = xhalo.below(pl.ds(sz.face_x, two))
    ids_above = xhalo.above(pl.ds(sz.face_x, two))
    ids_low = yhalo.below(pl.ds(sz.face_y, HALO_IDS))
    ids_high = yhalo.above(pl.ds(sz.face_y, HALO_IDS))
    for x in range(sz.cx + 4):
        if x < 2:
            rows = ids_below[x * sz.cy : (x + 1) * sz.cy]
        elif x >= sz.cx + 2:
            rows = ids_above[(x - sz.cx - 2) * sz.cy : (x - sz.cx - 1) * sz.cy]
        else:
            rows = (ids[pl.ds((x - 2) * sz.cy, sz.cy), :] + 1).astype(F32)
        id_box[pl.ds(x * pitch + 2, sz.cy), :] = rows
        id_box[pl.ds(x * pitch, 2), :] = ids_low[2 * x : 2 * x + 2]
        id_box[pl.ds(x * pitch + sz.cy + 2, 2), :] = ids_high[2 * x : 2 * x + 2]
    values = id_box[...]
    lane = lane_ids(values.shape[0])
    outer[...] = jnp.where(lane == LANES - 1, roll_lanes(values, 1), roll_lanes(values, -1))
    star[...] = jnp.zeros_like(star)
    lane8 = lane_ids(8)
    taken = jnp.zeros((8, LANES), F32)
    for x in range(sz.bx):
        for y in range(sz.by):
            place = x * sz.by + y
            row = (x + 1) * pitch + y + 1
            for j, shift in enumerate((0, -pitch, pitch, -1, 1)):
                star[pl.ds(place * 8 + j, 1), :] = id_box[pl.ds(row + shift, 1), :]
            star[pl.ds(place * 8 + 5, 1), :] = outer[pl.ds(row, 1), :]
    for place in range(sz.box):
        picked = roll_lanes(star[pl.ds(place * 8, 8), :], 2 * place + 1)
        taken = jnp.where((lane8 >> 1) == place, picked, taken)
    out[pl.ds(sz.face_z, HALO_IDS), :] = jnp.concatenate(
        [taken, jnp.zeros((HALO_IDS - 8, LANES), F32)], axis=0
    ).astype(BF16)
    lane_k = lane_ids(sz.loads)
    for comp in range(sz.comps):
        total = jnp.zeros((sz.loads, LANES), F32)
        for x in range(sz.bx):
            for y in range(sz.by):
                place = x * sz.by + y
                tile = box_tile(sz, res, xhalo, yhalo, comp, x, y)
                total = jnp.where(
                    (lane_k >> 1) == place, roll_lanes(tile, 2 * place + 1), total
                )
        out[pl.ds(comp * sz.loads, sz.loads), :] = total.astype(BF16)


def place_pieces(
    sz, gathered, inverse, after, message, starts_out, vector, wide, heads, starts, sem
):
    del after
    devices = gathered.shape[0]
    for device in range(devices):
        heads[pl.ds(device, 1), :] = gathered[device].astype(F32)[0:1]
    values = heads[...]
    ranks = jnp.transpose(values)[sz.slots + 1 : sz.slots + 2, :]
    earlier = values[:, sz.slots + 1 : sz.slots + 2] < ranks
    total = jnp.sum(jnp.where(earlier, values[:, sz.slots : sz.slots + 1], 0.0), axis=0, keepdims=True)
    starts_out[...] = jnp.zeros_like(starts_out)
    starts_out[:, pl.ds(0, devices)] = jnp.broadcast_to(total.astype(jnp.int32), (8, devices))
    copy = pltpu.make_async_copy(starts_out, starts, sem)
    copy.start()
    half = sz.loads // 2
    lane = lane_ids(half)
    vector[...] = jnp.zeros_like(vector)
    copy.wait()

    def place(device, carry):
        start = starts[0, device]
        block = start // LANES
        offset = start - block * LANES
        packed = gathered[device].astype(F32)
        low = jnp.where(lane < sz.slots, packed, 0.0)
        high = jnp.where((lane >= 64) & (lane < 64 + sz.slots), packed, 0.0)
        both = jnp.concatenate(
            [
                pltpu.roll(low, offset, axis=1),
                pltpu.roll(high, lax.rem(offset + 64, LANES), axis=1),
            ],
            axis=0,
        )
        wide_lane = lane_ids(sz.loads)
        vector[block] = vector[block] + jnp.where(wide_lane >= offset, both, 0.0)
        vector[block + 1] = vector[block + 1] + jnp.where(wide_lane < offset, both, 0.0)
        return carry

    lax.fori_loop(0, gathered.shape[0], place, 0, unroll=8)
    total = jnp.zeros((sz.loads, sz.block_rows), F32)
    for block in range(sz.total_rows // LANES):
        total = total + lax.dot_general(
            vector[block].astype(BF16),
            inverse[:, pl.ds(block * LANES, LANES)],
            TRANSPOSED,
            preferred_element_type=F32,
        )
    if sz.block_rows == 64:
        wide[...] = jnp.zeros_like(wide)
        wide[:, pl.ds(0, 64)] = total
        packed = jnp.where(lane < 64, wide[:half, :], roll_lanes(wide[half:, :], 64))
        for device in range(message.shape[0]):
            message[device, 0] = packed
    else:
        for device in range(message.shape[0]):
            for block in range(sz.block_rows // LANES):
                message[device, block] = total[:, block * LANES : (block + 1) * LANES]


def own_coefs(sz, coefs, start):
    if sz.block_rows == 64:
        half = sz.loads // 2
        block = start // 64
        offset = start - block * 64
        first = coefs[block]
        second = coefs[jnp.minimum(block + 1, coefs.shape[0] - 1)]
        lane = lane_ids(half)
        top = jnp.where(lane < 64, first, roll_lanes(second, 64))
        bottom = jnp.where(lane < 64, roll_lanes(first, 64), second)
        both = jnp.concatenate([top, bottom], axis=0)
    else:
        block = start // LANES
        offset = start - block * LANES
        first = coefs[block]
        second = coefs[jnp.minimum(block + 1, coefs.shape[0] - 1)]
        both = jnp.where(lane_ids(sz.loads) >= offset, first, second)
    return pltpu.roll(both, lax.rem(LANES - offset, LANES), axis=1)


def look_up(table, row, ids):
    result = jnp.zeros_like(ids)
    for material in range(table.shape[1]):
        result = jnp.where(ids == material + 1, table[row, material], result)
    return result


DINV, KEEP, DLAM, WXM, WXP, WYM, WYP, WZM, WZP = range(9)


def spread_row(ref, index, row):
    return ref[index, pl.ds(row, 8, stride=0), :]


def make_coefs(sz, table, id_box, halo_ids, coefs, halo_coefs, own, mu_box, halo_mu):
    pitch = sz.pitch
    mu_box[...] = look_up(table, 0, id_box[...])
    lam_box = look_up(table, 1, id_box[...])
    mu_halo = look_up(table, 0, halo_ids)
    lam_halo = look_up(table, 1, halo_ids)
    lane8 = lane_ids(8)
    center = jnp.broadcast_to(mu_halo[0:1], (8, LANES))
    inner = jnp.zeros((8, LANES), F32)
    for place in range(sz.box):
        row = (place // sz.by + 1) * pitch + place % sz.by + 1
        halo_mu[pl.ds(row, 1), :] = roll_lanes(center, -2 * place)[0:1]
        spread = jnp.broadcast_to(mu_box[pl.ds(row, 1), :], (8, LANES))
        here = (((lane8 + 1) >> 1) & 63) == place
        inner = jnp.where(here, roll_lanes(spread, 2 * place), inner)
    rows_id = lax.broadcasted_iota(jnp.int32, (pitch, LANES), 0)
    lane = lane_ids(pitch)
    for x in range(1, sz.bx + 1):
        mu = mu_box[pl.ds(x * pitch, pitch), :]
        edge = halo_mu[pl.ds(x * pitch, pitch), :]
        lam = lam_box[x * pitch : (x + 1) * pitch]
        faces = [
            0.5 * (mu + mu_box[pl.ds((x - 1) * pitch, pitch), :]),
            0.5 * (mu + mu_box[pl.ds((x + 1) * pitch, pitch), :]),
            0.5 * (mu + mu_box[pl.ds(x * pitch - 1, pitch), :]),
            0.5 * (mu + mu_box[pl.ds(x * pitch + 1, pitch), :]),
            0.5 * (mu + jnp.where(lane == 0, edge, roll_lanes(mu, 1))),
            0.5 * (mu + jnp.where(lane == LANES - 1, edge, roll_lanes(mu, -1))),
        ]
        diag = 1.0 + sum(faces)
        dinv = DAMPING / (diag + lam)
        rows = pl.ds(x * pitch, pitch)
        coefs[DINV, rows, :] = dinv
        coefs[KEEP, rows, :] = (1.0 - DAMPING) + dinv * lam
        coefs[DLAM, rows, :] = dinv * lam
        weights = [dinv * face for face in faces]
        if x == 1:
            weights[0] = jnp.zeros_like(dinv)
        if x == sz.bx:
            weights[1] = jnp.zeros_like(dinv)
        weights[2] = jnp.where(rows_id == 1, 0.0, weights[2])
        weights[3] = jnp.where(rows_id == sz.by, 0.0, weights[3])
        for j in range(6):
            coefs[WXM + j, rows, :] = weights[j]
        if 2 <= x <= sz.cx + 1:
            target = pl.ds((x - 2) * sz.cy, sz.cy)
            for j, value in enumerate([diag, lam] + faces):
                own[j, target, :] = value[2 : 2 + sz.cy]
    place = ((lane8 + 1) >> 1) & 63
    column = jnp.zeros_like(place)
    for x in range(1, sz.bx):
        column = column + (place >= x * sz.by).astype(jnp.int32)
    y_place = place - column * sz.by
    others = [jnp.broadcast_to(mu_halo[j : j + 1], (8, LANES)) for j in range(1, 6)]
    faces = [0.5 * (center + other) for other in others] + [0.5 * (center + inner)]
    lam = jnp.broadcast_to(lam_halo[0:1], (8, LANES))
    dinv = DAMPING / (1.0 + lam + sum(faces))
    live = place < sz.box
    keep = [
        live & (column > 0),
        live & (column < sz.bx - 1),
        live & (y_place > 0),
        live & (y_place < sz.by - 1),
        None,
        live,
    ]
    halo_coefs[DINV] = dinv
    halo_coefs[KEEP] = (1.0 - DAMPING) + dinv * lam
    halo_coefs[DLAM] = dinv * lam
    for j, target in ((0, WXM), (1, WXP), (2, WYM), (3, WYP), (5, WZM)):
        halo_coefs[target] = jnp.where(keep[j], dinv * faces[j], 0.0)


def neighbour_matrix(copies, spread):
    width = (3 if spread else 2) * LANES
    parts = []
    for copy in range(copies + 1):
        row = lax.broadcasted_iota(jnp.int32, (LANES, width), 0)
        lane = lax.broadcasted_iota(jnp.int32, (LANES, width), 1)
        even = (row & 1) == 0
        if copy < copies:
            hit = ((lane < LANES) & (row == lane - 1)) | (
                (lane >= LANES) & (lane < 2 * LANES) & (row == lane - LANES + 1)
            )
            if spread:
                source = jnp.where((lane & 1) == 0, 0, LANES - 1)
                hit = hit | ((lane >= 2 * LANES) & (row == source))
        else:
            hit = ((lane == 0) & even) | ((lane == 2 * LANES - 1) & jnp.logical_not(even))
        parts.append(jnp.where(hit, 1.0, 0.0).astype(BF16))
    return jnp.concatenate(parts, axis=0)


def z_halo(zhalo, rows):
    down, up = zhalo.below(rows), zhalo.above(rows)
    even = (lane_ids(down.shape[0]) & 1) == 0
    return jnp.where(even, down, roll_lanes(up, -2))


def solve_and_direct(sz, count, table, starts_in, res, id_box, coarse, split, *refs):
    xhalo, yhalo, zhalo, refs = take_halos(refs, "gx", "gy", "col")
    direction, own, zface = refs[:3]
    xsend, ysend, refs = take_halos(refs[3:], "gx", "gy")
    first, second, third, halos, inner, coefs, halo_coefs, mu_box, halo_mu, left, zedge = refs[:11]
    wide, own_rows_coef, weights, both_lhs, both_near, starts, sem = refs[11:]
    copy = pltpu.make_async_copy(starts_in, starts, sem)
    copy.start()
    loads, comps = sz.loads, sz.comps
    groups = loads // 8
    lane8 = lane_ids(8)

    halo_mu[...] = jnp.zeros_like(halo_mu)
    inner[...] = jnp.zeros_like(inner)
    make_coefs(
        sz, table, id_box, z_halo(zhalo, pl.ds(sz.face_z, HALO_IDS))[:8], coefs, halo_coefs, own_rows_coef,
        mu_box, halo_mu,
    )

    weights[...] = neighbour_matrix(1, True)

    def spread(place, carry):
        x = place // sz.by
        row = (x + 1) * sz.pitch + place - x * sz.by + 1
        for j in range(9):
            wide[j, place] = jnp.broadcast_to(coefs[j, pl.ds(row, 1), :], (8, LANES))
        return carry

    lax.fori_loop(0, sz.box, spread, 0, unroll=4)

    def spread_own(cell, carry):
        for j in range(8):
            own[j, cell] = jnp.broadcast_to(own_rows_coef[j, pl.ds(cell, 1), :], (8, LANES))
        return carry

    lax.fori_loop(0, sz.cells, spread_own, 0, unroll=4)

    for comp in range(comps):
        halo = z_halo(zhalo, pl.ds(comp * loads, loads))
        dinv = jnp.concatenate([halo_coefs[DINV]] * groups, axis=0)
        halos[0, comp] = dinv * halo
        for x in range(sz.bx):
            for y in range(sz.by):
                place = x * sz.by + y
                tile = box_tile(sz, res, xhalo, yhalo, comp, x, y)
                first[comp, place] = tile * jnp.concatenate([wide[DINV, place]] * groups, axis=0)

    lane_k = lane_ids(loads)

    def relax(source, level, x, ys, put, buffer):
        count = len(ys)
        lhs, near = both_lhs.at[buffer], both_near.at[buffer]
        for j, y in enumerate(ys):
            place = x * sz.by + y
            here = (((lane_k + 1) >> 1) & 63) == place
            for comp in range(comps):
                rows = pl.ds((j * comps + comp) * loads, loads)
                lhs[rows, pl.ds(0, LANES)] = source[comp, place].astype(BF16)
                lhs[rows, pl.ds(LANES, LANES)] = jnp.where(here, halos[level, comp], 0.0).astype(BF16)
        size = count * comps * loads
        cut = 3 * LANES if level < 2 else 2 * LANES
        near[pl.ds(0, size), pl.ds(0, cut)] = jnp.dot(
            lhs[pl.ds(0, size), :], weights[:, pl.ds(0, cut)], preferred_element_type=F32
        )
        for j, y in enumerate(ys):
            place = x * sz.by + y
            coef = [wide[i, place] for i in range(9)]
            here = (((lane8 + 1) >> 1) & 63) == place
            xm, xp = jnp.maximum(place - sz.by, 0), jnp.minimum(place + sz.by, sz.box - 1)
            ym, yp = jnp.maximum(place - 1, 0), jnp.minimum(place + 1, sz.box - 1)
            for group in range(groups):
                rows = pl.ds(group * 8, 8)
                center = [source[comp, place, rows, :] for comp in range(comps)]
                coupled = coef[DLAM] * (center[0] + center[1] + center[2])
                for comp in range(comps):
                    value = center[comp]
                    at = pl.ds((j * comps + comp) * loads + group * 8, 8)
                    out = (first[comp, place, rows, :] - coupled) + coef[KEEP] * value
                    out = out + coef[WXM] * source[comp, xm, rows, :]
                    out = out + coef[WXP] * source[comp, xp, rows, :]
                    out = out + coef[WYM] * source[comp, ym, rows, :]
                    out = out + coef[WYP] * source[comp, yp, rows, :]
                    out = out + coef[WZM] * near[at, pl.ds(0, LANES)]
                    out = out + coef[WZP] * near[at, pl.ds(LANES, LANES)]
                    put(j, place, comp, group, out)
                    if level < 2:
                        pltpu.store(
                            inner.at[level, comp, rows, :],
                            near[at, pl.ds(2 * LANES, LANES)],
                            mask=here,
                        )

    def sweep(source, target, level):
        def put(j, place, comp, group, out):
            target[comp, place, pl.ds(group * 8, 8), :] = out

        def at(pair, carry):
            for buffer in range(2):
                relax(source, level, 2 * pair + buffer, range(sz.by), put, buffer)
            return carry

        lax.fori_loop(0, sz.bx // 2, at, 0)
        coef = [halo_coefs[j] for j in range(8)]
        for group in range(groups):
            rows = pl.ds(group * 8, 8)
            center = [halos[level, comp, rows, :] for comp in range(comps)]
            coupled = coef[DLAM] * (center[0] + center[1] + center[2])
            for comp in range(comps):
                value = center[comp]
                out = (halos[0, comp, rows, :] - coupled) + coef[KEEP] * value
                out = out + coef[WXM] * roll_lanes(value, 2 * sz.by)
                out = out + coef[WXP] * roll_lanes(value, -2 * sz.by)
                out = out + coef[WYM] * roll_lanes(value, 2)
                out = out + coef[WYP] * roll_lanes(value, -2)
                out = out + coef[WZM] * inner[level, comp, rows, :]
                halos[level + 1, comp, rows, :] = out

    sweep(first, second, 0)
    sweep(second, third, 1)

    copy.wait()
    mine = own_coefs(sz, coarse, starts[0, own_index()])
    mine = jnp.where(lane_ids(loads) < jnp.minimum(count[0], sz.slots), mine, 0.0)
    left[...] = paired_left(mine, sz.slots, left)
    zedge[...] = jnp.zeros_like(zedge)

    def final(pair, carry):
        for buffer in range(2):
            finish_plane(2 * pair + buffer, buffer)
        return carry

    def finish_plane(x, buffer):
        lhs, near = both_lhs.at[buffer], both_near.at[buffer]

        def put(j, place, comp, group, out):
            direction[comp, x * sz.cy + j, pl.ds(group * 8, 8), :] = out

        relax(third, 2, x + 1, range(1, sz.cy + 1), put, buffer)
        for y in range(sz.cy):
            cell = x * sz.cy + y
            for comp in range(comps):
                part = jnp.dot(
                    left[:, : sz.slots],
                    split[comp * sz.cells + cell],
                    preferred_element_type=F32,
                )
                value = direction[comp, cell] + (part[:loads] + part[loads:])
                direction[comp, cell] = value
                lhs[pl.ds((y * comps + comp) * loads, loads), pl.ds(0, LANES)] = value.astype(BF16)
        size = sz.cy * comps * loads
        near[pl.ds(0, size), pl.ds(0, LANES)] = jnp.dot(
            lhs[pl.ds(0, size), pl.ds(0, LANES)], edges, preferred_element_type=F32
        )
        for y in range(sz.cy):
            place = (x + 1) * sz.by + y + 1
            for comp in range(comps):
                pltpu.store(
                    zedge.at[pl.ds(comp * loads, loads), :],
                    near[pl.ds((y * comps + comp) * loads, loads), pl.ds(0, LANES)],
                    mask=(lane_k >> 1) == place,
                )

    edge_row = lax.broadcasted_iota(jnp.int32, (LANES, LANES), 0)
    even_lane = (lane_ids(LANES) & 1) == 0
    edges = jnp.where(jnp.where(even_lane, LANES - 1, 0) == edge_row, 1.0, 0.0).astype(BF16)
    lax.fori_loop(0, sz.cx // 2, final, 0)
    zface[...] = zedge[...].astype(BF16)
    for comp in range(comps):
        for y in range(sz.cy):
            rows = pl.ds((comp * sz.cy + y) * loads, loads)
            xsend.send(rows, direction[comp, y], direction[comp, (sz.cx - 1) * sz.cy + y])
        for x in range(sz.cx):
            rows = pl.ds((comp * sz.cx + x) * loads, loads)
            ysend.send(rows, direction[comp, x * sz.cy], direction[comp, (x + 1) * sz.cy - 1])


def make_image(sz, res, own, direction, *refs):
    xhalo, yhalo, zhalo, refs = take_halos(refs, "gx", "gy", "col")
    dir_split, image_split, message, halo, weights, both_lhs, both_near = refs
    weights[...] = neighbour_matrix(2, False)
    loads, comps = sz.loads, sz.comps
    groups = loads // 8
    for comp in range(comps):
        halo[comp] = z_halo(zhalo, pl.ds(comp * loads, loads))
    lane_k = lane_ids(loads)
    total = jnp.zeros((2 * loads, 4 * loads), F32)

    def field_at(comp, x, y):
        if x < 0 or x == sz.cx:
            side = xhalo.below if x < 0 else xhalo.above
            return side(pl.ds((comp * sz.cy + y) * loads, loads))
        if y < 0 or y == sz.cy:
            side = yhalo.below if y < 0 else yhalo.above
            return side(pl.ds((comp * sz.cx + x) * loads, loads))
        return direction[comp, x * sz.cy + y]

    for x in range(sz.cx):
        lhs, near = both_lhs.at[x % 2], both_near.at[x % 2]
        for y in range(sz.cy):
            cell = x * sz.cy + y
            here = (((lane_k + 1) >> 1) & 63) == (x + 1) * sz.by + y + 1
            for comp in range(comps):
                hi, lo = split_hi_lo(direction[comp, cell])
                dir_split[comp * sz.cells + cell] = jnp.concatenate([hi, lo], axis=0)
                rows = pl.ds((y * comps + comp) * loads, loads)
                lhs[rows, pl.ds(0, LANES)] = hi
                lhs[rows, pl.ds(LANES, LANES)] = lo
                lhs[rows, pl.ds(2 * LANES, LANES)] = jnp.where(here, halo[comp], 0.0).astype(BF16)
        near[...] = jnp.dot(lhs[...], weights[...], preferred_element_type=F32)
        sides = {}
        for y in range(sz.cy):
            cell = x * sz.cy + y
            coef = [jnp.concatenate([own[j, cell]] * groups, axis=0) for j in range(8)]
            center = [field_at(comp, x, y) for comp in range(comps)]
            coupled = coef[1] * (center[0] + center[1] + center[2])
            for comp in range(comps):
                tile = comp * sz.cells + cell
                line = pl.ds((y * comps + comp) * loads, loads)
                out = coef[0] * center[comp] + coupled
                out = out - coef[2] * field_at(comp, x - 1, y)
                out = out - coef[3] * field_at(comp, x + 1, y)
                out = out - coef[4] * field_at(comp, x, y - 1)
                out = out - coef[5] * field_at(comp, x, y + 1)
                out = out - coef[6] * near[line, pl.ds(0, LANES)]
                out = out - coef[7] * near[line, pl.ds(LANES, LANES)]
                both = jnp.concatenate(split_hi_lo(out), axis=0)
                image_split[tile] = both
                right = jnp.concatenate((both,) + split_hi_lo(own_rows(sz, res, comp, cell)), axis=0)
                sides[y, comp] = (dir_split[tile], right)
            if y % 2 == 1:
                for comp in range(comps):
                    pair = zip(sides[y - 1, comp], sides[y, comp])
                    left, right = (jnp.concatenate(items, axis=1) for items in pair)
                    total = total + lax.dot_general(
                        left, right, TRANSPOSED, preferred_element_type=F32
                    )
    high, low = total[:loads], total[loads:]
    sums = high + roll_lanes(high, -loads) + low
    half = loads // 2
    lane = lane_ids(half)
    packed = jnp.where((lane & (2 * loads - 1)) < loads, sums[:half], roll_lanes(sums[half:], loads))
    message[...] = packed


def share_sums(sz, mine, *refs):
    message = refs[-1]
    total = mine[...]
    for other in refs[:-1]:
        total = total + other[...]
    for device in range(message.shape[0]):
        message[device] = total


def finish(
    sz, sums, iterate, res, dir_split, image_split, new_iterate, new_residual, parts
):
    loads = sz.loads
    total = sums[0]
    for device in range(1, sums.shape[0]):
        total = total + sums[device]
    system = jnp.concatenate([total, roll_lanes(total, -loads)], axis=0)
    lane = lane_ids(loads)
    system = jnp.where((lane & (2 * loads - 1)) < loads, system, 0.0)
    row_ids = lax.broadcasted_iota(jnp.int32, (loads, LANES), 0)
    for base in range(0, loads, 8):
        columns = [
            jnp.broadcast_to(system[:, i : i + 1], (loads, LANES)) for i in range(base, base + 8)
        ]
        for j in range(8):
            i = base + j
            here = row_ids == i
            scale = 1.0 / columns[j][i : i + 1, :]
            row = system[i : i + 1, :] * scale
            system = jnp.where(here, row, system - columns[j] * row)
            for other in range(j + 1, 8):
                entry = columns[other][i : i + 1, :] * scale
                columns[other] = jnp.where(here, entry, columns[other] - columns[j] * entry)
    step = jnp.transpose(system)[2 * loads : 3 * loads, :]
    padded = jnp.concatenate([step, jnp.zeros((loads, LANES - loads), F32)], axis=1) if (
        step.shape[1] < LANES
    ) else step
    left = paired_left(padded, loads, parts)[:, : 2 * loads]

    def at(cell, carry):
        for comp in range(sz.comps):
            tile = comp * sz.cells + cell
            right = jnp.concatenate([dir_split[tile], image_split[tile]], axis=1)
            part = jnp.dot(left, right, preferred_element_type=F32)
            part = part[:loads] + part[loads:]
            rows = pl.ds(comp * loads * sz.cells + cell, loads, stride=sz.cells)
            new_iterate[rows, :] = iterate[rows, :] + part[:, :LANES]
            new_residual[rows, :] = res[rows, :] - part[:, LANES:]
        return carry

    lax.fori_loop(0, sz.cells, at, 0, unroll=8)


def body(
    iterate, residual, cell_ids, materials, eigen_counts, coarse_rank, eigen_basis, coarse_inverse
):
    sz = Sizes(residual, eigen_basis, coarse_inverse)
    shape = jax.ShapeDtypeStruct
    devices = 1
    for axis in AXES:
        devices = devices * lax.axis_size(axis)
    blocks = sz.total_rows // sz.block_rows
    smem, vmem, scratch, dma = pltpu.SMEM, pltpu.VMEM, pltpu.VMEM, pltpu.SemaphoreType.DMA
    res = residual.reshape(-1, LANES)
    old = iterate.reshape(-1, LANES)
    ids = cell_ids.reshape(-1, LANES)

    def call(name, kernel, *args, **kwargs):
        return vmem_call(name, lambda *refs: kernel(sz, *refs), *args, **kwargs)

    face = shape((sz.face_x + 2 * sz.cy, LANES), BF16)
    faces = call(
        "pack_x",
        pack_x,
        [face] * swaps("gx"),
        [scratch((sz.comps * sz.loads, sz.cy, LANES), F32)] * 2
        + [scratch((sz.cells, LANES), jnp.int32), dma((3,))],
        8,
        1 << 20,
        2 << 20,
        [residual.reshape(-1, sz.cells, LANES), ids],
        spaces=[pl.ANY, pl.ANY],
    )
    xhalo = exchange(faces, "gx")

    packed, split = call(
        "pieces",
        make_pieces,
        [
            shape((sz.loads // 2, LANES), BF16),
            shape((sz.tiles, sz.slots, LANES), BF16),
        ],
        [
            scratch((sz.loads, LANES), F32),
            scratch((sz.slots, sz.tiles, LANES), F32),
            scratch((sz.comps, sz.loads * sz.cells, LANES), F32),
            dma((2, sz.comps)),
        ],
        12,
        1 << 27,
        7 << 20,
        [
            eigen_counts,
            coarse_rank,
            eigen_basis.reshape(sz.slots, sz.tiles, LANES),
            residual.reshape(sz.comps, -1, LANES),
            faces[0],
        ],
        spaces=[smem, smem, pl.ANY, pl.ANY, pl.ANY],
    )

    yface = shape((sz.face_y + HALO_IDS, LANES), BF16)
    message, *faces = call(
        "pack_y",
        pack_y,
        [shape((devices,) + packed.shape, BF16)] + [yface] * swaps("gy"),
        [scratch((HALO_IDS, LANES), F32)] * 2,
        8,
        1 << 20,
        2 << 20,
        [res, ids, packed] + xhalo,
    )
    yhalo = exchange(faces, "gy")
    gathered = lax.all_to_all(message, AXES, 0, 0, tiled=True)
    rows = (sz.cx + 4) * sz.pitch
    zmessage, id_box = call(
        "pack_z",
        pack_z,
        [shape((sz.face_z + HALO_IDS, LANES), BF16), shape((rows, LANES), F32)],
        [scratch((sz.box * 8, LANES), F32), scratch((rows, LANES), F32)],
        8,
        1 << 22,
        3 << 20,
        [res, ids] + xhalo + yhalo,
    )
    zhalo = exchange([zmessage] * 2, "col")

    tile = (1, sz.loads // 2, LANES)
    if sz.block_rows != 64:
        tile = (sz.block_rows // LANES, sz.loads, LANES)
    wide = (8, max(LANES, devices))
    partial, starts = call(
        "coarse",
        place_pieces,
        [shape((blocks,) + tile, F32), shape(wide, jnp.int32)],
        [
            scratch((sz.total_rows // LANES + 1, sz.loads, LANES), F32),
            scratch((sz.loads, LANES), F32),
            scratch((devices, LANES), F32),
            smem(wide, jnp.int32),
            dma,
        ],
        12,
        1 << 23,
        1 << 20,
        [gathered, coarse_inverse, zmessage],
        spaces=[vmem, vmem, pl.ANY],
    )
    coarse = lax.all_to_all(partial, ("gx", "col"), 0, 0, tiled=True)
    coarse = coarse.reshape((-1,) + tile[1:])

    field = scratch((sz.comps, sz.box, sz.loads, LANES), F32)
    direction, own, zface, *faces = call(
        "solve",
        solve_and_direct,
        [
            shape((sz.comps, sz.cells, sz.loads, LANES), F32),
            shape((8, sz.cells, 8, LANES), F32),
            shape((sz.face_z, LANES), BF16),
        ]
        + [shape((sz.face_x, LANES), BF16)] * swaps("gx")
        + [shape((sz.inner_y, LANES), BF16)] * swaps("gy"),
        [
            field,
            field,
            field,
            scratch((3, sz.comps, sz.loads, LANES), F32),
            scratch((2, sz.comps, sz.loads, LANES), F32),
            scratch((9, rows, LANES), F32),
            scratch((9, 8, LANES), F32),
            scratch((rows, LANES), F32),
            scratch((rows, LANES), F32),
            scratch((2 * sz.loads, LANES), BF16),
            scratch((sz.face_z, LANES), F32),
            scratch((9, sz.box, 8, LANES), F32),
            scratch((8, sz.cells, LANES), F32),
            scratch((2 * LANES, 3 * LANES), BF16),
            scratch((2, sz.by * sz.comps * sz.loads, 2 * LANES), BF16),
            scratch((2, sz.by * sz.comps * sz.loads, 3 * LANES), F32),
            smem(starts.shape, jnp.int32),
            dma,
        ],
        28,
        1 << 28,
        8 << 20,
        [eigen_counts, materials, starts, res, id_box, coarse, split] + xhalo + yhalo + zhalo,
        spaces=[smem, smem, pl.ANY] + [vmem] * (4 + len(xhalo + yhalo + zhalo)),
    )
    xhalo = exchange(faces[: swaps("gx")], "gx")
    yhalo = exchange(faces[swaps("gx") :], "gy")
    zhalo = exchange([zface] * 2, "col")
    sums_shape = (sz.loads // 2, LANES)
    dir_split, image_split, sums = call(
        "image",
        make_image,
        [
            shape((sz.tiles, 2 * sz.loads, LANES), BF16),
            shape((sz.tiles, 2 * sz.loads, LANES), BF16),
            shape(sums_shape, F32),
        ],
        [
            scratch((sz.comps, sz.loads, LANES), F32),
            scratch((3 * LANES, 2 * LANES), BF16),
            scratch((2, sz.cy * sz.comps * sz.loads, 3 * LANES), BF16),
            scratch((2, sz.cy * sz.comps * sz.loads, 2 * LANES), F32),
        ],
        20,
        1 << 28,
        8 << 20,
        [res, own, direction] + xhalo + yhalo + zhalo,
        spaces=[vmem] * (3 + len(xhalo + yhalo + zhalo)),
    )
    over, operands = AXES, [sums]
    if lax.axis_size("gy") == 2:
        over = ("gx", "col")
        operands += exchange([sums], "gy")
        devices = devices // 2
    spread = call(
        "share_sums", share_sums, shape((devices,) + sums_shape, F32), [], 4, 1 << 12, 1 << 17,
        operands,
    )
    sums = lax.all_to_all(spread, over, 0, 0, tiled=True)
    flat = shape(res.shape, F32)
    new_iterate, new_residual = call(
        "finish",
        finish,
        [flat, flat],
        [scratch((2 * sz.loads, LANES), BF16)],
        16,
        1 << 27,
        9 << 20,
        [sums, old, res, dir_split, image_split],
    )
    return (new_iterate.reshape(iterate.shape), new_residual.reshape(residual.shape))


def solution(mesh):
    placed = (
        P(None, None, "gx", "gy", "col"),
        P(None, None, "gx", "gy", "col"),
        P("gx", "gy", "col"),
        P(),
        P(("gx", "gy", "col")),
        P(("gx", "gy", "col")),
        P(None, None, "gx", "gy", "col"),
        P(("gx", "col"), None),
    )
    return jax.shard_map(
        body,
        mesh=mesh,
        in_specs=placed,
        out_specs=(P(None, None, "gx", "gy", "col"), P(None, None, "gx", "gy", "col")),
        check_vma=False,
    )
```

```python
import jax
import jax.numpy as jnp
from jax import lax
from jax.experimental import pallas as pl
from jax.experimental.pallas import tpu as pltpu
from jax.sharding import PartitionSpec as P

DAMPING = 0.6
F32 = jnp.float32
BF16 = jnp.bfloat16
LANES = 128
HALO_IDS = 16
AXES = ("gx", "gy", "col")
TRANSPOSED = (((1,), (1,)), ((), ()))


def split_hi_lo(value):
    hi = value.astype(BF16)
    return hi, (value - hi.astype(F32)).astype(BF16)


def paired_left(value, width, parts):
    rows = value.shape[0]
    hi, lo = split_hi_lo(value)
    parts[pl.ds(0, rows), :] = hi
    parts[pl.ds(rows, rows), :] = lo
    high = parts[pl.ds(0, rows), :].astype(F32)
    low = parts[pl.ds(rows, rows), :].astype(F32)
    return jnp.concatenate([high + roll_lanes(high, width), low], axis=0).astype(BF16)


def lane_ids(rows):
    return lax.broadcasted_iota(jnp.int32, (rows, LANES), 1)


def roll_lanes(value, shift):
    if isinstance(shift, int):
        shift = shift % LANES
        if shift == 0:
            return value
    return pltpu.roll(value, shift, axis=1)


def vmem_call(
    name, kernel, outs, scratch, limit_mib, flops, moved, operands, spaces=None,
    out_space=pltpu.VMEM,
):
    spaces = spaces or [pltpu.VMEM] * len(operands)
    return pl.pallas_call(
        kernel,
        name=name,
        out_shape=outs,
        in_specs=[pl.BlockSpec(memory_space=space) for space in spaces],
        out_specs=jax.tree.map(lambda _: pl.BlockSpec(memory_space=out_space), outs),
        scratch_shapes=scratch,
        compiler_params=pltpu.CompilerParams(vmem_limit_bytes=limit_mib << 20),
        cost_estimate=pl.CostEstimate(flops=flops, bytes_accessed=moved, transcendentals=0),
    )(*operands)


def own_index():
    index = 0
    for axis in AXES:
        index = index * lax.axis_size(axis) + lax.axis_index(axis)
    return index


class Sizes:
    def __init__(self, residual, eigen_basis, coarse_inverse):
        self.comps, self.loads, self.cx, self.cy, _ = residual.shape
        self.slots = eigen_basis.shape[0]
        self.block_rows, self.total_rows = coarse_inverse.shape
        self.cells = self.cx * self.cy
        self.bx, self.by = self.cx + 2, self.cy + 2
        self.box = self.bx * self.by
        self.tiles = self.comps * self.cells
        self.face_x = self.comps * self.cy * self.loads
        self.face_y = self.comps * self.bx * self.loads
        self.inner_y = self.comps * self.cx * self.loads
        self.face_z = self.comps * self.loads
        self.pitch = 16


class Halo:
    def __init__(self, axis, refs):
        self.refs = refs
        self.even = lax.rem(lax.axis_index(axis), 2) == 0

    def side(self, rows, first):
        value = self.refs[0][rows, :].astype(F32)
        other = self.refs[1][rows, :].astype(F32) if len(self.refs) > 1 else jnp.zeros_like(value)
        return jnp.where(self.even, value, other) if first else jnp.where(self.even, other, value)

    def below(self, rows):
        return self.side(rows, False)

    def above(self, rows):
        return self.side(rows, True)

    def send(self, rows, low, high):
        self.refs[0][rows, :] = jnp.where(self.even, high, low).astype(BF16)
        if len(self.refs) > 1:
            self.refs[1][rows, :] = jnp.where(self.even, low, high).astype(BF16)


def swaps(axis):
    return 1 if lax.axis_size(axis) == 2 else 2


def exchange(faces, axis):
    devices = lax.axis_size(axis)
    result = []
    for parity in range(swaps(axis)):
        pairs = []
        for low in range(parity, devices - 1, 2):
            pairs += [(low, low + 1), (low + 1, low)]
        result.append(lax.ppermute(faces[parity], axis, pairs))
    return result


def take_halos(refs, *axes):
    refs = list(refs)
    halos = []
    for axis in axes:
        count = swaps(axis)
        halos.append(Halo(axis, refs[:count]))
        refs = refs[count:]
    return halos + [refs]


def own_rows(sz, ref, comp, cell):
    start = comp * sz.loads * sz.cells + cell
    return ref[pl.ds(start, sz.loads, stride=sz.cells), :]


def pack_x(sz, res, ids, *refs):
    xsend, (low, high, id_rows, sem) = take_halos(refs, "gx")
    copies = [
        pltpu.make_async_copy(res.at[:, pl.ds(0, sz.cy)], low, sem.at[0]),
        pltpu.make_async_copy(res.at[:, pl.ds(sz.cells - sz.cy, sz.cy)], high, sem.at[1]),
        pltpu.make_async_copy(ids, id_rows, sem.at[2]),
    ]
    for copy in copies:
        copy.start()
    for copy in copies:
        copy.wait()
    low, high = (ref.reshape(sz.comps * sz.loads * sz.cy, LANES) for ref in (low, high))
    for comp in range(sz.comps):
        for y in range(sz.cy):
            rows = pl.ds((comp * sz.cy + y) * sz.loads, sz.loads)
            taken = pl.ds(comp * sz.loads * sz.cy + y, sz.loads, stride=sz.cy)
            xsend.send(rows, low[taken, :], high[taken, :])
    two = 2 * sz.cy
    first = (id_rows[pl.ds(0, two), :] + 1).astype(F32)
    last = (id_rows[pl.ds(sz.cells - two, two), :] + 1).astype(F32)
    xsend.send(pl.ds(sz.face_x, two), first, last)


def make_pieces(
    sz, count, rank, basis_in, res_in, after, message, split, wide, basis_rows, res_rows, sem
):
    del after
    slots, loads = sz.slots, sz.loads
    copies = []
    for comp in range(sz.comps):
        part = pl.ds(comp * sz.cells, sz.cells)
        copies.append(
            (
                pltpu.make_async_copy(
                    basis_in.at[:, part], basis_rows.at[:, part], sem.at[0, comp]
                ),
                pltpu.make_async_copy(res_in.at[comp], res_rows.at[comp], sem.at[1, comp]),
            )
        )
    for pair in copies:
        for copy in pair:
            copy.start()
    basis = basis_rows.reshape(slots * sz.tiles, LANES)
    res = res_rows.reshape(sz.tiles * loads, LANES)

    def step(index, carry):
        both, low = carry
        basis_hi, basis_lo, res_hi, res_both = [], [], [], []
        for half in range(2):
            tile = index * 2 + half
            comp = tile // sz.cells
            hi, lo = split_hi_lo(basis[pl.ds(tile, slots, stride=sz.tiles), :])
            split[tile, pl.ds(0, slots), :] = hi
            split[tile, pl.ds(slots, slots), :] = lo
            value_hi, value_lo = split_hi_lo(own_rows(sz, res, comp, tile - comp * sz.cells))
            basis_hi.append(hi)
            basis_lo.append(lo)
            res_hi.append(value_hi)
            res_both.append(jnp.concatenate([value_hi, value_lo], axis=0))
        both = both + lax.dot_general(
            jnp.concatenate(res_both, axis=1),
            jnp.concatenate(basis_hi, axis=1),
            TRANSPOSED,
            preferred_element_type=F32,
        )
        low = low + lax.dot_general(
            jnp.concatenate(res_hi, axis=1),
            jnp.concatenate(basis_lo, axis=1),
            TRANSPOSED,
            preferred_element_type=F32,
        )
        return both, low

    carry = (jnp.zeros((2 * loads, slots), F32), jnp.zeros((loads, slots), F32))
    for comp in range(sz.comps):
        for copy in copies[comp]:
            copy.wait()
        for index in range(comp * sz.cells // 2, (comp + 1) * sz.cells // 2):
            carry = step(index, carry)
    both, low = carry
    pieces = both[:loads] + both[loads:] + low
    slot = lax.broadcasted_iota(jnp.int32, pieces.shape, 1)
    wide[...] = jnp.zeros_like(wide)
    wide[:, pl.ds(0, slots)] = jnp.where(slot < count[0], pieces, 0.0)
    half = loads // 2
    lane = lane_ids(half)
    packed = jnp.where(lane < 64, wide[:half, :], roll_lanes(wide[half:, :], 64))
    packed = jnp.where(lane == slots, count[0].astype(F32), packed)
    packed = jnp.where(lane == slots + 1, rank[0].astype(F32), packed)
    message[...] = packed.astype(BF16)


def pack_y(sz, res, ids, packed, *refs):
    xhalo, refs = take_halos(refs, "gx")
    message = refs[0]
    ysend, (side_low, side_high) = take_halos(refs[1:], "gy")
    for device in range(message.shape[0]):
        message[device] = packed[...]
    last = sz.cy - 1
    for comp in range(sz.comps):
        for x in range(sz.bx):
            rows = pl.ds((comp * sz.bx + x) * sz.loads, sz.loads)
            if 0 < x < sz.bx - 1:
                low, high = (own_rows(sz, res, comp, (x - 1) * sz.cy + y) for y in (0, last))
            else:
                side = xhalo.below if x == 0 else xhalo.above
                low, high = (
                    side(pl.ds((comp * sz.cy + y) * sz.loads, sz.loads)) for y in (0, last)
                )
            ysend.send(rows, low, high)
    ids_below = xhalo.below(pl.ds(sz.face_x, 2 * sz.cy))
    ids_above = xhalo.above(pl.ds(sz.face_x, 2 * sz.cy))
    for x in range(sz.cx + 4):
        if x < 2:
            rows = ids_below[x * sz.cy : (x + 1) * sz.cy]
        elif x >= sz.cx + 2:
            rows = ids_above[(x - sz.cx - 2) * sz.cy : (x - sz.cx - 1) * sz.cy]
        else:
            rows = (ids[pl.ds((x - 2) * sz.cy, sz.cy), :] + 1).astype(F32)
        side_low[pl.ds(2 * x, 2), :] = rows[:2]
        side_high[pl.ds(2 * x, 2), :] = rows[sz.cy - 2 :]
    ysend.send(pl.ds(sz.face_y, HALO_IDS), side_low[...], side_high[...])


def box_tile(sz, res, xhalo, yhalo, comp, x, y):
    if y == 0 or y == sz.by - 1:
        side = yhalo.below if y == 0 else yhalo.above
        return side(pl.ds((comp * sz.bx + x) * sz.loads, sz.loads))
    if x == 0 or x == sz.bx - 1:
        side = xhalo.below if x == 0 else xhalo.above
        return side(pl.ds((comp * sz.cy + y - 1) * sz.loads, sz.loads))
    return own_rows(sz, res, comp, (x - 1) * sz.cy + y - 1)


def pack_z(sz, res, ids, *refs):
    xhalo, yhalo, (out, id_box, star, outer) = take_halos(refs, "gx", "gy")
    pitch = sz.pitch
    id_box[...] = jnp.zeros_like(id_box)
    two = 2 * sz.cy
    ids_below = xhalo.below(pl.ds(sz.face_x, two))
    ids_above = xhalo.above(pl.ds(sz.face_x, two))
    ids_low = yhalo.below(pl.ds(sz.face_y, HALO_IDS))
    ids_high = yhalo.above(pl.ds(sz.face_y, HALO_IDS))
    for x in range(sz.cx + 4):
        if x < 2:
            rows = ids_below[x * sz.cy : (x + 1) * sz.cy]
        elif x >= sz.cx + 2:
            rows = ids_above[(x - sz.cx - 2) * sz.cy : (x - sz.cx - 1) * sz.cy]
        else:
            rows = (ids[pl.ds((x - 2) * sz.cy, sz.cy), :] + 1).astype(F32)
        id_box[pl.ds(x * pitch + 2, sz.cy), :] = rows
        id_box[pl.ds(x * pitch, 2), :] = ids_low[2 * x : 2 * x + 2]
        id_box[pl.ds(x * pitch + sz.cy + 2, 2), :] = ids_high[2 * x : 2 * x + 2]
    values = id_box[...]
    lane = lane_ids(values.shape[0])
    outer[...] = jnp.where(lane == LANES - 1, roll_lanes(values, 1), roll_lanes(values, -1))
    star[...] = jnp.zeros_like(star)
    lane8 = lane_ids(8)
    taken = jnp.zeros((8, LANES), F32)
    for x in range(sz.bx):
        for y in range(sz.by):
            place = x * sz.by + y
            row = (x + 1) * pitch + y + 1
            for j, shift in enumerate((0, -pitch, pitch, -1, 1)):
                star[pl.ds(place * 8 + j, 1), :] = id_box[pl.ds(row + shift, 1), :]
            star[pl.ds(place * 8 + 5, 1), :] = outer[pl.ds(row, 1), :]
    for place in range(sz.box):
        picked = roll_lanes(star[pl.ds(place * 8, 8), :], 2 * place + 1)
        taken = jnp.where((lane8 >> 1) == place, picked, taken)
    out[pl.ds(sz.face_z, HALO_IDS), :] = jnp.concatenate(
        [taken, jnp.zeros((HALO_IDS - 8, LANES), F32)], axis=0
    ).astype(BF16)
    lane_k = lane_ids(sz.loads)
    for comp in range(sz.comps):
        total = jnp.zeros((sz.loads, LANES), F32)
        for x in range(sz.bx):
            for y in range(sz.by):
                place = x * sz.by + y
                tile = box_tile(sz, res, xhalo, yhalo, comp, x, y)
                total = jnp.where(
                    (lane_k >> 1) == place, roll_lanes(tile, 2 * place + 1), total
                )
        out[pl.ds(comp * sz.loads, sz.loads), :] = total.astype(BF16)


def place_pieces(
    sz, gathered, inverse, after, message, starts_out, vector, wide, heads, starts, sem
):
    del after
    devices = gathered.shape[0]
    for device in range(devices):
        heads[pl.ds(device, 1), :] = gathered[device].astype(F32)[0:1]
    values = heads[...]
    ranks = jnp.transpose(values)[sz.slots + 1 : sz.slots + 2, :]
    earlier = values[:, sz.slots + 1 : sz.slots + 2] < ranks
    total = jnp.sum(jnp.where(earlier, values[:, sz.slots : sz.slots + 1], 0.0), axis=0, keepdims=True)
    starts_out[...] = jnp.zeros_like(starts_out)
    starts_out[:, pl.ds(0, devices)] = jnp.broadcast_to(total.astype(jnp.int32), (8, devices))
    copy = pltpu.make_async_copy(starts_out, starts, sem)
    copy.start()
    half = sz.loads // 2
    lane = lane_ids(half)
    vector[...] = jnp.zeros_like(vector)
    copy.wait()

    def place(device, carry):
        start = starts[0, device]
        block = start // LANES
        offset = start - block * LANES
        packed = gathered[device].astype(F32)
        low = jnp.where(lane < sz.slots, packed, 0.0)
        high = jnp.where((lane >= 64) & (lane < 64 + sz.slots), packed, 0.0)
        both = jnp.concatenate(
            [
                pltpu.roll(low, offset, axis=1),
                pltpu.roll(high, lax.rem(offset + 64, LANES), axis=1),
            ],
            axis=0,
        )
        wide_lane = lane_ids(sz.loads)
        vector[block] = vector[block] + jnp.where(wide_lane >= offset, both, 0.0)
        vector[block + 1] = vector[block + 1] + jnp.where(wide_lane < offset, both, 0.0)
        return carry

    lax.fori_loop(0, gathered.shape[0], place, 0, unroll=8)
    total = jnp.zeros((sz.loads, sz.block_rows), F32)
    for block in range(sz.total_rows // LANES):
        total = total + lax.dot_general(
            vector[block].astype(BF16),
            inverse[:, pl.ds(block * LANES, LANES)],
            TRANSPOSED,
            preferred_element_type=F32,
        )
    if sz.block_rows == 64:
        wide[...] = jnp.zeros_like(wide)
        wide[:, pl.ds(0, 64)] = total
        packed = jnp.where(lane < 64, wide[:half, :], roll_lanes(wide[half:, :], 64))
        for device in range(message.shape[0]):
            message[device, 0] = packed
    else:
        for device in range(message.shape[0]):
            for block in range(sz.block_rows // LANES):
                message[device, block] = total[:, block * LANES : (block + 1) * LANES]


def own_coefs(sz, coefs, start):
    if sz.block_rows == 64:
        half = sz.loads // 2
        block = start // 64
        offset = start - block * 64
        first = coefs[block]
        second = coefs[jnp.minimum(block + 1, coefs.shape[0] - 1)]
        lane = lane_ids(half)
        top = jnp.where(lane < 64, first, roll_lanes(second, 64))
        bottom = jnp.where(lane < 64, roll_lanes(first, 64), second)
        both = jnp.concatenate([top, bottom], axis=0)
    else:
        block = start // LANES
        offset = start - block * LANES
        first = coefs[block]
        second = coefs[jnp.minimum(block + 1, coefs.shape[0] - 1)]
        both = jnp.where(lane_ids(sz.loads) >= offset, first, second)
    return pltpu.roll(both, lax.rem(LANES - offset, LANES), axis=1)


def look_up(table, row, ids):
    result = jnp.zeros_like(ids)
    for material in range(table.shape[1]):
        result = jnp.where(ids == material + 1, table[row, material], result)
    return result


DINV, KEEP, DLAM, WXM, WXP, WYM, WYP, WZM, WZP = range(9)


def spread_row(ref, index, row):
    return ref[index, pl.ds(row, 8, stride=0), :]


def make_coefs(sz, table, id_box, halo_ids, coefs, halo_coefs, own, mu_box, halo_mu):
    pitch = sz.pitch
    mu_box[...] = look_up(table, 0, id_box[...])
    lam_box = look_up(table, 1, id_box[...])
    mu_halo = look_up(table, 0, halo_ids)
    lam_halo = look_up(table, 1, halo_ids)
    lane8 = lane_ids(8)
    center = jnp.broadcast_to(mu_halo[0:1], (8, LANES))
    inner = jnp.zeros((8, LANES), F32)
    for place in range(sz.box):
        row = (place // sz.by + 1) * pitch + place % sz.by + 1
        halo_mu[pl.ds(row, 1), :] = roll_lanes(center, -2 * place)[0:1]
        spread = jnp.broadcast_to(mu_box[pl.ds(row, 1), :], (8, LANES))
        here = (((lane8 + 1) >> 1) & 63) == place
        inner = jnp.where(here, roll_lanes(spread, 2 * place), inner)
    rows_id = lax.broadcasted_iota(jnp.int32, (pitch, LANES), 0)
    lane = lane_ids(pitch)
    for x in range(1, sz.bx + 1):
        mu = mu_box[pl.ds(x * pitch, pitch), :]
        edge = halo_mu[pl.ds(x * pitch, pitch), :]
        lam = lam_box[x * pitch : (x + 1) * pitch]
        faces = [
            0.5 * (mu + mu_box[pl.ds((x - 1) * pitch, pitch), :]),
            0.5 * (mu + mu_box[pl.ds((x + 1) * pitch, pitch), :]),
            0.5 * (mu + mu_box[pl.ds(x * pitch - 1, pitch), :]),
            0.5 * (mu + mu_box[pl.ds(x * pitch + 1, pitch), :]),
            0.5 * (mu + jnp.where(lane == 0, edge, roll_lanes(mu, 1))),
            0.5 * (mu + jnp.where(lane == LANES - 1, edge, roll_lanes(mu, -1))),
        ]
        diag = 1.0 + sum(faces)
        dinv = DAMPING / (diag + lam)
        rows = pl.ds(x * pitch, pitch)
        coefs[DINV, rows, :] = dinv
        coefs[KEEP, rows, :] = (1.0 - DAMPING) + dinv * lam
        coefs[DLAM, rows, :] = dinv * lam
        weights = [dinv * face for face in faces]
        if x == 1:
            weights[0] = jnp.zeros_like(dinv)
        if x == sz.bx:
            weights[1] = jnp.zeros_like(dinv)
        weights[2] = jnp.where(rows_id == 1, 0.0, weights[2])
        weights[3] = jnp.where(rows_id == sz.by, 0.0, weights[3])
        for j in range(6):
            coefs[WXM + j, rows, :] = weights[j]
        if 2 <= x <= sz.cx + 1:
            target = pl.ds((x - 2) * sz.cy, sz.cy)
            for j, value in enumerate([diag, lam] + faces):
                own[j, target, :] = value[2 : 2 + sz.cy]
    place = ((lane8 + 1) >> 1) & 63
    column = jnp.zeros_like(place)
    for x in range(1, sz.bx):
        column = column + (place >= x * sz.by).astype(jnp.int32)
    y_place = place - column * sz.by
    others = [jnp.broadcast_to(mu_halo[j : j + 1], (8, LANES)) for j in range(1, 6)]
    faces = [0.5 * (center + other) for other in others] + [0.5 * (center + inner)]
    lam = jnp.broadcast_to(lam_halo[0:1], (8, LANES))
    dinv = DAMPING / (1.0 + lam + sum(faces))
    live = place < sz.box
    keep = [
        live & (column > 0),
        live & (column < sz.bx - 1),
        live & (y_place > 0),
        live & (y_place < sz.by - 1),
        None,
        live,
    ]
    halo_coefs[DINV] = dinv
    halo_coefs[KEEP] = (1.0 - DAMPING) + dinv * lam
    halo_coefs[DLAM] = dinv * lam
    for j, target in ((0, WXM), (1, WXP), (2, WYM), (3, WYP), (5, WZM)):
        halo_coefs[target] = jnp.where(keep[j], dinv * faces[j], 0.0)


def neighbour_matrix(copies):
    width = 2 * LANES
    parts = []
    for copy in range(copies + 1):
        row = lax.broadcasted_iota(jnp.int32, (LANES, width), 0)
        lane = lax.broadcasted_iota(jnp.int32, (LANES, width), 1)
        even = (row & 1) == 0
        if copy < copies:
            hit = ((lane < LANES) & (row == lane - 1)) | (
                (lane >= LANES) & (row == lane - LANES + 1)
            )
        else:
            hit = ((lane == 0) & even) | ((lane == width - 1) & jnp.logical_not(even))
        parts.append(jnp.where(hit, 1.0, 0.0).astype(BF16))
    return jnp.concatenate(parts, axis=0)


def z_halo(zhalo, rows):
    down, up = zhalo.below(rows), zhalo.above(rows)
    even = (lane_ids(down.shape[0]) & 1) == 0
    return jnp.where(even, down, roll_lanes(up, -2))


def solve_and_direct(sz, count, table, starts_in, res, id_box, coarse, split, *refs):
    xhalo, yhalo, zhalo, refs = take_halos(refs, "gx", "gy", "col")
    direction, own, zface = refs[:3]
    xsend, ysend, refs = take_halos(refs[3:], "gx", "gy")
    first, second, third, halos, inner, coefs, halo_coefs, mu_box, halo_mu, left, zedge = refs[:11]
    wide, own_rows_coef, weights, both_lhs, both_near, starts, sem = refs[11:]
    copy = pltpu.make_async_copy(starts_in, starts, sem)
    copy.start()
    loads, comps = sz.loads, sz.comps
    groups = loads // 8
    lane8 = lane_ids(8)

    halo_mu[...] = jnp.zeros_like(halo_mu)
    inner[...] = jnp.zeros_like(inner)
    make_coefs(
        sz, table, id_box, z_halo(zhalo, pl.ds(sz.face_z, HALO_IDS))[:8], coefs, halo_coefs, own_rows_coef,
        mu_box, halo_mu,
    )

    weights[...] = neighbour_matrix(1)

    def spread(place, carry):
        x = place // sz.by
        row = (x + 1) * sz.pitch + place - x * sz.by + 1
        for j in range(9):
            wide[j, place] = jnp.broadcast_to(coefs[j, pl.ds(row, 1), :], (8, LANES))
        return carry

    lax.fori_loop(0, sz.box, spread, 0, unroll=4)

    def spread_own(cell, carry):
        for j in range(8):
            own[j, cell] = jnp.broadcast_to(own_rows_coef[j, pl.ds(cell, 1), :], (8, LANES))
        return carry

    lax.fori_loop(0, sz.cells, spread_own, 0, unroll=4)

    for comp in range(comps):
        halo = z_halo(zhalo, pl.ds(comp * loads, loads))
        dinv = jnp.concatenate([halo_coefs[DINV]] * groups, axis=0)
        halos[0, comp] = dinv * halo
        for x in range(sz.bx):
            for y in range(sz.by):
                place = x * sz.by + y
                tile = box_tile(sz, res, xhalo, yhalo, comp, x, y)
                first[comp, place] = tile * jnp.concatenate([wide[DINV, place]] * groups, axis=0)

    lane_k = lane_ids(loads)

    def relax(source, level, x, ys, put, buffer):
        count = len(ys)
        lhs, near = both_lhs.at[buffer], both_near.at[buffer]
        for j, y in enumerate(ys):
            place = x * sz.by + y
            here = (((lane_k + 1) >> 1) & 63) == place
            for comp in range(comps):
                rows = pl.ds((j * comps + comp) * loads, loads)
                lhs[rows, pl.ds(0, LANES)] = source[comp, place].astype(BF16)
                lhs[rows, pl.ds(LANES, LANES)] = jnp.where(here, halos[level, comp], 0.0).astype(BF16)
        size = count * comps * loads
        near[pl.ds(0, size), :] = jnp.dot(
            lhs[pl.ds(0, size), :], weights[...], preferred_element_type=F32
        )
        for j, y in enumerate(ys):
            place = x * sz.by + y
            coef = [wide[i, place] for i in range(9)]
            here = (((lane8 + 1) >> 1) & 63) == place
            xm, xp = jnp.maximum(place - sz.by, 0), jnp.minimum(place + sz.by, sz.box - 1)
            ym, yp = jnp.maximum(place - 1, 0), jnp.minimum(place + 1, sz.box - 1)
            for group in range(groups):
                rows = pl.ds(group * 8, 8)
                center = [source[comp, place, rows, :] for comp in range(comps)]
                coupled = coef[DLAM] * (center[0] + center[1] + center[2])
                for comp in range(comps):
                    value = center[comp]
                    at = pl.ds((j * comps + comp) * loads + group * 8, 8)
                    out = (first[comp, place, rows, :] - coupled) + coef[KEEP] * value
                    out = out + coef[WXM] * source[comp, xm, rows, :]
                    out = out + coef[WXP] * source[comp, xp, rows, :]
                    out = out + coef[WYM] * source[comp, ym, rows, :]
                    out = out + coef[WYP] * source[comp, yp, rows, :]
                    out = out + coef[WZM] * near[at, pl.ds(0, LANES)]
                    out = out + coef[WZP] * near[at, pl.ds(LANES, LANES)]
                    put(j, place, comp, group, out)
                    if level < 2:
                        pltpu.store(
                            inner.at[level, comp, rows, :],
                            pltpu.roll(value, 2 * place, axis=1),
                            mask=here,
                        )

    def sweep(source, target, level):
        def put(j, place, comp, group, out):
            target[comp, place, pl.ds(group * 8, 8), :] = out

        def at(pair, carry):
            for buffer in range(2):
                relax(source, level, 2 * pair + buffer, range(sz.by), put, buffer)
            return carry

        lax.fori_loop(0, sz.bx // 2, at, 0)
        coef = [halo_coefs[j] for j in range(8)]
        for group in range(groups):
            rows = pl.ds(group * 8, 8)
            center = [halos[level, comp, rows, :] for comp in range(comps)]
            coupled = coef[DLAM] * (center[0] + center[1] + center[2])
            for comp in range(comps):
                value = center[comp]
                out = (halos[0, comp, rows, :] - coupled) + coef[KEEP] * value
                out = out + coef[WXM] * roll_lanes(value, 2 * sz.by)
                out = out + coef[WXP] * roll_lanes(value, -2 * sz.by)
                out = out + coef[WYM] * roll_lanes(value, 2)
                out = out + coef[WYP] * roll_lanes(value, -2)
                out = out + coef[WZM] * inner[level, comp, rows, :]
                halos[level + 1, comp, rows, :] = out

    sweep(first, second, 0)
    sweep(second, third, 1)

    copy.wait()
    mine = own_coefs(sz, coarse, starts[0, own_index()])
    mine = jnp.where(lane_ids(loads) < jnp.minimum(count[0], sz.slots), mine, 0.0)
    left[...] = paired_left(mine, sz.slots, left)
    zedge[...] = jnp.zeros_like(zedge)

    def final(pair, carry):
        for buffer in range(2):
            finish_plane(2 * pair + buffer, buffer)
        return carry

    def finish_plane(x, buffer):
        lhs, near = both_lhs.at[buffer], both_near.at[buffer]

        def put(j, place, comp, group, out):
            direction[comp, x * sz.cy + j, pl.ds(group * 8, 8), :] = out

        relax(third, 2, x + 1, range(1, sz.cy + 1), put, buffer)
        for y in range(sz.cy):
            cell = x * sz.cy + y
            for comp in range(comps):
                part = jnp.dot(
                    left[:, : 2 * sz.slots],
                    split[comp * sz.cells + cell],
                    preferred_element_type=F32,
                )
                value = direction[comp, cell] + (part[:loads] + part[loads:])
                direction[comp, cell] = value
                lhs[pl.ds((y * comps + comp) * loads, loads), pl.ds(0, LANES)] = value.astype(BF16)
        size = sz.cy * comps * loads
        near[pl.ds(0, size), pl.ds(0, LANES)] = jnp.dot(
            lhs[pl.ds(0, size), pl.ds(0, LANES)], edges, preferred_element_type=F32
        )
        for y in range(sz.cy):
            place = (x + 1) * sz.by + y + 1
            for comp in range(comps):
                pltpu.store(
                    zedge.at[pl.ds(comp * loads, loads), :],
                    near[pl.ds((y * comps + comp) * loads, loads), pl.ds(0, LANES)],
                    mask=(lane_k >> 1) == place,
                )

    edge_row = lax.broadcasted_iota(jnp.int32, (LANES, LANES), 0)
    even_lane = (lane_ids(LANES) & 1) == 0
    edges = jnp.where(jnp.where(even_lane, LANES - 1, 0) == edge_row, 1.0, 0.0).astype(BF16)
    lax.fori_loop(0, sz.cx // 2, final, 0)
    zface[...] = zedge[...].astype(BF16)
    for comp in range(comps):
        for y in range(sz.cy):
            rows = pl.ds((comp * sz.cy + y) * loads, loads)
            xsend.send(rows, direction[comp, y], direction[comp, (sz.cx - 1) * sz.cy + y])
        for x in range(sz.cx):
            rows = pl.ds((comp * sz.cx + x) * loads, loads)
            ysend.send(rows, direction[comp, x * sz.cy], direction[comp, (x + 1) * sz.cy - 1])


def make_image(sz, res, own, direction, *refs):
    xhalo, yhalo, zhalo, refs = take_halos(refs, "gx", "gy", "col")
    dir_split, image_split, message, halo, weights, both_lhs, both_near = refs
    weights[...] = neighbour_matrix(2)
    loads, comps = sz.loads, sz.comps
    groups = loads // 8
    for comp in range(comps):
        halo[comp] = z_halo(zhalo, pl.ds(comp * loads, loads))
    lane_k = lane_ids(loads)
    total = jnp.zeros((2 * loads, 4 * loads), F32)

    def field_at(comp, x, y):
        if x < 0 or x == sz.cx:
            side = xhalo.below if x < 0 else xhalo.above
            return side(pl.ds((comp * sz.cy + y) * loads, loads))
        if y < 0 or y == sz.cy:
            side = yhalo.below if y < 0 else yhalo.above
            return side(pl.ds((comp * sz.cx + x) * loads, loads))
        return direction[comp, x * sz.cy + y]

    for x in range(sz.cx):
        lhs, near = both_lhs.at[x % 2], both_near.at[x % 2]
        for y in range(sz.cy):
            cell = x * sz.cy + y
            here = (((lane_k + 1) >> 1) & 63) == (x + 1) * sz.by + y + 1
            for comp in range(comps):
                hi, lo = split_hi_lo(direction[comp, cell])
                dir_split[comp * sz.cells + cell] = jnp.concatenate([hi, lo], axis=0)
                rows = pl.ds((y * comps + comp) * loads, loads)
                lhs[rows, pl.ds(0, LANES)] = hi
                lhs[rows, pl.ds(LANES, LANES)] = lo
                lhs[rows, pl.ds(2 * LANES, LANES)] = jnp.where(here, halo[comp], 0.0).astype(BF16)
        near[...] = jnp.dot(lhs[...], weights[...], preferred_element_type=F32)
        sides = {}
        for y in range(sz.cy):
            cell = x * sz.cy + y
            coef = [jnp.concatenate([own[j, cell]] * groups, axis=0) for j in range(8)]
            center = [field_at(comp, x, y) for comp in range(comps)]
            coupled = coef[1] * (center[0] + center[1] + center[2])
            for comp in range(comps):
                tile = comp * sz.cells + cell
                line = pl.ds((y * comps + comp) * loads, loads)
                out = coef[0] * center[comp] + coupled
                out = out - coef[2] * field_at(comp, x - 1, y)
                out = out - coef[3] * field_at(comp, x + 1, y)
                out = out - coef[4] * field_at(comp, x, y - 1)
                out = out - coef[5] * field_at(comp, x, y + 1)
                out = out - coef[6] * near[line, pl.ds(0, LANES)]
                out = out - coef[7] * near[line, pl.ds(LANES, LANES)]
                both = jnp.concatenate(split_hi_lo(out), axis=0)
                image_split[tile] = both
                right = jnp.concatenate((both,) + split_hi_lo(own_rows(sz, res, comp, cell)), axis=0)
                sides[y, comp] = (dir_split[tile], right)
            if y % 2 == 1:
                for comp in range(comps):
                    pair = zip(sides[y - 1, comp], sides[y, comp])
                    left, right = (jnp.concatenate(items, axis=1) for items in pair)
                    total = total + lax.dot_general(
                        left, right, TRANSPOSED, preferred_element_type=F32
                    )
    high, low = total[:loads], total[loads:]
    sums = high + roll_lanes(high, -loads) + low
    half = loads // 2
    lane = lane_ids(half)
    packed = jnp.where((lane & (2 * loads - 1)) < loads, sums[:half], roll_lanes(sums[half:], loads))
    message[...] = packed


def share_sums(sz, mine, *refs):
    message = refs[-1]
    total = mine[...]
    for other in refs[:-1]:
        total = total + other[...]
    for device in range(message.shape[0]):
        message[device] = total


def finish(
    sz, sums, iterate, res, dir_split, image_split, iterate_out, residual_out, parts, new_iterate,
    new_residual, sem,
):
    loads = sz.loads
    total = sums[0]
    for device in range(1, sums.shape[0]):
        total = total + sums[device]
    system = jnp.concatenate([total, roll_lanes(total, -loads)], axis=0)
    lane = lane_ids(loads)
    system = jnp.where((lane & (2 * loads - 1)) < loads, system, 0.0)
    row_ids = lax.broadcasted_iota(jnp.int32, (loads, LANES), 0)
    for base in range(0, loads, 8):
        columns = [
            jnp.broadcast_to(system[:, i : i + 1], (loads, LANES)) for i in range(base, base + 8)
        ]
        for j in range(8):
            i = base + j
            here = row_ids == i
            scale = 1.0 / columns[j][i : i + 1, :]
            row = system[i : i + 1, :] * scale
            system = jnp.where(here, row, system - columns[j] * row)
            for other in range(j + 1, 8):
                entry = columns[other][i : i + 1, :] * scale
                columns[other] = jnp.where(here, entry, columns[other] - columns[j] * entry)
    step = jnp.transpose(system)[2 * loads : 3 * loads, :]
    padded = jnp.concatenate([step, jnp.zeros((loads, LANES - loads), F32)], axis=1) if (
        step.shape[1] < LANES
    ) else step
    left = paired_left(padded, loads, parts)[:, : 2 * loads]

    writes = []
    for comp in range(sz.comps):
        for cell in range(sz.cells):
            tile = comp * sz.cells + cell
            right = jnp.concatenate([dir_split[tile], image_split[tile]], axis=1)
            part = jnp.dot(left, right, preferred_element_type=F32)
            part = part[:loads] + part[loads:]
            rows = pl.ds(comp * loads * sz.cells + cell, loads, stride=sz.cells)
            new_iterate[rows, :] = iterate[rows, :] + part[:, :LANES]
            new_residual[rows, :] = res[rows, :] - part[:, LANES:]
        done = pl.ds(comp * loads * sz.cells, loads * sz.cells)
        for j, (source, out) in enumerate(
            ((new_iterate, iterate_out), (new_residual, residual_out))
        ):
            writes.append(pltpu.make_async_copy(source.at[done], out.at[done], sem.at[j, comp]))
            writes[-1].start()
    for copy in writes:
        copy.wait()


def body(
    iterate, residual, cell_ids, materials, eigen_counts, coarse_rank, eigen_basis, coarse_inverse
):
    sz = Sizes(residual, eigen_basis, coarse_inverse)
    shape = jax.ShapeDtypeStruct
    devices = 1
    for axis in AXES:
        devices = devices * lax.axis_size(axis)
    blocks = sz.total_rows // sz.block_rows
    smem, vmem, scratch, dma = pltpu.SMEM, pltpu.VMEM, pltpu.VMEM, pltpu.SemaphoreType.DMA
    res = residual.reshape(-1, LANES)
    old = iterate.reshape(-1, LANES)
    ids = cell_ids.reshape(-1, LANES)

    def call(name, kernel, *args, **kwargs):
        return vmem_call(name, lambda *refs: kernel(sz, *refs), *args, **kwargs)

    face = shape((sz.face_x + 2 * sz.cy, LANES), BF16)
    faces = call(
        "pack_x",
        pack_x,
        [face] * swaps("gx"),
        [scratch((sz.comps * sz.loads, sz.cy, LANES), F32)] * 2
        + [scratch((sz.cells, LANES), jnp.int32), dma((3,))],
        8,
        1 << 20,
        2 << 20,
        [residual.reshape(-1, sz.cells, LANES), ids],
        spaces=[pl.ANY, pl.ANY],
    )
    xhalo = exchange(faces, "gx")

    packed, split = call(
        "pieces",
        make_pieces,
        [
            shape((sz.loads // 2, LANES), BF16),
            shape((sz.tiles, 2 * sz.slots, LANES), BF16),
        ],
        [
            scratch((sz.loads, LANES), F32),
            scratch((sz.slots, sz.tiles, LANES), F32),
            scratch((sz.comps, sz.loads * sz.cells, LANES), F32),
            dma((2, sz.comps)),
        ],
        12,
        1 << 27,
        7 << 20,
        [
            eigen_counts,
            coarse_rank,
            eigen_basis.reshape(sz.slots, sz.tiles, LANES),
            residual.reshape(sz.comps, -1, LANES),
            faces[0],
        ],
        spaces=[smem, smem, pl.ANY, pl.ANY, pl.ANY],
    )

    yface = shape((sz.face_y + HALO_IDS, LANES), BF16)
    message, *faces = call(
        "pack_y",
        pack_y,
        [shape((devices,) + packed.shape, BF16)] + [yface] * swaps("gy"),
        [scratch((HALO_IDS, LANES), F32)] * 2,
        8,
        1 << 20,
        2 << 20,
        [res, ids, packed] + xhalo,
    )
    yhalo = exchange(faces, "gy")
    gathered = lax.all_to_all(message, AXES, 0, 0, tiled=True)
    rows = (sz.cx + 4) * sz.pitch
    zmessage, id_box = call(
        "pack_z",
        pack_z,
        [shape((sz.face_z + HALO_IDS, LANES), BF16), shape((rows, LANES), F32)],
        [scratch((sz.box * 8, LANES), F32), scratch((rows, LANES), F32)],
        8,
        1 << 22,
        3 << 20,
        [res, ids] + xhalo + yhalo,
    )
    zhalo = exchange([zmessage] * 2, "col")

    tile = (1, sz.loads // 2, LANES)
    if sz.block_rows != 64:
        tile = (sz.block_rows // LANES, sz.loads, LANES)
    wide = (8, max(LANES, devices))
    partial, starts = call(
        "coarse",
        place_pieces,
        [shape((blocks,) + tile, F32), shape(wide, jnp.int32)],
        [
            scratch((sz.total_rows // LANES + 1, sz.loads, LANES), F32),
            scratch((sz.loads, LANES), F32),
            scratch((devices, LANES), F32),
            smem(wide, jnp.int32),
            dma,
        ],
        12,
        1 << 23,
        1 << 20,
        [gathered, coarse_inverse, zmessage],
        spaces=[vmem, vmem, pl.ANY],
    )
    coarse = lax.all_to_all(partial, ("gx", "col"), 0, 0, tiled=True)
    coarse = coarse.reshape((-1,) + tile[1:])

    field = scratch((sz.comps, sz.box, sz.loads, LANES), F32)
    direction, own, zface, *faces = call(
        "solve",
        solve_and_direct,
        [
            shape((sz.comps, sz.cells, sz.loads, LANES), F32),
            shape((8, sz.cells, 8, LANES), F32),
            shape((sz.face_z, LANES), BF16),
        ]
        + [shape((sz.face_x, LANES), BF16)] * swaps("gx")
        + [shape((sz.inner_y, LANES), BF16)] * swaps("gy"),
        [
            field,
            field,
            field,
            scratch((3, sz.comps, sz.loads, LANES), F32),
            scratch((2, sz.comps, sz.loads, LANES), F32),
            scratch((9, rows, LANES), F32),
            scratch((9, 8, LANES), F32),
            scratch((rows, LANES), F32),
            scratch((rows, LANES), F32),
            scratch((2 * sz.loads, LANES), BF16),
            scratch((sz.face_z, LANES), F32),
            scratch((9, sz.box, 8, LANES), F32),
            scratch((8, sz.cells, LANES), F32),
            scratch((2 * LANES, 2 * LANES), BF16),
            scratch((2, sz.by * sz.comps * sz.loads, 2 * LANES), BF16),
            scratch((2, sz.by * sz.comps * sz.loads, 2 * LANES), F32),
            smem(starts.shape, jnp.int32),
            dma,
        ],
        28,
        1 << 28,
        8 << 20,
        [eigen_counts, materials, starts, res, id_box, coarse, split] + xhalo + yhalo + zhalo,
        spaces=[smem, smem, pl.ANY] + [vmem] * (4 + len(xhalo + yhalo + zhalo)),
    )
    xhalo = exchange(faces[: swaps("gx")], "gx")
    yhalo = exchange(faces[swaps("gx") :], "gy")
    zhalo = exchange([zface] * 2, "col")
    sums_shape = (sz.loads // 2, LANES)
    dir_split, image_split, sums = call(
        "image",
        make_image,
        [
            shape((sz.tiles, 2 * sz.loads, LANES), BF16),
            shape((sz.tiles, 2 * sz.loads, LANES), BF16),
            shape(sums_shape, F32),
        ],
        [
            scratch((sz.comps, sz.loads, LANES), F32),
            scratch((3 * LANES, 2 * LANES), BF16),
            scratch((2, sz.cy * sz.comps * sz.loads, 3 * LANES), BF16),
            scratch((2, sz.cy * sz.comps * sz.loads, 2 * LANES), F32),
        ],
        20,
        1 << 28,
        8 << 20,
        [res, own, direction] + xhalo + yhalo + zhalo,
        spaces=[vmem] * (3 + len(xhalo + yhalo + zhalo)),
    )
    over, operands = AXES, [sums]
    if lax.axis_size("gy") == 2:
        over = ("gx", "col")
        operands += exchange([sums], "gy")
        devices = devices // 2
    spread = call(
        "share_sums", share_sums, shape((devices,) + sums_shape, F32), [], 4, 1 << 12, 1 << 17,
        operands,
    )
    sums = lax.all_to_all(spread, over, 0, 0, tiled=True)
    flat = shape(res.shape, F32)
    new_iterate, new_residual = call(
        "finish",
        finish,
        [flat, flat],
        [
            scratch((2 * sz.loads, LANES), BF16),
            scratch(res.shape, F32),
            scratch(res.shape, F32),
            dma((2, sz.comps)),
        ],
        20,
        1 << 27,
        9 << 20,
        [sums, old, res, dir_split, image_split],
        out_space=pl.ANY,
    )
    return (new_iterate.reshape(iterate.shape), new_residual.reshape(residual.shape))


def solution(mesh):
    placed = (
        P(None, None, "gx", "gy", "col"),
        P(None, None, "gx", "gy", "col"),
        P("gx", "gy", "col"),
        P(),
        P(("gx", "gy", "col")),
        P(("gx", "gy", "col")),
        P(None, None, "gx", "gy", "col"),
        P(("gx", "col"), None),
    )
    return jax.shard_map(
        body,
        mesh=mesh,
        in_specs=placed,
        out_specs=(P(None, None, "gx", "gy", "col"), P(None, None, "gx", "gy", "col")),
        check_vma=False,
    )
```

```python
import jax
import jax.numpy as jnp
from jax import lax
from jax.experimental import pallas as pl
from jax.experimental.pallas import tpu as pltpu
from jax.sharding import PartitionSpec as P

DAMPING = 0.6
F32 = jnp.float32
BF16 = jnp.bfloat16
LANES = 128
HALO_IDS = 16
AXES = ("gx", "gy", "col")
TRANSPOSED = (((1,), (1,)), ((), ()))


def split_hi_lo(value):
    hi = value.astype(BF16)
    return hi, (value - hi.astype(F32)).astype(BF16)


def paired_left(value, width, parts):
    rows = value.shape[0]
    hi, lo = split_hi_lo(value)
    parts[pl.ds(0, rows), :] = hi
    parts[pl.ds(rows, rows), :] = lo
    high = parts[pl.ds(0, rows), :].astype(F32)
    low = parts[pl.ds(rows, rows), :].astype(F32)
    return jnp.concatenate([high + roll_lanes(high, width), low], axis=0).astype(BF16)


def lane_ids(rows):
    return lax.broadcasted_iota(jnp.int32, (rows, LANES), 1)


def roll_lanes(value, shift):
    if isinstance(shift, int):
        shift = shift % LANES
        if shift == 0:
            return value
    return pltpu.roll(value, shift, axis=1)


def vmem_call(
    name, kernel, outs, scratch, limit_mib, flops, moved, operands, spaces=None,
    out_space=pltpu.VMEM,
):
    spaces = spaces or [pltpu.VMEM] * len(operands)
    return pl.pallas_call(
        kernel,
        name=name,
        out_shape=outs,
        in_specs=[pl.BlockSpec(memory_space=space) for space in spaces],
        out_specs=jax.tree.map(lambda _: pl.BlockSpec(memory_space=out_space), outs),
        scratch_shapes=scratch,
        compiler_params=pltpu.CompilerParams(vmem_limit_bytes=limit_mib << 20),
        cost_estimate=pl.CostEstimate(flops=flops, bytes_accessed=moved, transcendentals=0),
    )(*operands)


def own_index():
    index = 0
    for axis in AXES:
        index = index * lax.axis_size(axis) + lax.axis_index(axis)
    return index


class Sizes:
    def __init__(self, residual, eigen_basis, coarse_inverse):
        self.comps, self.loads, self.cx, self.cy, _ = residual.shape
        self.slots = eigen_basis.shape[0]
        self.block_rows, self.total_rows = coarse_inverse.shape
        self.cells = self.cx * self.cy
        self.bx, self.by = self.cx + 2, self.cy + 2
        self.box = self.bx * self.by
        self.tiles = self.comps * self.cells
        self.face_x = self.comps * self.cy * self.loads
        self.face_y = self.comps * self.bx * self.loads
        self.inner_y = self.comps * self.cx * self.loads
        self.face_z = self.comps * self.loads
        self.pitch = 16


class Halo:
    def __init__(self, axis, refs):
        self.refs = refs
        self.even = lax.rem(lax.axis_index(axis), 2) == 0

    def side(self, rows, first):
        value = self.refs[0][rows, :].astype(F32)
        other = self.refs[1][rows, :].astype(F32) if len(self.refs) > 1 else jnp.zeros_like(value)
        return jnp.where(self.even, value, other) if first else jnp.where(self.even, other, value)

    def below(self, rows):
        return self.side(rows, False)

    def above(self, rows):
        return self.side(rows, True)

    def send(self, rows, low, high):
        self.refs[0][rows, :] = jnp.where(self.even, high, low).astype(BF16)
        if len(self.refs) > 1:
            self.refs[1][rows, :] = jnp.where(self.even, low, high).astype(BF16)


def swaps(axis):
    return 1 if lax.axis_size(axis) == 2 else 2


def exchange(faces, axis):
    devices = lax.axis_size(axis)
    result = []
    for parity in range(swaps(axis)):
        pairs = []
        for low in range(parity, devices - 1, 2):
            pairs += [(low, low + 1), (low + 1, low)]
        result.append(lax.ppermute(faces[parity], axis, pairs))
    return result


def take_halos(refs, *axes):
    refs = list(refs)
    halos = []
    for axis in axes:
        count = swaps(axis)
        halos.append(Halo(axis, refs[:count]))
        refs = refs[count:]
    return halos + [refs]


def own_rows(sz, ref, comp, cell):
    start = comp * sz.loads * sz.cells + cell
    return ref[pl.ds(start, sz.loads, stride=sz.cells), :]


def pack_x(sz, res, ids, *refs):
    xsend, (low, high, id_rows, sem) = take_halos(refs, "gx")
    copies = [
        pltpu.make_async_copy(res.at[:, pl.ds(0, sz.cy)], low, sem.at[0]),
        pltpu.make_async_copy(res.at[:, pl.ds(sz.cells - sz.cy, sz.cy)], high, sem.at[1]),
        pltpu.make_async_copy(ids, id_rows, sem.at[2]),
    ]
    for copy in copies:
        copy.start()
    for copy in copies:
        copy.wait()
    low, high = (ref.reshape(sz.comps * sz.loads * sz.cy, LANES) for ref in (low, high))
    for comp in range(sz.comps):
        for y in range(sz.cy):
            rows = pl.ds((comp * sz.cy + y) * sz.loads, sz.loads)
            taken = pl.ds(comp * sz.loads * sz.cy + y, sz.loads, stride=sz.cy)
            xsend.send(rows, low[taken, :], high[taken, :])
    two = 2 * sz.cy
    first = (id_rows[pl.ds(0, two), :] + 1).astype(F32)
    last = (id_rows[pl.ds(sz.cells - two, two), :] + 1).astype(F32)
    xsend.send(pl.ds(sz.face_x, two), first, last)


def make_pieces(
    sz, count, rank, basis_in, res_in, after, message, split, wide, basis_rows, res_rows, sem
):
    del after
    slots, loads = sz.slots, sz.loads
    copies = []
    for comp in range(sz.comps):
        part = pl.ds(comp * sz.cells, sz.cells)
        copies.append(
            (
                pltpu.make_async_copy(
                    basis_in.at[:, part], basis_rows.at[:, part], sem.at[0, comp]
                ),
                pltpu.make_async_copy(res_in.at[comp], res_rows.at[comp], sem.at[1, comp]),
            )
        )
    for pair in copies:
        for copy in pair:
            copy.start()
    basis = basis_rows.reshape(slots * sz.tiles, LANES)
    res = res_rows.reshape(sz.tiles * loads, LANES)

    def step(index, carry):
        both, low = carry
        basis_hi, basis_lo, res_hi, res_both = [], [], [], []
        for half in range(2):
            tile = index * 2 + half
            comp = tile // sz.cells
            hi, lo = split_hi_lo(basis[pl.ds(tile, slots, stride=sz.tiles), :])
            split[tile, pl.ds(0, slots), :] = hi
            split[tile, pl.ds(slots, slots), :] = lo
            value_hi, value_lo = split_hi_lo(own_rows(sz, res, comp, tile - comp * sz.cells))
            basis_hi.append(hi)
            basis_lo.append(lo)
            res_hi.append(value_hi)
            res_both.append(jnp.concatenate([value_hi, value_lo], axis=0))
        both = both + lax.dot_general(
            jnp.concatenate(res_both, axis=1),
            jnp.concatenate(basis_hi, axis=1),
            TRANSPOSED,
            preferred_element_type=F32,
        )
        low = low + lax.dot_general(
            jnp.concatenate(res_hi, axis=1),
            jnp.concatenate(basis_lo, axis=1),
            TRANSPOSED,
            preferred_element_type=F32,
        )
        return both, low

    carry = (jnp.zeros((2 * loads, slots), F32), jnp.zeros((loads, slots), F32))
    for comp in range(sz.comps):
        for copy in copies[comp]:
            copy.wait()
        for index in range(comp * sz.cells // 2, (comp + 1) * sz.cells // 2):
            carry = step(index, carry)
    both, low = carry
    pieces = both[:loads] + both[loads:] + low
    slot = lax.broadcasted_iota(jnp.int32, pieces.shape, 1)
    wide[...] = jnp.zeros_like(wide)
    wide[:, pl.ds(0, slots)] = jnp.where(slot < count[0], pieces, 0.0)
    half = loads // 2
    lane = lane_ids(half)
    packed = jnp.where(lane < 64, wide[:half, :], roll_lanes(wide[half:, :], 64))
    packed = jnp.where(lane == slots, count[0].astype(F32), packed)
    packed = jnp.where(lane == slots + 1, rank[0].astype(F32), packed)
    message[...] = packed.astype(BF16)


def pack_y(sz, res, ids, packed, *refs):
    xhalo, refs = take_halos(refs, "gx")
    message = refs[0]
    ysend, (side_low, side_high) = take_halos(refs[1:], "gy")
    for device in range(message.shape[0]):
        message[device] = packed[...]
    last = sz.cy - 1
    for comp in range(sz.comps):
        for x in range(sz.bx):
            rows = pl.ds((comp * sz.bx + x) * sz.loads, sz.loads)
            if 0 < x < sz.bx - 1:
                low, high = (own_rows(sz, res, comp, (x - 1) * sz.cy + y) for y in (0, last))
            else:
                side = xhalo.below if x == 0 else xhalo.above
                low, high = (
                    side(pl.ds((comp * sz.cy + y) * sz.loads, sz.loads)) for y in (0, last)
                )
            ysend.send(rows, low, high)
    ids_below = xhalo.below(pl.ds(sz.face_x, 2 * sz.cy))
    ids_above = xhalo.above(pl.ds(sz.face_x, 2 * sz.cy))
    for x in range(sz.cx + 4):
        if x < 2:
            rows = ids_below[x * sz.cy : (x + 1) * sz.cy]
        elif x >= sz.cx + 2:
            rows = ids_above[(x - sz.cx - 2) * sz.cy : (x - sz.cx - 1) * sz.cy]
        else:
            rows = (ids[pl.ds((x - 2) * sz.cy, sz.cy), :] + 1).astype(F32)
        side_low[pl.ds(2 * x, 2), :] = rows[:2]
        side_high[pl.ds(2 * x, 2), :] = rows[sz.cy - 2 :]
    ysend.send(pl.ds(sz.face_y, HALO_IDS), side_low[...], side_high[...])


def box_tile(sz, res, xhalo, yhalo, comp, x, y):
    if y == 0 or y == sz.by - 1:
        side = yhalo.below if y == 0 else yhalo.above
        return side(pl.ds((comp * sz.bx + x) * sz.loads, sz.loads))
    if x == 0 or x == sz.bx - 1:
        side = xhalo.below if x == 0 else xhalo.above
        return side(pl.ds((comp * sz.cy + y - 1) * sz.loads, sz.loads))
    return own_rows(sz, res, comp, (x - 1) * sz.cy + y - 1)


def pack_z(sz, res, ids, *refs):
    xhalo, yhalo, (out, id_box, star, outer) = take_halos(refs, "gx", "gy")
    pitch = sz.pitch
    id_box[...] = jnp.zeros_like(id_box)
    two = 2 * sz.cy
    ids_below = xhalo.below(pl.ds(sz.face_x, two))
    ids_above = xhalo.above(pl.ds(sz.face_x, two))
    ids_low = yhalo.below(pl.ds(sz.face_y, HALO_IDS))
    ids_high = yhalo.above(pl.ds(sz.face_y, HALO_IDS))
    for x in range(sz.cx + 4):
        if x < 2:
            rows = ids_below[x * sz.cy : (x + 1) * sz.cy]
        elif x >= sz.cx + 2:
            rows = ids_above[(x - sz.cx - 2) * sz.cy : (x - sz.cx - 1) * sz.cy]
        else:
            rows = (ids[pl.ds((x - 2) * sz.cy, sz.cy), :] + 1).astype(F32)
        id_box[pl.ds(x * pitch + 2, sz.cy), :] = rows
        id_box[pl.ds(x * pitch, 2), :] = ids_low[2 * x : 2 * x + 2]
        id_box[pl.ds(x * pitch + sz.cy + 2, 2), :] = ids_high[2 * x : 2 * x + 2]
    values = id_box[...]
    lane = lane_ids(values.shape[0])
    outer[...] = jnp.where(lane == LANES - 1, roll_lanes(values, 1), roll_lanes(values, -1))
    star[...] = jnp.zeros_like(star)
    lane8 = lane_ids(8)
    taken = jnp.zeros((8, LANES), F32)
    for x in range(sz.bx):
        for y in range(sz.by):
            place = x * sz.by + y
            row = (x + 1) * pitch + y + 1
            for j, shift in enumerate((0, -pitch, pitch, -1, 1)):
                star[pl.ds(place * 8 + j, 1), :] = id_box[pl.ds(row + shift, 1), :]
            star[pl.ds(place * 8 + 5, 1), :] = outer[pl.ds(row, 1), :]
    for place in range(sz.box):
        picked = roll_lanes(star[pl.ds(place * 8, 8), :], 2 * place + 1)
        taken = jnp.where((lane8 >> 1) == place, picked, taken)
    out[pl.ds(sz.face_z, HALO_IDS), :] = jnp.concatenate(
        [taken, jnp.zeros((HALO_IDS - 8, LANES), F32)], axis=0
    ).astype(BF16)
    lane_k = lane_ids(sz.loads)
    for comp in range(sz.comps):
        total = jnp.zeros((sz.loads, LANES), F32)
        for x in range(sz.bx):
            for y in range(sz.by):
                place = x * sz.by + y
                tile = box_tile(sz, res, xhalo, yhalo, comp, x, y)
                total = jnp.where(
                    (lane_k >> 1) == place, roll_lanes(tile, 2 * place + 1), total
                )
        out[pl.ds(comp * sz.loads, sz.loads), :] = total.astype(BF16)


def place_pieces(
    sz, gathered, inverse, after, message, starts_out, vector, wide, heads, starts, sem
):
    del after
    devices = gathered.shape[0]
    for device in range(devices):
        heads[pl.ds(device, 1), :] = gathered[device].astype(F32)[0:1]
    values = heads[...]
    ranks = jnp.transpose(values)[sz.slots + 1 : sz.slots + 2, :]
    earlier = values[:, sz.slots + 1 : sz.slots + 2] < ranks
    total = jnp.sum(jnp.where(earlier, values[:, sz.slots : sz.slots + 1], 0.0), axis=0, keepdims=True)
    starts_out[...] = jnp.zeros_like(starts_out)
    starts_out[:, pl.ds(0, devices)] = jnp.broadcast_to(total.astype(jnp.int32), (8, devices))
    copy = pltpu.make_async_copy(starts_out, starts, sem)
    copy.start()
    half = sz.loads // 2
    lane = lane_ids(half)
    vector[...] = jnp.zeros_like(vector)
    copy.wait()

    def place(device, carry):
        start = starts[0, device]
        block = start // LANES
        offset = start - block * LANES
        packed = gathered[device].astype(F32)
        low = jnp.where(lane < sz.slots, packed, 0.0)
        high = jnp.where((lane >= 64) & (lane < 64 + sz.slots), packed, 0.0)
        both = jnp.concatenate(
            [
                pltpu.roll(low, offset, axis=1),
                pltpu.roll(high, lax.rem(offset + 64, LANES), axis=1),
            ],
            axis=0,
        )
        wide_lane = lane_ids(sz.loads)
        vector[block] = vector[block] + jnp.where(wide_lane >= offset, both, 0.0)
        vector[block + 1] = vector[block + 1] + jnp.where(wide_lane < offset, both, 0.0)
        return carry

    lax.fori_loop(0, gathered.shape[0], place, 0, unroll=8)
    total = jnp.zeros((sz.loads, sz.block_rows), F32)
    for block in range(sz.total_rows // LANES):
        total = total + lax.dot_general(
            vector[block].astype(BF16),
            inverse[:, pl.ds(block * LANES, LANES)],
            TRANSPOSED,
            preferred_element_type=F32,
        )
    if sz.block_rows == 64:
        wide[...] = jnp.zeros_like(wide)
        wide[:, pl.ds(0, 64)] = total
        packed = jnp.where(lane < 64, wide[:half, :], roll_lanes(wide[half:, :], 64))
        for device in range(message.shape[0]):
            message[device, 0] = packed
    else:
        for device in range(message.shape[0]):
            for block in range(sz.block_rows // LANES):
                message[device, block] = total[:, block * LANES : (block + 1) * LANES]


def own_coefs(sz, coefs, start):
    if sz.block_rows == 64:
        half = sz.loads // 2
        block = start // 64
        offset = start - block * 64
        first = coefs[block]
        second = coefs[jnp.minimum(block + 1, coefs.shape[0] - 1)]
        lane = lane_ids(half)
        top = jnp.where(lane < 64, first, roll_lanes(second, 64))
        bottom = jnp.where(lane < 64, roll_lanes(first, 64), second)
        both = jnp.concatenate([top, bottom], axis=0)
    else:
        block = start // LANES
        offset = start - block * LANES
        first = coefs[block]
        second = coefs[jnp.minimum(block + 1, coefs.shape[0] - 1)]
        both = jnp.where(lane_ids(sz.loads) >= offset, first, second)
    return pltpu.roll(both, lax.rem(LANES - offset, LANES), axis=1)


def look_up(table, row, ids):
    result = jnp.zeros_like(ids)
    for material in range(table.shape[1]):
        result = jnp.where(ids == material + 1, table[row, material], result)
    return result


DINV, KEEP, DLAM, WXM, WXP, WYM, WYP, WZM, WZP = range(9)


def spread_row(ref, index, row):
    return ref[index, pl.ds(row, 8, stride=0), :]


def make_coefs(sz, table, id_box, halo_ids, coefs, halo_coefs, own, mu_box, halo_mu):
    pitch = sz.pitch
    mu_box[...] = look_up(table, 0, id_box[...])
    lam_box = look_up(table, 1, id_box[...])
    mu_halo = look_up(table, 0, halo_ids)
    lam_halo = look_up(table, 1, halo_ids)
    lane8 = lane_ids(8)
    center = jnp.broadcast_to(mu_halo[0:1], (8, LANES))
    inner = jnp.zeros((8, LANES), F32)
    for place in range(sz.box):
        row = (place // sz.by + 1) * pitch + place % sz.by + 1
        halo_mu[pl.ds(row, 1), :] = roll_lanes(center, -2 * place)[0:1]
        spread = jnp.broadcast_to(mu_box[pl.ds(row, 1), :], (8, LANES))
        here = (((lane8 + 1) >> 1) & 63) == place
        inner = jnp.where(here, roll_lanes(spread, 2 * place), inner)
    rows_id = lax.broadcasted_iota(jnp.int32, (pitch, LANES), 0)
    lane = lane_ids(pitch)
    for x in range(1, sz.bx + 1):
        mu = mu_box[pl.ds(x * pitch, pitch), :]
        edge = halo_mu[pl.ds(x * pitch, pitch), :]
        lam = lam_box[x * pitch : (x + 1) * pitch]
        faces = [
            0.5 * (mu + mu_box[pl.ds((x - 1) * pitch, pitch), :]),
            0.5 * (mu + mu_box[pl.ds((x + 1) * pitch, pitch), :]),
            0.5 * (mu + mu_box[pl.ds(x * pitch - 1, pitch), :]),
            0.5 * (mu + mu_box[pl.ds(x * pitch + 1, pitch), :]),
            0.5 * (mu + jnp.where(lane == 0, edge, roll_lanes(mu, 1))),
            0.5 * (mu + jnp.where(lane == LANES - 1, edge, roll_lanes(mu, -1))),
        ]
        diag = 1.0 + sum(faces)
        dinv = DAMPING / (diag + lam)
        rows = pl.ds(x * pitch, pitch)
        coefs[DINV, rows, :] = dinv
        coefs[KEEP, rows, :] = (1.0 - DAMPING) + dinv * lam
        coefs[DLAM, rows, :] = dinv * lam
        weights = [dinv * face for face in faces]
        if x == 1:
            weights[0] = jnp.zeros_like(dinv)
        if x == sz.bx:
            weights[1] = jnp.zeros_like(dinv)
        weights[2] = jnp.where(rows_id == 1, 0.0, weights[2])
        weights[3] = jnp.where(rows_id == sz.by, 0.0, weights[3])
        for j in range(6):
            coefs[WXM + j, rows, :] = weights[j]
        if 2 <= x <= sz.cx + 1:
            target = pl.ds((x - 2) * sz.cy, sz.cy)
            for j, value in enumerate([diag, lam] + faces):
                own[j, target, :] = value[2 : 2 + sz.cy]
    place = ((lane8 + 1) >> 1) & 63
    column = jnp.zeros_like(place)
    for x in range(1, sz.bx):
        column = column + (place >= x * sz.by).astype(jnp.int32)
    y_place = place - column * sz.by
    others = [jnp.broadcast_to(mu_halo[j : j + 1], (8, LANES)) for j in range(1, 6)]
    faces = [0.5 * (center + other) for other in others] + [0.5 * (center + inner)]
    lam = jnp.broadcast_to(lam_halo[0:1], (8, LANES))
    dinv = DAMPING / (1.0 + lam + sum(faces))
    live = place < sz.box
    keep = [
        live & (column > 0),
        live & (column < sz.bx - 1),
        live & (y_place > 0),
        live & (y_place < sz.by - 1),
        None,
        live,
    ]
    halo_coefs[DINV] = dinv
    halo_coefs[KEEP] = (1.0 - DAMPING) + dinv * lam
    halo_coefs[DLAM] = dinv * lam
    for j, target in ((0, WXM), (1, WXP), (2, WYM), (3, WYP), (5, WZM)):
        halo_coefs[target] = jnp.where(keep[j], dinv * faces[j], 0.0)


def neighbour_matrix(copies):
    width = 2 * LANES
    parts = []
    for copy in range(copies + 1):
        row = lax.broadcasted_iota(jnp.int32, (LANES, width), 0)
        lane = lax.broadcasted_iota(jnp.int32, (LANES, width), 1)
        even = (row & 1) == 0
        if copy < copies:
            hit = ((lane < LANES) & (row == lane - 1)) | (
                (lane >= LANES) & (row == lane - LANES + 1)
            )
        else:
            hit = ((lane == 0) & even) | ((lane == width - 1) & jnp.logical_not(even))
        parts.append(jnp.where(hit, 1.0, 0.0).astype(BF16))
    return jnp.concatenate(parts, axis=0)


def z_halo(zhalo, rows):
    down, up = zhalo.below(rows), zhalo.above(rows)
    even = (lane_ids(down.shape[0]) & 1) == 0
    return jnp.where(even, down, roll_lanes(up, -2))


def solve_and_direct(sz, count, table, starts_in, res, id_box, coarse, split, *refs):
    xhalo, yhalo, zhalo, refs = take_halos(refs, "gx", "gy", "col")
    direction, own, zface = refs[:3]
    xsend, ysend, refs = take_halos(refs[3:], "gx", "gy")
    first, second, third, halos, inner, coefs, halo_coefs, mu_box, halo_mu, left, zedge = refs[:11]
    wide, own_rows_coef, weights, both_lhs, both_near, starts, sem = refs[11:]
    copy = pltpu.make_async_copy(starts_in, starts, sem)
    copy.start()
    loads, comps = sz.loads, sz.comps
    groups = loads // 8
    lane8 = lane_ids(8)

    halo_mu[...] = jnp.zeros_like(halo_mu)
    inner[...] = jnp.zeros_like(inner)
    make_coefs(
        sz, table, id_box, z_halo(zhalo, pl.ds(sz.face_z, HALO_IDS))[:8], coefs, halo_coefs, own_rows_coef,
        mu_box, halo_mu,
    )

    weights[...] = neighbour_matrix(1)

    def spread(place, carry):
        x = place // sz.by
        row = (x + 1) * sz.pitch + place - x * sz.by + 1
        for j in range(9):
            wide[j, place] = jnp.broadcast_to(coefs[j, pl.ds(row, 1), :], (8, LANES))
        return carry

    lax.fori_loop(0, sz.box, spread, 0, unroll=4)

    def spread_own(cell, carry):
        for j in range(8):
            own[j, cell] = jnp.broadcast_to(own_rows_coef[j, pl.ds(cell, 1), :], (8, LANES))
        return carry

    lax.fori_loop(0, sz.cells, spread_own, 0, unroll=4)

    for comp in range(comps):
        halo = z_halo(zhalo, pl.ds(comp * loads, loads))
        dinv = jnp.concatenate([halo_coefs[DINV]] * groups, axis=0)
        halos[0, comp] = dinv * halo
        for x in range(sz.bx):
            for y in range(sz.by):
                place = x * sz.by + y
                tile = box_tile(sz, res, xhalo, yhalo, comp, x, y)
                first[comp, place] = tile * jnp.concatenate([wide[DINV, place]] * groups, axis=0)

    lane_k = lane_ids(loads)

    def relax(source, level, x, ys, put, buffer):
        count = len(ys)
        lhs, near = both_lhs.at[buffer], both_near.at[buffer]
        for j, y in enumerate(ys):
            place = x * sz.by + y
            here = (((lane_k + 1) >> 1) & 63) == place
            for comp in range(comps):
                rows = pl.ds((j * comps + comp) * loads, loads)
                lhs[rows, pl.ds(0, LANES)] = source[comp, place].astype(BF16)
                lhs[rows, pl.ds(LANES, LANES)] = jnp.where(here, halos[level, comp], 0.0).astype(BF16)
        size = count * comps * loads
        near[pl.ds(0, size), :] = jnp.dot(
            lhs[pl.ds(0, size), :], weights[...], preferred_element_type=F32
        )
        for j, y in enumerate(ys):
            place = x * sz.by + y
            coef = [wide[i, place] for i in range(9)]
            here = (((lane8 + 1) >> 1) & 63) == place
            sides = [
                (WXM, place - sz.by, x > 0),
                (WXP, place + sz.by, x < sz.bx - 1),
                (WYM, place - 1, y > 0),
                (WYP, place + 1, y < sz.by - 1),
            ]
            for group in range(groups):
                rows = pl.ds(group * 8, 8)
                center = [source[comp, place, rows, :] for comp in range(comps)]
                coupled = coef[DLAM] * (center[0] + center[1] + center[2])
                for comp in range(comps):
                    value = center[comp]
                    at = pl.ds((j * comps + comp) * loads + group * 8, 8)
                    out = (first[comp, place, rows, :] - coupled) + coef[KEEP] * value
                    for weight, other, inside in sides:
                        if inside:
                            out = out + coef[weight] * source[comp, other, rows, :]
                    out = out + coef[WZM] * near[at, pl.ds(0, LANES)]
                    out = out + coef[WZP] * near[at, pl.ds(LANES, LANES)]
                    put(j, place, comp, group, out)
                    if level < 2:
                        pltpu.store(
                            inner.at[level, comp, rows, :],
                            roll_lanes(value, 2 * place),
                            mask=here,
                        )

    def sweep(source, target, level):
        def put(j, place, comp, group, out):
            target[comp, place, pl.ds(group * 8, 8), :] = out

        for x in range(sz.bx):
            relax(source, level, x, range(sz.by), put, x % 2)
        coef = [halo_coefs[j] for j in range(8)]
        for group in range(groups):
            rows = pl.ds(group * 8, 8)
            center = [halos[level, comp, rows, :] for comp in range(comps)]
            coupled = coef[DLAM] * (center[0] + center[1] + center[2])
            for comp in range(comps):
                value = center[comp]
                out = (halos[0, comp, rows, :] - coupled) + coef[KEEP] * value
                out = out + coef[WXM] * roll_lanes(value, 2 * sz.by)
                out = out + coef[WXP] * roll_lanes(value, -2 * sz.by)
                out = out + coef[WYM] * roll_lanes(value, 2)
                out = out + coef[WYP] * roll_lanes(value, -2)
                out = out + coef[WZM] * inner[level, comp, rows, :]
                halos[level + 1, comp, rows, :] = out

    sweep(first, second, 0)
    sweep(second, third, 1)

    copy.wait()
    mine = own_coefs(sz, coarse, starts[0, own_index()])
    mine = jnp.where(lane_ids(loads) < jnp.minimum(count[0], sz.slots), mine, 0.0)
    left[...] = paired_left(mine, sz.slots, left)
    zedge[...] = jnp.zeros_like(zedge)

    def finish_plane(x, buffer):
        lhs, near = both_lhs.at[buffer], both_near.at[buffer]

        def put(j, place, comp, group, out):
            direction[comp, x * sz.cy + j, pl.ds(group * 8, 8), :] = out

        relax(third, 2, x + 1, range(1, sz.cy + 1), put, buffer)
        for y in range(sz.cy):
            cell = x * sz.cy + y
            for comp in range(comps):
                part = jnp.dot(
                    left[:, : 2 * sz.slots],
                    split[comp * sz.cells + cell],
                    preferred_element_type=F32,
                )
                value = direction[comp, cell] + (part[:loads] + part[loads:])
                direction[comp, cell] = value
                lhs[pl.ds((y * comps + comp) * loads, loads), pl.ds(0, LANES)] = value.astype(BF16)
        size = sz.cy * comps * loads
        near[pl.ds(0, size), pl.ds(0, LANES)] = jnp.dot(
            lhs[pl.ds(0, size), pl.ds(0, LANES)], edges, preferred_element_type=F32
        )
        for y in range(sz.cy):
            place = (x + 1) * sz.by + y + 1
            for comp in range(comps):
                pltpu.store(
                    zedge.at[pl.ds(comp * loads, loads), :],
                    near[pl.ds((y * comps + comp) * loads, loads), pl.ds(0, LANES)],
                    mask=(lane_k >> 1) == place,
                )

    edge_row = lax.broadcasted_iota(jnp.int32, (LANES, LANES), 0)
    even_lane = (lane_ids(LANES) & 1) == 0
    edges = jnp.where(jnp.where(even_lane, LANES - 1, 0) == edge_row, 1.0, 0.0).astype(BF16)
    for x in range(sz.cx):
        finish_plane(x, x % 2)
    zface[...] = zedge[...].astype(BF16)
    for comp in range(comps):
        for y in range(sz.cy):
            rows = pl.ds((comp * sz.cy + y) * loads, loads)
            xsend.send(rows, direction[comp, y], direction[comp, (sz.cx - 1) * sz.cy + y])
        for x in range(sz.cx):
            rows = pl.ds((comp * sz.cx + x) * loads, loads)
            ysend.send(rows, direction[comp, x * sz.cy], direction[comp, (x + 1) * sz.cy - 1])


def make_image(sz, res, own, direction, *refs):
    xhalo, yhalo, zhalo, refs = take_halos(refs, "gx", "gy", "col")
    dir_split, image_split, message, halo, weights, both_lhs, both_near = refs
    weights[...] = neighbour_matrix(2)
    loads, comps = sz.loads, sz.comps
    groups = loads // 8
    for comp in range(comps):
        halo[comp] = z_halo(zhalo, pl.ds(comp * loads, loads))
    lane_k = lane_ids(loads)
    total = jnp.zeros((2 * loads, 4 * loads), F32)

    def field_at(comp, x, y):
        if x < 0 or x == sz.cx:
            side = xhalo.below if x < 0 else xhalo.above
            return side(pl.ds((comp * sz.cy + y) * loads, loads))
        if y < 0 or y == sz.cy:
            side = yhalo.below if y < 0 else yhalo.above
            return side(pl.ds((comp * sz.cx + x) * loads, loads))
        return direction[comp, x * sz.cy + y]

    for x in range(sz.cx):
        lhs, near = both_lhs.at[x % 2], both_near.at[x % 2]
        for y in range(sz.cy):
            cell = x * sz.cy + y
            here = (((lane_k + 1) >> 1) & 63) == (x + 1) * sz.by + y + 1
            for comp in range(comps):
                hi, lo = split_hi_lo(direction[comp, cell])
                dir_split[comp * sz.cells + cell] = jnp.concatenate([hi, lo], axis=0)
                rows = pl.ds((y * comps + comp) * loads, loads)
                lhs[rows, pl.ds(0, LANES)] = hi
                lhs[rows, pl.ds(LANES, LANES)] = lo
                lhs[rows, pl.ds(2 * LANES, LANES)] = jnp.where(here, halo[comp], 0.0).astype(BF16)
        near[...] = jnp.dot(lhs[...], weights[...], preferred_element_type=F32)
        sides = {}
        for y in range(sz.cy):
            cell = x * sz.cy + y
            coef = [jnp.concatenate([own[j, cell]] * groups, axis=0) for j in range(8)]
            center = [field_at(comp, x, y) for comp in range(comps)]
            coupled = coef[1] * (center[0] + center[1] + center[2])
            for comp in range(comps):
                tile = comp * sz.cells + cell
                line = pl.ds((y * comps + comp) * loads, loads)
                out = coef[0] * center[comp] + coupled
                out = out - coef[2] * field_at(comp, x - 1, y)
                out = out - coef[3] * field_at(comp, x + 1, y)
                out = out - coef[4] * field_at(comp, x, y - 1)
                out = out - coef[5] * field_at(comp, x, y + 1)
                out = out - coef[6] * near[line, pl.ds(0, LANES)]
                out = out - coef[7] * near[line, pl.ds(LANES, LANES)]
                both = jnp.concatenate(split_hi_lo(out), axis=0)
                image_split[tile] = both
                right = jnp.concatenate((both,) + split_hi_lo(own_rows(sz, res, comp, cell)), axis=0)
                sides[y, comp] = (dir_split[tile], right)
            if y % 2 == 1:
                for comp in range(comps):
                    pair = zip(sides[y - 1, comp], sides[y, comp])
                    left, right = (jnp.concatenate(items, axis=1) for items in pair)
                    total = total + lax.dot_general(
                        left, right, TRANSPOSED, preferred_element_type=F32
                    )
    high, low = total[:loads], total[loads:]
    sums = high + roll_lanes(high, -loads) + low
    half = loads // 2
    lane = lane_ids(half)
    packed = jnp.where((lane & (2 * loads - 1)) < loads, sums[:half], roll_lanes(sums[half:], loads))
    message[...] = packed


def share_sums(sz, mine, *refs):
    message = refs[-1]
    total = mine[...]
    for other in refs[:-1]:
        total = total + other[...]
    for device in range(message.shape[0]):
        message[device] = total


def finish(
    sz, sums, iterate, res, dir_split, image_split, iterate_out, residual_out, parts, new_iterate,
    new_residual, sem,
):
    loads = sz.loads
    total = sums[0]
    for device in range(1, sums.shape[0]):
        total = total + sums[device]
    system = jnp.concatenate([total, roll_lanes(total, -loads)], axis=0)
    lane = lane_ids(loads)
    system = jnp.where((lane & (2 * loads - 1)) < loads, system, 0.0)
    row_ids = lax.broadcasted_iota(jnp.int32, (loads, LANES), 0)
    for base in range(0, loads, 8):
        columns = [
            jnp.broadcast_to(system[:, i : i + 1], (loads, LANES)) for i in range(base, base + 8)
        ]
        for j in range(8):
            i = base + j
            here = row_ids == i
            scale = 1.0 / columns[j][i : i + 1, :]
            row = system[i : i + 1, :] * scale
            system = jnp.where(here, row, system - columns[j] * row)
            for other in range(j + 1, 8):
                entry = columns[other][i : i + 1, :] * scale
                columns[other] = jnp.where(here, entry, columns[other] - columns[j] * entry)
    step = jnp.transpose(system)[2 * loads : 3 * loads, :]
    padded = jnp.concatenate([step, jnp.zeros((loads, LANES - loads), F32)], axis=1) if (
        step.shape[1] < LANES
    ) else step
    left = paired_left(padded, loads, parts)[:, : 2 * loads]

    writes = []
    for comp in range(sz.comps):
        for cell in range(sz.cells):
            tile = comp * sz.cells + cell
            right = jnp.concatenate([dir_split[tile], image_split[tile]], axis=1)
            part = jnp.dot(left, right, preferred_element_type=F32)
            part = part[:loads] + part[loads:]
            rows = pl.ds(comp * loads * sz.cells + cell, loads, stride=sz.cells)
            new_iterate[rows, :] = iterate[rows, :] + part[:, :LANES]
            new_residual[rows, :] = res[rows, :] - part[:, LANES:]
        done = pl.ds(comp * loads * sz.cells, loads * sz.cells)
        for j, (source, out) in enumerate(
            ((new_iterate, iterate_out), (new_residual, residual_out))
        ):
            writes.append(pltpu.make_async_copy(source.at[done], out.at[done], sem.at[j, comp]))
            writes[-1].start()
    for copy in writes:
        copy.wait()


def body(
    iterate, residual, cell_ids, materials, eigen_counts, coarse_rank, eigen_basis, coarse_inverse
):
    sz = Sizes(residual, eigen_basis, coarse_inverse)
    shape = jax.ShapeDtypeStruct
    devices = 1
    for axis in AXES:
        devices = devices * lax.axis_size(axis)
    blocks = sz.total_rows // sz.block_rows
    smem, vmem, scratch, dma = pltpu.SMEM, pltpu.VMEM, pltpu.VMEM, pltpu.SemaphoreType.DMA
    res = residual.reshape(-1, LANES)
    old = iterate.reshape(-1, LANES)
    ids = cell_ids.reshape(-1, LANES)

    def call(name, kernel, *args, **kwargs):
        return vmem_call(name, lambda *refs: kernel(sz, *refs), *args, **kwargs)

    face = shape((sz.face_x + 2 * sz.cy, LANES), BF16)
    faces = call(
        "pack_x",
        pack_x,
        [face] * swaps("gx"),
        [scratch((sz.comps * sz.loads, sz.cy, LANES), F32)] * 2
        + [scratch((sz.cells, LANES), jnp.int32), dma((3,))],
        8,
        1 << 20,
        2 << 20,
        [residual.reshape(-1, sz.cells, LANES), ids],
        spaces=[pl.ANY, pl.ANY],
    )
    xhalo = exchange(faces, "gx")

    packed, split = call(
        "pieces",
        make_pieces,
        [
            shape((sz.loads // 2, LANES), BF16),
            shape((sz.tiles, 2 * sz.slots, LANES), BF16),
        ],
        [
            scratch((sz.loads, LANES), F32),
            scratch((sz.slots, sz.tiles, LANES), F32),
            scratch((sz.comps, sz.loads * sz.cells, LANES), F32),
            dma((2, sz.comps)),
        ],
        12,
        1 << 27,
        7 << 20,
        [
            eigen_counts,
            coarse_rank,
            eigen_basis.reshape(sz.slots, sz.tiles, LANES),
            residual.reshape(sz.comps, -1, LANES),
            faces[0],
        ],
        spaces=[smem, smem, pl.ANY, pl.ANY, pl.ANY],
    )

    yface = shape((sz.face_y + HALO_IDS, LANES), BF16)
    message, *faces = call(
        "pack_y",
        pack_y,
        [shape((devices,) + packed.shape, BF16)] + [yface] * swaps("gy"),
        [scratch((HALO_IDS, LANES), F32)] * 2,
        8,
        1 << 20,
        2 << 20,
        [res, ids, packed] + xhalo,
    )
    yhalo = exchange(faces, "gy")
    gathered = lax.all_to_all(message, AXES, 0, 0, tiled=True)
    rows = (sz.cx + 4) * sz.pitch
    zmessage, id_box = call(
        "pack_z",
        pack_z,
        [shape((sz.face_z + HALO_IDS, LANES), BF16), shape((rows, LANES), F32)],
        [scratch((sz.box * 8, LANES), F32), scratch((rows, LANES), F32)],
        8,
        1 << 22,
        3 << 20,
        [res, ids] + xhalo + yhalo,
    )
    zhalo = exchange([zmessage] * 2, "col")

    tile = (1, sz.loads // 2, LANES)
    if sz.block_rows != 64:
        tile = (sz.block_rows // LANES, sz.loads, LANES)
    wide = (8, max(LANES, devices))
    partial, starts = call(
        "coarse",
        place_pieces,
        [shape((blocks,) + tile, F32), shape(wide, jnp.int32)],
        [
            scratch((sz.total_rows // LANES + 1, sz.loads, LANES), F32),
            scratch((sz.loads, LANES), F32),
            scratch((devices, LANES), F32),
            smem(wide, jnp.int32),
            dma,
        ],
        12,
        1 << 23,
        1 << 20,
        [gathered, coarse_inverse, zmessage],
        spaces=[vmem, vmem, pl.ANY],
    )
    coarse = lax.all_to_all(partial, ("gx", "col"), 0, 0, tiled=True)
    coarse = coarse.reshape((-1,) + tile[1:])

    field = scratch((sz.comps, sz.box, sz.loads, LANES), F32)
    direction, own, zface, *faces = call(
        "solve",
        solve_and_direct,
        [
            shape((sz.comps, sz.cells, sz.loads, LANES), F32),
            shape((8, sz.cells, 8, LANES), F32),
            shape((sz.face_z, LANES), BF16),
        ]
        + [shape((sz.face_x, LANES), BF16)] * swaps("gx")
        + [shape((sz.inner_y, LANES), BF16)] * swaps("gy"),
        [
            field,
            field,
            field,
            scratch((3, sz.comps, sz.loads, LANES), F32),
            scratch((2, sz.comps, sz.loads, LANES), F32),
            scratch((9, rows, LANES), F32),
            scratch((9, 8, LANES), F32),
            scratch((rows, LANES), F32),
            scratch((rows, LANES), F32),
            scratch((2 * sz.loads, LANES), BF16),
            scratch((sz.face_z, LANES), F32),
            scratch((9, sz.box, 8, LANES), F32),
            scratch((8, sz.cells, LANES), F32),
            scratch((2 * LANES, 2 * LANES), BF16),
            scratch((2, sz.by * sz.comps * sz.loads, 2 * LANES), BF16),
            scratch((2, sz.by * sz.comps * sz.loads, 2 * LANES), F32),
            smem(starts.shape, jnp.int32),
            dma,
        ],
        28,
        1 << 28,
        8 << 20,
        [eigen_counts, materials, starts, res, id_box, coarse, split] + xhalo + yhalo + zhalo,
        spaces=[smem, smem, pl.ANY] + [vmem] * (4 + len(xhalo + yhalo + zhalo)),
    )
    xhalo = exchange(faces[: swaps("gx")], "gx")
    yhalo = exchange(faces[swaps("gx") :], "gy")
    zhalo = exchange([zface] * 2, "col")
    sums_shape = (sz.loads // 2, LANES)
    dir_split, image_split, sums = call(
        "image",
        make_image,
        [
            shape((sz.tiles, 2 * sz.loads, LANES), BF16),
            shape((sz.tiles, 2 * sz.loads, LANES), BF16),
            shape(sums_shape, F32),
        ],
        [
            scratch((sz.comps, sz.loads, LANES), F32),
            scratch((3 * LANES, 2 * LANES), BF16),
            scratch((2, sz.cy * sz.comps * sz.loads, 3 * LANES), BF16),
            scratch((2, sz.cy * sz.comps * sz.loads, 2 * LANES), F32),
        ],
        20,
        1 << 28,
        8 << 20,
        [res, own, direction] + xhalo + yhalo + zhalo,
        spaces=[vmem] * (3 + len(xhalo + yhalo + zhalo)),
    )
    over, operands = AXES, [sums]
    if lax.axis_size("gy") == 2:
        over = ("gx", "col")
        operands += exchange([sums], "gy")
        devices = devices // 2
    spread = call(
        "share_sums", share_sums, shape((devices,) + sums_shape, F32), [], 4, 1 << 12, 1 << 17,
        operands,
    )
    sums = lax.all_to_all(spread, over, 0, 0, tiled=True)
    flat = shape(res.shape, F32)
    new_iterate, new_residual = call(
        "finish",
        finish,
        [flat, flat],
        [
            scratch((2 * sz.loads, LANES), BF16),
            scratch(res.shape, F32),
            scratch(res.shape, F32),
            dma((2, sz.comps)),
        ],
        20,
        1 << 27,
        9 << 20,
        [sums, old, res, dir_split, image_split],
        out_space=pl.ANY,
    )
    return (new_iterate.reshape(iterate.shape), new_residual.reshape(residual.shape))


def solution(mesh):
    placed = (
        P(None, None, "gx", "gy", "col"),
        P(None, None, "gx", "gy", "col"),
        P("gx", "gy", "col"),
        P(),
        P(("gx", "gy", "col")),
        P(("gx", "gy", "col")),
        P(None, None, "gx", "gy", "col"),
        P(("gx", "col"), None),
    )
    return jax.shard_map(
        body,
        mesh=mesh,
        in_specs=placed,
        out_specs=(P(None, None, "gx", "gy", "col"), P(None, None, "gx", "gy", "col")),
        check_vma=False,
    )
```

```python
import jax
import jax.numpy as jnp
from jax import lax
from jax.experimental import pallas as pl
from jax.experimental.pallas import tpu as pltpu
from jax.sharding import PartitionSpec as P

DAMPING = 0.6
F32 = jnp.float32
BF16 = jnp.bfloat16
LANES = 128
HALO_IDS = 16
AXES = ("gx", "gy", "col")
TRANSPOSED = (((1,), (1,)), ((), ()))


def split_hi_lo(value):
    hi = value.astype(BF16)
    return hi, (value - hi.astype(F32)).astype(BF16)


def paired_left(value, width, parts):
    rows = value.shape[0]
    hi, lo = split_hi_lo(value)
    parts[pl.ds(0, rows), :] = hi
    parts[pl.ds(rows, rows), :] = lo
    high = parts[pl.ds(0, rows), :].astype(F32)
    low = parts[pl.ds(rows, rows), :].astype(F32)
    return jnp.concatenate([high + roll_lanes(high, width), low], axis=0).astype(BF16)


def lane_ids(rows):
    return lax.broadcasted_iota(jnp.int32, (rows, LANES), 1)


def roll_lanes(value, shift):
    if isinstance(shift, int):
        shift = shift % LANES
        if shift == 0:
            return value
    return pltpu.roll(value, shift, axis=1)


def vmem_call(
    name, kernel, outs, scratch, limit_mib, flops, moved, operands, spaces=None,
    out_space=pltpu.VMEM,
):
    spaces = spaces or [pltpu.VMEM] * len(operands)
    return pl.pallas_call(
        kernel,
        name=name,
        out_shape=outs,
        in_specs=[pl.BlockSpec(memory_space=space) for space in spaces],
        out_specs=jax.tree.map(lambda _: pl.BlockSpec(memory_space=out_space), outs),
        scratch_shapes=scratch,
        compiler_params=pltpu.CompilerParams(vmem_limit_bytes=limit_mib << 20),
        cost_estimate=pl.CostEstimate(flops=flops, bytes_accessed=moved, transcendentals=0),
    )(*operands)


def own_index():
    index = 0
    for axis in AXES:
        index = index * lax.axis_size(axis) + lax.axis_index(axis)
    return index


class Sizes:
    def __init__(self, residual, eigen_basis, coarse_inverse):
        self.comps, self.loads, self.cx, self.cy, _ = residual.shape
        self.slots = eigen_basis.shape[0]
        self.block_rows, self.total_rows = coarse_inverse.shape
        self.cells = self.cx * self.cy
        self.bx, self.by = self.cx + 2, self.cy + 2
        self.box = self.bx * self.by
        self.tiles = self.comps * self.cells
        self.face_x = self.comps * self.cy * self.loads
        self.face_y = self.comps * self.bx * self.loads
        self.inner_y = self.comps * self.cx * self.loads
        self.face_z = self.comps * self.loads
        self.pitch = 16


class Halo:
    def __init__(self, axis, refs):
        self.refs = refs
        self.even = lax.rem(lax.axis_index(axis), 2) == 0

    def side(self, rows, first):
        value = self.refs[0][rows, :].astype(F32)
        other = self.refs[1][rows, :].astype(F32) if len(self.refs) > 1 else jnp.zeros_like(value)
        return jnp.where(self.even, value, other) if first else jnp.where(self.even, other, value)

    def below(self, rows):
        return self.side(rows, False)

    def above(self, rows):
        return self.side(rows, True)

    def send(self, rows, low, high):
        self.refs[0][rows, :] = jnp.where(self.even, high, low).astype(BF16)
        if len(self.refs) > 1:
            self.refs[1][rows, :] = jnp.where(self.even, low, high).astype(BF16)


def swaps(axis):
    return 1 if lax.axis_size(axis) == 2 else 2


def exchange(faces, axis):
    devices = lax.axis_size(axis)
    result = []
    for parity in range(swaps(axis)):
        pairs = []
        for low in range(parity, devices - 1, 2):
            pairs += [(low, low + 1), (low + 1, low)]
        result.append(lax.ppermute(faces[parity], axis, pairs))
    return result


def take_halos(refs, *axes):
    refs = list(refs)
    halos = []
    for axis in axes:
        count = swaps(axis)
        halos.append(Halo(axis, refs[:count]))
        refs = refs[count:]
    return halos + [refs]


def own_rows(sz, ref, comp, cell):
    start = comp * sz.loads * sz.cells + cell
    return ref[pl.ds(start, sz.loads, stride=sz.cells), :]


def pack_x(sz, res, ids, *refs):
    xsend, (low, high, id_rows, sem) = take_halos(refs, "gx")
    copies = [
        pltpu.make_async_copy(res.at[:, pl.ds(0, sz.cy)], low, sem.at[0]),
        pltpu.make_async_copy(res.at[:, pl.ds(sz.cells - sz.cy, sz.cy)], high, sem.at[1]),
        pltpu.make_async_copy(ids, id_rows, sem.at[2]),
    ]
    for copy in copies:
        copy.start()
    for copy in copies:
        copy.wait()
    low, high = (ref.reshape(sz.comps * sz.loads * sz.cy, LANES) for ref in (low, high))
    for comp in range(sz.comps):
        for y in range(sz.cy):
            rows = pl.ds((comp * sz.cy + y) * sz.loads, sz.loads)
            taken = pl.ds(comp * sz.loads * sz.cy + y, sz.loads, stride=sz.cy)
            xsend.send(rows, low[taken, :], high[taken, :])
    two = 2 * sz.cy
    first = (id_rows[pl.ds(0, two), :] + 1).astype(F32)
    last = (id_rows[pl.ds(sz.cells - two, two), :] + 1).astype(F32)
    xsend.send(pl.ds(sz.face_x, two), first, last)


def make_pieces(
    sz, count, rank, basis_in, res_in, after, message, split, wide, basis_rows, res_rows, sem
):
    del after
    slots, loads = sz.slots, sz.loads
    copies = []
    for comp in range(sz.comps):
        part = pl.ds(comp * sz.cells, sz.cells)
        copies.append(
            (
                pltpu.make_async_copy(
                    basis_in.at[:, part], basis_rows.at[:, part], sem.at[0, comp]
                ),
                pltpu.make_async_copy(res_in.at[comp], res_rows.at[comp], sem.at[1, comp]),
            )
        )
    for pair in copies:
        for copy in pair:
            copy.start()
    basis = basis_rows.reshape(slots * sz.tiles, LANES)
    res = res_rows.reshape(sz.tiles * loads, LANES)

    def step(index, carry):
        both, low = carry
        basis_hi, basis_lo, res_hi, res_both = [], [], [], []
        for half in range(2):
            tile = index * 2 + half
            comp = tile // sz.cells
            hi, lo = split_hi_lo(basis[pl.ds(tile, slots, stride=sz.tiles), :])
            split[tile, pl.ds(0, slots), :] = hi
            split[tile, pl.ds(slots, slots), :] = lo
            value_hi, value_lo = split_hi_lo(own_rows(sz, res, comp, tile - comp * sz.cells))
            basis_hi.append(hi)
            basis_lo.append(lo)
            res_hi.append(value_hi)
            res_both.append(jnp.concatenate([value_hi, value_lo], axis=0))
        both = both + lax.dot_general(
            jnp.concatenate(res_both, axis=1),
            jnp.concatenate(basis_hi, axis=1),
            TRANSPOSED,
            preferred_element_type=F32,
        )
        low = low + lax.dot_general(
            jnp.concatenate(res_hi, axis=1),
            jnp.concatenate(basis_lo, axis=1),
            TRANSPOSED,
            preferred_element_type=F32,
        )
        return both, low

    carry = (jnp.zeros((2 * loads, slots), F32), jnp.zeros((loads, slots), F32))
    for comp in range(sz.comps):
        for copy in copies[comp]:
            copy.wait()
        for index in range(comp * sz.cells // 2, (comp + 1) * sz.cells // 2):
            carry = step(index, carry)
    both, low = carry
    pieces = both[:loads] + both[loads:] + low
    slot = lax.broadcasted_iota(jnp.int32, pieces.shape, 1)
    wide[...] = jnp.zeros_like(wide)
    wide[:, pl.ds(0, slots)] = jnp.where(slot < count[0], pieces, 0.0)
    half = loads // 2
    lane = lane_ids(half)
    packed = jnp.where(lane < 64, wide[:half, :], roll_lanes(wide[half:, :], 64))
    packed = jnp.where(lane == slots, count[0].astype(F32), packed)
    packed = jnp.where(lane == slots + 1, rank[0].astype(F32), packed)
    message[...] = packed.astype(BF16)


def pack_y(sz, res, ids, packed, *refs):
    xhalo, refs = take_halos(refs, "gx")
    message = refs[0]
    ysend, (side_low, side_high) = take_halos(refs[1:], "gy")
    for device in range(message.shape[0]):
        message[device] = packed[...]
    last = sz.cy - 1
    for comp in range(sz.comps):
        for x in range(sz.bx):
            rows = pl.ds((comp * sz.bx + x) * sz.loads, sz.loads)
            if 0 < x < sz.bx - 1:
                low, high = (own_rows(sz, res, comp, (x - 1) * sz.cy + y) for y in (0, last))
            else:
                side = xhalo.below if x == 0 else xhalo.above
                low, high = (
                    side(pl.ds((comp * sz.cy + y) * sz.loads, sz.loads)) for y in (0, last)
                )
            ysend.send(rows, low, high)
    ids_below = xhalo.below(pl.ds(sz.face_x, 2 * sz.cy))
    ids_above = xhalo.above(pl.ds(sz.face_x, 2 * sz.cy))
    for x in range(sz.cx + 4):
        if x < 2:
            rows = ids_below[x * sz.cy : (x + 1) * sz.cy]
        elif x >= sz.cx + 2:
            rows = ids_above[(x - sz.cx - 2) * sz.cy : (x - sz.cx - 1) * sz.cy]
        else:
            rows = (ids[pl.ds((x - 2) * sz.cy, sz.cy), :] + 1).astype(F32)
        side_low[pl.ds(2 * x, 2), :] = rows[:2]
        side_high[pl.ds(2 * x, 2), :] = rows[sz.cy - 2 :]
    ysend.send(pl.ds(sz.face_y, HALO_IDS), side_low[...], side_high[...])


def box_tile(sz, res, xhalo, yhalo, comp, x, y):
    if y == 0 or y == sz.by - 1:
        side = yhalo.below if y == 0 else yhalo.above
        return side(pl.ds((comp * sz.bx + x) * sz.loads, sz.loads))
    if x == 0 or x == sz.bx - 1:
        side = xhalo.below if x == 0 else xhalo.above
        return side(pl.ds((comp * sz.cy + y - 1) * sz.loads, sz.loads))
    return own_rows(sz, res, comp, (x - 1) * sz.cy + y - 1)


def pack_z(sz, res, ids, *refs):
    xhalo, yhalo, (out, id_box, star, outer) = take_halos(refs, "gx", "gy")
    pitch = sz.pitch
    id_box[...] = jnp.zeros_like(id_box)
    two = 2 * sz.cy
    ids_below = xhalo.below(pl.ds(sz.face_x, two))
    ids_above = xhalo.above(pl.ds(sz.face_x, two))
    ids_low = yhalo.below(pl.ds(sz.face_y, HALO_IDS))
    ids_high = yhalo.above(pl.ds(sz.face_y, HALO_IDS))
    for x in range(sz.cx + 4):
        if x < 2:
            rows = ids_below[x * sz.cy : (x + 1) * sz.cy]
        elif x >= sz.cx + 2:
            rows = ids_above[(x - sz.cx - 2) * sz.cy : (x - sz.cx - 1) * sz.cy]
        else:
            rows = (ids[pl.ds((x - 2) * sz.cy, sz.cy), :] + 1).astype(F32)
        id_box[pl.ds(x * pitch + 2, sz.cy), :] = rows
        id_box[pl.ds(x * pitch, 2), :] = ids_low[2 * x : 2 * x + 2]
        id_box[pl.ds(x * pitch + sz.cy + 2, 2), :] = ids_high[2 * x : 2 * x + 2]
    values = id_box[...]
    lane = lane_ids(values.shape[0])
    outer[...] = jnp.where(lane == LANES - 1, roll_lanes(values, 1), roll_lanes(values, -1))
    star[...] = jnp.zeros_like(star)
    lane8 = lane_ids(8)
    taken = jnp.zeros((8, LANES), F32)
    for x in range(sz.bx):
        for y in range(sz.by):
            place = x * sz.by + y
            row = (x + 1) * pitch + y + 1
            for j, shift in enumerate((0, -pitch, pitch, -1, 1)):
                star[pl.ds(place * 8 + j, 1), :] = id_box[pl.ds(row + shift, 1), :]
            star[pl.ds(place * 8 + 5, 1), :] = outer[pl.ds(row, 1), :]
    for place in range(sz.box):
        picked = roll_lanes(star[pl.ds(place * 8, 8), :], 2 * place + 1)
        taken = jnp.where((lane8 >> 1) == place, picked, taken)
    out[pl.ds(sz.face_z, HALO_IDS), :] = jnp.concatenate(
        [taken, jnp.zeros((HALO_IDS - 8, LANES), F32)], axis=0
    ).astype(BF16)
    lane_k = lane_ids(sz.loads)
    for comp in range(sz.comps):
        total = jnp.zeros((sz.loads, LANES), F32)
        for x in range(sz.bx):
            for y in range(sz.by):
                place = x * sz.by + y
                tile = box_tile(sz, res, xhalo, yhalo, comp, x, y)
                total = jnp.where(
                    (lane_k >> 1) == place, roll_lanes(tile, 2 * place + 1), total
                )
        out[pl.ds(comp * sz.loads, sz.loads), :] = total.astype(BF16)


def place_pieces(
    sz, gathered, inverse, after, message, starts_out, vector, wide, heads, starts, sem
):
    del after
    devices = gathered.shape[0]
    for device in range(devices):
        heads[pl.ds(device, 1), :] = gathered[device].astype(F32)[0:1]
    values = heads[...]
    ranks = jnp.transpose(values)[sz.slots + 1 : sz.slots + 2, :]
    earlier = values[:, sz.slots + 1 : sz.slots + 2] < ranks
    total = jnp.sum(jnp.where(earlier, values[:, sz.slots : sz.slots + 1], 0.0), axis=0, keepdims=True)
    starts_out[...] = jnp.zeros_like(starts_out)
    starts_out[:, pl.ds(0, devices)] = jnp.broadcast_to(total.astype(jnp.int32), (8, devices))
    copy = pltpu.make_async_copy(starts_out, starts, sem)
    copy.start()
    half = sz.loads // 2
    lane = lane_ids(half)
    vector[...] = jnp.zeros_like(vector)
    copy.wait()

    def place(device, carry):
        start = starts[0, device]
        block = start // LANES
        offset = start - block * LANES
        packed = gathered[device].astype(F32)
        low = jnp.where(lane < sz.slots, packed, 0.0)
        high = jnp.where((lane >= 64) & (lane < 64 + sz.slots), packed, 0.0)
        both = jnp.concatenate(
            [
                pltpu.roll(low, offset, axis=1),
                pltpu.roll(high, lax.rem(offset + 64, LANES), axis=1),
            ],
            axis=0,
        )
        wide_lane = lane_ids(sz.loads)
        vector[block] = vector[block] + jnp.where(wide_lane >= offset, both, 0.0)
        vector[block + 1] = vector[block + 1] + jnp.where(wide_lane < offset, both, 0.0)
        return carry

    lax.fori_loop(0, gathered.shape[0], place, 0, unroll=32)
    total = jnp.zeros((sz.loads, sz.block_rows), F32)
    for block in range(sz.total_rows // LANES):
        total = total + lax.dot_general(
            vector[block].astype(BF16),
            inverse[:, pl.ds(block * LANES, LANES)],
            TRANSPOSED,
            preferred_element_type=F32,
        )
    if sz.block_rows == 64:
        wide[...] = jnp.zeros_like(wide)
        wide[:, pl.ds(0, 64)] = total
        packed = jnp.where(lane < 64, wide[:half, :], roll_lanes(wide[half:, :], 64))
        for device in range(message.shape[0]):
            message[device, 0] = packed
    else:
        for device in range(message.shape[0]):
            for block in range(sz.block_rows // LANES):
                message[device, block] = total[:, block * LANES : (block + 1) * LANES]


def own_coefs(sz, coefs, start):
    if sz.block_rows == 64:
        half = sz.loads // 2
        block = start // 64
        offset = start - block * 64
        first = coefs[block]
        second = coefs[jnp.minimum(block + 1, coefs.shape[0] - 1)]
        lane = lane_ids(half)
        top = jnp.where(lane < 64, first, roll_lanes(second, 64))
        bottom = jnp.where(lane < 64, roll_lanes(first, 64), second)
        both = jnp.concatenate([top, bottom], axis=0)
    else:
        block = start // LANES
        offset = start - block * LANES
        first = coefs[block]
        second = coefs[jnp.minimum(block + 1, coefs.shape[0] - 1)]
        both = jnp.where(lane_ids(sz.loads) >= offset, first, second)
    return pltpu.roll(both, lax.rem(LANES - offset, LANES), axis=1)


def look_up(table, row, ids):
    result = jnp.zeros_like(ids)
    for material in range(table.shape[1]):
        result = jnp.where(ids == material + 1, table[row, material], result)
    return result


DINV, KEEP, DLAM, WXM, WXP, WYM, WYP, WZM, WZP = range(9)


def spread_row(ref, index, row):
    return ref[index, pl.ds(row, 8, stride=0), :]


def make_coefs(sz, table, id_box, halo_ids, coefs, halo_coefs, own, mu_box, halo_mu):
    pitch = sz.pitch
    mu_box[...] = look_up(table, 0, id_box[...])
    lam_box = look_up(table, 1, id_box[...])
    mu_halo = look_up(table, 0, halo_ids)
    lam_halo = look_up(table, 1, halo_ids)
    lane8 = lane_ids(8)
    center = jnp.broadcast_to(mu_halo[0:1], (8, LANES))
    inner = jnp.zeros((8, LANES), F32)
    for place in range(sz.box):
        row = (place // sz.by + 1) * pitch + place % sz.by + 1
        halo_mu[pl.ds(row, 1), :] = roll_lanes(center, -2 * place)[0:1]
        spread = jnp.broadcast_to(mu_box[pl.ds(row, 1), :], (8, LANES))
        here = (((lane8 + 1) >> 1) & 63) == place
        inner = jnp.where(here, roll_lanes(spread, 2 * place), inner)
    rows_id = lax.broadcasted_iota(jnp.int32, (pitch, LANES), 0)
    lane = lane_ids(pitch)
    for x in range(1, sz.bx + 1):
        mu = mu_box[pl.ds(x * pitch, pitch), :]
        edge = halo_mu[pl.ds(x * pitch, pitch), :]
        lam = lam_box[x * pitch : (x + 1) * pitch]
        faces = [
            0.5 * (mu + mu_box[pl.ds((x - 1) * pitch, pitch), :]),
            0.5 * (mu + mu_box[pl.ds((x + 1) * pitch, pitch), :]),
            0.5 * (mu + mu_box[pl.ds(x * pitch - 1, pitch), :]),
            0.5 * (mu + mu_box[pl.ds(x * pitch + 1, pitch), :]),
            0.5 * (mu + jnp.where(lane == 0, edge, roll_lanes(mu, 1))),
            0.5 * (mu + jnp.where(lane == LANES - 1, edge, roll_lanes(mu, -1))),
        ]
        diag = 1.0 + sum(faces)
        dinv = DAMPING / (diag + lam)
        rows = pl.ds(x * pitch, pitch)
        coefs[DINV, rows, :] = dinv
        coefs[KEEP, rows, :] = (1.0 - DAMPING) + dinv * lam
        coefs[DLAM, rows, :] = dinv * lam
        weights = [dinv * face for face in faces]
        if x == 1:
            weights[0] = jnp.zeros_like(dinv)
        if x == sz.bx:
            weights[1] = jnp.zeros_like(dinv)
        weights[2] = jnp.where(rows_id == 1, 0.0, weights[2])
        weights[3] = jnp.where(rows_id == sz.by, 0.0, weights[3])
        for j in range(6):
            coefs[WXM + j, rows, :] = weights[j]
        if 2 <= x <= sz.cx + 1:
            target = pl.ds((x - 2) * sz.cy, sz.cy)
            for j, value in enumerate([diag, lam] + faces):
                own[j, target, :] = value[2 : 2 + sz.cy]
    place = ((lane8 + 1) >> 1) & 63
    column = jnp.zeros_like(place)
    for x in range(1, sz.bx):
        column = column + (place >= x * sz.by).astype(jnp.int32)
    y_place = place - column * sz.by
    others = [jnp.broadcast_to(mu_halo[j : j + 1], (8, LANES)) for j in range(1, 6)]
    faces = [0.5 * (center + other) for other in others] + [0.5 * (center + inner)]
    lam = jnp.broadcast_to(lam_halo[0:1], (8, LANES))
    dinv = DAMPING / (1.0 + lam + sum(faces))
    live = place < sz.box
    keep = [
        live & (column > 0),
        live & (column < sz.bx - 1),
        live & (y_place > 0),
        live & (y_place < sz.by - 1),
        None,
        live,
    ]
    halo_coefs[DINV] = dinv
    halo_coefs[KEEP] = (1.0 - DAMPING) + dinv * lam
    halo_coefs[DLAM] = dinv * lam
    for j, target in ((0, WXM), (1, WXP), (2, WYM), (3, WYP), (5, WZM)):
        halo_coefs[target] = jnp.where(keep[j], dinv * faces[j], 0.0)


def neighbour_matrix(copies):
    width = 2 * LANES
    parts = []
    for copy in range(copies + 1):
        row = lax.broadcasted_iota(jnp.int32, (LANES, width), 0)
        lane = lax.broadcasted_iota(jnp.int32, (LANES, width), 1)
        even = (row & 1) == 0
        if copy < copies:
            hit = ((lane < LANES) & (row == lane - 1)) | (
                (lane >= LANES) & (row == lane - LANES + 1)
            )
        else:
            hit = ((lane == 0) & even) | ((lane == width - 1) & jnp.logical_not(even))
        parts.append(jnp.where(hit, 1.0, 0.0).astype(BF16))
    return jnp.concatenate(parts, axis=0)


def z_halo(zhalo, rows):
    down, up = zhalo.below(rows), zhalo.above(rows)
    even = (lane_ids(down.shape[0]) & 1) == 0
    return jnp.where(even, down, roll_lanes(up, -2))


def solve_and_direct(sz, count, table, starts_in, res, id_box, coarse, split, *refs):
    xhalo, yhalo, zhalo, refs = take_halos(refs, "gx", "gy", "col")
    direction, own, zface = refs[:3]
    xsend, ysend, refs = take_halos(refs[3:], "gx", "gy")
    first, second, third, halos, inner, coefs, halo_coefs, mu_box, halo_mu, left, zedge = refs[:11]
    wide, own_rows_coef, weights, both_lhs, both_near, starts, sem = refs[11:]
    copy = pltpu.make_async_copy(starts_in, starts, sem)
    copy.start()
    loads, comps = sz.loads, sz.comps
    groups = loads // 8
    lane8 = lane_ids(8)

    halo_mu[...] = jnp.zeros_like(halo_mu)
    inner[...] = jnp.zeros_like(inner)
    make_coefs(
        sz, table, id_box, z_halo(zhalo, pl.ds(sz.face_z, HALO_IDS))[:8], coefs, halo_coefs, own_rows_coef,
        mu_box, halo_mu,
    )

    weights[...] = neighbour_matrix(1)

    def spread(place, carry):
        x = place // sz.by
        row = (x + 1) * sz.pitch + place - x * sz.by + 1
        for j in range(9):
            wide[j, place] = jnp.broadcast_to(coefs[j, pl.ds(row, 1), :], (8, LANES))
        return carry

    lax.fori_loop(0, sz.box, spread, 0, unroll=4)

    def spread_own(cell, carry):
        for j in range(8):
            own[j, cell] = jnp.broadcast_to(own_rows_coef[j, pl.ds(cell, 1), :], (8, LANES))
        return carry

    lax.fori_loop(0, sz.cells, spread_own, 0, unroll=4)

    for comp in range(comps):
        halo = z_halo(zhalo, pl.ds(comp * loads, loads))
        dinv = jnp.concatenate([halo_coefs[DINV]] * groups, axis=0)
        halos[0, comp] = dinv * halo
        for x in range(sz.bx):
            for y in range(sz.by):
                place = x * sz.by + y
                tile = box_tile(sz, res, xhalo, yhalo, comp, x, y)
                first[comp, place] = tile * jnp.concatenate([wide[DINV, place]] * groups, axis=0)

    lane_k = lane_ids(loads)

    def relax(source, level, x, ys, put, buffer):
        count = len(ys)
        lhs, near = both_lhs.at[buffer], both_near.at[buffer]
        for j, y in enumerate(ys):
            place = x * sz.by + y
            here = (((lane_k + 1) >> 1) & 63) == place
            for comp in range(comps):
                rows = pl.ds((j * comps + comp) * loads, loads)
                lhs[rows, pl.ds(0, LANES)] = source[comp, place].astype(BF16)
                lhs[rows, pl.ds(LANES, LANES)] = jnp.where(here, halos[level, comp], 0.0).astype(BF16)
        size = count * comps * loads
        near[pl.ds(0, size), :] = jnp.dot(
            lhs[pl.ds(0, size), :], weights[...], preferred_element_type=F32
        )
        for j, y in enumerate(ys):
            place = x * sz.by + y
            coef = [wide[i, place] for i in range(9)]
            here = (((lane8 + 1) >> 1) & 63) == place
            sides = [
                (WXM, place - sz.by, x > 0),
                (WXP, place + sz.by, x < sz.bx - 1),
                (WYM, place - 1, y > 0),
                (WYP, place + 1, y < sz.by - 1),
            ]
            for group in range(groups):
                rows = pl.ds(group * 8, 8)
                center = [source[comp, place, rows, :] for comp in range(comps)]
                coupled = coef[DLAM] * (center[0] + center[1] + center[2])
                for comp in range(comps):
                    value = center[comp]
                    at = pl.ds((j * comps + comp) * loads + group * 8, 8)
                    out = (first[comp, place, rows, :] - coupled) + coef[KEEP] * value
                    for weight, other, inside in sides:
                        if inside:
                            out = out + coef[weight] * source[comp, other, rows, :]
                    out = out + coef[WZM] * near[at, pl.ds(0, LANES)]
                    out = out + coef[WZP] * near[at, pl.ds(LANES, LANES)]
                    put(j, place, comp, group, out)
                    if level < 2:
                        pltpu.store(
                            inner.at[level, comp, rows, :],
                            roll_lanes(value, 2 * place),
                            mask=here,
                        )

    def sweep(source, target, level):
        def put(j, place, comp, group, out):
            target[comp, place, pl.ds(group * 8, 8), :] = out

        for x in range(sz.bx):
            relax(source, level, x, range(sz.by), put, x % 2)
        coef = [halo_coefs[j] for j in range(8)]
        for group in range(groups):
            rows = pl.ds(group * 8, 8)
            center = [halos[level, comp, rows, :] for comp in range(comps)]
            coupled = coef[DLAM] * (center[0] + center[1] + center[2])
            for comp in range(comps):
                value = center[comp]
                out = (halos[0, comp, rows, :] - coupled) + coef[KEEP] * value
                out = out + coef[WXM] * roll_lanes(value, 2 * sz.by)
                out = out + coef[WXP] * roll_lanes(value, -2 * sz.by)
                out = out + coef[WYM] * roll_lanes(value, 2)
                out = out + coef[WYP] * roll_lanes(value, -2)
                out = out + coef[WZM] * inner[level, comp, rows, :]
                halos[level + 1, comp, rows, :] = out

    sweep(first, second, 0)
    sweep(second, third, 1)

    copy.wait()
    mine = own_coefs(sz, coarse, starts[0, own_index()])
    mine = jnp.where(lane_ids(loads) < jnp.minimum(count[0], sz.slots), mine, 0.0)
    left[...] = paired_left(mine, sz.slots, left)
    zedge[...] = jnp.zeros_like(zedge)

    def finish_plane(x, buffer):
        lhs, near = both_lhs.at[buffer], both_near.at[buffer]

        def put(j, place, comp, group, out):
            direction[comp, x * sz.cy + j, pl.ds(group * 8, 8), :] = out

        relax(third, 2, x + 1, range(1, sz.cy + 1), put, buffer)
        for y in range(sz.cy):
            cell = x * sz.cy + y
            for comp in range(comps):
                part = jnp.dot(
                    left[:, : 2 * sz.slots],
                    split[comp * sz.cells + cell],
                    preferred_element_type=F32,
                )
                value = direction[comp, cell] + (part[:loads] + part[loads:])
                direction[comp, cell] = value
                lhs[pl.ds((y * comps + comp) * loads, loads), pl.ds(0, LANES)] = value.astype(BF16)
        size = sz.cy * comps * loads
        near[pl.ds(0, size), pl.ds(0, LANES)] = jnp.dot(
            lhs[pl.ds(0, size), pl.ds(0, LANES)], edges, preferred_element_type=F32
        )
        for y in range(sz.cy):
            place = (x + 1) * sz.by + y + 1
            for comp in range(comps):
                pltpu.store(
                    zedge.at[pl.ds(comp * loads, loads), :],
                    near[pl.ds((y * comps + comp) * loads, loads), pl.ds(0, LANES)],
                    mask=(lane_k >> 1) == place,
                )

    edge_row = lax.broadcasted_iota(jnp.int32, (LANES, LANES), 0)
    even_lane = (lane_ids(LANES) & 1) == 0
    edges = jnp.where(jnp.where(even_lane, LANES - 1, 0) == edge_row, 1.0, 0.0).astype(BF16)
    for x in range(sz.cx):
        finish_plane(x, x % 2)
    zface[...] = zedge[...].astype(BF16)
    for comp in range(comps):
        for y in range(sz.cy):
            rows = pl.ds((comp * sz.cy + y) * loads, loads)
            xsend.send(rows, direction[comp, y], direction[comp, (sz.cx - 1) * sz.cy + y])
        for x in range(sz.cx):
            rows = pl.ds((comp * sz.cx + x) * loads, loads)
            ysend.send(rows, direction[comp, x * sz.cy], direction[comp, (x + 1) * sz.cy - 1])


def make_image(sz, res, own, direction, *refs):
    xhalo, yhalo, zhalo, refs = take_halos(refs, "gx", "gy", "col")
    dir_split, image_split, message, halo, weights, both_lhs, both_near = refs
    weights[...] = neighbour_matrix(2)
    loads, comps = sz.loads, sz.comps
    groups = loads // 8
    for comp in range(comps):
        halo[comp] = z_halo(zhalo, pl.ds(comp * loads, loads))
    lane_k = lane_ids(loads)
    total = jnp.zeros((2 * loads, 4 * loads), F32)

    def field_at(comp, x, y):
        if x < 0 or x == sz.cx:
            side = xhalo.below if x < 0 else xhalo.above
            return side(pl.ds((comp * sz.cy + y) * loads, loads))
        if y < 0 or y == sz.cy:
            side = yhalo.below if y < 0 else yhalo.above
            return side(pl.ds((comp * sz.cx + x) * loads, loads))
        return direction[comp, x * sz.cy + y]

    for x in range(sz.cx):
        lhs, near = both_lhs.at[x % 2], both_near.at[x % 2]
        for y in range(sz.cy):
            cell = x * sz.cy + y
            here = (((lane_k + 1) >> 1) & 63) == (x + 1) * sz.by + y + 1
            for comp in range(comps):
                hi, lo = split_hi_lo(direction[comp, cell])
                dir_split[comp * sz.cells + cell] = jnp.concatenate([hi, lo], axis=0)
                rows = pl.ds((y * comps + comp) * loads, loads)
                lhs[rows, pl.ds(0, LANES)] = hi
                lhs[rows, pl.ds(LANES, LANES)] = lo
                lhs[rows, pl.ds(2 * LANES, LANES)] = jnp.where(here, halo[comp], 0.0).astype(BF16)
        near[...] = jnp.dot(lhs[...], weights[...], preferred_element_type=F32)
        sides = {}
        for y in range(sz.cy):
            cell = x * sz.cy + y
            coef = [jnp.concatenate([own[j, cell]] * groups, axis=0) for j in range(8)]
            center = [field_at(comp, x, y) for comp in range(comps)]
            coupled = coef[1] * (center[0] + center[1] + center[2])
            for comp in range(comps):
                tile = comp * sz.cells + cell
                line = pl.ds((y * comps + comp) * loads, loads)
                out = coef[0] * center[comp] + coupled
                out = out - coef[2] * field_at(comp, x - 1, y)
                out = out - coef[3] * field_at(comp, x + 1, y)
                out = out - coef[4] * field_at(comp, x, y - 1)
                out = out - coef[5] * field_at(comp, x, y + 1)
                out = out - coef[6] * near[line, pl.ds(0, LANES)]
                out = out - coef[7] * near[line, pl.ds(LANES, LANES)]
                both = jnp.concatenate(split_hi_lo(out), axis=0)
                image_split[tile] = both
                right = jnp.concatenate((both,) + split_hi_lo(own_rows(sz, res, comp, cell)), axis=0)
                sides[y, comp] = (dir_split[tile], right)
            if y % 2 == 1:
                for comp in range(comps):
                    pair = zip(sides[y - 1, comp], sides[y, comp])
                    left, right = (jnp.concatenate(items, axis=1) for items in pair)
                    total = total + lax.dot_general(
                        left, right, TRANSPOSED, preferred_element_type=F32
                    )
    high, low = total[:loads], total[loads:]
    sums = high + roll_lanes(high, -loads) + low
    half = loads // 2
    lane = lane_ids(half)
    packed = jnp.where((lane & (2 * loads - 1)) < loads, sums[:half], roll_lanes(sums[half:], loads))
    message[...] = packed


def share_sums(sz, mine, *refs):
    message = refs[-1]
    total = mine[...]
    for other in refs[:-1]:
        total = total + other[...]
    for device in range(message.shape[0]):
        message[device] = total


def finish(
    sz, sums, iterate, res, dir_split, image_split, iterate_out, residual_out, parts, new_iterate,
    new_residual, sem,
):
    loads = sz.loads
    total = sums[0]
    for device in range(1, sums.shape[0]):
        total = total + sums[device]
    system = jnp.concatenate([total, roll_lanes(total, -loads)], axis=0)
    lane = lane_ids(loads)
    system = jnp.where((lane & (2 * loads - 1)) < loads, system, 0.0)
    row_ids = lax.broadcasted_iota(jnp.int32, (loads, LANES), 0)
    for base in range(0, loads, 8):
        columns = [
            jnp.broadcast_to(system[:, i : i + 1], (loads, LANES)) for i in range(base, base + 8)
        ]
        for j in range(8):
            i = base + j
            here = row_ids == i
            scale = 1.0 / columns[j][i : i + 1, :]
            row = system[i : i + 1, :] * scale
            system = jnp.where(here, row, system - columns[j] * row)
            for other in range(j + 1, 8):
                entry = columns[other][i : i + 1, :] * scale
                columns[other] = jnp.where(here, entry, columns[other] - columns[j] * entry)
    step = jnp.transpose(system)[2 * loads : 3 * loads, :]
    padded = jnp.concatenate([step, jnp.zeros((loads, LANES - loads), F32)], axis=1) if (
        step.shape[1] < LANES
    ) else step
    left = paired_left(padded, loads, parts)[:, : 2 * loads]

    writes = []
    for comp in range(sz.comps):
        for cell in range(sz.cells):
            tile = comp * sz.cells + cell
            right = jnp.concatenate([dir_split[tile], image_split[tile]], axis=1)
            part = jnp.dot(left, right, preferred_element_type=F32)
            part = part[:loads] + part[loads:]
            rows = pl.ds(comp * loads * sz.cells + cell, loads, stride=sz.cells)
            new_iterate[rows, :] = iterate[rows, :] + part[:, :LANES]
            new_residual[rows, :] = res[rows, :] - part[:, LANES:]
        done = pl.ds(comp * loads * sz.cells, loads * sz.cells)
        for j, (source, out) in enumerate(
            ((new_iterate, iterate_out), (new_residual, residual_out))
        ):
            writes.append(pltpu.make_async_copy(source.at[done], out.at[done], sem.at[j, comp]))
            writes[-1].start()
    for copy in writes:
        copy.wait()


def body(
    iterate, residual, cell_ids, materials, eigen_counts, coarse_rank, eigen_basis, coarse_inverse
):
    sz = Sizes(residual, eigen_basis, coarse_inverse)
    shape = jax.ShapeDtypeStruct
    devices = 1
    for axis in AXES:
        devices = devices * lax.axis_size(axis)
    blocks = sz.total_rows // sz.block_rows
    smem, vmem, scratch, dma = pltpu.SMEM, pltpu.VMEM, pltpu.VMEM, pltpu.SemaphoreType.DMA
    res = residual.reshape(-1, LANES)
    old = iterate.reshape(-1, LANES)
    ids = cell_ids.reshape(-1, LANES)

    def call(name, kernel, *args, **kwargs):
        return vmem_call(name, lambda *refs: kernel(sz, *refs), *args, **kwargs)

    face = shape((sz.face_x + 2 * sz.cy, LANES), BF16)
    faces = call(
        "pack_x",
        pack_x,
        [face] * swaps("gx"),
        [scratch((sz.comps * sz.loads, sz.cy, LANES), F32)] * 2
        + [scratch((sz.cells, LANES), jnp.int32), dma((3,))],
        8,
        1 << 20,
        2 << 20,
        [residual.reshape(-1, sz.cells, LANES), ids],
        spaces=[pl.ANY, pl.ANY],
    )
    xhalo = exchange(faces, "gx")

    packed, split = call(
        "pieces",
        make_pieces,
        [
            shape((sz.loads // 2, LANES), BF16),
            shape((sz.tiles, 2 * sz.slots, LANES), BF16),
        ],
        [
            scratch((sz.loads, LANES), F32),
            scratch((sz.slots, sz.tiles, LANES), F32),
            scratch((sz.comps, sz.loads * sz.cells, LANES), F32),
            dma((2, sz.comps)),
        ],
        12,
        1 << 27,
        7 << 20,
        [
            eigen_counts,
            coarse_rank,
            eigen_basis.reshape(sz.slots, sz.tiles, LANES),
            residual.reshape(sz.comps, -1, LANES),
            faces[0],
        ],
        spaces=[smem, smem, pl.ANY, pl.ANY, pl.ANY],
    )

    yface = shape((sz.face_y + HALO_IDS, LANES), BF16)
    message, *faces = call(
        "pack_y",
        pack_y,
        [shape((devices,) + packed.shape, BF16)] + [yface] * swaps("gy"),
        [scratch((HALO_IDS, LANES), F32)] * 2,
        8,
        1 << 20,
        2 << 20,
        [res, ids, packed] + xhalo,
    )
    yhalo = exchange(faces, "gy")
    gathered = lax.all_to_all(message, AXES, 0, 0, tiled=True)
    rows = (sz.cx + 4) * sz.pitch
    zmessage, id_box = call(
        "pack_z",
        pack_z,
        [shape((sz.face_z + HALO_IDS, LANES), BF16), shape((rows, LANES), F32)],
        [scratch((sz.box * 8, LANES), F32), scratch((rows, LANES), F32)],
        8,
        1 << 22,
        3 << 20,
        [res, ids] + xhalo + yhalo,
    )
    zhalo = exchange([zmessage] * 2, "col")

    tile = (1, sz.loads // 2, LANES)
    if sz.block_rows != 64:
        tile = (sz.block_rows // LANES, sz.loads, LANES)
    wide = (8, max(LANES, devices))
    partial, starts = call(
        "coarse",
        place_pieces,
        [shape((blocks,) + tile, F32), shape(wide, jnp.int32)],
        [
            scratch((sz.total_rows // LANES + 1, sz.loads, LANES), F32),
            scratch((sz.loads, LANES), F32),
            scratch((devices, LANES), F32),
            smem(wide, jnp.int32),
            dma,
        ],
        12,
        1 << 23,
        1 << 20,
        [gathered, coarse_inverse, zmessage],
        spaces=[vmem, vmem, pl.ANY],
    )
    coarse = lax.all_to_all(partial, ("gx", "col"), 0, 0, tiled=True)
    coarse = coarse.reshape((-1,) + tile[1:])

    field = scratch((sz.comps, sz.box, sz.loads, LANES), F32)
    direction, own, zface, *faces = call(
        "solve",
        solve_and_direct,
        [
            shape((sz.comps, sz.cells, sz.loads, LANES), F32),
            shape((8, sz.cells, 8, LANES), F32),
            shape((sz.face_z, LANES), BF16),
        ]
        + [shape((sz.face_x, LANES), BF16)] * swaps("gx")
        + [shape((sz.inner_y, LANES), BF16)] * swaps("gy"),
        [
            field,
            field,
            field,
            scratch((3, sz.comps, sz.loads, LANES), F32),
            scratch((2, sz.comps, sz.loads, LANES), F32),
            scratch((9, rows, LANES), F32),
            scratch((9, 8, LANES), F32),
            scratch((rows, LANES), F32),
            scratch((rows, LANES), F32),
            scratch((2 * sz.loads, LANES), BF16),
            scratch((sz.face_z, LANES), F32),
            scratch((9, sz.box, 8, LANES), F32),
            scratch((8, sz.cells, LANES), F32),
            scratch((2 * LANES, 2 * LANES), BF16),
            scratch((2, sz.by * sz.comps * sz.loads, 2 * LANES), BF16),
            scratch((2, sz.by * sz.comps * sz.loads, 2 * LANES), F32),
            smem(starts.shape, jnp.int32),
            dma,
        ],
        28,
        1 << 28,
        8 << 20,
        [eigen_counts, materials, starts, res, id_box, coarse, split] + xhalo + yhalo + zhalo,
        spaces=[smem, smem, pl.ANY] + [vmem] * (4 + len(xhalo + yhalo + zhalo)),
    )
    xhalo = exchange(faces[: swaps("gx")], "gx")
    yhalo = exchange(faces[swaps("gx") :], "gy")
    zhalo = exchange([zface] * 2, "col")
    sums_shape = (sz.loads // 2, LANES)
    dir_split, image_split, sums = call(
        "image",
        make_image,
        [
            shape((sz.tiles, 2 * sz.loads, LANES), BF16),
            shape((sz.tiles, 2 * sz.loads, LANES), BF16),
            shape(sums_shape, F32),
        ],
        [
            scratch((sz.comps, sz.loads, LANES), F32),
            scratch((3 * LANES, 2 * LANES), BF16),
            scratch((2, sz.cy * sz.comps * sz.loads, 3 * LANES), BF16),
            scratch((2, sz.cy * sz.comps * sz.loads, 2 * LANES), F32),
        ],
        20,
        1 << 28,
        8 << 20,
        [res, own, direction] + xhalo + yhalo + zhalo,
        spaces=[vmem] * (3 + len(xhalo + yhalo + zhalo)),
    )
    over, operands = AXES, [sums]
    if lax.axis_size("gy") == 2:
        over = ("gx", "col")
        operands += exchange([sums], "gy")
        devices = devices // 2
    spread = call(
        "share_sums", share_sums, shape((devices,) + sums_shape, F32), [], 4, 1 << 12, 1 << 17,
        operands,
    )
    sums = lax.all_to_all(spread, over, 0, 0, tiled=True)
    flat = shape(res.shape, F32)
    new_iterate, new_residual = call(
        "finish",
        finish,
        [flat, flat],
        [
            scratch((2 * sz.loads, LANES), BF16),
            scratch(res.shape, F32),
            scratch(res.shape, F32),
            dma((2, sz.comps)),
        ],
        20,
        1 << 27,
        9 << 20,
        [sums, old, res, dir_split, image_split],
        out_space=pl.ANY,
    )
    return (new_iterate.reshape(iterate.shape), new_residual.reshape(residual.shape))


def solution(mesh):
    placed = (
        P(None, None, "gx", "gy", "col"),
        P(None, None, "gx", "gy", "col"),
        P("gx", "gy", "col"),
        P(),
        P(("gx", "gy", "col")),
        P(("gx", "gy", "col")),
        P(None, None, "gx", "gy", "col"),
        P(("gx", "col"), None),
    )
    return jax.shard_map(
        body,
        mesh=mesh,
        in_specs=placed,
        out_specs=(P(None, None, "gx", "gy", "col"), P(None, None, "gx", "gy", "col")),
        check_vma=False,
    )
```
